128 devices in a mesh: fsdp: 8 (over y, core), ctx: 4 (over z), tp: 4 (over x).
Axes of the slice: x: 4, y: 4, z: 4, core: 2. Of those that a mesh axis runs over, the one named last changes fastest.
Arguments:
- hidden_in: bfloat16 [16384, 768], P(('fsdp', 'ctx', 'tp')), may hold values from -6 to 6
- out_grad: bfloat16 [16384, 768], P(('fsdp', 'ctx', 'tp')), may hold values from -6 to 6
- seq_lengths: int32 [8, 3], P('fsdp'), may hold values from 64 to 1920, as said below
- norm_gains: float32 [2, 2, 768], replicated, may hold values from 0.5 to 1.5
- gain_first: float32 [2, 2, 768], replicated
- gain_second: float32 [2, 2, 768], replicated, as said below
- attend_in: float32 [2, 3, 768, 768], P(None, None, ('fsdp', 'ctx'), 'tp'), may hold values from -0.21875 to 0.21875
- attend_out: float32 [2, 768, 768], P(None, 'tp', ('fsdp', 'ctx')), may hold values from -2.5 to 2.5
- expand: float32 [2, 2, 768, 2048], P(None, None, ('fsdp', 'ctx'), 'tp'), may hold values from -0.21875 to 0.21875
- shrink: float32 [2, 2048, 768], P(None, 'tp', ('fsdp', 'ctx')), may hold values from -0.125 to 0.125
- attend_in_moment: float32 [2, 3, 768, 768], P(None, None, ('fsdp', 'ctx'), 'tp')
- attend_out_moment: float32 [2, 768, 768], P(None, 'tp', ('fsdp', 'ctx'))
- expand_moment: float32 [2, 2, 768, 2048], P(None, None, ('fsdp', 'ctx'), 'tp')
- shrink_moment: float32 [2, 2048, 768], P(None, 'tp', ('fsdp', 'ctx'))
Outputs:
- hidden_out: float32 [16384, 768], P(('fsdp', 'ctx', 'tp'))
- hidden_grad: float32 [16384, 768], P(('fsdp', 'ctx', 'tp'))
- gain_first_new: float32 [2, 2, 768], replicated
- gain_second_new: float32 [2, 2, 768], replicated
- norm_gains_new: float32 [2, 2, 768], replicated
- attend_in_moment_new: float32 [2, 3, 768, 768], P(None, None, ('fsdp', 'ctx'), 'tp')
- attend_out_moment_new: float32 [2, 768, 768], P(None, 'tp', ('fsdp', 'ctx'))
- expand_moment_new: float32 [2, 2, 768, 2048], P(None, None, ('fsdp', 'ctx'), 'tp')
- shrink_moment_new: float32 [2, 2048, 768], P(None, 'tp', ('fsdp', 'ctx'))
- attend_in_new: float32 [2, 3, 768, 768], P(None, None, ('fsdp', 'ctx'), 'tp')
- attend_out_new: float32 [2, 768, 768], P(None, 'tp', ('fsdp', 'ctx'))
- expand_new: float32 [2, 2, 768, 2048], P(None, None, ('fsdp', 'ctx'), 'tp')
- shrink_new: float32 [2, 2048, 768], P(None, 'tp', ('fsdp', 'ctx'))
The draws below stay inside these ranges and needn't reach their ends.
Inputs may be any that keep to these rules, and one draw needn't show every extreme that they name: `seq_lengths`: each row sums to 2048; its first and last lengths are at most 512 - max(64, 1). `gain_second`: Positive.
All inputs are finite; a program needn't handle non-finite values.
Results may differ from the reference program's by a relative error of at most 0.04.
Values may be sent and summed in bfloat16 or wider, within the bound.
A program may use at most 192 MiB of HBM per device.

```python
import math
import jax
import jax.numpy as jnp
from jax import lax

D = 768
HEADS = 12
HEAD_DIM = 64
FF = 2048
LAYERS = 2
NS_STEPS = 4
STEP = 5
CTX_TOK = 512
GROUP_TOK = 2048
TOKENS = 16384
N_FSDP = 8


def draw_seq_lengths(key, part):
    key = jax.random.fold_in(key, 11)
    least = max(CTX_TOK // 8, 1)
    edges = jax.random.randint(key, (N_FSDP, 2), least, CTX_TOK - least + 1)
    edges = edges.at[0].set(least)
    first_len = edges[:, 0]
    last_len = edges[:, 1]
    middle_len = GROUP_TOK - first_len - last_len
    return jnp.stack([first_len, middle_len, last_len], axis=1).astype(jnp.int32)


def draw_attend_in_moment(key, part):
    key = jax.random.fold_in(key, 21)
    spread = 0.5 * math.sqrt(TOKENS)
    return spread * jax.random.truncated_normal(key, -4.0, 4.0, (LAYERS, 3, D, D), jnp.float32)


def draw_attend_out_moment(key, part):
    key = jax.random.fold_in(key, 22)
    spread = 0.05 * math.sqrt(TOKENS)
    return spread * jax.random.truncated_normal(key, -4.0, 4.0, (LAYERS, D, D), jnp.float32)


def draw_expand_moment(key, part):
    key = jax.random.fold_in(key, 23)
    spread = 0.4 * math.sqrt(TOKENS)
    return spread * jax.random.truncated_normal(key, -4.0, 4.0, (LAYERS, 2, D, FF), jnp.float32)


def draw_shrink_moment(key, part):
    key = jax.random.fold_in(key, 24)
    spread = 0.5 * math.sqrt(TOKENS)
    return spread * jax.random.truncated_normal(key, -4.0, 4.0, (LAYERS, FF, D), jnp.float32)


def draw_gain_first(key, part):
    key = jax.random.fold_in(key, 31)
    spread = 0.111 * math.sqrt(TOKENS)
    return spread * jax.random.truncated_normal(key, -4.0, 4.0, (LAYERS, 2, D), jnp.float32)


def draw_gain_second(key, part):
    key = jax.random.fold_in(key, 32)
    base_level = 0.05 / 0.95 * TOKENS
    return base_level * jnp.exp(jax.random.uniform(key, (LAYERS, 2, D), jnp.float32, math.log(0.5), math.log(8.0)))


def block_levels(rng, extent, pieces, low, top_value):
    gain, own = 1.0, jax.random.fold_in(rng, 6)
    for dim, shards_of in pieces:
        steps = jnp.exp(jax.random.uniform(jax.random.fold_in(own, dim), (shards_of,), jnp.float32, low / len(pieces), top_value / len(pieces)))
        gain = gain * jnp.repeat(steps, extent[dim] // shards_of).reshape([-1 if axis == dim else 1 for axis in range(len(extent))])
    return gain


def noise(rng, extent, width, limit, pieces=(), held_as=jnp.bfloat16):
    entries = jax.random.normal(rng, extent, jnp.float32) * width
    if len(pieces) > 0:
        entries = block_levels(rng, extent, pieces, -0.22, 0.18) * entries
    return jnp.clip(entries, min=-limit, max=limit).astype(held_as)


def setup_inputs(seed: int = 0) -> dict:
    key_of = jax.random.split(jax.random.key(seed), 15)
    hidden_in = noise(key_of[0], (TOKENS, D), 1.0, 6.0, ((0, 128),))
    out_grad = noise(key_of[1], (TOKENS, D), 1.0, 6.0, ((0, 128),))
    seq_lengths = draw_seq_lengths(jax.random.fold_in(key_of[14], 71), 0)
    norm_gains = jnp.clip(1.0 + 0.1 * jax.random.normal(key_of[3], (LAYERS, 2, D), jnp.float32), 0.5, 1.5)
    gain_first = draw_gain_first(jax.random.fold_in(key_of[14], 71), 0)
    gain_second = draw_gain_second(jax.random.fold_in(key_of[14], 71), 0)
    attend_in = noise(key_of[6], (LAYERS, 3, D, D), D ** -0.5, 0.21875, ((2, 32), (3, 4)), jnp.float32)
    attend_out = noise(key_of[7], (LAYERS, D, D), (max(D // 128, 1)) ** -0.5, 2.5, ((1, 4), (2, 32)), jnp.float32)
    expand = noise(key_of[8], (LAYERS, 2, D, FF), D ** -0.5, 0.21875, ((2, 32), (3, 4)), jnp.float32)
    shrink = noise(key_of[9], (LAYERS, FF, D), FF ** -0.5, 0.125, ((1, 4), (2, 32)), jnp.float32)
    attend_in_moment = draw_attend_in_moment(jax.random.fold_in(key_of[14], 71), 0)
    attend_out_moment = draw_attend_out_moment(jax.random.fold_in(key_of[14], 71), 0)
    expand_moment = draw_expand_moment(jax.random.fold_in(key_of[14], 71), 0)
    shrink_moment = draw_shrink_moment(jax.random.fold_in(key_of[14], 71), 0)
    return {"hidden_in": hidden_in, "out_grad": out_grad, "seq_lengths": seq_lengths, "norm_gains": norm_gains, "gain_first": gain_first, "gain_second": gain_second, "attend_in": attend_in, "attend_out": attend_out, "expand": expand, "shrink": shrink, "attend_in_moment": attend_in_moment, "attend_out_moment": attend_out_moment, "expand_moment": expand_moment, "shrink_moment": shrink_moment}


best_precision = lax.Precision.HIGHEST
norm_eps = 1e-05
rope_base = 10000.0
mask_fill = -1e+30
quintic_one = 3.4445
quintic_two = -4.775
quintic_three = 2.0315
moment_decay = 0.95
matrix_rate = 0.1
project_rate = 0.8
matrix_decay = 0.1
gain_rate = 0.8
first_decay = 0.9
second_decay = 0.95
adam_eps = 1e-08
ortho_eps = 1e-07

@jax.custom_vjp
def low(v):
    return lax.optimization_barrier(v.astype(jnp.bfloat16)).astype(jnp.float32)

@jax.custom_vjp
def low_back(v):
    return v

def low_keep(v):
    return (low(v), None)

def low_pass(kept, grad):
    return (grad,)

def back_keep(v):
    return (v, None)

def back_low(kept, grad):
    return (low(grad),)
low.defvjp(low_keep, low_pass)
low_back.defvjp(back_keep, back_low)

def doc_layout(lengths, row_count):
    doc_ends = jnp.cumsum(lengths).astype(jnp.int32)
    starts = (doc_ends - lengths).astype(jnp.int32)
    places = jnp.arange(row_count, dtype=jnp.int32)
    document = lax.optimization_barrier(jnp.sum((places[:, None] >= doc_ends[None, :]).astype(jnp.int32), axis=1)).astype(jnp.int32)
    member = document[:, None] == jnp.arange(lengths.shape[0], dtype=jnp.int32)[None, :]
    offset = lax.optimization_barrier(jnp.sum(jnp.where(member, starts[None, :], 0), axis=1)).astype(jnp.int32)
    return (document, (places - offset).astype(jnp.int32), places)

def rotate(values, positions):
    half_dim = values.shape[-1] // 2
    frequency = rope_base ** (-jnp.arange(half_dim, dtype=jnp.float32) * 2.0 / values.shape[-1])
    angles = positions.astype(jnp.float32)[:, None] * frequency[None, :]
    cosine = jnp.cos(angles)[:, None, :]
    sine_part = jnp.sin(angles)[:, None, :]
    first_half = values[..., :half_dim]
    second_half = values[..., half_dim:]
    return jnp.concatenate([first_half * cosine - second_half * sine_part, second_half * cosine + first_half * sine_part], axis=-1)

def normalize(row_values, gain_row):
    return row_values * lax.rsqrt(lax.optimization_barrier(jnp.mean(row_values * row_values, axis=-1, keepdims=True)) + norm_eps) * gain_row

def orthogonalize(matrix):
    scaled = matrix / (jnp.sqrt(jnp.sum(matrix * matrix)) + ortho_eps)
    flipped = matrix.shape[0] > matrix.shape[1]
    current = scaled.astype(jnp.bfloat16)
    if flipped:
        current = current.T
    for ns_index in range(NS_STEPS):
        square = jnp.dot(current, current.T, preferred_element_type=jnp.float32).astype(jnp.bfloat16)
        polynomial = (quintic_two * square.astype(jnp.float32) + quintic_three * jnp.dot(square, square, preferred_element_type=jnp.float32)).astype(jnp.bfloat16)
        current = (quintic_one * current.astype(jnp.float32) + jnp.dot(polynomial, current, preferred_element_type=jnp.float32)).astype(jnp.bfloat16)
    if flipped:
        current = current.T
    return current

def attend_block(queries, query_doc, query_place, key_rows, value_rows, key_doc, key_place):
    score_scale = 1.0 / math.sqrt(queries.shape[-1])
    raw_scores = jnp.einsum('qhd,khd->hqk', queries, key_rows, precision=best_precision) * score_scale
    scores = low_back(raw_scores)
    allowed = (query_doc[:, None] == key_doc[None, :]) & (query_place[:, None] >= key_place[None, :])
    masked = jnp.where(allowed[None], scores, mask_fill)
    log_total = jax.nn.logsumexp(masked, axis=-1, keepdims=True)
    probability = low(jnp.exp(masked - log_total))
    return jnp.einsum('hqk,khd->qhd', probability, value_rows, precision=best_precision)

def split_rows(array_in):
    return array_in.reshape((array_in.shape[0] // CTX_TOK, CTX_TOK) + array_in.shape[1:])

def layer_forward(row_values, gain_rows, in_weight, out_weight, expand_weight, shrink_weight, document, position, places):
    row_count = row_values.shape[0]
    normed = low(normalize(row_values, gain_rows[0]))
    projected = low_back(jnp.einsum('rd,kdc->rkc', normed, low(in_weight), precision=best_precision))
    head_shape = (row_count, HEADS, HEAD_DIM)
    queries = low(rotate(projected[:, 0].reshape(head_shape), position))
    key_rows = low(rotate(projected[:, 1].reshape(head_shape), position))
    value_rows = low(projected[:, 2].reshape(head_shape))
    attend = jax.checkpoint(attend_block)
    attended = lax.map(lambda block_items: attend(block_items[0], block_items[1], block_items[2], key_rows, value_rows, document, places), (split_rows(queries), split_rows(document), split_rows(places)))
    attended = low_back(low(attended.reshape(row_count, D)))
    mid_rows = row_values + low_back(jnp.dot(attended, low(out_weight), precision=best_precision))
    normed_mid = low(normalize(mid_rows, gain_rows[1]))
    gate_up = low_back(jnp.einsum('rd,kdf->rkf', normed_mid, low(expand_weight), precision=best_precision))
    active = low(jax.nn.silu(gate_up[:, 0]) * gate_up[:, 1])
    return mid_rows + low_back(jnp.dot(active, low(shrink_weight), precision=best_precision))

def refresh(weight, moment_new, rate_value):
    orthogonal = orthogonalize(moment_new).astype(jnp.float32)
    factor = 0.2 * math.sqrt(max(weight.shape))
    return weight - rate_value * (factor * orthogonal + matrix_decay * weight)

def reference(hidden_in, out_grad, seq_lengths, norm_gains, gain_first, gain_second, attend_in, attend_out, expand, shrink, attend_in_moment, attend_out_moment, expand_moment, shrink_moment):
    params = (norm_gains, attend_in, attend_out, expand, shrink)

    def forward(row_values, weights_all, document, position, places):
        gain_all, in_all, out_all, expand_all, shrink_all = weights_all
        for layer_index in range(LAYERS):
            row_values = layer_forward(row_values, gain_all[layer_index], in_all[layer_index], out_all[layer_index], expand_all[layer_index], shrink_all[layer_index], document, position, places)
        return row_values

    def group_step(totals, group_items):
        row_values, cotangent, lengths = group_items
        document, position, places = doc_layout(lengths, GROUP_TOK)
        result, pullback = jax.vjp(lambda inputs, weights_all: forward(inputs, weights_all, document, position, places), row_values, params)
        row_grad, weight_grad = pullback(cotangent)
        return (jax.tree.map(lambda left_sum, right_sum: left_sum + right_sum, totals, weight_grad), (result, row_grad))
    zero_grads = jax.tree.map(jnp.zeros_like, params)
    group_inputs = (hidden_in.astype(jnp.float32).reshape(N_FSDP, GROUP_TOK, D), out_grad.astype(jnp.float32).reshape(N_FSDP, GROUP_TOK, D), seq_lengths)
    totals, (outputs, row_grads) = lax.scan(group_step, zero_grads, group_inputs)
    gain_grad, in_grad, out_weight_grad, expand_grad, shrink_grad = totals
    gain_first_new = first_decay * gain_first + (1.0 - first_decay) * gain_grad
    gain_second_new = second_decay * gain_second + (1.0 - second_decay) * gain_grad * gain_grad
    norm_gains_new = norm_gains - gain_rate * (gain_first_new / (1.0 - first_decay ** STEP)) / (jnp.sqrt(gain_second_new / (1.0 - second_decay ** STEP)) + adam_eps)
    in_moment_new = moment_decay * attend_in_moment + in_grad
    out_moment_new = moment_decay * attend_out_moment + out_weight_grad
    expand_moment_new = moment_decay * expand_moment + expand_grad
    shrink_moment_new = moment_decay * shrink_moment + shrink_grad
    attend_in_new = jnp.stack([jnp.stack([refresh(attend_in[layer_index, part_index], in_moment_new[layer_index, part_index], matrix_rate) for part_index in range(3)]) for layer_index in range(LAYERS)])
    attend_out_new = jnp.stack([refresh(attend_out[layer_index], out_moment_new[layer_index], project_rate) for layer_index in range(LAYERS)])
    expand_new = jnp.stack([jnp.stack([refresh(expand[layer_index, part_index], expand_moment_new[layer_index, part_index], matrix_rate) for part_index in range(2)]) for layer_index in range(LAYERS)])
    shrink_new = jnp.stack([refresh(shrink[layer_index], shrink_moment_new[layer_index], matrix_rate) for layer_index in range(LAYERS)])
    return (outputs.reshape(TOKENS, D), row_grads.reshape(TOKENS, D), gain_first_new, gain_second_new, norm_gains_new, in_moment_new, out_moment_new, expand_moment_new, shrink_moment_new, attend_in_new, attend_out_new, expand_new, shrink_new)
```

```python
import math

import jax
import jax.numpy as jnp
from jax import lax
from jax.experimental import pallas as pl
from jax.experimental.pallas import tpu as pltpu
from jax.sharding import PartitionSpec as P

D = 768
HEAD_DIM = 64
FF = 2048
NS_STEPS = 4
STEP = 5
KEY_BLOCK = 512


norm_eps = 1e-05
rope_base = 10000.0
mask_fill = -1e30
quintic_one = 3.4445
quintic_two = -4.775
quintic_three = 2.0315
moment_decay = 0.95
matrix_rate = 0.1
project_rate = 0.8
matrix_decay = 0.1
gain_rate = 0.8
first_decay = 0.9
second_decay = 0.95
adam_eps = 1e-08
ortho_eps = 1e-07


def doc_layout(lengths, row_count):
    doc_ends = jnp.cumsum(lengths)
    starts = doc_ends - lengths
    places = jnp.arange(row_count, dtype=jnp.int32)
    document = jnp.sum((places[:, None] >= doc_ends[None, :]).astype(jnp.int32), axis=1)
    member = document[:, None] == jnp.arange(lengths.shape[0], dtype=jnp.int32)[None, :]
    offset = jnp.sum(jnp.where(member, starts[None, :], 0), axis=1)
    return (document, places - offset, places)


def rope_tables(head_dim, positions):
    half_dim = head_dim // 2
    frequency = rope_base ** (-jnp.arange(half_dim, dtype=jnp.float32) * 2.0 / head_dim)
    angles = positions.astype(jnp.float32)[:, None] * frequency[None, :]
    return (jnp.cos(angles)[:, None, :], jnp.sin(angles)[:, None, :])


def rotate(values, positions):
    half_dim = values.shape[-1] // 2
    cosine, sine_part = rope_tables(values.shape[-1], positions)
    first_half = values[..., :half_dim]
    second_half = values[..., half_dim:]
    return jnp.concatenate(
        [
            first_half * cosine - second_half * sine_part,
            second_half * cosine + first_half * sine_part,
        ],
        axis=-1,
    )


def unrotate(gradient, positions):
    half_dim = gradient.shape[-1] // 2
    cosine, sine_part = rope_tables(gradient.shape[-1], positions)
    first_half = gradient[..., :half_dim]
    second_half = gradient[..., half_dim:]
    return jnp.concatenate(
        [
            first_half * cosine + second_half * sine_part,
            second_half * cosine - first_half * sine_part,
        ],
        axis=-1,
    )


def normalize(row_values, gain_row):
    return (
        row_values
        * lax.rsqrt(jnp.mean(row_values * row_values, axis=-1, keepdims=True) + norm_eps)
        * gain_row
    )


MESH_ID = pl.DeviceIdType.MESH
ROW_SHARD = 24
PACK_COLS = 2304
HALF_COLS = PACK_COLS // 2
HALVES = (pl.ds(0, HALF_COLS), pl.ds(HALF_COLS, HALF_COLS))


def whereami():
    fsdp_index = lax.axis_index("fsdp")
    return (lax.div(fsdp_index, 2), lax.rem(fsdp_index, 2), lax.axis_index("ctx"), lax.axis_index("tp"))


def device_at(y, c, z, x):
    return (y * 2 + c, z, x)


def ring(index, offset):
    return lax.rem(index + offset, 4)


def remote(source, target, send_sem, recv_sem, device):
    return pltpu.make_async_remote_copy(
        src_ref=source,
        dst_ref=target,
        send_sem=send_sem,
        recv_sem=recv_sem,
        device_id=device,
        device_id_type=MESH_ID,
    )


def greet(devices):
    barrier = pltpu.get_barrier_semaphore()
    for device in devices:
        pl.semaphore_signal(barrier, inc=1, device_id=device, device_id_type=MESH_ID)
    pl.semaphore_wait(barrier, len(devices))


def gather_kernel(own, full, send, recv, local):
    y, c, z, x = whereami()
    other = 1 - c
    y_peer = [device_at(ring(y, d), c, z, x) for d in (1, 2, 3)]
    z_peer = [device_at(y, c, ring(z, d), x) for d in (1, 2, 3)]
    sibling = device_at(y, other, z, x)
    greet(y_peer + z_peer + [sibling])
    a_cols, b_cols = HALVES
    started = []

    def start(source, target, slot, device):
        copy = remote(source, target, send.at[slot], recv.at[slot], device)
        copy.start()
        started.append(copy)
        return copy

    def arrived(view, slot):
        remote(view, view, send.at[slot], recv.at[slot], sibling).wait_recv()

    mine_a = full.at[y, c, z, :, a_cols]
    mine_b = full.at[y, c, z, :, b_cols]
    for d in range(3):
        start(own.at[:, a_cols], mine_a, d, z_peer[d])
        start(own.at[:, b_cols], mine_b, 3 + d, y_peer[d])
    start(own, full.at[y, c, z], 24, sibling)
    keep = pltpu.make_async_copy(own, full.at[y, c, z], local)
    keep.start()
    keep.wait()
    for d in range(3):
        arrived(full.at[y, c, ring(z, 3 - d), :, a_cols], d)
        arrived(full.at[ring(y, 3 - d), c, z, :, b_cols], 3 + d)
    line_a = full.at[y, c, :, :, a_cols]
    line_b = full.at[:, c, z, :, b_cols]
    for d in range(3):
        start(line_a, line_a, 6 + d, y_peer[d])
        start(line_b, line_b, 9 + d, z_peer[d])
    for d in range(3):
        view = full.at[y, c, ring(z, 3 - d), :, a_cols]
        start(view, view, 12 + d, sibling)
        view = full.at[ring(y, 3 - d), c, z, :, b_cols]
        start(view, view, 15 + d, sibling)
    for d in range(3):
        view = full.at[ring(y, 3 - d), c, :, :, a_cols]
        arrived(view, 6 + d)
        start(view, view, 18 + d, sibling)
        view = full.at[:, c, ring(z, 3 - d), :, b_cols]
        arrived(view, 9 + d)
        start(view, view, 21 + d, sibling)
    arrived(full.at[y, other, z], 24)
    for d in range(3):
        arrived(full.at[y, other, ring(z, 3 - d), :, a_cols], 12 + d)
        arrived(full.at[ring(y, 3 - d), other, z, :, b_cols], 15 + d)
        arrived(full.at[ring(y, 3 - d), other, :, :, a_cols], 18 + d)
        arrived(full.at[:, other, ring(z, 3 - d), :, b_cols], 21 + d)
    for copy in started:
        copy.wait_send()


def gather_weights(own):
    return pl.pallas_call(
        gather_kernel,
        out_shape=jax.ShapeDtypeStruct((4, 2, 4) + own.shape, own.dtype),
        in_specs=[pl.BlockSpec(memory_space=pltpu.VMEM)],
        out_specs=pl.BlockSpec(memory_space=pltpu.HBM),
        scratch_shapes=[
            pltpu.SemaphoreType.DMA((25,)),
            pltpu.SemaphoreType.DMA((25,)),
            pltpu.SemaphoreType.DMA,
        ],
        compiler_params=pltpu.CompilerParams(
            collective_id=0, has_side_effects=True, vmem_limit_bytes=48 * 1024 * 1024
        ),
        name="gather_weights",
    )(own)


def reduce_kernel(
    grads, gains, total, gain_total, twin, summed, got_a, got_b, sum_a, sum_b, last, gain_box, send, recv
):
    y, c, z, x = whereami()
    other = 1 - c
    y_peer = [device_at(ring(y, d), c, z, x) for d in (1, 2, 3)]
    z_peer = [device_at(y, c, ring(z, d), x) for d in (1, 2, 3)]
    x_peer = [device_at(y, c, z, ring(x, d)) for d in (1, 2, 3)]
    sibling = device_at(y, other, z, x)
    greet(y_peer + z_peer + x_peer + [sibling])
    a_cols, b_cols = HALVES
    started = []

    def start(source, target, slot, device):
        copy = remote(source, target, send.at[slot], recv.at[slot], device)
        copy.start()
        started.append(copy)

    def arrived(view, slot):
        remote(view, view, send.at[slot], recv.at[slot], sibling).wait_recv()

    gain_total[...] = gains[...]
    start(gains, gain_box.at[0], 16, sibling)
    for step in range(4):
        row = ring(y, step + 1)
        start(grads.at[row, other], twin.at[row], step, sibling)
    arrived(gain_box.at[0], 16)
    gain_total[...] += gain_box[0]
    gain_box[10] = gain_total[...]
    for d in range(3):
        start(gain_box.at[10], gain_box.at[1 + d], 17 + d, y_peer[d])
    for step in range(4):
        row = ring(y, step + 1)
        arrived(twin.at[row], step)

        def add_pair(zz, carry, row=row):
            summed[row, zz] = (
                grads[row, c, zz].astype(jnp.float32) + twin[row, zz].astype(jnp.float32)
            ).astype(jnp.bfloat16)
            return carry

        lax.fori_loop(0, 4, add_pair, 0)
        if step < 3:
            start(summed.at[row, :, :, a_cols], got_a.at[step], 4 + step, y_peer[step])
    for d in range(3):
        start(summed.at[:, ring(z, d + 1), :, b_cols], got_b.at[d], 7 + d, z_peer[d])
    for d in range(3):
        arrived(gain_box.at[1 + d], 17 + d)
    gain_total[...] += gain_box[1] + gain_box[2] + gain_box[3]
    gain_box[11] = gain_total[...]
    for d in range(3):
        start(gain_box.at[11], gain_box.at[4 + d], 20 + d, z_peer[d])
    for d in range(3):
        arrived(got_a.at[d], 4 + d)

    def add_a(zz, carry):
        value = summed[y, zz, :, a_cols].astype(jnp.float32)
        for d in range(3):
            value = value + got_a[d, zz].astype(jnp.float32)
        sum_a[zz] = value.astype(jnp.bfloat16)
        return carry

    lax.fori_loop(0, 4, add_a, 0)
    for d in range(3):
        start(sum_a.at[ring(z, d + 1)], last.at[0, d], 10 + d, z_peer[d])
    for d in range(3):
        arrived(got_b.at[d], 7 + d)

    def add_b(yy, carry):
        value = summed[yy, z, :, b_cols].astype(jnp.float32)
        for d in range(3):
            value = value + got_b[d, yy].astype(jnp.float32)
        sum_b[yy] = value.astype(jnp.bfloat16)
        return carry

    lax.fori_loop(0, 4, add_b, 0)
    for d in range(3):
        start(sum_b.at[ring(y, d + 1)], last.at[1, d], 13 + d, y_peer[d])
    for d in range(3):
        arrived(gain_box.at[4 + d], 20 + d)
    gain_total[...] += gain_box[4] + gain_box[5] + gain_box[6]
    gain_box[12] = gain_total[...]
    for d in range(3):
        start(gain_box.at[12], gain_box.at[7 + d], 23 + d, x_peer[d])
    for d in range(3):
        arrived(last.at[0, d], 10 + d)
    value = sum_a[z].astype(jnp.float32)
    for d in range(3):
        value = value + last[0, d].astype(jnp.float32)
    total[:, a_cols] = value
    for d in range(3):
        arrived(last.at[1, d], 13 + d)
    value = sum_b[y].astype(jnp.float32)
    for d in range(3):
        value = value + last[1, d].astype(jnp.float32)
    total[:, b_cols] = value
    for d in range(3):
        arrived(gain_box.at[7 + d], 23 + d)
    gain_total[...] += gain_box[7] + gain_box[8] + gain_box[9]
    for copy in started:
        copy.wait_send()


def reduce_grads(grads, gains):
    rows = grads.shape[3]
    return pl.pallas_call(
        reduce_kernel,
        out_shape=[
            jax.ShapeDtypeStruct((rows, PACK_COLS), jnp.float32),
            jax.ShapeDtypeStruct(gains.shape, jnp.float32),
        ],
        in_specs=[pl.BlockSpec(memory_space=pltpu.VMEM)] * 2,
        out_specs=[pl.BlockSpec(memory_space=pltpu.VMEM)] * 2,
        scratch_shapes=[
            pltpu.VMEM((4, 4, rows, PACK_COLS), jnp.bfloat16),
            pltpu.VMEM((4, 4, rows, PACK_COLS), jnp.bfloat16),
            pltpu.VMEM((3, 4, rows, HALF_COLS), jnp.bfloat16),
            pltpu.VMEM((3, 4, rows, HALF_COLS), jnp.bfloat16),
            pltpu.VMEM((4, rows, HALF_COLS), jnp.bfloat16),
            pltpu.VMEM((4, rows, HALF_COLS), jnp.bfloat16),
            pltpu.VMEM((2, 3, rows, HALF_COLS), jnp.bfloat16),
            pltpu.VMEM((13,) + gains.shape, jnp.float32),
            pltpu.SemaphoreType.DMA((26,)),
            pltpu.SemaphoreType.DMA((26,)),
        ],
        compiler_params=pltpu.CompilerParams(
            collective_id=1, has_side_effects=True, vmem_limit_bytes=56 * 1024 * 1024
        ),
        name="reduce_grads",
    )(grads, gains)


SQUARE_COUNT = 8
WIDE_COUNT = 6
OWNERS = SQUARE_COUNT + WIDE_COUNT
PAIR_ROWS = 2 * ROW_SHARD


def owner_place(matrix):
    return (matrix // 4, 0, (matrix // 4 + matrix % 4) % 4, matrix % 4)


def device_of_index(index):
    return (lax.div(index, 16), lax.rem(lax.div(index, 4), 4), lax.rem(index, 4))


def ns_step(source, target, gram, columns):
    blocks = D // 256

    def gram_rows(block, carry):
        rows = pl.ds(pl.multiple_of(block * 256, 256), 256)
        gram[rows, :] = lax.dot_general(
            source[rows, 0:columns],
            source[:, 0:columns],
            (((1,), (1,)), ((), ())),
            preferred_element_type=jnp.float32,
        ).astype(jnp.bfloat16)
        return carry

    lax.fori_loop(0, blocks, gram_rows, 0)

    def update_rows(block, carry):
        rows = pl.ds(pl.multiple_of(block * 256, 256), 256)
        gram_block = gram[rows, :]
        polynomial = (
            quintic_two * gram_block.astype(jnp.float32)
            + quintic_three
            * jnp.dot(gram_block, gram[...], preferred_element_type=jnp.float32)
        ).astype(jnp.bfloat16)
        for start in range(0, columns, 512):
            part = slice(start, start + 512)
            target[rows, part] = (
                quintic_one * source[rows, part].astype(jnp.float32)
                + jnp.dot(polynomial, source[:, part], preferred_element_type=jnp.float32)
            ).astype(jnp.bfloat16)
        return carry

    lax.fori_loop(0, blocks, update_rows, 0)


def orthogonal_owner(slots, front, back, gram, wide):
    columns = 2048 if wide else 1024
    slot_rows = PAIR_ROWS if wide else 32

    def add_squares(index, carry):
        value = slots[index, 0:slot_rows, :].astype(jnp.float32)
        return carry + jnp.sum(value * value, axis=0, keepdims=True)

    squares = lax.fori_loop(0, 128, add_squares, jnp.zeros((1, 256), jnp.float32))
    norm = jnp.sqrt(jnp.sum(squares, axis=1, keepdims=True)) + ortho_eps
    scale = 1.0 / norm

    def assemble(pair, carry):
        rows = pl.ds(pl.multiple_of(pair * PAIR_ROWS, PAIR_ROWS), PAIR_ROWS)
        for part in range(4):
            first = slots[pair * 8 + part, 0:slot_rows, :].astype(jnp.float32) * scale
            second = slots[pair * 8 + 4 + part, 0:slot_rows, :].astype(jnp.float32) * scale
            joined = jnp.concatenate([first[0:24], second[0:24]], axis=0).astype(jnp.bfloat16)
            if wide:
                front[rows, part * 512 : part * 512 + 256] = joined
                front[rows, part * 512 + 256 : part * 512 + 512] = jnp.concatenate(
                    [first[24:48], second[24:48]], axis=0
                ).astype(jnp.bfloat16)
            else:
                front[rows, part * 256 : part * 256 + 256] = joined
        return carry

    lax.fori_loop(0, 16, assemble, 0)

    def two_steps(index, carry):
        ns_step(front, back, gram, columns)
        ns_step(back, front, gram, columns)
        return carry

    lax.fori_loop(0, NS_STEPS // 2, two_steps, 0)

    def take_apart(pair, carry):
        rows = pl.ds(pl.multiple_of(pair * PAIR_ROWS, PAIR_ROWS), PAIR_ROWS)
        for part in range(4):
            if wide:
                left = front[rows, part * 512 : part * 512 + 256].astype(jnp.float32)
                right = front[rows, part * 512 + 256 : part * 512 + 512].astype(jnp.float32)
                slots[pair * 8 + part] = jnp.concatenate([left[0:24], right[0:24]], axis=0).astype(
                    jnp.bfloat16
                )
                slots[pair * 8 + 4 + part] = jnp.concatenate(
                    [left[24:48], right[24:48]], axis=0
                ).astype(jnp.bfloat16)
            else:
                left = front[rows, part * 256 : part * 256 + 256].astype(jnp.float32)
                slots[pair * 8 + part, 0:32] = left[0:32].astype(jnp.bfloat16)
                slots[pair * 8 + 4 + part, 0:32] = jnp.concatenate(
                    [left[24:48], left[0:8]], axis=0
                ).astype(jnp.bfloat16)
        return carry

    lax.fori_loop(0, 16, take_apart, 0)


def muon_kernel(square, wide, square_new, wide_new, slots, front, back, gram, send, recv, slot_recv, slot_send):
    y, c, z, x = whereami()
    mine = (y * 2 + c) * 16 + z * 4 + x
    barrier = pltpu.get_barrier_semaphore()
    owns = [None] * OWNERS
    places = [owner_place(m) for m in range(OWNERS)]
    indices = [(p[0] * 2 + p[1]) * 16 + p[2] * 4 + p[3] for p in places]
    is_square_owner = (c == 0) & (z == ring(x, y)) & (y < 2)
    is_wide_owner = (c == 0) & (z == ring(x, y)) & ((y == 2) | ((y == 3) & (x < 2)))
    is_owner = is_square_owner | is_wide_owner

    @pl.when(is_owner)
    def _():
        def greet_one(index, carry):
            @pl.when(index != mine)
            def _():
                pl.semaphore_signal(
                    barrier, inc=1, device_id=device_of_index(index), device_id_type=MESH_ID
                )

            return carry

        lax.fori_loop(0, 128, greet_one, 0)
        pl.semaphore_wait(barrier, 127)

    @pl.when(jnp.logical_not(is_owner))
    def _():
        for m in range(OWNERS):
            pl.semaphore_signal(
                barrier, inc=1, device_id=device_at(*places[m]), device_id_type=MESH_ID
            )
        pl.semaphore_wait(barrier, OWNERS)

    def tile_of(m, source, width):
        return source.at[m] if width else source.at[m - SQUARE_COUNT]

    def outbound(m):
        if m < SQUARE_COUNT:
            return square.at[m], slots.at[mine, pl.ds(0, 32)]
        return wide.at[m - SQUARE_COUNT], slots.at[mine]

    def inbound(m):
        return square_new.at[m] if m < SQUARE_COUNT else wide_new.at[m - SQUARE_COUNT]

    for m in range(OWNERS):
        source, target = outbound(m)

        @pl.when(mine != indices[m])
        def _(source=source, target=target, m=m):
            remote(source, target, send.at[m], slot_recv, device_at(*places[m])).start()

        @pl.when(mine == indices[m])
        def _(source=source, target=target, m=m):
            copy = pltpu.make_async_copy(source, target, send.at[m])
            copy.start()
            copy.wait()

    def serve(is_wide):
        slot_rows = PAIR_ROWS if is_wide else 32
        whole = slots.at[pl.ds(0, 127), pl.ds(0, slot_rows)]
        remote(whole, whole, slot_send, slot_recv, device_at(y, c, z, x)).wait_recv()
        orthogonal_owner(slots, front, back, gram, is_wide)
        matrix = y * 4 + x

        def answer(index, carry):
            @pl.when(index != mine)
            def _():
                if is_wide:
                    remote(
                        slots.at[index],
                        wide_new.at[matrix - SQUARE_COUNT],
                        slot_send,
                        recv.at[matrix],
                        device_of_index(index),
                    ).start()
                else:
                    remote(
                        slots.at[index, pl.ds(0, 32)],
                        square_new.at[matrix],
                        slot_send,
                        recv.at[matrix],
                        device_of_index(index),
                    ).start()

            return carry

        lax.fori_loop(0, 128, answer, 0)
        if is_wide:
            wide_new[matrix - SQUARE_COUNT] = slots[mine]
        else:
            square_new[matrix] = slots[mine, 0:32]
        remote(whole, whole, slot_send, slot_recv, device_at(y, c, z, x)).wait_send()

    @pl.when(is_square_owner)
    def _():
        serve(False)

    @pl.when(is_wide_owner)
    def _():
        serve(True)

    for m in range(OWNERS):
        source, target = outbound(m)

        @pl.when(mine != indices[m])
        def _(source=source, target=target, m=m):
            copy = remote(source, inbound(m), send.at[m], recv.at[m], device_at(*places[m]))
            copy.wait_send()
            copy.wait_recv()


def muon(square, wide):
    return pl.pallas_call(
        muon_kernel,
        out_shape=[
            jax.ShapeDtypeStruct(square.shape, jnp.bfloat16),
            jax.ShapeDtypeStruct(wide.shape, jnp.bfloat16),
        ],
        in_specs=[pl.BlockSpec(memory_space=pltpu.VMEM)] * 2,
        out_specs=[pl.BlockSpec(memory_space=pltpu.VMEM)] * 2,
        scratch_shapes=[
            pltpu.VMEM((128, PAIR_ROWS, 256), jnp.bfloat16),
            pltpu.VMEM((D, FF), jnp.bfloat16),
            pltpu.VMEM((D, FF), jnp.bfloat16),
            pltpu.VMEM((D, D), jnp.bfloat16),
            pltpu.SemaphoreType.DMA((OWNERS,)),
            pltpu.SemaphoreType.DMA((OWNERS,)),
            pltpu.SemaphoreType.DMA,
            pltpu.SemaphoreType.DMA,
        ],
        compiler_params=pltpu.CompilerParams(
            collective_id=2, has_side_effects=True, vmem_limit_bytes=56 * 1024 * 1024
        ),
        name="muon",
    )(square, wide)


def pack_layers(attend_in, attend_out, expand, shrink):
    return jnp.concatenate(
        [
            attend_in[:, 0],
            attend_in[:, 1],
            attend_in[:, 2],
            jnp.swapaxes(attend_out, 1, 2),
            expand[:, 0],
            expand[:, 1],
            jnp.swapaxes(shrink, 1, 2),
        ],
        axis=2,
    )


def unpack_layers(packed):
    attend_in = jnp.stack([packed[:, :, 192 * k : 192 * k + 192] for k in range(3)], axis=1)
    attend_out = jnp.swapaxes(packed[:, :, 576:768], 1, 2)
    expand = jnp.stack([packed[:, :, 768:1280], packed[:, :, 1280:1792]], axis=1)
    shrink = jnp.swapaxes(packed[:, :, 1792:2304], 1, 2)
    return attend_in, attend_out, expand, shrink


def square_tiles(packed):
    tiles = packed[:, :, 0:768].reshape(2, 24, 4, 192).transpose(0, 2, 1, 3).reshape(8, 24, 192)
    return jnp.pad(tiles, ((0, 0), (0, 8), (0, 64)))


def wide_tiles(packed):
    tiles = packed[:, :, 768:2304].reshape(2, 24, 3, 2, 256).transpose(0, 2, 3, 1, 4)
    return tiles.reshape(6, 48, 256)


def untile(square_new, wide_new):
    left = square_new[:, 0:24, 0:192].reshape(2, 4, 24, 192).transpose(0, 2, 1, 3).reshape(2, 24, 768)
    right = wide_new.reshape(2, 3, 2, 24, 256).transpose(0, 3, 1, 2, 4).reshape(2, 24, 1536)
    return jnp.concatenate([left, right], axis=2)


def gather_rows(normed):
    return lax.all_gather(normed, "tp", axis=0, tiled=True)


def gather_grads(gradient):
    return lax.all_gather(gradient, "tp", axis=0, tiled=True)


def branch_sum(operand, weight):
    return lax.psum_scatter(
        jnp.einsum("rc,dc->rd", operand, weight, preferred_element_type=jnp.float32).astype(
            jnp.bfloat16
        ),
        "tp",
        scatter_dimension=0,
        tiled=True,
    ).astype(jnp.float32)


def input_sum(operand, weight, pattern):
    return lax.psum_scatter(
        jnp.einsum(pattern, operand, weight, preferred_element_type=jnp.float32).astype(
            jnp.bfloat16
        ),
        "tp",
        scatter_dimension=0,
        tiled=True,
    ).astype(jnp.float32)


def block_scores(queries, key_all, layout, key_start, score_scale):
    document, places, query_doc, query_place = layout
    key_block = lax.dynamic_slice_in_dim(key_all, key_start, KEY_BLOCK)
    key_doc = lax.dynamic_slice_in_dim(document, key_start, KEY_BLOCK)
    key_place = lax.dynamic_slice_in_dim(places, key_start, KEY_BLOCK)
    raw_scores = (
        jnp.einsum("qhd,khd->hqk", queries, key_block, preferred_element_type=jnp.float32)
        * score_scale
    )
    allowed = (query_doc[:, None] == key_doc[None, :]) & (
        query_place[:, None] >= key_place[None, :]
    )
    return jnp.where(allowed[None], raw_scores, mask_fill)


def attend_forward(queries, key_all, value_all, layout, score_scale):
    block_count = key_all.shape[0] // KEY_BLOCK
    stat_shape = (queries.shape[1], queries.shape[0], 1)

    def measure(block_step, state_carry):
        running_max, running_sum = state_carry
        scores = block_scores(queries, key_all, layout, block_step * KEY_BLOCK, score_scale)
        new_max = jnp.maximum(running_max, jnp.max(scores, axis=-1, keepdims=True))
        running_sum = running_sum * jnp.exp(running_max - new_max) + jnp.sum(
            jnp.exp(scores - new_max), axis=-1, keepdims=True
        )
        return (new_max, running_sum)

    running_max, running_sum = lax.fori_loop(
        0,
        block_count,
        measure,
        (jnp.full(stat_shape, mask_fill, jnp.float32), jnp.zeros(stat_shape, jnp.float32)),
    )
    log_total = running_max + jnp.log(running_sum)

    def collect(block_step, output):
        key_start = block_step * KEY_BLOCK
        scores = block_scores(queries, key_all, layout, key_start, score_scale)
        probability = jnp.exp(scores - log_total).astype(jnp.bfloat16)
        value_block = lax.dynamic_slice_in_dim(value_all, key_start, KEY_BLOCK)
        return output + jnp.einsum(
            "hqk,khd->qhd", probability, value_block, preferred_element_type=jnp.float32
        )

    output = lax.fori_loop(0, block_count, collect, jnp.zeros(queries.shape, jnp.float32))
    return (output, log_total)


def attend_backward(queries, key_all, value_all, attended_grad, log_total, layout, score_scale):
    block_count = key_all.shape[0] // KEY_BLOCK

    def rowwise(block_step, row_total):
        key_start = block_step * KEY_BLOCK
        scores = block_scores(queries, key_all, layout, key_start, score_scale)
        probability = jnp.exp(scores - log_total)
        value_block = lax.dynamic_slice_in_dim(value_all, key_start, KEY_BLOCK)
        prob_grad = jnp.einsum(
            "qhd,khd->hqk", attended_grad, value_block, preferred_element_type=jnp.float32
        )
        return row_total + jnp.sum(probability * prob_grad, axis=-1, keepdims=True)

    row_total = lax.fori_loop(0, block_count, rowwise, jnp.zeros(log_total.shape, jnp.float32))

    def spread(block_step, state_carry):
        query_grad, key_terms = state_carry
        key_start = block_step * KEY_BLOCK
        scores = block_scores(queries, key_all, layout, key_start, score_scale)
        probability = jnp.exp(scores - log_total)
        key_block = lax.dynamic_slice_in_dim(key_all, key_start, KEY_BLOCK)
        value_block = lax.dynamic_slice_in_dim(value_all, key_start, KEY_BLOCK)
        prob_grad = jnp.einsum(
            "qhd,khd->hqk", attended_grad, value_block, preferred_element_type=jnp.float32
        )
        score_grad = (probability * (prob_grad - row_total)).astype(jnp.bfloat16)
        query_grad = (
            query_grad
            + jnp.einsum("hqk,khd->qhd", score_grad, key_block, preferred_element_type=jnp.float32)
            * score_scale
        )
        key_grad = (
            jnp.einsum("hqk,qhd->khd", score_grad, queries, preferred_element_type=jnp.float32)
            * score_scale
        )
        value_grad = jnp.einsum(
            "hqk,qhd->khd",
            probability.astype(jnp.bfloat16),
            attended_grad,
            preferred_element_type=jnp.float32,
        )
        key_terms = lax.dynamic_update_slice_in_dim(
            key_terms, jnp.stack([key_grad, value_grad], axis=1), key_start, 0
        )
        return (query_grad, key_terms)

    start_state = (
        jnp.zeros(queries.shape, jnp.float32),
        jnp.zeros((key_all.shape[0], 2) + key_all.shape[1:], jnp.float32),
    )
    return lax.fori_loop(0, block_count, spread, start_state)


def body(
    hidden_in,
    out_grad,
    seq_lengths,
    norm_gains,
    gain_first,
    gain_second,
    attend_in,
    attend_out,
    expand,
    shrink,
    attend_in_moment,
    attend_out_moment,
    expand_moment,
    shrink_moment,
):
    layer_count = attend_in.shape[0]
    tensor_count = lax.axis_size("tp")
    context_count = lax.axis_size("ctx")
    local_rows = hidden_in.shape[0]
    context_rows = local_rows * tensor_count
    group_rows = context_rows * context_count
    local_width = attend_in.shape[3]
    head_shape = (context_rows, local_width // HEAD_DIM, HEAD_DIM)
    score_scale = 1.0 / math.sqrt(HEAD_DIM)
    document, position, places = doc_layout(seq_lengths[0], group_rows)
    row_start = lax.axis_index("ctx") * context_rows
    query_position = lax.dynamic_slice_in_dim(position, row_start, context_rows)
    layout = (
        document,
        places,
        lax.dynamic_slice_in_dim(document, row_start, context_rows),
        lax.dynamic_slice_in_dim(places, row_start, context_rows),
    )
    weights_packed = pack_layers(attend_in, attend_out, expand, shrink)
    weights_all = gather_weights(weights_packed.astype(jnp.bfloat16).reshape(48, PACK_COLS))
    tiles_by_layer = []
    for layer_index in range(layer_count):
        rows = slice(24 * layer_index, 24 * layer_index + 24)
        whole = weights_all[:, :, :, rows, :].reshape(D, PACK_COLS)
        tiles_by_layer.append(
            (
                whole[:, 0:576].reshape(D, 3, 192).transpose(1, 0, 2),
                whole[:, 576:768],
                whole[:, 768:1792].reshape(D, 2, 512).transpose(1, 0, 2),
                whole[:, 1792:2304],
            )
        )
    row_values = hidden_in.astype(jnp.float32)
    kept_state = []
    for layer_index in range(layer_count):
        in_tile, out_tile, expand_tile, shrink_tile = tiles_by_layer[layer_index]
        gain_rows = norm_gains[layer_index]
        normed = gather_rows(normalize(row_values, gain_rows[0]).astype(jnp.bfloat16))
        projected = jnp.einsum("rd,kdc->rkc", normed, in_tile, preferred_element_type=jnp.float32)
        queries = rotate(projected[:, 0].reshape(head_shape), query_position).astype(jnp.bfloat16)
        key_rows = rotate(projected[:, 1].reshape(head_shape), query_position).astype(jnp.bfloat16)
        value_rows = projected[:, 2].reshape(head_shape).astype(jnp.bfloat16)
        key_all, value_all = (
            lax.all_gather(key_rows, "ctx", axis=0, tiled=True),
            lax.all_gather(value_rows, "ctx", axis=0, tiled=True),
        )
        attended, log_total = attend_forward(queries, key_all, value_all, layout, score_scale)
        attended = attended.reshape(context_rows, local_width).astype(jnp.bfloat16)
        mid_rows = row_values + branch_sum(attended, out_tile)
        normed_mid = gather_rows(normalize(mid_rows, gain_rows[1]).astype(jnp.bfloat16))
        gate_up = jnp.einsum(
            "rd,kdf->rkf", normed_mid, expand_tile, preferred_element_type=jnp.float32
        )
        active = (jax.nn.silu(gate_up[:, 0]) * gate_up[:, 1]).astype(jnp.bfloat16)
        kept_state.append(
            (
                row_values,
                normed,
                queries,
                key_all,
                value_all,
                log_total,
                attended,
                mid_rows,
                normed_mid,
                gate_up,
                active,
                (in_tile, out_tile, expand_tile, shrink_tile),
            )
        )
        row_values = mid_rows + branch_sum(active, shrink_tile)
    row_grad = out_grad.astype(jnp.float32)
    gain_terms = [None] * layer_count
    weight_terms = [None] * layer_count
    for layer_index in reversed(range(layer_count)):
        (
            rows_before,
            normed,
            queries,
            key_all,
            value_all,
            log_total,
            attended,
            mid_rows,
            normed_mid,
            gate_up,
            active,
            tile_set,
        ) = kept_state[layer_index]
        in_tile, out_tile, expand_tile, shrink_tile = tiles_by_layer[layer_index]
        gain_rows = norm_gains[layer_index]
        down_grad = gather_grads(row_grad.astype(jnp.bfloat16))
        active_grad = jnp.einsum(
            "rd,df->rf", down_grad, shrink_tile, preferred_element_type=jnp.float32
        )
        shrink_grad = jnp.einsum("rf,rd->df", active, down_grad, preferred_element_type=jnp.float32)
        gate_part = gate_up[:, 0]
        up_part = gate_up[:, 1]
        sigmoid_gate = jax.nn.sigmoid(gate_part)
        gate_grad = active_grad * up_part * sigmoid_gate * (1.0 + gate_part * (1.0 - sigmoid_gate))
        up_grad = active_grad * gate_part * sigmoid_gate
        gate_up_grad = jnp.stack([gate_grad, up_grad], axis=1).astype(jnp.bfloat16)
        expand_grad = jnp.einsum(
            "rd,rkf->kdf", normed_mid, gate_up_grad, preferred_element_type=jnp.float32
        )
        normed_mid_grad = input_sum(gate_up_grad, expand_tile, "rkf,kdf->rd")
        mid_pull = jax.vjp(normalize, mid_rows, gain_rows[1])[1]
        mid_part, second_gain_grad = mid_pull(normed_mid_grad)
        mid_row_grad = row_grad + mid_part
        branch_grad = gather_grads(mid_row_grad.astype(jnp.bfloat16))
        attended_grad = jnp.einsum(
            "rd,dc->rc", branch_grad, out_tile, preferred_element_type=jnp.float32
        ).astype(jnp.bfloat16)
        out_weight_grad = jnp.einsum(
            "rc,rd->dc", attended, branch_grad, preferred_element_type=jnp.float32
        )
        query_grad, key_terms = attend_backward(
            queries,
            key_all,
            value_all,
            attended_grad.reshape(head_shape),
            log_total,
            layout,
            score_scale,
        )
        key_value_grad = (
            lax.psum_scatter(
                key_terms.reshape(group_rows, 2 * local_width).astype(jnp.bfloat16),
                "ctx",
                scatter_dimension=0,
                tiled=True,
            )
            .astype(jnp.float32)
            .reshape(context_rows, 2, head_shape[1], HEAD_DIM)
        )
        mixed_grad = jnp.stack(
            [
                unrotate(query_grad, query_position).reshape(context_rows, local_width),
                unrotate(key_value_grad[:, 0], query_position).reshape(context_rows, local_width),
                key_value_grad[:, 1].reshape(context_rows, local_width),
            ],
            axis=1,
        ).astype(jnp.bfloat16)
        in_weight_grad = jnp.einsum(
            "rd,rkc->kdc", normed, mixed_grad, preferred_element_type=jnp.float32
        )
        normed_grad = input_sum(mixed_grad, in_tile, "rkc,kdc->rd")
        first_pull = jax.vjp(normalize, rows_before, gain_rows[0])[1]
        first_part, first_gain_grad = first_pull(normed_grad)
        row_grad = mid_row_grad + first_part
        gain_terms[layer_index] = jnp.stack([first_gain_grad, second_gain_grad])
        weight_terms[layer_index] = jnp.concatenate(
            [
                in_weight_grad[0],
                in_weight_grad[1],
                in_weight_grad[2],
                out_weight_grad,
                expand_grad[0],
                expand_grad[1],
                shrink_grad,
            ],
            axis=1,
        ).astype(jnp.bfloat16)
    grads_packed = jnp.concatenate(
        [term.reshape(4, 2, 4, 24, PACK_COLS) for term in weight_terms], axis=3
    )
    gains_packed = jnp.pad(jnp.stack(gain_terms).reshape(4, D), ((0, 4), (0, 0)))
    grad_total, gain_total = reduce_grads(grads_packed, gains_packed)
    gain_grad = gain_total[0:4].reshape(2, 2, D)
    gain_first_new = first_decay * gain_first + (1.0 - first_decay) * gain_grad
    gain_second_new = second_decay * gain_second + (1.0 - second_decay) * gain_grad * gain_grad
    norm_gains_new = norm_gains - gain_rate * (gain_first_new / (1.0 - first_decay**STEP)) / (
        jnp.sqrt(gain_second_new / (1.0 - second_decay**STEP)) + adam_eps
    )
    moment_packed = pack_layers(
        attend_in_moment, attend_out_moment, expand_moment, shrink_moment
    )
    moment_new = moment_decay * moment_packed + grad_total.reshape(2, 24, PACK_COLS)
    sent = moment_new.astype(jnp.bfloat16)
    square_new, wide_new = muon(square_tiles(sent), wide_tiles(sent))
    orthogonal = untile(square_new, wide_new).astype(jnp.float32)
    column = jnp.arange(PACK_COLS, dtype=jnp.int32)
    rate = jnp.where((column >= 576) & (column < 768), project_rate, matrix_rate)
    factor = jnp.where(column < 768, 0.2 * math.sqrt(D), 0.2 * math.sqrt(FF))
    weights_new = weights_packed - rate * (factor * orthogonal + matrix_decay * weights_packed)
    return (
        row_values,
        row_grad,
        gain_first_new,
        gain_second_new,
        norm_gains_new,
        *unpack_layers(moment_new),
        *unpack_layers(weights_new),
    )


def solution(mesh):
    placed = (
        P(("fsdp", "ctx", "tp"), None),
        P(("fsdp", "ctx", "tp"), None),
        P("fsdp", None),
        P(),
        P(),
        P(),
        P(None, None, ("fsdp", "ctx"), "tp"),
        P(None, "tp", ("fsdp", "ctx")),
        P(None, None, ("fsdp", "ctx"), "tp"),
        P(None, "tp", ("fsdp", "ctx")),
        P(None, None, ("fsdp", "ctx"), "tp"),
        P(None, "tp", ("fsdp", "ctx")),
        P(None, None, ("fsdp", "ctx"), "tp"),
        P(None, "tp", ("fsdp", "ctx")),
    )
    return jax.shard_map(
        body,
        mesh=mesh,
        in_specs=placed,
        out_specs=(
            P(("fsdp", "ctx", "tp"), None),
            P(("fsdp", "ctx", "tp"), None),
            P(),
            P(),
            P(),
            P(None, None, ("fsdp", "ctx"), "tp"),
            P(None, "tp", ("fsdp", "ctx")),
            P(None, None, ("fsdp", "ctx"), "tp"),
            P(None, "tp", ("fsdp", "ctx")),
            P(None, None, ("fsdp", "ctx"), "tp"),
            P(None, "tp", ("fsdp", "ctx")),
            P(None, None, ("fsdp", "ctx"), "tp"),
            P(None, "tp", ("fsdp", "ctx")),
        ),
        check_vma=False,
    )
```

```python
import math

import jax
import jax.numpy as jnp
from jax import lax
from jax.experimental import pallas as pl
from jax.experimental.pallas import tpu as pltpu
from jax.sharding import PartitionSpec as P

D = 768
HEAD_DIM = 64
FF = 2048
NS_STEPS = 4
STEP = 5


norm_eps = 1e-05
rope_base = 10000.0
mask_fill = -1e30
quintic_one = 3.4445
quintic_two = -4.775
quintic_three = 2.0315
moment_decay = 0.95
matrix_rate = 0.1
project_rate = 0.8
matrix_decay = 0.1
gain_rate = 0.8
first_decay = 0.9
second_decay = 0.95
adam_eps = 1e-08
ortho_eps = 1e-07


def doc_layout(lengths, row_count):
    doc_ends = jnp.cumsum(lengths)
    starts = doc_ends - lengths
    places = jnp.arange(row_count, dtype=jnp.int32)
    document = jnp.sum((places[:, None] >= doc_ends[None, :]).astype(jnp.int32), axis=1)
    member = document[:, None] == jnp.arange(lengths.shape[0], dtype=jnp.int32)[None, :]
    offset = jnp.sum(jnp.where(member, starts[None, :], 0), axis=1)
    return (document, places - offset, places)


MESH_ID = pl.DeviceIdType.MESH
ROW_SHARD = 24
PAIR_ROWS = 2 * ROW_SHARD
PACK_COLS = 2304
PART_COLS = 768
HALF_COLS = PART_COLS // 2
LAYERS = 2
MIB = 1024 * 1024


def whereami():
    fsdp_index = lax.axis_index("fsdp")
    return (lax.div(fsdp_index, 2), lax.rem(fsdp_index, 2), lax.axis_index("ctx"), lax.axis_index("tp"))


def device_at(y, c, z, x):
    return (y * 2 + c, z, x)


def ring(index, offset):
    return lax.rem(index + offset, 4)


def remote(source, target, send_sem, recv_sem, device):
    return pltpu.make_async_remote_copy(
        src_ref=source,
        dst_ref=target,
        send_sem=send_sem,
        recv_sem=recv_sem,
        device_id=device,
        device_id_type=MESH_ID,
    )


def greet(devices):
    barrier = pltpu.get_barrier_semaphore()
    for device in devices:
        pl.semaphore_signal(barrier, inc=1, device_id=device, device_id_type=MESH_ID)
    pl.semaphore_wait(barrier, len(devices))


def neighbour(axis, offset):
    y, c, z, x = whereami()
    if axis == "y":
        return device_at(ring(y, offset), c, z, x)
    if axis == "z":
        return device_at(y, c, ring(z, offset), x)
    return device_at(y, c, z, ring(x, offset))


def six_neighbours():
    return [neighbour(axis, offset) for axis in ("x", "y", "z") for offset in (1, 3)]


PART_ORDER = (("x", "y", "z"), ("y", "z", "x"), ("z", "x", "y"))


def part_view(ref, part, done, axis, place, half):
    y, c, z, x = whereami()
    whole = slice(None)

    def index(name, own):
        if name == axis:
            return place
        return whole if name in done else own

    if axis == "x":
        pick_x = lax.rem(place, 2)
    else:
        pick_x = whole if "x" in done else lax.rem(x, 2)
    start = part * PART_COLS
    width = PART_COLS
    if half is not None:
        start += half * HALF_COLS
        width = HALF_COLS
    return ref.at[pick_x, index("y", y), index("z", z), :, pl.ds(start, width)]


def ring_exists(axis, done, place):
    y, c, z, x = whereami()
    if axis == "x":
        return lax.div(place, 2) == c
    if "x" in done:
        return None
    return lax.div(x, 2) == c


def run_if(condition, action):
    if condition is None:
        action()
    else:
        pl.when(condition)(action)


class GatherLane:
    def __init__(self, ref, part, send, recv, base):
        self.ref, self.part, self.send, self.recv, self.base = ref, part, send, recv, base

    def parts(self, phase):
        axis = PART_ORDER[self.part][phase]
        done = PART_ORDER[self.part][:phase]
        y, c, z, x = whereami()
        return axis, done, {"x": x, "y": y, "z": z}[axis], self.base + 4 * phase

    def copy(self, phase, slot, place, half, offset):
        axis, done, me, base = self.parts(phase)
        view = part_view(self.ref, self.part, done, axis, place, half)
        return remote(
            view, view, self.send.at[base + slot], self.recv.at[base + slot], neighbour(axis, offset)
        )

    def first(self, phase):
        axis, done, me, base = self.parts(phase)

        def action():
            self.copy(phase, 0, me, None, 1).start()
            self.copy(phase, 1, me, None, 3).start()

        run_if(ring_exists(axis, done, me), action)

    def second(self, phase):
        axis, done, me, base = self.parts(phase)
        left, right = ring(me, 3), ring(me, 1)

        def from_left():
            self.copy(phase, 0, left, None, 1).wait_recv()
            self.copy(phase, 2, left, 0, 1).start()

        def from_right():
            self.copy(phase, 1, right, None, 1).wait_recv()
            self.copy(phase, 3, right, 1, 3).start()

        run_if(ring_exists(axis, done, left), from_left)
        run_if(ring_exists(axis, done, right), from_right)

    def third(self, phase):
        axis, done, me, base = self.parts(phase)
        far = ring(me, 2)

        def action():
            self.copy(phase, 2, far, 0, 1).wait_recv()
            self.copy(phase, 3, far, 1, 1).wait_recv()

        run_if(ring_exists(axis, done, far), action)

    def drain(self, phase):
        axis, done, me, base = self.parts(phase)
        left, right = ring(me, 3), ring(me, 1)

        def own():
            self.copy(phase, 0, me, None, 1).wait_send()
            self.copy(phase, 1, me, None, 3).wait_send()

        run_if(ring_exists(axis, done, me), own)
        run_if(ring_exists(axis, done, left), lambda: self.copy(phase, 2, left, 0, 1).wait_send())
        run_if(ring_exists(axis, done, right), lambda: self.copy(phase, 3, right, 1, 3).wait_send())


def gather_kernel(own, table, full, tables, twin, piece, send, recv, local):
    y, c, z, x = whereami()
    holder = lax.div(x, 2)
    sibling = device_at(y, 1 - c, z, x)
    greet(six_neighbours() + [sibling])
    swap = remote(table, tables.at[c], send.at[73], recv.at[73], sibling)
    swap.start()
    tables[c] = table[...]

    @pl.when(c != holder)
    def _():
        remote(own, twin, send.at[72], recv.at[72], sibling).start()

    @pl.when(c == holder)
    def _():
        remote(twin, twin, send.at[72], recv.at[72], sibling).wait_recv()
        mine = own[...].astype(jnp.float32)
        theirs = twin[...].astype(jnp.float32)
        first = jnp.where(c == 0, mine, theirs)
        second = jnp.where(c == 0, theirs, mine)
        for layer in range(LAYERS):
            rows = slice(layer * ROW_SHARD, layer * ROW_SHARD + ROW_SHARD)
            piece[layer] = jnp.concatenate([first[rows], second[rows]], axis=0).astype(jnp.bfloat16)
            keep = pltpu.make_async_copy(
                piece.at[layer], full.at[layer, lax.rem(x, 2), y, z], local.at[layer]
            )
            keep.start()
        for layer in range(LAYERS):
            pltpu.make_async_copy(
                piece.at[layer], full.at[layer, lax.rem(x, 2), y, z], local.at[layer]
            ).wait()

    lanes = [
        GatherLane(full.at[layer], part, send, recv, 12 * (3 * layer + part))
        for layer in range(LAYERS)
        for part in range(3)
    ]
    for phase in range(3):
        for lane in lanes:
            lane.first(phase)
        for lane in lanes:
            lane.second(phase)
        for lane in lanes:
            lane.third(phase)
    for phase in range(3):
        for lane in lanes:
            lane.drain(phase)

    @pl.when(c != holder)
    def _():
        remote(own, twin, send.at[72], recv.at[72], sibling).wait_send()

    swap.wait_send()
    remote(table, tables.at[1 - c], send.at[73], recv.at[73], sibling).wait_recv()


def gather_weights(own, table):
    return pl.pallas_call(
        gather_kernel,
        out_shape=[
            jax.ShapeDtypeStruct((LAYERS, 2, 4, 4, PAIR_ROWS, PACK_COLS), jnp.bfloat16),
            jax.ShapeDtypeStruct((2,) + table.shape, jnp.float32),
        ],
        in_specs=[pl.BlockSpec(memory_space=pltpu.VMEM)] * 2,
        out_specs=[pl.BlockSpec(memory_space=pltpu.HBM), pl.BlockSpec(memory_space=pltpu.VMEM)],
        scratch_shapes=[
            pltpu.VMEM((LAYERS * ROW_SHARD, PACK_COLS), jnp.bfloat16),
            pltpu.VMEM((LAYERS, PAIR_ROWS, PACK_COLS), jnp.bfloat16),
            pltpu.SemaphoreType.DMA((74,)),
            pltpu.SemaphoreType.DMA((74,)),
            pltpu.SemaphoreType.DMA((LAYERS,)),
        ],
        compiler_params=pltpu.CompilerParams(
            collective_id=0, has_side_effects=True, vmem_limit_bytes=32 * MIB
        ),
        name="gather_weights",
    )(own, table)


class ReduceLane:
    def __init__(self, ref, boxes, part, send, recv, base):
        self.ref, self.boxes, self.part, self.send, self.recv, self.base = (
            ref,
            boxes,
            part,
            send,
            recv,
            base,
        )

    def parts(self, phase):
        axis = PART_ORDER[self.part][2 - phase]
        done = PART_ORDER[self.part][: 2 - phase]
        y, c, z, x = whereami()
        return axis, done, {"x": x, "y": y, "z": z}[axis], self.base + 4 * phase

    def copy(self, phase, slot, place, half, offset):
        axis, done, me, base = self.parts(phase)
        view = part_view(self.ref, self.part, done, axis, place, half)
        return remote(
            view,
            self.boxes[phase][slot],
            self.send.at[base + slot],
            self.recv.at[base + slot],
            neighbour(axis, offset),
        )

    def add(self, phase, place, half, boxes):
        axis, done, me, base = self.parts(phase)
        view = part_view(self.ref, self.part, done, axis, place, half)
        lead = view.shape[:-2]

        def add_one(index, carry):
            where = []
            for extent in reversed(lead):
                where.insert(0, lax.rem(index, extent))
                index = lax.div(index, extent)
            where = tuple(where)
            value = view[where].astype(jnp.float32)
            for box in boxes:
                value = value + box[where].astype(jnp.float32)
            view[where] = value.astype(jnp.bfloat16)
            return carry

        if len(lead) == 0:
            value = view[...].astype(jnp.float32)
            for box in boxes:
                value = value + box[...].astype(jnp.float32)
            view[...] = value.astype(jnp.bfloat16)
        else:
            lax.fori_loop(0, math.prod(lead), add_one, 0)

    def first(self, phase):
        axis, done, me, base = self.parts(phase)
        far = ring(me, 2)

        def action():
            self.copy(phase, 0, far, 0, 1).start()
            self.copy(phase, 1, far, 1, 3).start()

        run_if(ring_exists(axis, done, far), action)

    def second(self, phase):
        axis, done, me, base = self.parts(phase)
        left, right = ring(me, 3), ring(me, 1)

        def to_right():
            self.copy(phase, 0, right, 0, 1).wait_recv()
            self.add(phase, right, 0, [self.boxes[phase][0]])
            self.copy(phase, 2, right, None, 1).start()

        def to_left():
            self.copy(phase, 1, left, 1, 1).wait_recv()
            self.add(phase, left, 1, [self.boxes[phase][1]])
            self.copy(phase, 3, left, None, 3).start()

        run_if(ring_exists(axis, done, right), to_right)
        run_if(ring_exists(axis, done, left), to_left)

    def third(self, phase):
        axis, done, me, base = self.parts(phase)

        def action():
            self.copy(phase, 2, me, None, 1).wait_recv()
            self.copy(phase, 3, me, None, 1).wait_recv()
            self.add(phase, me, None, [self.boxes[phase][2], self.boxes[phase][3]])

        run_if(ring_exists(axis, done, me), action)

    def drain(self, phase):
        axis, done, me, base = self.parts(phase)
        far, left, right = ring(me, 2), ring(me, 3), ring(me, 1)

        def own():
            self.copy(phase, 0, far, 0, 1).wait_send()
            self.copy(phase, 1, far, 1, 3).wait_send()

        run_if(ring_exists(axis, done, far), own)
        run_if(ring_exists(axis, done, right), lambda: self.copy(phase, 2, right, None, 1).wait_send())
        run_if(ring_exists(axis, done, left), lambda: self.copy(phase, 3, left, None, 3).wait_send())


def box_shape(part, phase):
    order = PART_ORDER[part]
    axis, done = order[2 - phase], order[: 2 - phase]
    lead = []
    for name, extent in (("x", 2), ("y", 4), ("z", 4)):
        if name != axis and name in done:
            lead.append(extent)
    return tuple(lead)


def reduce_kernel(first, second, gains, total, gain_total, work, pair, gain_box, *rest):
    boxes_flat, (send, recv, local) = rest[:-3], rest[-3:]
    y, c, z, x = whereami()
    holder = lax.div(x, 2)
    sibling = device_at(y, 1 - c, z, x)
    greet(six_neighbours() + [sibling])
    loads = [
        pltpu.make_async_copy(grads, work.at[i], local.at[i])
        for i, grads in enumerate((first, second))
    ]
    for load in loads:
        load.start()
    gain_total[...] = gains[...]
    lanes = []
    for layer in range(LAYERS):
        for part in range(3):
            boxes = []
            for phase in range(3):
                at = 4 * (3 * part + phase)
                boxes.append([box.at[layer] for box in boxes_flat[at : at + 4]])
            lanes.append(
                ReduceLane(work.at[layer], boxes, part, send, recv, 12 * (3 * layer + part))
            )

    def swap_gains(slot, box, device):
        copy = remote(gain_total, gain_box.at[box], send.at[slot], recv.at[slot], device)
        copy.start()
        return copy

    hops = [(72, sibling)]
    slot = 73
    for axis in ("x", "y", "z"):
        y_, c_, z_, x_ = whereami()
        me = {"x": x_, "y": y_, "z": z_}[axis]
        odd = lax.rem(me, 2)
        near = me + 1 - 2 * odd
        cross = 3 - me
        for place in (near, cross):
            where = {"x": x_, "y": y_, "z": z_}
            where[axis] = place
            hops.append((slot, device_at(where["y"], c_, where["z"], where["x"])))
            slot += 1

    def gain_hop(number):
        slot, device = hops[number]
        copy = swap_gains(slot, number, device)
        copy.wait_send()
        copy.wait_recv()
        gain_total[...] += gain_box[number]

    for layer in range(LAYERS):
        loads[layer].wait()
        for lane in lanes[3 * layer : 3 * layer + 3]:
            lane.first(0)
    gain_hop(0)
    for phase in range(3):
        if phase > 0:
            for lane in lanes:
                lane.first(phase)
        gain_hop(2 * phase + 1)
        for lane in lanes:
            lane.second(phase)
        gain_hop(2 * phase + 2)
        for lane in lanes:
            lane.third(phase)

    @pl.when(c == holder)
    def _():
        for layer in range(LAYERS):
            whole = work[layer, lax.rem(x, 2), y, z].astype(jnp.float32)
            first, second = whole[0:ROW_SHARD], whole[ROW_SHARD:PAIR_ROWS]
            rows = slice(layer * ROW_SHARD, layer * ROW_SHARD + ROW_SHARD)
            total[rows] = jnp.where(c == 0, first, second)
            pair[rows] = jnp.where(c == 0, second, first)
        copy = remote(pair, total, send.at[79], recv.at[79], sibling)
        copy.start()
        copy.wait_send()

    @pl.when(c != holder)
    def _():
        remote(pair, total, send.at[79], recv.at[79], sibling).wait_recv()

    for phase in range(3):
        for lane in lanes:
            lane.drain(phase)


def reduce_grads(first, second, gains):
    box_scratch = []
    for part in range(3):
        for phase in range(3):
            lead = (LAYERS,) + box_shape(part, phase) + (PAIR_ROWS,)
            box_scratch += [pltpu.VMEM(lead + (HALF_COLS,), jnp.bfloat16)] * 2
            box_scratch += [pltpu.VMEM(lead + (PART_COLS,), jnp.bfloat16)] * 2
    return pl.pallas_call(
        reduce_kernel,
        out_shape=[
            jax.ShapeDtypeStruct((LAYERS * ROW_SHARD, PACK_COLS), jnp.float32),
            jax.ShapeDtypeStruct(gains.shape, jnp.float32),
        ],
        in_specs=[pl.BlockSpec(memory_space=pltpu.HBM)] * 2
        + [pl.BlockSpec(memory_space=pltpu.VMEM)],
        out_specs=[pl.BlockSpec(memory_space=pltpu.VMEM)] * 2,
        scratch_shapes=[
            pltpu.VMEM((LAYERS, 2, 4, 4, PAIR_ROWS, PACK_COLS), jnp.bfloat16),
            pltpu.VMEM((LAYERS * ROW_SHARD, PACK_COLS), jnp.float32),
            pltpu.VMEM((7,) + gains.shape, jnp.float32),
            *box_scratch,
            pltpu.SemaphoreType.DMA((80,)),
            pltpu.SemaphoreType.DMA((80,)),
            pltpu.SemaphoreType.DMA((LAYERS,)),
        ],
        compiler_params=pltpu.CompilerParams(
            collective_id=1, has_side_effects=True, vmem_limit_bytes=56 * MIB
        ),
        name="reduce_grads",
    )(first, second, gains)


HEADS_HERE = 6
TOKENS_HERE = 128
CHIP_TOKENS = 256
GROUP = 2048
Q_BLOCK = 256
K_BLOCK = 512
IN_COLS = 640
OUT_AT = 512
GATE_AT = 768
UP_AT = 1280
DOWN_AT = 1792
MESSAGE_ROWS = 192
bf16 = jnp.bfloat16
f32 = jnp.float32


def dot_nn(left, right):
    return jnp.dot(left, right, preferred_element_type=f32)


def dot_nt(left, right):
    return lax.dot_general(left, right, (((1,), (1,)), ((), ())), preferred_element_type=f32)


def dot_tn(left, right):
    return lax.dot_general(left, right, (((0,), (0,)), ((), ())), preferred_element_type=f32)


def sigmoid(value):
    return 1.0 / (1.0 + jnp.exp(-value))


def norm_scale(rows):
    return lax.rsqrt(jnp.mean(rows * rows, axis=-1, keepdims=True) + norm_eps)


def norm_back(rows, gain, grad):
    scale = norm_scale(rows)
    unit = rows * scale
    inner = grad * gain
    back = scale * (inner - unit * jnp.mean(inner * unit, axis=-1, keepdims=True))
    return back, jnp.sum(grad * unit, axis=0, keepdims=True)


def lower_half(shape):
    return lax.rem(lax.broadcasted_iota(jnp.int32, shape, 1), 64) < 32


def swap_halves(values):
    return jnp.where(
        lower_half(values.shape), pltpu.roll(values, 96, 1), pltpu.roll(values, 32, 1)
    )


def head_owner(y, group, head):
    z = lax.div(head, 3)
    return device_at(y, group, z, lax.rem(lax.rem(head, 3) + z, 4))


def plane_peers():
    y, c, z, x = whereami()
    peers = []
    for core in range(2):
        for dz in range(4):
            for dx in range(4):
                if core + dz + dx > 0:
                    peers.append(device_at(y, lax.rem(c + core, 2), ring(z, dz), ring(x, dx)))
    return peers


def is_owner_here():
    y, c, z, x = whereami()
    return lax.rem(x - z + 4, 4) < 3


def head_here():
    y, c, z, x = whereami()
    return 3 * z + lax.rem(x - z + 4, 4)


class Swap:
    def __init__(self, send, recv, slot):
        self.send, self.recv, self.slot = send, recv, slot

    def start(self, source, target):
        y, c, z, x = whereami()
        self.copy = remote(
            source, target, self.send.at[self.slot], self.recv.at[self.slot], device_at(y, 1 - c, z, x)
        )
        self.copy.start()

    def wait(self):
        self.copy.wait_send()
        self.copy.wait_recv()


class HeadTraffic:
    def __init__(self, outbox, inbox, sems, recv_sem):
        self.outbox, self.inbox, self.sems, self.recv_sem = outbox, inbox, sems, recv_sem

    def to_owner(self, head, group):
        y, c, z, x = whereami()
        block = z * 4 + x
        owner_z = 2 * c + head // 3
        owner_x = lax.rem(head % 3 + owner_z, 4)
        here = (owner_z == z) & (owner_x == x) & (c == group)
        return remote(
            self.outbox.at[head, group],
            self.inbox.at[block],
            self.sems.at[head, group],
            self.recv_sem,
            device_at(y, group, owner_z, owner_x),
        ), here, pltpu.make_async_copy(
            self.outbox.at[head, group], self.inbox.at[block], self.recv_sem
        )

    def send_to_owner(self, head, group):
        copy, here, keep = self.to_owner(head, group)
        pl.when(here)(keep.start)
        pl.when(jnp.logical_not(here))(copy.start)

    def drain_to_owner(self):
        for head in range(HEADS_HERE):
            for group in range(2):
                copy, here, keep = self.to_owner(head, group)
                pl.when(jnp.logical_not(here))(copy.wait_send)

    def to_tokens(self, block):
        y, c, z, x = whereami()
        core = lax.div(z, 2)
        slot = head_here() - HEADS_HERE * core
        block_z, block_x = lax.div(block, 4), lax.rem(block, 4)
        here = (block_z == z) & (block_x == x) & (core == c)
        return remote(
            self.outbox.at[block],
            self.inbox.at[slot, c],
            self.sems.at[block],
            self.recv_sem,
            device_at(y, core, block_z, block_x),
        ), here, pltpu.make_async_copy(self.outbox.at[block], self.inbox.at[slot, c], self.recv_sem)

    def send_to_tokens(self, block):
        copy, here, keep = self.to_tokens(block)
        pl.when(here)(keep.start)
        pl.when(jnp.logical_not(here))(copy.start)

    def drain_to_tokens(self):
        def drain(block, carry):
            copy, here, keep = self.to_tokens(block)
            pl.when(jnp.logical_not(here))(copy.wait_send)
            return carry

        lax.fori_loop(0, 16, drain, 0)

    def arrived(self):
        pltpu.make_async_copy(self.inbox, self.inbox, self.recv_sem).wait()


def allowed_block(start, query_at, key_at):
    shape = (Q_BLOCK, K_BLOCK)
    query = query_at + lax.broadcasted_iota(jnp.int32, shape, 0)
    key = key_at + lax.broadcasted_iota(jnp.int32, shape, 1)
    return (key <= query) & (key >= start)


def attend_forward(queries, keys, values, starts, score_box, output, log_total, blocks_done):
    def one_block(block, carry):
        query_at = pl.multiple_of(block * Q_BLOCK, Q_BLOCK)
        rows = pl.ds(query_at, Q_BLOCK)
        query = queries[rows, :]
        start = starts[rows, :]
        key_blocks = lax.div(block, 2) + 1

        def scores(step, top):
            key_at = pl.multiple_of(step * K_BLOCK, K_BLOCK)
            raw = dot_nt(query, keys[pl.ds(key_at, K_BLOCK), :])
            masked = jnp.where(allowed_block(start, query_at, key_at), raw, mask_fill)
            score_box[step] = masked
            for lane in range(K_BLOCK // 128):
                top = jnp.maximum(top, masked[:, 128 * lane : 128 * lane + 128])
            return top

        top = lax.fori_loop(0, key_blocks, scores, jnp.full((Q_BLOCK, 128), mask_fill, f32))
        top = jnp.max(top, axis=1, keepdims=True)

        def collect(step, state):
            total, gathered = state
            key_at = pl.multiple_of(step * K_BLOCK, K_BLOCK)
            probability = jnp.exp(score_box[step] - top)
            for lane in range(K_BLOCK // 128):
                total = total + probability[:, 128 * lane : 128 * lane + 128]
            return total, gathered + dot_nn(
                probability.astype(bf16), values[pl.ds(key_at, K_BLOCK), :]
            )

        total, gathered = lax.fori_loop(
            0,
            key_blocks,
            collect,
            (jnp.zeros((Q_BLOCK, 128), f32), jnp.zeros((Q_BLOCK, HEAD_DIM), f32)),
        )
        total = jnp.sum(total, axis=1, keepdims=True)
        output[rows, :] = gathered / total
        log_total[rows, :] = top + jnp.log(total)
        blocks_done(block)
        return carry

    lax.fori_loop(0, GROUP // Q_BLOCK, one_block, 0)


def attend_backward(
    queries, keys, values, output_grad, output, log_total, starts, query_grad, key_grad, value_grad
):
    key_grad[...] = jnp.zeros_like(key_grad)
    value_grad[...] = jnp.zeros_like(value_grad)

    def one_block(block, carry):
        query_at = pl.multiple_of(block * Q_BLOCK, Q_BLOCK)
        rows = pl.ds(query_at, Q_BLOCK)
        query = queries[rows, :]
        grad = output_grad[rows, :]
        start = starts[rows, :]
        logs = log_total[rows, :]
        inner = jnp.sum(grad.astype(f32) * output[rows, :], axis=1, keepdims=True)

        def one_key(step, total):
            key_at = pl.multiple_of(step * K_BLOCK, K_BLOCK)
            keys_here = pl.ds(key_at, K_BLOCK)
            raw = dot_nt(query, keys[keys_here, :])
            masked = jnp.where(allowed_block(start, query_at, key_at), raw, mask_fill)
            probability = jnp.exp(masked - logs)
            probability_grad = dot_nt(grad, values[keys_here, :])
            score_grad = (probability * (probability_grad - inner)).astype(bf16)
            key_grad[keys_here, :] += dot_tn(score_grad, query)
            value_grad[keys_here, :] += dot_tn(probability.astype(bf16), grad)
            return total + dot_nn(score_grad, keys[keys_here, :])

        query_grad[rows, :] = lax.fori_loop(
            0, lax.div(block, 2) + 1, one_key, jnp.zeros((Q_BLOCK, HEAD_DIM), f32)
        )
        return carry

    lax.fori_loop(0, GROUP // Q_BLOCK, one_block, 0)


def forward_kernel(
    layer,
    rows_in,
    gains,
    weights_hbm,
    tables,
    starts,
    rows_out,
    mid_rows,
    normed,
    normed_mid,
    gate_up,
    attended,
    queries,
    keys,
    values,
    log_total,
    output,
    weights,
    message,
    inbox,
    reply,
    reply_box,
    score_box,
    partial_out,
    partial_in,
    load_sem,
    swap_send,
    swap_recv,
    ask_send,
    reply_send,
    traffic_recv,
):
    y, c, z, x = whereami()
    first_load = pltpu.make_async_copy(
        weights_hbm.at[layer, :, :, pl.ds(0, GATE_AT)],
        weights.at[:, :, pl.ds(0, GATE_AT)],
        load_sem.at[0],
    )
    second_load = pltpu.make_async_copy(
        weights_hbm.at[layer, :, :, pl.ds(GATE_AT, PACK_COLS - GATE_AT)],
        weights.at[:, :, pl.ds(GATE_AT, PACK_COLS - GATE_AT)],
        load_sem.at[1],
    )
    first_load.start()
    second_load.start()
    swaps = [Swap(swap_send, swap_recv, slot) for slot in range(4)]
    rows = rows_in[...]
    normed[c] = (rows * norm_scale(rows) * gains[0:1, :]).astype(bf16)
    greet(plane_peers())
    swaps[0].start(normed.at[c], normed.at[c])
    first_load.wait()
    swaps[0].wait()
    ask = HeadTraffic(message, inbox, ask_send, traffic_recv.at[0])
    chip_normed = normed[...].reshape(CHIP_TOKENS, D)
    cosine = tables[:, :, 0:128].reshape(CHIP_TOKENS, 128)
    sine = tables[:, :, 128:256].reshape(CHIP_TOKENS, 128)
    for side in range(2):
        mixed = dot_nn(chip_normed, weights[side, :, 0:IN_COLS])
        for inner in range(3):
            head = 3 * side + inner
            pair = mixed[:, 128 * inner : 128 * inner + 128]
            pair = (pair * cosine + swap_halves(pair) * sine).astype(bf16)
            value = mixed[:, 384 + 64 * inner : 448 + 64 * inner]
            for group in range(2):
                at = TOKENS_HERE * group
                message[head, group, 0:128] = pair[at : at + 128]
                message[head, group, 128:192] = jnp.concatenate(
                    [value[at : at + 64], value[at + 64 : at + 128]], axis=1
                ).astype(bf16)
                ask.send_to_owner(head, group)

    answer = HeadTraffic(reply, reply_box, reply_send, traffic_recv.at[1])

    @pl.when(is_owner_here())
    def _():
        ask.arrived()

        def place(block, carry):
            at = pl.multiple_of(block * TOKENS_HERE, TOKENS_HERE)
            pair = inbox[block, 0:128].astype(f32)
            queries[pl.ds(at, 128), :] = (pair[:, 0:64] * (1.0 / math.sqrt(HEAD_DIM))).astype(bf16)
            keys[pl.ds(at, 128), :] = pair[:, 64:128].astype(bf16)
            both = inbox[block, 128:192].astype(f32)
            values[pl.ds(at, 128), :] = jnp.concatenate([both[:, 0:64], both[:, 64:128]], axis=0).astype(
                bf16
            )
            return carry

        lax.fori_loop(0, 16, place, 0)

        def send_rows(block):
            for half in range(2):
                at = pl.multiple_of(block * Q_BLOCK + half * 128, 128)
                first = output[pl.ds(at, 64), :]
                second = output[pl.ds(at + 64, 64), :]
                reply[2 * block + half] = jnp.concatenate([first, second], axis=1).astype(bf16)
                answer.send_to_tokens(2 * block + half)

        attend_forward(queries, keys, values, starts, score_box, output, log_total, send_rows)

    answer.arrived()
    partial = None
    for side in range(2):
        columns = [jnp.zeros((CHIP_TOKENS, 64), f32)]
        for inner in range(3):
            pieces = []
            for group in range(2):
                both = reply_box[3 * side + inner, group].astype(f32)
                pieces += [both[:, 0:64], both[:, 64:128]]
            columns.append(jnp.concatenate(pieces, axis=0))
        attended[side] = jnp.concatenate(columns, axis=1).astype(bf16)
        term = dot_nt(attended[side], weights[side, :, OUT_AT:GATE_AT])
        partial = term if partial is None else partial + term
    partial_out[0] = partial.astype(bf16)
    mine = pl.ds(pl.multiple_of(c * TOKENS_HERE, TOKENS_HERE), TOKENS_HERE)
    theirs = pl.ds(pl.multiple_of((1 - c) * TOKENS_HERE, TOKENS_HERE), TOKENS_HERE)
    swaps[1].start(partial_out.at[0, theirs], partial_in.at[0])
    own_part = jnp.where(c == 0, partial[0:TOKENS_HERE], partial[TOKENS_HERE:CHIP_TOKENS])
    swaps[1].wait()
    middle = rows_in[...] + (own_part + partial_in[0].astype(f32))
    mid_rows[...] = middle
    normed_mid[c] = (middle * norm_scale(middle) * gains[1:2, :]).astype(bf16)
    swaps[2].start(normed_mid.at[c], normed_mid.at[c])
    second_load.wait()
    swaps[2].wait()
    chip_mid = normed_mid[...].reshape(CHIP_TOKENS, D)
    partial = None
    for side in range(2):
        gate = dot_nn(chip_mid, weights[side, :, GATE_AT:UP_AT])
        up = dot_nn(chip_mid, weights[side, :, UP_AT:DOWN_AT])
        gate_up[side, 0] = gate
        gate_up[side, 1] = up
        active = (gate * sigmoid(gate) * up).astype(bf16)
        term = dot_nt(active, weights[side, :, DOWN_AT:PACK_COLS])
        partial = term if partial is None else partial + term
    partial_out[1] = partial.astype(bf16)
    swaps[3].start(partial_out.at[1, theirs], partial_in.at[1])
    own_part = jnp.where(c == 0, partial[0:TOKENS_HERE], partial[TOKENS_HERE:CHIP_TOKENS])
    swaps[3].wait()
    rows_out[...] = mid_rows[...] + (own_part + partial_in[1].astype(f32))
    ask.drain_to_owner()

    @pl.when(is_owner_here())
    def _():
        answer.drain_to_tokens()


def vmem_specs(count):
    return [pl.BlockSpec(memory_space=pltpu.VMEM)] * count


def forward_layer(layer, rows, gains, weights_all, tables, starts):
    shape = jax.ShapeDtypeStruct
    return pl.pallas_call(
        lambda *refs: forward_kernel(layer, *refs),
        out_shape=[
            shape((TOKENS_HERE, D), f32),
            shape((TOKENS_HERE, D), f32),
            shape((2, TOKENS_HERE, D), bf16),
            shape((2, TOKENS_HERE, D), bf16),
            shape((2, 2, CHIP_TOKENS, 512), f32),
            shape((2, CHIP_TOKENS, 256), bf16),
            shape((GROUP, HEAD_DIM), bf16),
            shape((GROUP, HEAD_DIM), bf16),
            shape((GROUP, HEAD_DIM), bf16),
            shape((GROUP, 1), f32),
            shape((GROUP, HEAD_DIM), f32),
        ],
        in_specs=vmem_specs(2) + [pl.BlockSpec(memory_space=pltpu.HBM)] + vmem_specs(2),
        out_specs=vmem_specs(11),
        scratch_shapes=[
            pltpu.VMEM((2, D, PACK_COLS), bf16),
            pltpu.VMEM((HEADS_HERE, 2, MESSAGE_ROWS, 128), bf16),
            pltpu.VMEM((16, MESSAGE_ROWS, 128), bf16),
            pltpu.VMEM((16, 64, 128), bf16),
            pltpu.VMEM((HEADS_HERE, 2, 64, 128), bf16),
            pltpu.VMEM((GROUP // K_BLOCK, Q_BLOCK, K_BLOCK), f32),
            pltpu.VMEM((2, CHIP_TOKENS, D), bf16),
            pltpu.VMEM((2, TOKENS_HERE, D), bf16),
            pltpu.SemaphoreType.DMA((2,)),
            pltpu.SemaphoreType.DMA((4,)),
            pltpu.SemaphoreType.DMA((4,)),
            pltpu.SemaphoreType.DMA((HEADS_HERE, 2)),
            pltpu.SemaphoreType.DMA((16,)),
            pltpu.SemaphoreType.DMA((2,)),
        ],
        compiler_params=pltpu.CompilerParams(
            collective_id=3 + layer, has_side_effects=True, vmem_limit_bytes=52 * MIB
        ),
        name="forward_layer",
    )(rows, gains, weights_all, tables, starts)


def backward_kernel(
    layer,
    rows_grad,
    rows_in,
    mid_rows,
    gains,
    weights_hbm,
    tables,
    starts,
    normed,
    normed_mid,
    gate_up,
    attended,
    queries,
    keys,
    values,
    log_total,
    output,
    grad_out,
    gain_grads,
    grads,
    weights,
    grad_swap,
    partial_out,
    partial_in,
    message,
    inbox,
    output_grad,
    query_grad,
    key_grad,
    value_grad,
    reply,
    reply_box,
    mixed_grad,
    load_sem,
    swap_send,
    swap_recv,
    ask_send,
    reply_send,
    traffic_recv,
):
    y, c, z, x = whereami()
    load = pltpu.make_async_copy(weights_hbm.at[layer], weights, load_sem.at[0])
    load.start()
    swaps = [Swap(swap_send, swap_recv, slot) for slot in range(4)]
    theirs = pl.ds(pl.multiple_of((1 - c) * TOKENS_HERE, TOKENS_HERE), TOKENS_HERE)

    def own_of(partial):
        return jnp.where(c == 0, partial[0:TOKENS_HERE], partial[TOKENS_HERE:CHIP_TOKENS])

    def weight_grad(side, columns, left_t, right):
        grads[side, :, columns] = dot_nn(left_t, right).astype(bf16)

    grad_swap[0, c] = rows_grad[...].astype(bf16)
    greet(plane_peers())
    swaps[0].start(grad_swap.at[0, c], grad_swap.at[0, c])
    load.wait()
    swaps[0].wait()
    down = grad_swap[0].reshape(CHIP_TOKENS, D)
    down_t = down.T
    mid_t = normed_mid[...].reshape(CHIP_TOKENS, D).T
    partial = None
    for side in range(2):
        gate = gate_up[side, 0]
        up = gate_up[side, 1]
        active_grad = dot_nn(down, weights[side, :, DOWN_AT:PACK_COLS])
        sigma = sigmoid(gate)
        active = gate * sigma
        gate_grad = (active_grad * up * sigma * (1.0 + gate * (1.0 - sigma))).astype(bf16)
        up_grad = (active_grad * active).astype(bf16)
        weight_grad(side, slice(DOWN_AT, PACK_COLS), down_t, (active * up).astype(bf16))
        weight_grad(side, slice(GATE_AT, UP_AT), mid_t, gate_grad)
        weight_grad(side, slice(UP_AT, DOWN_AT), mid_t, up_grad)
        term = dot_nt(gate_grad, weights[side, :, GATE_AT:UP_AT]) + dot_nt(
            up_grad, weights[side, :, UP_AT:DOWN_AT]
        )
        partial = term if partial is None else partial + term
    partial_out[0] = partial.astype(bf16)
    swaps[1].start(partial_out.at[0, theirs], partial_in.at[0])
    own_part = own_of(partial)
    swaps[1].wait()
    back, gain_grad = norm_back(
        mid_rows[...], gains[1:2, :], own_part + partial_in[0].astype(f32)
    )
    mid_grad = rows_grad[...] + back
    gain_grads[1:2, :] = gain_grad
    grad_swap[1, c] = mid_grad.astype(bf16)
    swaps[2].start(grad_swap.at[1, c], grad_swap.at[1, c])
    swaps[2].wait()
    branch = grad_swap[1].reshape(CHIP_TOKENS, D)
    ask = HeadTraffic(message, inbox, ask_send, traffic_recv.at[0])
    for side in range(2):
        heads_grad = dot_nn(branch, weights[side, :, OUT_AT:GATE_AT])
        for inner in range(3):
            head = 3 * side + inner
            piece = heads_grad[:, 64 + 64 * inner : 128 + 64 * inner]
            for group in range(2):
                at = TOKENS_HERE * group
                message[head, group] = jnp.concatenate(
                    [piece[at : at + 64], piece[at + 64 : at + 128]], axis=1
                ).astype(bf16)
                ask.send_to_owner(head, group)
    branch_t = branch.T
    for side in range(2):
        weight_grad(side, slice(OUT_AT, GATE_AT), branch_t, attended[side])
    answer = HeadTraffic(reply, reply_box, reply_send, traffic_recv.at[1])

    @pl.when(is_owner_here())
    def _():
        ask.arrived()

        def place(block, carry):
            at = pl.multiple_of(block * TOKENS_HERE, TOKENS_HERE)
            both = inbox[block].astype(f32)
            output_grad[pl.ds(at, 128), :] = jnp.concatenate(
                [both[:, 0:64], both[:, 64:128]], axis=0
            ).astype(bf16)
            return carry

        lax.fori_loop(0, 16, place, 0)
        attend_backward(
            queries,
            keys,
            values,
            output_grad,
            output,
            log_total,
            starts,
            query_grad,
            key_grad,
            value_grad,
        )

        def give(block, carry):
            at = pl.multiple_of(block * TOKENS_HERE, TOKENS_HERE)
            reply[block, 0:128] = jnp.concatenate(
                [
                    query_grad[pl.ds(at, 128), :] * (1.0 / math.sqrt(HEAD_DIM)),
                    key_grad[pl.ds(at, 128), :],
                ],
                axis=1,
            ).astype(bf16)
            reply[block, 128:192] = jnp.concatenate(
                [value_grad[pl.ds(at, 64), :], value_grad[pl.ds(at + 64, 64), :]], axis=1
            ).astype(bf16)
            answer.send_to_tokens(block)
            return carry

        lax.fori_loop(0, 16, give, 0)

    answer.arrived()
    cosine = tables[:, :, 0:128].reshape(CHIP_TOKENS, 128)
    sine = tables[:, :, 128:256].reshape(CHIP_TOKENS, 128)
    normed_t = normed[...].reshape(CHIP_TOKENS, D).T
    partial = None
    for side in range(2):
        pieces = []
        for inner in range(3):
            head = 3 * side + inner
            pair = jnp.concatenate([reply_box[head, 0, 0:128], reply_box[head, 1, 0:128]], axis=0)
            pair = pair.astype(f32)
            pair = pair * cosine - swap_halves(pair) * sine
            mixed_grad[side, :, 128 * inner : 128 * inner + 128] = pair.astype(bf16)
            rows = []
            for group in range(2):
                both = reply_box[head, group, 128:192].astype(f32)
                rows += [both[:, 0:64], both[:, 64:128]]
            pieces.append(jnp.concatenate(rows, axis=0))
        pieces.append(jnp.zeros((CHIP_TOKENS, 64), f32))
        mixed_grad[side, :, 384:IN_COLS] = jnp.concatenate(pieces, axis=1).astype(bf16)
        weight_grad(side, slice(0, OUT_AT), normed_t, mixed_grad[side, :, 0:OUT_AT])
        last = dot_nn(normed_t, mixed_grad[side, :, OUT_AT:IN_COLS])
        grads[side, :, OUT_AT:IN_COLS] = (
            grads[side, :, OUT_AT:IN_COLS].astype(f32) + last
        ).astype(bf16)
        term = dot_nt(mixed_grad[side], weights[side, :, 0:IN_COLS])
        partial = term if partial is None else partial + term
    partial_out[1] = partial.astype(bf16)
    swaps[3].start(partial_out.at[1, theirs], partial_in.at[1])
    own_part = own_of(partial)
    swaps[3].wait()
    back, gain_grad = norm_back(rows_in[...], gains[0:1, :], own_part + partial_in[1].astype(f32))
    gain_grads[0:1, :] = gain_grad
    grad_out[...] = mid_grad + back
    ask.drain_to_owner()

    @pl.when(is_owner_here())
    def _():
        answer.drain_to_tokens()


def backward_layer(layer, rows_grad, rows_in, mid_rows, gains, weights_all, tables, starts, kept):
    shape = jax.ShapeDtypeStruct
    return pl.pallas_call(
        lambda *refs: backward_kernel(layer, *refs),
        out_shape=[
            shape((TOKENS_HERE, D), f32),
            shape((8, D), f32),
            shape((2, D, PACK_COLS), bf16),
        ],
        in_specs=vmem_specs(4) + [pl.BlockSpec(memory_space=pltpu.HBM)] + vmem_specs(11),
        out_specs=vmem_specs(3),
        scratch_shapes=[
            pltpu.VMEM((2, D, PACK_COLS), bf16),
            pltpu.VMEM((2, 2, TOKENS_HERE, D), bf16),
            pltpu.VMEM((2, CHIP_TOKENS, D), bf16),
            pltpu.VMEM((2, TOKENS_HERE, D), bf16),
            pltpu.VMEM((HEADS_HERE, 2, 64, 128), bf16),
            pltpu.VMEM((16, 64, 128), bf16),
            pltpu.VMEM((GROUP, HEAD_DIM), bf16),
            pltpu.VMEM((GROUP, HEAD_DIM), f32),
            pltpu.VMEM((GROUP, HEAD_DIM), f32),
            pltpu.VMEM((GROUP, HEAD_DIM), f32),
            pltpu.VMEM((16, MESSAGE_ROWS, 128), bf16),
            pltpu.VMEM((HEADS_HERE, 2, MESSAGE_ROWS, 128), bf16),
            pltpu.VMEM((2, CHIP_TOKENS, IN_COLS), bf16),
            pltpu.SemaphoreType.DMA((1,)),
            pltpu.SemaphoreType.DMA((4,)),
            pltpu.SemaphoreType.DMA((4,)),
            pltpu.SemaphoreType.DMA((HEADS_HERE, 2)),
            pltpu.SemaphoreType.DMA((16,)),
            pltpu.SemaphoreType.DMA((2,)),
        ],
        compiler_params=pltpu.CompilerParams(
            collective_id=5 + layer, has_side_effects=True, vmem_limit_bytes=56 * MIB
        ),
        name="backward_layer",
    )(rows_grad, rows_in, mid_rows, gains, weights_all, tables, starts, *kept)


SQUARE_COUNT = 8
WIDE_COUNT = 6
OWNERS = SQUARE_COUNT + WIDE_COUNT


def owner_place(matrix):
    return (matrix // 4, 0, (matrix // 4 + matrix % 4) % 4, matrix % 4)


def device_of_index(index):
    return (lax.div(index, 16), lax.rem(lax.div(index, 4), 4), lax.rem(index, 4))


def ns_step(source, target, gram, columns):
    blocks = D // 256

    def gram_rows(block, carry):
        rows = pl.ds(pl.multiple_of(block * 256, 256), 256)
        gram[rows, :] = lax.dot_general(
            source[rows, 0:columns],
            source[:, 0:columns],
            (((1,), (1,)), ((), ())),
            preferred_element_type=jnp.float32,
        ).astype(jnp.bfloat16)
        return carry

    lax.fori_loop(0, blocks, gram_rows, 0)

    def update_rows(block, carry):
        rows = pl.ds(pl.multiple_of(block * 256, 256), 256)
        gram_block = gram[rows, :]
        polynomial = (
            quintic_two * gram_block.astype(jnp.float32)
            + quintic_three
            * jnp.dot(gram_block, gram[...], preferred_element_type=jnp.float32)
        ).astype(jnp.bfloat16)
        for start in range(0, columns, 512):
            part = slice(start, start + 512)
            target[rows, part] = (
                quintic_one * source[rows, part].astype(jnp.float32)
                + jnp.dot(polynomial, source[:, part], preferred_element_type=jnp.float32)
            ).astype(jnp.bfloat16)
        return carry

    lax.fori_loop(0, blocks, update_rows, 0)


def orthogonal_owner(slots, front, back, gram, wide):
    columns = 2048 if wide else 1024
    slot_rows = PAIR_ROWS if wide else 32

    def add_squares(index, carry):
        value = slots[index, 0:slot_rows, :].astype(jnp.float32)
        return carry + jnp.sum(value * value, axis=0, keepdims=True)

    squares = lax.fori_loop(0, 128, add_squares, jnp.zeros((1, 256), jnp.float32))
    norm = jnp.sqrt(jnp.sum(squares, axis=1, keepdims=True)) + ortho_eps
    scale = 1.0 / norm

    def assemble(pair, carry):
        rows = pl.ds(pl.multiple_of(pair * PAIR_ROWS, PAIR_ROWS), PAIR_ROWS)
        for part in range(4):
            first = slots[pair * 8 + part, 0:slot_rows, :].astype(jnp.float32) * scale
            second = slots[pair * 8 + 4 + part, 0:slot_rows, :].astype(jnp.float32) * scale
            joined = jnp.concatenate([first[0:24], second[0:24]], axis=0).astype(jnp.bfloat16)
            if wide:
                front[rows, part * 512 : part * 512 + 256] = joined
                front[rows, part * 512 + 256 : part * 512 + 512] = jnp.concatenate(
                    [first[24:48], second[24:48]], axis=0
                ).astype(jnp.bfloat16)
            else:
                front[rows, part * 256 : part * 256 + 256] = joined
        return carry

    lax.fori_loop(0, 16, assemble, 0)

    def two_steps(index, carry):
        ns_step(front, back, gram, columns)
        ns_step(back, front, gram, columns)
        return carry

    lax.fori_loop(0, NS_STEPS // 2, two_steps, 0)

    def take_apart(pair, carry):
        rows = pl.ds(pl.multiple_of(pair * PAIR_ROWS, PAIR_ROWS), PAIR_ROWS)
        for part in range(4):
            if wide:
                left = front[rows, part * 512 : part * 512 + 256].astype(jnp.float32)
                right = front[rows, part * 512 + 256 : part * 512 + 512].astype(jnp.float32)
                slots[pair * 8 + part] = jnp.concatenate([left[0:24], right[0:24]], axis=0).astype(
                    jnp.bfloat16
                )
                slots[pair * 8 + 4 + part] = jnp.concatenate(
                    [left[24:48], right[24:48]], axis=0
                ).astype(jnp.bfloat16)
            else:
                left = front[rows, part * 256 : part * 256 + 256].astype(jnp.float32)
                slots[pair * 8 + part, 0:32] = left[0:32].astype(jnp.bfloat16)
                slots[pair * 8 + 4 + part, 0:32] = jnp.concatenate(
                    [left[24:48], left[0:8]], axis=0
                ).astype(jnp.bfloat16)
        return carry

    lax.fori_loop(0, 16, take_apart, 0)


def muon_kernel(square, wide, square_new, wide_new, slots, front, back, gram, send, recv, slot_recv, slot_send):
    y, c, z, x = whereami()
    mine = (y * 2 + c) * 16 + z * 4 + x
    barrier = pltpu.get_barrier_semaphore()
    places = [owner_place(m) for m in range(OWNERS)]
    indices = [(p[0] * 2 + p[1]) * 16 + p[2] * 4 + p[3] for p in places]
    is_square_owner = (c == 0) & (z == ring(x, y)) & (y < 2)
    is_wide_owner = (c == 0) & (z == ring(x, y)) & ((y == 2) | ((y == 3) & (x < 2)))
    is_owner = is_square_owner | is_wide_owner

    @pl.when(is_owner)
    def _():
        def greet_one(index, carry):
            @pl.when(index != mine)
            def _():
                pl.semaphore_signal(
                    barrier, inc=1, device_id=device_of_index(index), device_id_type=MESH_ID
                )

            return carry

        lax.fori_loop(0, 128, greet_one, 0)
        pl.semaphore_wait(barrier, 127)

    @pl.when(jnp.logical_not(is_owner))
    def _():
        for m in range(OWNERS):
            pl.semaphore_signal(
                barrier, inc=1, device_id=device_at(*places[m]), device_id_type=MESH_ID
            )
        pl.semaphore_wait(barrier, OWNERS)

    def outbound(m):
        if m < SQUARE_COUNT:
            return square.at[m], slots.at[mine, pl.ds(0, 32)]
        return wide.at[m - SQUARE_COUNT], slots.at[mine]

    def inbound(m):
        return square_new.at[m] if m < SQUARE_COUNT else wide_new.at[m - SQUARE_COUNT]

    for m in range(OWNERS):
        source, target = outbound(m)

        @pl.when(mine != indices[m])
        def _(source=source, target=target, m=m):
            remote(source, target, send.at[m], slot_recv, device_at(*places[m])).start()

        @pl.when(mine == indices[m])
        def _(source=source, target=target, m=m):
            copy = pltpu.make_async_copy(source, target, send.at[m])
            copy.start()
            copy.wait()

    def serve(is_wide):
        slot_rows = PAIR_ROWS if is_wide else 32
        whole = slots.at[pl.ds(0, 127), pl.ds(0, slot_rows)]
        remote(whole, whole, slot_send, slot_recv, device_at(y, c, z, x)).wait_recv()
        orthogonal_owner(slots, front, back, gram, is_wide)
        matrix = y * 4 + x

        def answer(index, carry):
            @pl.when(index != mine)
            def _():
                if is_wide:
                    remote(
                        slots.at[index],
                        wide_new.at[matrix - SQUARE_COUNT],
                        slot_send,
                        recv.at[matrix],
                        device_of_index(index),
                    ).start()
                else:
                    remote(
                        slots.at[index, pl.ds(0, 32)],
                        square_new.at[matrix],
                        slot_send,
                        recv.at[matrix],
                        device_of_index(index),
                    ).start()

            return carry

        lax.fori_loop(0, 128, answer, 0)
        if is_wide:
            wide_new[matrix - SQUARE_COUNT] = slots[mine]
        else:
            square_new[matrix] = slots[mine, 0:32]
        remote(whole, whole, slot_send, slot_recv, device_at(y, c, z, x)).wait_send()

    @pl.when(is_square_owner)
    def _():
        serve(False)

    @pl.when(is_wide_owner)
    def _():
        serve(True)

    for m in range(OWNERS):
        source, target = outbound(m)

        @pl.when(mine != indices[m])
        def _(source=source, target=target, m=m):
            copy = remote(source, inbound(m), send.at[m], recv.at[m], device_at(*places[m]))
            copy.wait_send()
            copy.wait_recv()


def muon(square, wide):
    return pl.pallas_call(
        muon_kernel,
        out_shape=[
            jax.ShapeDtypeStruct(square.shape, jnp.bfloat16),
            jax.ShapeDtypeStruct(wide.shape, jnp.bfloat16),
        ],
        in_specs=[pl.BlockSpec(memory_space=pltpu.VMEM)] * 2,
        out_specs=[pl.BlockSpec(memory_space=pltpu.VMEM)] * 2,
        scratch_shapes=[
            pltpu.VMEM((128, PAIR_ROWS, 256), jnp.bfloat16),
            pltpu.VMEM((D, FF), jnp.bfloat16),
            pltpu.VMEM((D, FF), jnp.bfloat16),
            pltpu.VMEM((D, D), jnp.bfloat16),
            pltpu.SemaphoreType.DMA((OWNERS,)),
            pltpu.SemaphoreType.DMA((OWNERS,)),
            pltpu.SemaphoreType.DMA,
            pltpu.SemaphoreType.DMA,
        ],
        compiler_params=pltpu.CompilerParams(
            collective_id=2, has_side_effects=True, vmem_limit_bytes=56 * MIB
        ),
        name="muon",
    )(square, wide)


def pack_layers(attend_in, attend_out, expand, shrink):
    query_key = jnp.stack(
        [attend_in[:, k].reshape(LAYERS, ROW_SHARD, 3, HEAD_DIM) for k in range(2)], axis=3
    )
    return jnp.concatenate(
        [
            query_key.reshape(LAYERS, ROW_SHARD, 384),
            attend_in[:, 2],
            jnp.swapaxes(attend_out, 1, 2),
            expand[:, 0],
            expand[:, 1],
            jnp.swapaxes(shrink, 1, 2),
        ],
        axis=2,
    )


def four_squares(packed):
    query_key = packed[:, :, 0:384].reshape(LAYERS, ROW_SHARD, 3, 2, HEAD_DIM)
    return [
        query_key[:, :, :, 0].reshape(LAYERS, ROW_SHARD, 192),
        query_key[:, :, :, 1].reshape(LAYERS, ROW_SHARD, 192),
        packed[:, :, 384:576],
        packed[:, :, 576:768],
    ]


def unpack_layers(packed):
    query, key, value, out = four_squares(packed)
    return (
        jnp.stack([query, key, value], axis=1),
        jnp.swapaxes(out, 1, 2),
        jnp.stack([packed[:, :, 768:1280], packed[:, :, 1280:1792]], axis=1),
        jnp.swapaxes(packed[:, :, 1792:2304], 1, 2),
    )


def square_tiles(packed):
    tiles = jnp.stack(four_squares(packed), axis=1).reshape(SQUARE_COUNT, ROW_SHARD, 192)
    return jnp.pad(tiles, ((0, 0), (0, 8), (0, 64)))


def wide_tiles(packed):
    tiles = packed[:, :, 768:2304].reshape(LAYERS, ROW_SHARD, 3, 2, 256).transpose(0, 2, 3, 1, 4)
    return tiles.reshape(WIDE_COUNT, PAIR_ROWS, 256)


def untile(square_new, wide_new):
    square = square_new[:, 0:ROW_SHARD, 0:192].reshape(LAYERS, 4, ROW_SHARD, 192)
    query_key = jnp.stack(
        [square[:, k].reshape(LAYERS, ROW_SHARD, 3, HEAD_DIM) for k in range(2)], axis=3
    )
    wide = wide_new.reshape(LAYERS, 3, 2, ROW_SHARD, 256).transpose(0, 3, 1, 2, 4)
    return jnp.concatenate(
        [
            query_key.reshape(LAYERS, ROW_SHARD, 384),
            square[:, 2],
            square[:, 3],
            wide.reshape(LAYERS, ROW_SHARD, 1536),
        ],
        axis=2,
    )


def to_chip_order(values):
    split = values.reshape(values.shape[:-1] + (4, 2, 4, ROW_SHARD))
    return jnp.swapaxes(split, -3, -2).reshape(values.shape)


def from_chip_order(values):
    split = values.reshape(values.shape[:-1] + (4, 4, 2, ROW_SHARD))
    return jnp.swapaxes(split, -3, -2).reshape(values.shape)


def rope_table(positions):
    frequency = rope_base ** (-jnp.arange(HEAD_DIM // 2, dtype=jnp.float32) * 2.0 / HEAD_DIM)
    angles = positions.astype(jnp.float32)[:, None] * frequency[None, :]
    cosine, sine_part = jnp.cos(angles), jnp.sin(angles)
    return jnp.concatenate(
        [cosine, cosine, cosine, cosine, -sine_part, sine_part, -sine_part, sine_part], axis=1
    )


def body(
    hidden_in,
    out_grad,
    seq_lengths,
    norm_gains,
    gain_first,
    gain_second,
    attend_in,
    attend_out,
    expand,
    shrink,
    attend_in_moment,
    attend_out_moment,
    expand_moment,
    shrink_moment,
):
    document, position, places = doc_layout(seq_lengths[0], GROUP)
    starts = (places - position)[:, None]
    token_block = lax.axis_index("ctx") * 4 + lax.axis_index("tp")
    table = rope_table(
        lax.dynamic_slice_in_dim(position, token_block * TOKENS_HERE, TOKENS_HERE)
    )
    weights_packed = pack_layers(attend_in, attend_out, expand, shrink)
    weights_all, tables = gather_weights(
        weights_packed.astype(jnp.bfloat16).reshape(LAYERS * ROW_SHARD, PACK_COLS), table
    )
    weights_all = weights_all.reshape(LAYERS, 2, D, PACK_COLS)
    gains = jnp.pad(to_chip_order(norm_gains), ((0, 0), (0, 6), (0, 0)))
    rows = to_chip_order(hidden_in).astype(jnp.float32)
    saved = []
    for layer in range(LAYERS):
        rows_in = rows
        rows, mid_rows, *kept = forward_layer(
            layer, rows_in, gains[layer], weights_all, tables, starts
        )
        saved.append((rows_in, mid_rows, kept))
    rows_grad = to_chip_order(out_grad).astype(jnp.float32)
    grads = [None] * LAYERS
    gain_terms = [None] * LAYERS
    for layer in reversed(range(LAYERS)):
        rows_in, mid_rows, kept = saved[layer]
        rows_grad, gain_rows, grads[layer] = backward_layer(
            layer, rows_grad, rows_in, mid_rows, gains[layer], weights_all, tables, starts, kept
        )
        gain_terms[layer] = gain_rows[0:2]
    gains_packed = jnp.pad(jnp.concatenate(gain_terms, axis=0), ((0, 4), (0, 0)))
    split = (2, 4, 4, PAIR_ROWS, PACK_COLS)
    grad_total, gain_total = reduce_grads(
        grads[0].reshape(split), grads[1].reshape(split), gains_packed
    )
    gain_grad = from_chip_order(gain_total[0:4]).reshape(LAYERS, 2, D)
    gain_first_new = first_decay * gain_first + (1.0 - first_decay) * gain_grad
    gain_second_new = second_decay * gain_second + (1.0 - second_decay) * gain_grad * gain_grad
    norm_gains_new = norm_gains - gain_rate * (gain_first_new / (1.0 - first_decay**STEP)) / (
        jnp.sqrt(gain_second_new / (1.0 - second_decay**STEP)) + adam_eps
    )
    moment_packed = pack_layers(attend_in_moment, attend_out_moment, expand_moment, shrink_moment)
    moment_new = moment_decay * moment_packed + grad_total.reshape(LAYERS, ROW_SHARD, PACK_COLS)
    sent = moment_new.astype(jnp.bfloat16)
    square_new, wide_new = muon(square_tiles(sent), wide_tiles(sent))
    orthogonal = untile(square_new, wide_new).astype(jnp.float32)
    column = jnp.arange(PACK_COLS, dtype=jnp.int32)
    rate = jnp.where((column >= 576) & (column < 768), project_rate, matrix_rate)
    factor = jnp.where(column < 768, 0.2 * math.sqrt(D), 0.2 * math.sqrt(FF))
    weights_new = weights_packed - rate * (factor * orthogonal + matrix_decay * weights_packed)
    return (
        from_chip_order(rows),
        from_chip_order(rows_grad),
        gain_first_new,
        gain_second_new,
        norm_gains_new,
        *unpack_layers(moment_new),
        *unpack_layers(weights_new),
    )


def solution(mesh):
    placed = (
        P(("fsdp", "ctx", "tp"), None),
        P(("fsdp", "ctx", "tp"), None),
        P("fsdp", None),
        P(),
        P(),
        P(),
        P(None, None, ("fsdp", "ctx"), "tp"),
        P(None, "tp", ("fsdp", "ctx")),
        P(None, None, ("fsdp", "ctx"), "tp"),
        P(None, "tp", ("fsdp", "ctx")),
        P(None, None, ("fsdp", "ctx"), "tp"),
        P(None, "tp", ("fsdp", "ctx")),
        P(None, None, ("fsdp", "ctx"), "tp"),
        P(None, "tp", ("fsdp", "ctx")),
    )
    return jax.shard_map(
        body,
        mesh=mesh,
        in_specs=placed,
        out_specs=(
            P(("fsdp", "ctx", "tp"), None),
            P(("fsdp", "ctx", "tp"), None),
            P(),
            P(),
            P(),
            P(None, None, ("fsdp", "ctx"), "tp"),
            P(None, "tp", ("fsdp", "ctx")),
            P(None, None, ("fsdp", "ctx"), "tp"),
            P(None, "tp", ("fsdp", "ctx")),
            P(None, None, ("fsdp", "ctx"), "tp"),
            P(None, "tp", ("fsdp", "ctx")),
            P(None, None, ("fsdp", "ctx"), "tp"),
            P(None, "tp", ("fsdp", "ctx")),
        ),
        check_vma=False,
    )
```

```python
import math
import types

import jax
import jax.numpy as jnp
from jax import lax
from jax.experimental import pallas as pl
from jax.experimental.pallas import tpu as pltpu
from jax.sharding import PartitionSpec as P

D = 768
HEAD_DIM = 64
FF = 2048
NS_STEPS = 4
STEP = 5


norm_eps = 1e-05
rope_base = 10000.0
mask_fill = -1e30
quintic_one = 3.4445
quintic_two = -4.775
quintic_three = 2.0315
moment_decay = 0.95
matrix_rate = 0.1
project_rate = 0.8
matrix_decay = 0.1
gain_rate = 0.8
first_decay = 0.9
second_decay = 0.95
adam_eps = 1e-08
ortho_eps = 1e-07


def doc_layout(lengths, row_count):
    doc_ends = jnp.cumsum(lengths)
    starts = doc_ends - lengths
    places = jnp.arange(row_count, dtype=jnp.int32)
    document = jnp.sum((places[:, None] >= doc_ends[None, :]).astype(jnp.int32), axis=1)
    member = document[:, None] == jnp.arange(lengths.shape[0], dtype=jnp.int32)[None, :]
    offset = jnp.sum(jnp.where(member, starts[None, :], 0), axis=1)
    return (document, places - offset, places)


MESH_ID = pl.DeviceIdType.MESH
ROW_SHARD = 24
PAIR_ROWS = 2 * ROW_SHARD
PACK_COLS = 2304
LAYERS = 2
MIB = 1024 * 1024
DEVICES = 128


def whereami():
    fsdp_index = lax.axis_index("fsdp")
    return (lax.div(fsdp_index, 2), lax.rem(fsdp_index, 2), lax.axis_index("ctx"), lax.axis_index("tp"))


def device_at(y, c, z, x):
    return (y * 2 + c, z, x)


def device_of_index(index):
    return (lax.div(index, 16), lax.rem(lax.div(index, 4), 4), lax.rem(index, 4))


def index_here():
    y, c, z, x = whereami()
    return (y * 2 + c) * 16 + z * 4 + x


def sibling_here():
    y, c, z, x = whereami()
    return device_at(y, 1 - c, z, x)


def ring(index, offset):
    return lax.rem(index + offset, 4)


def remote(source, target, send_sem, recv_sem, device):
    return pltpu.make_async_remote_copy(
        src_ref=source,
        dst_ref=target,
        send_sem=send_sem,
        recv_sem=recv_sem,
        device_id=device,
        device_id_type=MESH_ID,
    )


def signal_everyone():
    barrier = pltpu.get_barrier_semaphore()
    mine = index_here()

    def signal_one(offset, carry):
        device = device_of_index(lax.rem(mine + offset, DEVICES))
        pl.semaphore_signal(barrier, inc=1, device_id=device, device_id_type=MESH_ID)
        return carry

    lax.fori_loop(1, DEVICES, signal_one, 0)


def wait_for_everyone():
    pl.semaphore_wait(pltpu.get_barrier_semaphore(), DEVICES - 1)


def neighbour(axis, offset):
    y, c, z, x = whereami()
    if axis == "y":
        return device_at(ring(y, offset), c, z, x)
    if axis == "z":
        return device_at(y, c, ring(z, offset), x)
    return device_at(y, c, z, ring(x, offset))


PART_ORDER = (("x", "y", "z"), ("y", "z", "x"), ("z", "x", "y"))


def part_view(ref, columns, done, axis, place, half):
    y, c, z, x = whereami()
    whole = slice(None)

    def index(name, own):
        if name == axis:
            return place
        return whole if name in done else own

    if axis == "x":
        pick_x = lax.rem(place, 2)
    else:
        pick_x = whole if "x" in done else lax.rem(x, 2)
    start, width = columns
    if half is not None:
        width = width // 2
        start = start + half * width
    return ref.at[pick_x, index("y", y), index("z", z), :, pl.ds(start, width)]


def ring_exists(axis, done, place):
    y, c, z, x = whereami()
    if axis == "x":
        return lax.div(place, 2) == c
    if "x" in done:
        return None
    return lax.div(x, 2) == c


def run_if(condition, action):
    if condition is None:
        action()
    else:
        pl.when(condition)(action)


class GatherLane:
    def __init__(self, ref, part, columns, send, recv, base, direct):
        self.ref, self.part, self.columns = ref, part, columns
        self.send, self.recv, self.base, self.direct = send, recv, base, direct

    def parts(self, phase):
        axis = PART_ORDER[self.part][phase]
        done = PART_ORDER[self.part][:phase]
        y, c, z, x = whereami()
        return axis, done, {"x": x, "y": y, "z": z}[axis], self.base + 4 * phase

    def copy(self, phase, slot, place, half, offset):
        axis, done, me, base = self.parts(phase)
        view = part_view(self.ref, self.columns, done, axis, place, half)
        return remote(
            view, view, self.send.at[base + slot], self.recv.at[base + slot], neighbour(axis, offset)
        )

    def first(self, phase):
        axis, done, me, base = self.parts(phase)

        def action():
            if phase in self.direct:
                for offset in (1, 2, 3):
                    self.copy(phase, offset - 1, me, None, offset).start()
            else:
                self.copy(phase, 0, me, None, 1).start()
                self.copy(phase, 1, me, None, 3).start()

        run_if(ring_exists(axis, done, me), action)

    def second(self, phase):
        axis, done, me, base = self.parts(phase)
        left, right = ring(me, 3), ring(me, 1)

        def from_left():
            self.copy(phase, 0, left, None, 1).wait_recv()
            self.copy(phase, 2, left, 0, 1).start()

        def from_right():
            self.copy(phase, 1, right, None, 1).wait_recv()
            self.copy(phase, 3, right, 1, 3).start()

        run_if(ring_exists(axis, done, left), from_left)
        run_if(ring_exists(axis, done, right), from_right)

    def third(self, phase):
        axis, done, me, base = self.parts(phase)
        far = ring(me, 2)

        def action():
            self.copy(phase, 2, far, 0, 1).wait_recv()
            self.copy(phase, 3, far, 1, 1).wait_recv()

        if phase in self.direct:
            for offset in (1, 2, 3):
                place = ring(me, 4 - offset)
                run_if(
                    ring_exists(axis, done, place),
                    lambda place=place, offset=offset: self.copy(
                        phase, offset - 1, place, None, 1
                    ).wait_recv(),
                )
        else:
            run_if(ring_exists(axis, done, far), action)

    def drain(self, phase):
        axis, done, me, base = self.parts(phase)
        left, right = ring(me, 3), ring(me, 1)

        def own():
            for slot in range(3 if phase in self.direct else 2):
                self.copy(phase, slot, me, None, 1).wait_send()

        run_if(ring_exists(axis, done, me), own)
        if phase not in self.direct:
            run_if(
                ring_exists(axis, done, left), lambda: self.copy(phase, 2, left, 0, 1).wait_send()
            )
            run_if(
                ring_exists(axis, done, right), lambda: self.copy(phase, 3, right, 1, 3).wait_send()
            )


class ReduceLane:
    def __init__(self, ref, boxes, part, columns, send, recv, base, direct, gives=None, takes=None):
        self.ref, self.boxes, self.part, self.columns = ref, boxes, part, columns
        self.send, self.recv, self.base, self.direct = send, recv, base, direct
        self.gives, self.takes = gives, takes

    def parts(self, phase):
        axis = PART_ORDER[self.part][2 - phase]
        done = PART_ORDER[self.part][: 2 - phase]
        y, c, z, x = whereami()
        return axis, done, {"x": x, "y": y, "z": z}[axis], self.base + 4 * phase

    def copy(self, phase, slot, place, half, offset):
        axis, done, me, base = self.parts(phase)
        view = part_view(self.ref, self.columns, done, axis, place, half)
        return remote(
            view,
            self.boxes[phase][slot],
            self.send.at[base + slot],
            self.recv.at[base + slot],
            neighbour(axis, offset),
        )

    def add(self, phase, place, half, boxes):
        axis, done, me, base = self.parts(phase)
        view = part_view(self.ref, self.columns, done, axis, place, half)
        lead = view.shape[:-2]

        def summed(where):
            terms = [view[where]] + [box[where] for box in boxes]
            while len(terms) > 1:
                terms = [
                    terms[i] + terms[i + 1] if i + 1 < len(terms) else terms[i]
                    for i in range(0, len(terms), 2)
                ]
            return terms[0]

        def add_one(index, carry):
            where = []
            for extent in reversed(lead):
                where.insert(0, lax.rem(index, extent))
                index = lax.div(index, extent)
            view[tuple(where)] = summed(tuple(where))
            return carry

        if len(lead) == 0:
            view[...] = summed(...)
        else:
            lax.fori_loop(0, math.prod(lead), add_one, 0)

    def first(self, phase):
        axis, done, me, base = self.parts(phase)
        far = ring(me, 2)

        def action():
            self.copy(phase, 0, far, 0, 1).start()
            self.copy(phase, 1, far, 1, 3).start()

        if phase in self.direct:
            for offset in (1, 2, 3):
                place = ring(me, offset)
                run_if(
                    ring_exists(axis, done, place),
                    lambda place=place, offset=offset: self.copy(
                        phase, offset - 1, place, None, offset
                    ).start(),
                )
        else:
            run_if(ring_exists(axis, done, far), action)

    def second(self, phase):
        axis, done, me, base = self.parts(phase)
        left, right = ring(me, 3), ring(me, 1)

        def to_right():
            self.copy(phase, 0, right, 0, 1).wait_recv()
            self.add(phase, right, 0, [self.boxes[phase][0]])
            if phase == 0 and self.takes is not None:
                pl.semaphore_wait(self.takes[0], 1)
            self.copy(phase, 2, right, None, 1).start()

        def to_left():
            self.copy(phase, 1, left, 1, 1).wait_recv()
            self.add(phase, left, 1, [self.boxes[phase][1]])
            if phase == 0 and self.takes is not None:
                pl.semaphore_wait(self.takes[1], 1)
            self.copy(phase, 3, left, None, 3).start()

        run_if(ring_exists(axis, done, right), to_right)
        run_if(ring_exists(axis, done, left), to_left)

    def third(self, phase):
        axis, done, me, base = self.parts(phase)

        def action():
            if phase in self.direct:
                slots = (0, 1, 2)
            else:
                slots = (2, 3)
            for slot in slots:
                self.copy(phase, slot, me, None, 1).wait_recv()
            self.add(phase, me, None, [self.boxes[phase][slot] for slot in slots])
            if phase == 0 and self.gives is not None:
                for sem, offset in zip(self.gives, (3, 1)):
                    pl.semaphore_signal(
                        sem, inc=1, device_id=neighbour(axis, offset), device_id_type=MESH_ID
                    )

        run_if(ring_exists(axis, done, me), action)

    def drain(self, phase):
        axis, done, me, base = self.parts(phase)
        far, left, right = ring(me, 2), ring(me, 3), ring(me, 1)

        def own():
            self.copy(phase, 0, far, 0, 1).wait_send()
            self.copy(phase, 1, far, 1, 3).wait_send()

        if phase in self.direct:
            for offset in (1, 2, 3):
                place = ring(me, offset)
                run_if(
                    ring_exists(axis, done, place),
                    lambda place=place, offset=offset: self.copy(
                        phase, offset - 1, place, None, offset
                    ).wait_send(),
                )
            return
        run_if(ring_exists(axis, done, far), own)
        run_if(ring_exists(axis, done, right), lambda: self.copy(phase, 2, right, None, 1).wait_send())
        run_if(ring_exists(axis, done, left), lambda: self.copy(phase, 3, left, None, 3).wait_send())


def box_shape(part, phase):
    order = PART_ORDER[part]
    axis, done = order[2 - phase], order[: 2 - phase]
    lead = []
    for name, extent in (("x", 2), ("y", 4), ("z", 4)):
        if name != axis and name in done:
            lead.append(extent)
    return tuple(lead)


def each(lanes, step, phase):
    for lane in lanes:
        getattr(lane, step)(phase)


HEADS_HERE = 6
TOKENS_HERE = 128
CHIP_TOKENS = 256
GROUP = 2048
Q_BLOCK = 256
K_BLOCK = 512
Q_BLOCKS = GROUP // Q_BLOCK
IN_COLS = 640
OUT_AT = 512
GATE_AT = 768
UP_AT = 1280
DOWN_AT = 1792
ASK_ROWS = 192
REPLY_ROWS = 64
SQUARE_COUNT = 8
WIDE_COUNT = 6
OWNERS = SQUARE_COUNT + WIDE_COUNT
bf16 = jnp.bfloat16
f32 = jnp.float32


def dot_nn(left, right):
    return jnp.dot(left, right, preferred_element_type=f32)


def dot_nt(left, right):
    return lax.dot_general(left, right, (((1,), (1,)), ((), ())), preferred_element_type=f32)


def dot_tn(left, right):
    return lax.dot_general(left, right, (((0,), (0,)), ((), ())), preferred_element_type=f32)


def sigmoid(value):
    return 1.0 / (1.0 + jnp.exp(-value))


def norm_scale(rows):
    return lax.rsqrt(jnp.mean(rows * rows, axis=-1, keepdims=True) + norm_eps)


def norm_back(rows, gain, grad):
    scale = norm_scale(rows)
    unit = rows * scale
    inner = grad * gain
    back = scale * (inner - unit * jnp.mean(inner * unit, axis=-1, keepdims=True))
    return back, jnp.sum(grad * unit, axis=0, keepdims=True)


def swap_halves(values):
    lower = lax.rem(lax.broadcasted_iota(jnp.int32, values.shape, 1), 64) < 32
    return jnp.where(lower, pltpu.roll(values, 96, 1), pltpu.roll(values, 32, 1))


def is_owner_here():
    y, c, z, x = whereami()
    return z < 3


def head_here():
    y, c, z, x = whereami()
    return 4 * z + x


def own_half(both):
    y, c, z, x = whereami()
    return jnp.where(c == 0, both[0:TOKENS_HERE], both[TOKENS_HERE:CHIP_TOKENS])


class Swap:
    def __init__(self, e, slot):
        self.send, self.recv = e.swap_send.at[slot], e.swap_recv.at[slot]

    def start(self, source, target):
        self.copy = remote(source, target, self.send, self.recv, sibling_here())
        self.copy.start()

    def wait(self):
        self.copy.wait_send()
        self.copy.wait_recv()


class HeadTraffic:
    def __init__(self, outbox, inbox, sems, recv_sem):
        self.outbox, self.inbox, self.sems, self.recv_sem = outbox, inbox, sems, recv_sem

    def owner_place(self, head):
        y, c, z, x = whereami()
        number = HEADS_HERE * c + head
        return lax.div(number, 4), lax.rem(number, 4)

    def owner_is_here(self, head, group):
        y, c, z, x = whereami()
        owner_z, owner_x = self.owner_place(head)
        return (owner_z == z) & (owner_x == x) & (c == group)

    def to_owner(self, head, group):
        y, c, z, x = whereami()
        owner_z, owner_x = self.owner_place(head)
        return remote(
            self.outbox.at[head, group],
            self.inbox.at[z * 4 + x],
            self.sems.at[head, group],
            self.recv_sem,
            device_at(y, group, owner_z, owner_x),
        )

    def send_to_owner(self, head, group):
        y, c, z, x = whereami()
        here = self.owner_is_here(head, group)

        @pl.when(here)
        def _():
            pltpu.make_async_copy(
                self.outbox.at[head, group], self.inbox.at[z * 4 + x], self.recv_sem
            ).start()

        @pl.when(jnp.logical_not(here))
        def _():
            self.to_owner(head, group).start()

    def drain_to_owner(self):
        for head in range(HEADS_HERE):
            for group in range(2):

                @pl.when(jnp.logical_not(self.owner_is_here(head, group)))
                def _(head=head, group=group):
                    self.to_owner(head, group).wait_send()

    def tokens_are_here(self, block):
        y, c, z, x = whereami()
        core = lax.div(head_here(), HEADS_HERE)
        return (lax.div(block, 4) == z) & (lax.rem(block, 4) == x) & (core == c)

    def to_tokens(self, block):
        y, c, z, x = whereami()
        core = lax.div(head_here(), HEADS_HERE)
        slot = head_here() - HEADS_HERE * core
        return remote(
            self.outbox.at[block],
            self.inbox.at[slot, c],
            self.sems.at[block],
            self.recv_sem,
            device_at(y, core, lax.div(block, 4), lax.rem(block, 4)),
        )

    def send_to_tokens(self, block):
        y, c, z, x = whereami()
        here = self.tokens_are_here(block)

        @pl.when(here)
        def _():
            slot = head_here() - HEADS_HERE * lax.div(head_here(), HEADS_HERE)
            pltpu.make_async_copy(
                self.outbox.at[block], self.inbox.at[slot, c], self.recv_sem
            ).start()

        @pl.when(jnp.logical_not(here))
        def _():
            self.to_tokens(block).start()

    def drain_to_tokens(self):
        def drain(block, carry):
            @pl.when(jnp.logical_not(self.tokens_are_here(block)))
            def _():
                self.to_tokens(block).wait_send()

            return carry

        lax.fori_loop(0, 16, drain, 0)

    def arrived(self):
        pltpu.make_async_copy(self.inbox, self.inbox, self.recv_sem).wait()


def block_mask(ends, query_at, key_at):
    query_row = query_at + lax.broadcasted_iota(jnp.int32, (Q_BLOCK, 1), 0)
    first, second = ends[0:1, 0:1], ends[1:2, 0:1]
    start = jnp.where(query_row >= second, second, jnp.where(query_row >= first, first, 0))
    shape = (Q_BLOCK, K_BLOCK)
    query = query_at + lax.broadcasted_iota(jnp.int32, shape, 0)
    key = key_at + lax.broadcasted_iota(jnp.int32, shape, 1)
    return (key <= query) & (key >= start)


def run_pumps(pumps, block):
    for number, action in sorted(pumps.items()):
        pl.when(block == number)(action)


def score_rows(step, lane):
    at = (step * (K_BLOCK // 128) + lane) * Q_BLOCK
    return pl.ds(pl.multiple_of(at, Q_BLOCK), Q_BLOCK)


def attend_forward(queries, keys_values, ends, score_box, kept_output, pumps, block_done):
    def one_block(block, carry):
        run_pumps(pumps, block)
        query_at = pl.multiple_of(block * Q_BLOCK, Q_BLOCK)
        rows = pl.ds(query_at, Q_BLOCK)
        query = queries[rows, :]
        key_blocks = lax.div(block, 2) + 1

        def scores(step, top):
            key_at = pl.multiple_of(step * K_BLOCK, K_BLOCK)
            raw = dot_nt(query, keys_values[pl.ds(key_at, K_BLOCK), :])
            masked = jnp.where(block_mask(ends, query_at, key_at), raw, mask_fill)
            for lane in range(K_BLOCK // 128):
                tile = masked[:, 128 * lane : 128 * lane + 128]
                score_box[score_rows(step, lane), :] = tile
                top = jnp.maximum(top, tile)
            return top

        top = lax.fori_loop(0, key_blocks, scores, jnp.full((Q_BLOCK, 128), mask_fill, f32))
        top = jnp.max(top, axis=1, keepdims=True)

        def collect(step, state):
            total, gathered = state
            key_at = pl.multiple_of(step * K_BLOCK, K_BLOCK)
            tiles = []
            for lane in range(K_BLOCK // 128):
                tile = jnp.exp(score_box[score_rows(step, lane), :] - top)
                total = total + tile
                tiles.append(tile.astype(bf16))
            return total, gathered + dot_nn(
                jnp.concatenate(tiles, axis=1), keys_values[pl.ds(key_at, K_BLOCK), :]
            )

        total, gathered = lax.fori_loop(
            0,
            key_blocks,
            collect,
            (jnp.zeros((Q_BLOCK, 128), f32), jnp.zeros((Q_BLOCK, 128), f32)),
        )
        total = jnp.sum(total, axis=1, keepdims=True)
        lane = lax.broadcasted_iota(jnp.int32, (Q_BLOCK, 128), 1)
        kept_output[rows, :] = jnp.where(
            lane < HEAD_DIM, top + jnp.log(total), gathered / total
        )
        block_done(block)
        return carry

    lax.fori_loop(0, Q_BLOCKS, one_block, 0)


def attend_backward(
    queries, keys_values, output_grad, kept_output, ends, query_grad, key_value_grad, pumps
):
    key_value_grad[...] = jnp.zeros_like(key_value_grad)

    def one_block(block, carry):
        run_pumps(pumps, block)
        query_at = pl.multiple_of(block * Q_BLOCK, Q_BLOCK)
        rows = pl.ds(query_at, Q_BLOCK)
        query = queries[rows, :]
        grad = output_grad[rows, :]
        kept = kept_output[rows, :]
        logs = kept[:, 0:1]
        inner = jnp.sum(grad.astype(f32) * kept, axis=1, keepdims=True)

        def one_key(step, total):
            key_at = pl.multiple_of(step * K_BLOCK, K_BLOCK)
            keys_here = pl.ds(key_at, K_BLOCK)
            both = keys_values[keys_here, :]
            masked = jnp.where(
                block_mask(ends, query_at, key_at), dot_nt(query, both), mask_fill
            )
            probability = jnp.exp(masked - logs)
            probability_grad = dot_nt(grad, both)
            score_grad = (probability * (probability_grad - inner)).astype(bf16)
            key_value_grad[keys_here, :] += dot_tn(score_grad, query) + dot_tn(
                probability.astype(bf16), grad
            )
            return total + dot_nn(score_grad, both)

        query_grad[rows, :] = lax.fori_loop(
            0, lax.div(block, 2) + 1, one_key, jnp.zeros((Q_BLOCK, 128), f32)
        )
        return carry

    lax.fori_loop(0, Q_BLOCKS, one_block, 0)


class Weights:
    def __init__(self, e):
        self.e = e
        self.ranges = {"attend": (0, GATE_AT, 0), "units": (GATE_AT, PACK_COLS - GATE_AT, 1)}

    def copy(self, layer, name):
        start, width, slot = self.ranges[name]
        columns = pl.ds(start, width)
        return pltpu.make_async_copy(
            self.e.full.at[layer, :, :, :, :, columns],
            self.e.weights.at[:, :, :, :, columns],
            self.e.load_sem.at[slot],
        )

    def load(self, layer, name):
        self.copy(layer, name).start()

    def wait(self, layer, name):
        self.copy(layer, name).wait()

    def keep_copy(self):
        return pltpu.make_async_copy(self.e.weights, self.e.full.at[0], self.e.load_sem.at[3])

    def keep(self):
        self.keep_copy().start()

    def keep_wait(self):
        self.keep_copy().wait()

    def units(self, step, start):
        side, at = lax.div(step, 2), start + 256 * lax.rem(step, 2)
        columns = pl.ds(pl.multiple_of(at, 128), 256)
        return self.e.weights[side, :, :, :, columns].reshape(D, 256)

    def get(self, side, start, stop):
        return self.e.weights[side, :, :, :, start:stop].reshape(D, stop - start)


def nothing():
    pass


def forward_pass(e, layer, rows_ref, rows_out, pump):
    y, c, z, x = whereami()
    weights = Weights(e)
    swaps = [Swap(e, 4 * layer + slot) for slot in range(4)]
    ask = HeadTraffic(e.ask_out, e.ask_in, e.ask_send, e.traffic_recv.at[4 * layer])
    answer = HeadTraffic(e.reply_out, e.reply_in, e.reply_send, e.traffic_recv.at[4 * layer + 1])
    theirs = pl.ds(pl.multiple_of((1 - c) * TOKENS_HERE, TOKENS_HERE), TOKENS_HERE)
    swaps[0].start(e.normed.at[layer, c], e.normed.at[layer, c])
    pump("start")
    if layer == 1:
        weights.wait(layer, "attend")
    swaps[0].wait()
    chip_normed = e.normed[layer].reshape(CHIP_TOKENS, D)
    cosine = e.tables[:, :, 0:128].reshape(CHIP_TOKENS, 128)
    sine = e.tables[:, :, 128:256].reshape(CHIP_TOKENS, 128)
    for side in range(2):
        mixed = dot_nn(chip_normed, weights.get(side, 0, IN_COLS))
        for inner in range(3):
            head = 3 * side + inner
            pair = mixed[:, 128 * inner : 128 * inner + 128]
            pair = (pair * cosine + swap_halves(pair) * sine).astype(bf16)
            value = mixed[:, 384 + 64 * inner : 448 + 64 * inner]
            for group in range(2):
                at = TOKENS_HERE * group
                e.ask_out[head, group, 0:128] = pair[at : at + 128]
                e.ask_out[head, group, 128:192] = jnp.concatenate(
                    [value[at : at + 64], value[at + 64 : at + 128]], axis=1
                ).astype(bf16)
                ask.send_to_owner(head, group)
    pump("asked")
    queries, keys_values = e.queries.at[layer], e.keys_values.at[layer]
    kept_output = e.kept_output.at[layer]

    @pl.when(is_owner_here())
    def _():
        ask.arrived()

        def place(block, carry):
            at = pl.multiple_of(block * TOKENS_HERE, TOKENS_HERE)
            pair = e.ask_in[block, 0:128].astype(f32)
            zeros = jnp.zeros((TOKENS_HERE, HEAD_DIM), f32)
            queries[pl.ds(at, 128), :] = jnp.concatenate(
                [pair[:, 0:64] * (1.0 / math.sqrt(HEAD_DIM)), zeros], axis=1
            ).astype(bf16)
            both = e.ask_in[block, 128:192].astype(f32)
            value = jnp.concatenate([both[:, 0:64], both[:, 64:128]], axis=0)
            keys_values[pl.ds(at, 128), :] = jnp.concatenate(
                [pair[:, 64:128], value], axis=1
            ).astype(bf16)
            return carry

        lax.fori_loop(0, 16, place, 0)

        def send_rows(block):
            for half in range(2):
                at = pl.multiple_of(block * Q_BLOCK + half * 128, 128)
                first = kept_output[pl.ds(at, 64), :]
                second = kept_output[pl.ds(at + 64, 64), :]
                e.reply_out[2 * block + half] = jnp.concatenate(
                    [first[:, HEAD_DIM:], second[:, HEAD_DIM:]], axis=1
                ).astype(bf16)
                answer.send_to_tokens(2 * block + half)

        attend_forward(
            queries, keys_values, e.ends, e.score_box, kept_output, pump.blocks(), send_rows
        )

    @pl.when(jnp.logical_not(is_owner_here()))
    def _():
        for number, action in sorted(pump.blocks().items()):
            action()

    pump("attended")
    answer.arrived()
    partial = None
    for side in range(2):
        columns = [jnp.zeros((CHIP_TOKENS, 64), f32)]
        for inner in range(3):
            pieces = []
            for group in range(2):
                both = e.reply_in[3 * side + inner, group].astype(f32)
                pieces += [both[:, 0:64], both[:, 64:128]]
            columns.append(jnp.concatenate(pieces, axis=0))
        e.attended[layer, side] = jnp.concatenate(columns, axis=1).astype(bf16)
        term = dot_nt(e.attended[layer, side], weights.get(side, OUT_AT, GATE_AT))
        partial = term if partial is None else partial + term
    e.partial_out[...] = partial.astype(bf16)
    swaps[1].start(e.partial_out.at[theirs], e.partial_in.at[0])
    own_part = own_half(partial)
    swaps[1].wait()
    middle = rows_ref[...] + (own_part + e.partial_in[0].astype(f32))
    e.mid_rows[layer] = middle
    e.normed_mid[layer, c] = (middle * norm_scale(middle) * e.gains[layer, 1:2, :]).astype(bf16)
    swaps[2].start(e.normed_mid.at[layer, c], e.normed_mid.at[layer, c])
    if layer == 1:
        weights.wait(layer, "units")
    swaps[2].wait()
    e.partial[...] = jnp.zeros_like(e.partial)

    def some_units(step, carry):
        chip_mid = e.normed_mid[layer].reshape(CHIP_TOKENS, D)
        gate = dot_nn(chip_mid, weights.units(step, GATE_AT))
        up = dot_nn(chip_mid, weights.units(step, UP_AT))
        active = (gate * sigmoid(gate) * up).astype(bf16)
        e.partial[...] += dot_nt(active, weights.units(step, DOWN_AT))
        return carry

    lax.fori_loop(0, 4, some_units, 0)
    partial = e.partial[...]
    e.partial_out[...] = partial.astype(bf16)
    swaps[3].start(e.partial_out.at[theirs], e.partial_in.at[1])
    own_part = own_half(partial)
    pump("units")
    swaps[3].wait()
    rows_out[...] = e.mid_rows[layer] + (own_part + e.partial_in[1].astype(f32))
    ask.drain_to_owner()
    pl.when(is_owner_here())(answer.drain_to_tokens)
    pump("end")


def backward_pass(e, layer, grad_ref, rows_ref, grad_out, pump, next_layer):
    y, c, z, x = whereami()
    weights = Weights(e)
    swaps = [Swap(e, 8 + 4 * layer + slot) for slot in range(4)]
    ask = HeadTraffic(e.back_ask_out, e.back_ask_in, e.ask_send, e.traffic_recv.at[4 * layer + 2])
    answer = HeadTraffic(
        e.back_reply_out, e.back_reply_in, e.reply_send, e.traffic_recv.at[4 * layer + 3]
    )
    theirs = pl.ds(pl.multiple_of((1 - c) * TOKENS_HERE, TOKENS_HERE), TOKENS_HERE)

    def transpose_rows(which, value):
        e.left_t[which] = value.T.reshape(4, D // 4, CHIP_TOKENS)

    def weight_grad(side, start, width, which, right):
        columns = pl.ds(pl.multiple_of(start, 128), width)
        for block in range(4):
            e.grads[layer, side, block, :, :, columns] = (
                dot_nn(e.left_t[which, block], right).astype(bf16).reshape(4, PAIR_ROWS, width)
            )

    e.grad_swap[0, c] = grad_ref[...].astype(bf16)
    swaps[0].start(e.grad_swap.at[0, c], e.grad_swap.at[0, c])
    pump("start")
    if next_layer is None:
        weights.wait(layer, "units")
    swaps[0].wait()
    transpose_rows(0, e.grad_swap[0].reshape(CHIP_TOKENS, D))
    transpose_rows(1, e.normed_mid[layer].reshape(CHIP_TOKENS, D))
    e.partial[...] = jnp.zeros_like(e.partial)

    def some_units(step, carry):
        down = e.grad_swap[0].reshape(CHIP_TOKENS, D)
        chip_mid = e.normed_mid[layer].reshape(CHIP_TOKENS, D)
        gate = dot_nn(chip_mid, weights.units(step, GATE_AT))
        up = dot_nn(chip_mid, weights.units(step, UP_AT))
        active_grad = dot_nn(down, weights.units(step, DOWN_AT))
        sigma = sigmoid(gate)
        active = gate * sigma
        gate_grad = (active_grad * up * sigma * (1.0 + gate * (1.0 - sigma))).astype(bf16)
        up_grad = (active_grad * active).astype(bf16)
        side, at = lax.div(step, 2), 256 * lax.rem(step, 2)
        weight_grad(side, DOWN_AT + at, 256, 0, (active * up).astype(bf16))
        weight_grad(side, GATE_AT + at, 256, 1, gate_grad)
        weight_grad(side, UP_AT + at, 256, 1, up_grad)
        e.partial[...] += dot_nt(gate_grad, weights.units(step, GATE_AT)) + dot_nt(
            up_grad, weights.units(step, UP_AT)
        )
        return carry

    lax.fori_loop(0, 4, some_units, 0)
    partial = e.partial[...]
    e.partial_out[...] = partial.astype(bf16)
    swaps[1].start(e.partial_out.at[theirs], e.partial_in.at[0])
    own_part = own_half(partial)
    if next_layer is not None:
        weights.load(next_layer, "units")
    pump("units")
    swaps[1].wait()
    back, gain_grad = norm_back(
        e.mid_rows[layer], e.gains[layer, 1:2, :], own_part + e.partial_in[0].astype(f32)
    )
    e.mid_grad[...] = grad_ref[...] + back
    e.gain_total[2 * layer + 1 : 2 * layer + 2, :] = gain_grad
    e.grad_swap[1, c] = e.mid_grad[...].astype(bf16)
    swaps[2].start(e.grad_swap.at[1, c], e.grad_swap.at[1, c])
    if next_layer is None:
        weights.wait(layer, "attend")
    swaps[2].wait()
    branch = e.grad_swap[1].reshape(CHIP_TOKENS, D)
    for side in range(2):
        heads_grad = dot_nn(branch, weights.get(side, OUT_AT, GATE_AT))
        for inner in range(3):
            head = 3 * side + inner
            piece = heads_grad[:, 64 + 64 * inner : 128 + 64 * inner]
            for group in range(2):
                at = TOKENS_HERE * group
                e.back_ask_out[head, group] = jnp.concatenate(
                    [piece[at : at + 64], piece[at + 64 : at + 128]], axis=1
                ).astype(bf16)
                ask.send_to_owner(head, group)
    transpose_rows(0, branch)
    for side in range(2):
        weight_grad(side, OUT_AT, GATE_AT - OUT_AT, 0, e.attended[layer, side])
    pump("asked")

    @pl.when(is_owner_here())
    def _():
        ask.arrived()

        def place(block, carry):
            at = pl.multiple_of(block * TOKENS_HERE, TOKENS_HERE)
            both = e.back_ask_in[block].astype(f32)
            grad = jnp.concatenate([both[:, 0:64], both[:, 64:128]], axis=0)
            e.output_grad[pl.ds(at, 128), :] = jnp.concatenate(
                [jnp.zeros((TOKENS_HERE, HEAD_DIM), f32), grad], axis=1
            ).astype(bf16)
            return carry

        lax.fori_loop(0, 16, place, 0)
        attend_backward(
            e.queries.at[layer],
            e.keys_values.at[layer],
            e.output_grad,
            e.kept_output.at[layer],
            e.ends,
            e.query_grad,
            e.key_value_grad,
            pump.blocks(),
        )

        def give(block, carry):
            at = pl.multiple_of(block * TOKENS_HERE, TOKENS_HERE)
            e.back_reply_out[block, 0:128] = jnp.concatenate(
                [
                    e.query_grad[pl.ds(at, 128), 0:64] * (1.0 / math.sqrt(HEAD_DIM)),
                    e.key_value_grad[pl.ds(at, 128), 0:64],
                ],
                axis=1,
            ).astype(bf16)
            e.back_reply_out[block, 128:192] = jnp.concatenate(
                [
                    e.key_value_grad[pl.ds(at, 64), 64:128],
                    e.key_value_grad[pl.ds(at + 64, 64), 64:128],
                ],
                axis=1,
            ).astype(bf16)
            answer.send_to_tokens(block)
            return carry

        lax.fori_loop(0, 16, give, 0)

    @pl.when(jnp.logical_not(is_owner_here()))
    def _():
        for number, action in sorted(pump.blocks().items()):
            action()

    pump("attended")
    answer.arrived()
    cosine = e.tables[:, :, 0:128].reshape(CHIP_TOKENS, 128)
    sine = e.tables[:, :, 128:256].reshape(CHIP_TOKENS, 128)
    transpose_rows(1, e.normed[layer].reshape(CHIP_TOKENS, D))
    partial = None
    for side in range(2):
        pieces = []
        for inner in range(3):
            head = 3 * side + inner
            pair = jnp.concatenate(
                [e.back_reply_in[head, 0, 0:128], e.back_reply_in[head, 1, 0:128]], axis=0
            ).astype(f32)
            pair = pair * cosine - swap_halves(pair) * sine
            e.mixed_grad[side, :, 128 * inner : 128 * inner + 128] = pair.astype(bf16)
            rows = []
            for group in range(2):
                both = e.back_reply_in[head, group, 128:192].astype(f32)
                rows += [both[:, 0:64], both[:, 64:128]]
            pieces.append(jnp.concatenate(rows, axis=0))
        pieces.append(jnp.zeros((CHIP_TOKENS, 64), f32))
        e.mixed_grad[side, :, 384:IN_COLS] = jnp.concatenate(pieces, axis=1).astype(bf16)
        weight_grad(side, 0, OUT_AT, 1, e.mixed_grad[side, :, 0:OUT_AT])
        last = dot_nn(e.left_t[1].reshape(D, CHIP_TOKENS), e.mixed_grad[side, :, OUT_AT:IN_COLS])
        here = e.grads[layer, side, :, :, :, OUT_AT:IN_COLS].reshape(D, IN_COLS - OUT_AT)
        e.grads[layer, side, :, :, :, OUT_AT:IN_COLS] = (
            (here.astype(f32) + last).astype(bf16).reshape(4, 4, PAIR_ROWS, IN_COLS - OUT_AT)
        )
    pump("mixed")
    for side in range(2):
        term = dot_nt(e.mixed_grad[side], weights.get(side, 0, IN_COLS))
        partial = term if partial is None else partial + term
    e.partial_out[...] = partial.astype(bf16)
    swaps[3].start(e.partial_out.at[theirs], e.partial_in.at[1])
    own_part = own_half(partial)
    if next_layer is not None:
        weights.load(next_layer, "attend")
    swaps[3].wait()
    back, gain_grad = norm_back(
        rows_ref[...], e.gains[layer, 0:1, :], own_part + e.partial_in[1].astype(f32)
    )
    e.gain_total[2 * layer : 2 * layer + 1, :] = gain_grad
    grad_out[...] = e.mid_grad[...] + back
    ask.drain_to_owner()
    pl.when(is_owner_here())(answer.drain_to_tokens)
    pump("end")


class Pump:
    def __init__(self, actions=None):
        self.actions = actions or {}

    def __call__(self, point):
        for action in self.actions.get(point, []):
            action()

    def blocks(self):
        def run(actions):
            def action():
                for one in actions:
                    one()

            return action

        return {key: run(value) for key, value in self.actions.items() if isinstance(key, int)}


def owner_place(matrix):
    return (matrix // 4, 0, (matrix // 4 + matrix % 4) % 4, matrix % 4)


def square_columns(kind):
    if kind < 2:
        return [(128 * head + 64 * kind, 64) for head in range(3)]
    return [(384 + 192 * (kind - 2), 192)]


def ns_step(source, target, gram, columns):
    blocks = 4
    rows = D // blocks

    def gram_rows(block, carry):
        part = source[block, :, :, 0:columns].reshape(rows, columns)
        gram[block, :, :, 0:D] = (
            dot_nt(part, source[:, :, :, 0:columns].reshape(D, columns))
            .astype(bf16)
            .reshape(4, PAIR_ROWS, D)
        )
        return carry

    lax.fori_loop(0, blocks, gram_rows, 0)

    def update_rows(block, carry):
        gram_block = gram[block, :, :, 0:D].reshape(rows, D)
        polynomial = (
            quintic_two * gram_block.astype(f32)
            + quintic_three * dot_nn(gram_block, gram[:, :, :, 0:D].reshape(D, D))
        ).astype(bf16)
        for start in range(0, columns, 512):
            stop = start + 512
            target[block, :, :, start:stop] = (
                (
                    quintic_one * source[block, :, :, start:stop].reshape(rows, 512).astype(f32)
                    + dot_nn(polynomial, source[:, :, :, start:stop].reshape(D, 512))
                )
                .astype(bf16)
                .reshape(4, PAIR_ROWS, 512)
            )
        return carry

    lax.fori_loop(0, blocks, update_rows, 0)


def orthogonal_owner(slots, front, back, gram, wide, send_back):
    columns = FF if wide else 1024
    slot_rows = PAIR_ROWS if wide else 32

    def add_squares(index, carry):
        value = slots[index, 0:slot_rows, :].astype(f32)
        return carry + jnp.sum(value * value, axis=0, keepdims=True)

    squares = lax.fori_loop(0, DEVICES, add_squares, jnp.zeros((1, 256), f32))
    scale = 1.0 / (jnp.sqrt(jnp.sum(squares, axis=1, keepdims=True)) + ortho_eps)

    def assemble(pair, carry):
        outer, inner = lax.div(pair, 4), lax.rem(pair, 4)
        for part in range(4):
            first = slots[pair * 8 + part, 0:slot_rows, :].astype(f32) * scale
            second = slots[pair * 8 + 4 + part, 0:slot_rows, :].astype(f32) * scale
            joined = jnp.concatenate([first[0:24], second[0:24]], axis=0).astype(bf16)
            if wide:
                front[outer, inner, :, part * 512 : part * 512 + 256] = joined
                front[outer, inner, :, part * 512 + 256 : part * 512 + 512] = jnp.concatenate(
                    [first[24:48], second[24:48]], axis=0
                ).astype(bf16)
            else:
                front[outer, inner, :, part * 256 : part * 256 + 256] = joined
        return carry

    lax.fori_loop(0, 16, assemble, 0)

    def two_steps(index, carry):
        ns_step(front, back, gram, columns)
        ns_step(back, front, gram, columns)
        return carry

    lax.fori_loop(0, NS_STEPS // 2, two_steps, 0)

    def take_apart(pair, carry):
        outer, inner = lax.div(pair, 4), lax.rem(pair, 4)
        for part in range(4):
            if wide:
                left = front[outer, inner, :, part * 512 : part * 512 + 256].astype(f32)
                right = front[outer, inner, :, part * 512 + 256 : part * 512 + 512].astype(f32)
                slots[pair * 8 + part] = jnp.concatenate([left[0:24], right[0:24]], axis=0).astype(
                    bf16
                )
                slots[pair * 8 + 4 + part] = jnp.concatenate(
                    [left[24:48], right[24:48]], axis=0
                ).astype(bf16)
            else:
                left = front[outer, inner, :, part * 256 : part * 256 + 256].astype(f32)
                slots[pair * 8 + part, 0:32] = left[0:32].astype(bf16)
                slots[pair * 8 + 4 + part, 0:32] = jnp.concatenate(
                    [left[24:48], left[0:8]], axis=0
                ).astype(bf16)
        for part in range(8):
            send_back(pair * 8 + part)
        return carry

    lax.fori_loop(0, 16, take_apart, 0)


class Muon:
    def __init__(self, e):
        self.e = e
        self.places = [owner_place(m) for m in range(OWNERS)]
        self.indices = [(p[0] * 2 + p[1]) * 16 + p[2] * 4 + p[3] for p in self.places]

    def tile(self, m):
        return self.e.square.at[m] if m < SQUARE_COUNT else self.e.wide.at[m - SQUARE_COUNT]

    def returned(self, m):
        return self.e.square_new.at[m] if m < SQUARE_COUNT else self.e.wide_new.at[m - SQUARE_COUNT]

    def slot(self, m):
        if m < SQUARE_COUNT:
            return self.e.slots.at[index_here(), pl.ds(0, 32)]
        return self.e.slots.at[index_here()]

    def outbound(self, m):
        return remote(
            self.tile(m),
            self.slot(m),
            self.e.tile_send.at[m],
            self.e.slot_recv.at[0],
            device_at(*self.places[m]),
        )

    def update_moment(self, layer, start, stop):
        e = self.e
        rows = slice(ROW_SHARD * layer, ROW_SHARD * layer + ROW_SHARD)
        e.moment_new[rows, start:stop] = (
            moment_decay * e.moment[rows, start:stop] + e.total[rows, start:stop]
        )

    def send(self, m):
        e = self.e
        if m < SQUARE_COUNT:
            layer, kind = m // 4, m % 4
            rows = slice(ROW_SHARD * layer, ROW_SHARD * layer + ROW_SHARD)
            pieces = [e.moment_new[rows, at : at + width] for at, width in square_columns(kind)]
            tile = jnp.concatenate(pieces + [jnp.zeros((ROW_SHARD, 64), f32)], axis=1)
            e.square[m] = jnp.concatenate([tile, jnp.zeros((8, 256), f32)], axis=0).astype(bf16)
        else:
            layer, kind = (m - SQUARE_COUNT) // 3, (m - SQUARE_COUNT) % 3
            rows = slice(ROW_SHARD * layer, ROW_SHARD * layer + ROW_SHARD)
            at = GATE_AT + 512 * kind
            e.wide[m - SQUARE_COUNT] = jnp.concatenate(
                [e.moment_new[rows, at : at + 256], e.moment_new[rows, at + 256 : at + 512]], axis=0
            ).astype(bf16)

        @pl.when(index_here() != self.indices[m])
        def _():
            self.outbound(m).start()

        @pl.when(index_here() == self.indices[m])
        def _():
            copy = pltpu.make_async_copy(self.tile(m), self.slot(m), self.e.tile_send.at[m])
            copy.start()
            copy.wait()

    def serve(self, is_wide):
        e = self.e
        y, c, z, x = whereami()
        slot_rows = PAIR_ROWS if is_wide else 32
        whole = e.slots.at[pl.ds(0, DEVICES - 1), pl.ds(0, slot_rows)]
        pltpu.make_async_copy(whole, whole, e.slot_recv.at[0]).wait()
        matrix = y * 4 + x
        mine = index_here()

        def send_back(index):
            if is_wide:
                source, target = e.slots.at[index], e.wide_new.at[matrix - SQUARE_COUNT]
            else:
                source, target = e.slots.at[index, pl.ds(0, 32)], e.square_new.at[matrix]

            @pl.when(index != mine)
            def _():
                remote(
                    source, target, e.slot_recv.at[1], e.tile_recv.at[matrix], device_of_index(index)
                ).start()

            @pl.when(index == mine)
            def _():
                copy = pltpu.make_async_copy(source, target, e.tile_recv.at[matrix])
                copy.start()

        orthogonal_owner(
            e.slots, e.weights.at[0], e.weights.at[1], e.grads.at[1, 0], is_wide, send_back
        )
        pltpu.make_async_copy(whole, whole, e.slot_recv.at[1]).wait()

    def serve_all(self):
        y, c, z, x = whereami()
        placed = (c == 0) & (z == ring(x, y))
        square_owner = placed & (y < 2)
        wide_owner = placed & ((y == 2) | ((y == 3) & (x < 2)))
        pl.when(square_owner)(lambda: self.serve(False))
        pl.when(wide_owner)(lambda: self.serve(True))

    def finish(self):
        e = self.e
        for m in range(OWNERS):
            tile = self.returned(m)
            pltpu.make_async_copy(tile, tile, e.tile_recv.at[m]).wait()
            if m < SQUARE_COUNT:
                layer, kind = m // 4, m % 4
                rate = project_rate if kind == 3 else matrix_rate
                factor = 0.2 * math.sqrt(D)
                value = e.square_new[m].astype(f32)[0:ROW_SHARD]
                places = square_columns(kind)
            else:
                layer, kind = (m - SQUARE_COUNT) // 3, (m - SQUARE_COUNT) % 3
                rate, factor = matrix_rate, 0.2 * math.sqrt(FF)
                value = e.wide_new[m - SQUARE_COUNT].astype(f32)
                value = jnp.concatenate([value[0:ROW_SHARD], value[ROW_SHARD:PAIR_ROWS]], axis=1)
                places = [(GATE_AT + 512 * kind, 512)]
            rows = slice(ROW_SHARD * layer, ROW_SHARD * layer + ROW_SHARD)
            offset = 0
            for at, width in places:
                weight = e.weights_own[rows, at : at + width]
                e.weights_new[rows, at : at + width] = weight - rate * (
                    factor * value[:, offset : offset + width] + matrix_decay * weight
                )
                offset += width

            @pl.when(index_here() != self.indices[m])
            def _(m=m):
                self.outbound(m).wait_send()


def finish_sum(e, layer, start, stop, slot):
    y, c, z, x = whereami()
    rows = slice(ROW_SHARD * layer, ROW_SHARD * layer + ROW_SHARD)
    source, target = e.pair.at[rows, start:stop], e.total.at[rows, start:stop]
    copy = lambda: remote(source, target, e.pair_send.at[slot], e.pair_recv.at[slot], sibling_here())

    @pl.when(c == lax.div(x, 2))
    def _():
        whole = e.grads[layer, lax.rem(x, 2), y, z, :, start:stop].astype(f32)
        first, second = whole[0:ROW_SHARD], whole[ROW_SHARD:PAIR_ROWS]
        e.total[rows, start:stop] = jnp.where(c == 0, first, second)
        e.pair[rows, start:stop] = jnp.where(c == 0, second, first)
        copy().start()
        copy().wait_send()

    @pl.when(c != lax.div(x, 2))
    def _():
        copy().wait_recv()


def gain_copies(e, hop):
    if hop == 0:
        devices = [sibling_here()]
    else:
        devices = [neighbour("xyz"[hop - 1], offset) for offset in (1, 2, 3)]
    base = 3 * hop
    return [
        remote(
            e.gain_total,
            e.gain_box.at[base + i],
            e.gain_send.at[base + i],
            e.gain_recv.at[base + i],
            device,
        )
        for i, device in enumerate(devices)
    ]


def gain_start(e, hop):
    for copy in gain_copies(e, hop):
        copy.start()


def gain_finish(e, hop):
    copies = gain_copies(e, hop)
    for copy in copies:
        copy.wait_send()
        copy.wait_recv()
    for i in range(len(copies)):
        e.gain_total[...] += e.gain_box[3 * hop + i]


BOX_SHAPES = {}
for _part in range(3):
    for _phase in range(3):
        _lead = box_shape(_part, _phase) + (PAIR_ROWS,)
        if _phase == 0:
            BOX_SHAPES[f"late_half_{_part}"] = (2,) + _lead + (384,)
            BOX_SHAPES[f"both_block_{_part}"] = (2,) + _lead + (768,)
            BOX_SHAPES[f"early_half_{_part}"] = (2,) + _lead + (256,)
            BOX_SHAPES[f"early_last_{_part}"] = (3,) + _lead + (256,)
        else:
            BOX_SHAPES[f"late_{_part}{_phase}"] = (3,) + _lead + (768,)
            BOX_SHAPES[f"early_{_part}{_phase}"] = (3,) + _lead + (768,)


def boxes_of(e, kind, part):
    start, width = {"late": (0, 768), "units": (0, 512), "attend": (512, 256)}[kind]
    found = []
    for phase in range(3):
        cut = (slice(None),) * (len(box_shape(part, phase)) + 1) + (pl.ds(start, width),)
        if phase == 0:
            if kind == "attend":
                boxes = getattr(e, f"early_last_{part}")
                found.append([boxes.at[i] for i in range(3)])
            else:
                blocks = getattr(e, f"both_block_{part}")
                blocks = [blocks.at[(i,) + cut] for i in range(2)]
                halves = getattr(e, f"{'late' if kind == 'late' else 'early'}_half_{part}")
                found.append([halves.at[0], halves.at[1]] + blocks)
        else:
            boxes = getattr(e, f"{'late' if kind == 'late' else 'early'}_{part}{phase}")
            found.append([boxes.at[(i,) + cut] for i in range(3)])
    return found


def step_kernel(*refs):
    e = types.SimpleNamespace(**dict(zip(REF_NAMES, refs)))
    e.query_grad = e.score_box.at[pl.ds(0, GROUP)]
    e.key_value_grad = e.score_box.at[pl.ds(GROUP, GROUP)]
    e.pair, e.total = e.moment_new, e.weights_new
    e.back_ask_out, e.back_reply_out, e.back_reply_in = e.reply_in, e.ask_in, e.ask_out
    y, c, z, x = whereami()
    holder = lax.div(x, 2)
    signal_everyone()
    e.own[...] = e.weights_own[...].astype(bf16)
    e.tables[c] = e.table[...]
    rows = e.rows_in[...]
    e.normed[0, c] = (rows * norm_scale(rows) * e.gains[0, 0:1, :]).astype(bf16)
    e.gain_total[...] = jnp.zeros_like(e.gain_total)
    wait_for_everyone()

    hand_over = lambda: remote(e.own, e.twin, e.pair_send.at[3], e.pair_recv.at[3], sibling_here())
    pl.when(c != holder)(lambda: hand_over().start())
    table_swap = remote(
        e.table, e.tables.at[c], e.pair_send.at[4], e.pair_recv.at[4], sibling_here()
    )
    table_swap.start()

    @pl.when(c == holder)
    def _():
        hand_over().wait_recv()
        mine = e.own[...].astype(f32)
        theirs = e.twin[...].astype(f32)
        first = jnp.where(c == 0, mine, theirs)
        second = jnp.where(c == 0, theirs, mine)
        for layer in range(LAYERS):
            part = slice(layer * ROW_SHARD, layer * ROW_SHARD + ROW_SHARD)
            joined = jnp.concatenate([first[part], second[part]], axis=0).astype(bf16)
            if layer == 0:
                e.weights[lax.rem(x, 2), y, z] = joined
            else:
                e.piece[...] = joined
                keep = pltpu.make_async_copy(
                    e.piece, e.full.at[1, lax.rem(x, 2), y, z], e.load_sem.at[2]
                )
                keep.start()
                keep.wait()

    def gather_lanes(ref, at, width, base, direct):
        return [
            GatherLane(
                ref,
                part,
                (at + part * width, width),
                e.gather_send,
                e.gather_recv,
                base + 12 * part,
                direct,
            )
            for part in range(3)
        ]

    ga = gather_lanes(e.weights, 0, 256, 0, (0, 1, 2))
    gb = gather_lanes(e.weights, GATE_AT, 512, 36, (0, 1))
    gc = gather_lanes(e.full.at[1], 0, 256, 72, (0, 1))
    gd = gather_lanes(e.full.at[1], GATE_AT, 512, 108, (0, 1))
    do = lambda lanes, step, phase: lambda: each(lanes, step, phase)
    weights = Weights(e)
    for phase in range(3):
        for lanes in (ga, gb, gc, gd):
            if phase > 0:
                each(lanes, "third", phase - 1)
            each(lanes, "first", phase)
    table_swap.wait_send()
    remote(
        e.table, e.tables.at[1 - c], e.pair_send.at[4], e.pair_recv.at[4], sibling_here()
    ).wait_recv()
    each(ga, "third", 2)

    def turn_to_layer_1():
        each(gc, "third", 2)
        for phase in range(3):
            each(ga, "drain", phase)
            each(gb, "drain", phase)
        weights.keep_wait()
        weights.load(1, "attend")

    def units_of_layer_1():
        each(gd, "third", 2)
        weights.load(1, "units")

    forward_pass(
        e,
        0,
        e.rows_in,
        e.rows_mid,
        Pump(
            {
                "asked": [do(gb, "second", 2)],
                2: [do(gc, "second", 2)],
                4: [do(gd, "second", 2)],
                "attended": [do(gb, "third", 2), weights.keep],
                "end": [turn_to_layer_1],
            }
        ),
    )
    rows = e.rows_mid[...]
    e.normed[1, c] = (rows * norm_scale(rows) * e.gains[1, 0:1, :]).astype(bf16)
    forward_pass(e, 1, e.rows_mid, e.rows_out, Pump({"attended": [units_of_layer_1]}))
    backward_pass(e, 1, e.grad_in, e.rows_mid, e.grad_mid, Pump(), 0)

    def reduce_lanes(layer, kind, at, width, base, direct):
        lanes = []
        for part in range(3):
            credits = [e.credit.at[part, side] for side in range(2)]
            lanes.append(
                ReduceLane(
                    e.grads.at[layer],
                    boxes_of(e, kind, part),
                    part,
                    (at + part * width, width),
                    e.reduce_send,
                    e.reduce_recv,
                    base + 12 * part,
                    direct,
                    gives=credits if kind == "late" else None,
                    takes=credits if kind == "units" else None,
                )
            )
        return lanes

    r1 = reduce_lanes(1, "late", 0, 768, 0, (1, 2))
    rf = reduce_lanes(0, "units", GATE_AT, 512, 36, (1, 2))
    ra = reduce_lanes(0, "attend", 0, 256, 72, (0, 1, 2))
    muon = Muon(e)

    def late_done():
        finish_sum(e, 1, 0, PACK_COLS, 0)
        muon.update_moment(1, 0, PACK_COLS)
        for m in (4, 5, 6, 7, 11, 12, 13):
            muon.send(m)

    def units_done():
        finish_sum(e, 0, GATE_AT, PACK_COLS, 1)
        muon.update_moment(0, GATE_AT, PACK_COLS)
        for m in (8, 9, 10):
            muon.send(m)

    backward_pass(
        e,
        0,
        e.grad_mid,
        e.rows_in,
        e.grad_out,
        Pump(
            {
                "start": [do(r1, "first", 0)],
                "units": [do(r1, "second", 0), do(rf, "first", 0)],
                5: [do(r1, "third", 0), do(r1, "first", 1)],
                6: [do(rf, "second", 0)],
                7: [do(r1, "third", 1), do(r1, "first", 2)],
                "attended": [
                    do(r1, "third", 2),
                    late_done,
                    do(rf, "third", 0),
                    do(rf, "first", 1),
                ],
                "mixed": [do(ra, "first", 0), do(rf, "third", 1), do(rf, "first", 2)],
            }
        ),
        None,
    )
    gain_start(e, 0)
    each(ra, "third", 0)
    each(ra, "first", 1)
    gain_finish(e, 0)
    gain_start(e, 1)
    each(rf, "third", 2)
    units_done()
    each(ra, "third", 1)
    each(ra, "first", 2)
    gain_finish(e, 1)
    gain_start(e, 2)
    each(ra, "third", 2)
    finish_sum(e, 0, 0, GATE_AT, 2)
    muon.update_moment(0, 0, GATE_AT)
    for m in range(4):
        muon.send(m)
    gain_finish(e, 2)
    gain_start(e, 3)
    for lanes in (gc, gd, r1, rf, ra):
        for phase in range(3):
            each(lanes, "drain", phase)
    muon.serve_all()
    gain_finish(e, 3)
    pl.when(c != holder)(lambda: hand_over().wait_send())
    muon.finish()


REF_TABLE = [
    ("rows_in", "in", (TOKENS_HERE, D), f32),
    ("grad_in", "in", (TOKENS_HERE, D), f32),
    ("weights_own", "in", (LAYERS * ROW_SHARD, PACK_COLS), f32),
    ("moment", "in", (LAYERS * ROW_SHARD, PACK_COLS), f32),
    ("table", "in", (TOKENS_HERE, 256), f32),
    ("ends", "in", (8, 128), jnp.int32),
    ("gains", "in", (LAYERS, 8, D), f32),
    ("rows_out", "out", (TOKENS_HERE, D), f32),
    ("grad_out", "out", (TOKENS_HERE, D), f32),
    ("gain_total", "out", (8, D), f32),
    ("moment_new", "out", (LAYERS * ROW_SHARD, PACK_COLS), f32),
    ("weights_new", "out", (LAYERS * ROW_SHARD, PACK_COLS), f32),
    ("full", "hbm", (LAYERS, 2, 4, 4, PAIR_ROWS, PACK_COLS), bf16),
    ("weights", "vmem", (2, 4, 4, PAIR_ROWS, PACK_COLS), bf16),
    ("grads", "vmem", (LAYERS, 2, 4, 4, PAIR_ROWS, PACK_COLS), bf16),
    ("own", "vmem", (LAYERS * ROW_SHARD, PACK_COLS), bf16),
    ("twin", "vmem", (LAYERS * ROW_SHARD, PACK_COLS), bf16),
    ("piece", "vmem", (PAIR_ROWS, PACK_COLS), bf16),
    ("tables", "vmem", (2, TOKENS_HERE, 256), f32),
    ("rows_mid", "vmem", (TOKENS_HERE, D), f32),
    ("grad_mid", "vmem", (TOKENS_HERE, D), f32),
    ("mid_grad", "vmem", (TOKENS_HERE, D), f32),
    ("mid_rows", "vmem", (LAYERS, TOKENS_HERE, D), f32),
    ("normed", "vmem", (LAYERS, 2, TOKENS_HERE, D), bf16),
    ("normed_mid", "vmem", (LAYERS, 2, TOKENS_HERE, D), bf16),
    ("attended", "vmem", (LAYERS, 2, CHIP_TOKENS, 256), bf16),
    ("queries", "vmem", (LAYERS, GROUP, 128), bf16),
    ("keys_values", "vmem", (LAYERS, GROUP, 128), bf16),
    ("kept_output", "vmem", (LAYERS, GROUP, 2 * HEAD_DIM), f32),
    ("score_box", "vmem", (2 * GROUP, 128), f32),
    ("output_grad", "vmem", (GROUP, 128), bf16),
    ("partial", "vmem", (CHIP_TOKENS, D), f32),
    ("partial_out", "vmem", (CHIP_TOKENS, D), bf16),
    ("left_t", "vmem", (2, 4, D // 4, CHIP_TOKENS), bf16),
    ("partial_in", "vmem", (2, TOKENS_HERE, D), bf16),
    ("grad_swap", "vmem", (2, 2, TOKENS_HERE, D), bf16),
    ("mixed_grad", "vmem", (2, CHIP_TOKENS, IN_COLS), bf16),
    ("ask_out", "vmem", (HEADS_HERE, 2, ASK_ROWS, 128), bf16),
    ("ask_in", "vmem", (16, ASK_ROWS, 128), bf16),
    ("reply_out", "vmem", (16, REPLY_ROWS, 128), bf16),
    ("reply_in", "vmem", (HEADS_HERE, 2, REPLY_ROWS, 128), bf16),
    ("back_ask_in", "vmem", (16, REPLY_ROWS, 128), bf16),
    ("gain_box", "vmem", (12, 8, D), f32),
    ("square", "vmem", (SQUARE_COUNT, 32, 256), bf16),
    ("wide", "vmem", (WIDE_COUNT, PAIR_ROWS, 256), bf16),
    ("square_new", "vmem", (SQUARE_COUNT, 32, 256), bf16),
    ("wide_new", "vmem", (WIDE_COUNT, PAIR_ROWS, 256), bf16),
    ("slots", "vmem", (DEVICES, PAIR_ROWS, 256), bf16),
]
REF_TABLE += [(name, "vmem", shape, bf16) for name, shape in BOX_SHAPES.items()]
REF_TABLE += [
    ("gather_send", "dma", (144,), None),
    ("gather_recv", "dma", (144,), None),
    ("reduce_send", "dma", (108,), None),
    ("reduce_recv", "dma", (108,), None),
    ("load_sem", "dma", (4,), None),
    ("swap_send", "dma", (16,), None),
    ("swap_recv", "dma", (16,), None),
    ("ask_send", "dma", (HEADS_HERE, 2), None),
    ("reply_send", "dma", (16,), None),
    ("traffic_recv", "dma", (8,), None),
    ("pair_send", "dma", (5,), None),
    ("pair_recv", "dma", (5,), None),
    ("gain_send", "dma", (12,), None),
    ("gain_recv", "dma", (12,), None),
    ("tile_send", "dma", (OWNERS,), None),
    ("tile_recv", "dma", (OWNERS,), None),
    ("slot_recv", "dma", (2,), None),
    ("credit", "regular", (3, 2), None),
]
REF_NAMES = [row[0] for row in REF_TABLE]


def train_step(*inputs):
    scratch = []
    for name, where, shape, dtype in REF_TABLE:
        if where == "vmem":
            scratch.append(pltpu.VMEM(shape, dtype))
        elif where == "dma":
            scratch.append(pltpu.SemaphoreType.DMA(shape))
        elif where == "regular":
            scratch.append(pltpu.SemaphoreType.REGULAR(shape))
    outs = [row for row in REF_TABLE if row[1] in ("out", "hbm")]
    return pl.pallas_call(
        step_kernel,
        out_shape=[jax.ShapeDtypeStruct(shape, dtype) for _, _, shape, dtype in outs],
        in_specs=[pl.BlockSpec(memory_space=pltpu.VMEM)] * len(inputs),
        out_specs=[
            pl.BlockSpec(memory_space=pltpu.HBM if where == "hbm" else pltpu.VMEM)
            for _, where, _, _ in outs
        ],
        scratch_shapes=scratch,
        compiler_params=pltpu.CompilerParams(
            collective_id=0, has_side_effects=True, vmem_limit_bytes=63 * MIB
        ),
        name="train_step",
    )(*inputs)


def pack_layers(attend_in, attend_out, expand, shrink):
    query_key = jnp.stack(
        [attend_in[:, k].reshape(LAYERS, ROW_SHARD, 3, HEAD_DIM) for k in range(2)], axis=3
    )
    return jnp.concatenate(
        [
            query_key.reshape(LAYERS, ROW_SHARD, 384),
            attend_in[:, 2],
            jnp.swapaxes(attend_out, 1, 2),
            expand[:, 0],
            expand[:, 1],
            jnp.swapaxes(shrink, 1, 2),
        ],
        axis=2,
    )


def four_squares(packed):
    query_key = packed[:, :, 0:384].reshape(LAYERS, ROW_SHARD, 3, 2, HEAD_DIM)
    return [
        query_key[:, :, :, 0].reshape(LAYERS, ROW_SHARD, 192),
        query_key[:, :, :, 1].reshape(LAYERS, ROW_SHARD, 192),
        packed[:, :, 384:576],
        packed[:, :, 576:768],
    ]


def unpack_layers(packed):
    query, key, value, out = four_squares(packed)
    return (
        jnp.stack([query, key, value], axis=1),
        jnp.swapaxes(out, 1, 2),
        jnp.stack([packed[:, :, 768:1280], packed[:, :, 1280:1792]], axis=1),
        jnp.swapaxes(packed[:, :, 1792:2304], 1, 2),
    )


def to_chip_order(values):
    split = values.reshape(values.shape[:-1] + (4, 2, 4, ROW_SHARD))
    return jnp.swapaxes(split, -3, -2).reshape(values.shape)


def from_chip_order(values):
    split = values.reshape(values.shape[:-1] + (4, 4, 2, ROW_SHARD))
    return jnp.swapaxes(split, -3, -2).reshape(values.shape)


def rope_table(positions):
    frequency = rope_base ** (-jnp.arange(HEAD_DIM // 2, dtype=jnp.float32) * 2.0 / HEAD_DIM)
    angles = positions.astype(jnp.float32)[:, None] * frequency[None, :]
    cosine, sine_part = jnp.cos(angles), jnp.sin(angles)
    return jnp.concatenate(
        [cosine, cosine, cosine, cosine, -sine_part, sine_part, -sine_part, sine_part], axis=1
    )


def body(
    hidden_in,
    out_grad,
    seq_lengths,
    norm_gains,
    gain_first,
    gain_second,
    attend_in,
    attend_out,
    expand,
    shrink,
    attend_in_moment,
    attend_out_moment,
    expand_moment,
    shrink_moment,
):
    document, position, places = doc_layout(seq_lengths[0], GROUP)
    doc_ends = jnp.cumsum(seq_lengths[0])
    ends = jnp.pad(
        jnp.broadcast_to(doc_ends[0:2, None], (2, 128)).astype(jnp.int32), ((0, 6), (0, 0))
    )
    token_block = lax.axis_index("ctx") * 4 + lax.axis_index("tp")
    table = rope_table(
        lax.dynamic_slice_in_dim(position, token_block * TOKENS_HERE, TOKENS_HERE)
    )
    weights_packed = pack_layers(attend_in, attend_out, expand, shrink)
    moment_packed = pack_layers(attend_in_moment, attend_out_moment, expand_moment, shrink_moment)
    gains = jnp.pad(to_chip_order(norm_gains), ((0, 0), (0, 6), (0, 0)))
    flat = (LAYERS * ROW_SHARD, PACK_COLS)
    rows, rows_grad, gain_total, moment_new, weights_new, _ = train_step(
        to_chip_order(hidden_in).astype(jnp.float32),
        to_chip_order(out_grad).astype(jnp.float32),
        weights_packed.reshape(flat),
        moment_packed.reshape(flat),
        table,
        ends,
        gains,
    )
    moment_new = moment_new.reshape(LAYERS, ROW_SHARD, PACK_COLS)
    weights_new = weights_new.reshape(LAYERS, ROW_SHARD, PACK_COLS)
    gain_grad = from_chip_order(gain_total[0:4]).reshape(LAYERS, 2, D)
    gain_first_new = first_decay * gain_first + (1.0 - first_decay) * gain_grad
    gain_second_new = second_decay * gain_second + (1.0 - second_decay) * gain_grad * gain_grad
    norm_gains_new = norm_gains - gain_rate * (gain_first_new / (1.0 - first_decay**STEP)) / (
        jnp.sqrt(gain_second_new / (1.0 - second_decay**STEP)) + adam_eps
    )
    return (
        from_chip_order(rows),
        from_chip_order(rows_grad),
        gain_first_new,
        gain_second_new,
        norm_gains_new,
        *unpack_layers(moment_new),
        *unpack_layers(weights_new),
    )


def solution(mesh):
    placed = (
        P(("fsdp", "ctx", "tp"), None),
        P(("fsdp", "ctx", "tp"), None),
        P("fsdp", None),
        P(),
        P(),
        P(),
        P(None, None, ("fsdp", "ctx"), "tp"),
        P(None, "tp", ("fsdp", "ctx")),
        P(None, None, ("fsdp", "ctx"), "tp"),
        P(None, "tp", ("fsdp", "ctx")),
        P(None, None, ("fsdp", "ctx"), "tp"),
        P(None, "tp", ("fsdp", "ctx")),
        P(None, None, ("fsdp", "ctx"), "tp"),
        P(None, "tp", ("fsdp", "ctx")),
    )
    return jax.shard_map(
        body,
        mesh=mesh,
        in_specs=placed,
        out_specs=(
            P(("fsdp", "ctx", "tp"), None),
            P(("fsdp", "ctx", "tp"), None),
            P(),
            P(),
            P(),
            P(None, None, ("fsdp", "ctx"), "tp"),
            P(None, "tp", ("fsdp", "ctx")),
            P(None, None, ("fsdp", "ctx"), "tp"),
            P(None, "tp", ("fsdp", "ctx")),
            P(None, None, ("fsdp", "ctx"), "tp"),
            P(None, "tp", ("fsdp", "ctx")),
            P(None, None, ("fsdp", "ctx"), "tp"),
            P(None, "tp", ("fsdp", "ctx")),
        ),
        check_vma=False,
    )
```

```python
import math
import types

import jax
import jax.numpy as jnp
from jax import lax
from jax.experimental import pallas as pl
from jax.experimental.pallas import tpu as pltpu
from jax.sharding import PartitionSpec as P

D = 768
HEAD_DIM = 64
FF = 2048
NS_STEPS = 4
STEP = 5


norm_eps = 1e-05
rope_base = 10000.0
mask_fill = -1e30
quintic_one = 3.4445
quintic_two = -4.775
quintic_three = 2.0315
moment_decay = 0.95
matrix_rate = 0.1
project_rate = 0.8
matrix_decay = 0.1
gain_rate = 0.8
first_decay = 0.9
second_decay = 0.95
adam_eps = 1e-08
ortho_eps = 1e-07


def doc_layout(lengths, row_count):
    doc_ends = jnp.cumsum(lengths)
    starts = doc_ends - lengths
    places = jnp.arange(row_count, dtype=jnp.int32)
    document = jnp.sum((places[:, None] >= doc_ends[None, :]).astype(jnp.int32), axis=1)
    member = document[:, None] == jnp.arange(lengths.shape[0], dtype=jnp.int32)[None, :]
    offset = jnp.sum(jnp.where(member, starts[None, :], 0), axis=1)
    return (document, places - offset, places)


MESH_ID = pl.DeviceIdType.MESH
ROW_SHARD = 24
PAIR_ROWS = 2 * ROW_SHARD
PACK_COLS = 2304
LAYERS = 2
MIB = 1024 * 1024
DEVICES = 128


def whereami():
    fsdp_index = lax.axis_index("fsdp")
    return (lax.div(fsdp_index, 2), lax.rem(fsdp_index, 2), lax.axis_index("ctx"), lax.axis_index("tp"))


def device_at(y, c, z, x):
    return (y * 2 + c, z, x)


def device_of_index(index):
    return (lax.div(index, 16), lax.rem(lax.div(index, 4), 4), lax.rem(index, 4))


def index_here():
    y, c, z, x = whereami()
    return (y * 2 + c) * 16 + z * 4 + x


def sibling_here():
    y, c, z, x = whereami()
    return device_at(y, 1 - c, z, x)


def ring(index, offset):
    return lax.rem(index + offset, 4)


def remote(source, target, send_sem, recv_sem, device):
    return pltpu.make_async_remote_copy(
        src_ref=source,
        dst_ref=target,
        send_sem=send_sem,
        recv_sem=recv_sem,
        device_id=device,
        device_id_type=MESH_ID,
    )


def signal_everyone():
    barrier = pltpu.get_barrier_semaphore()
    mine = index_here()

    def signal_one(offset, carry):
        device = device_of_index(lax.rem(mine + offset, DEVICES))
        pl.semaphore_signal(barrier, inc=1, device_id=device, device_id_type=MESH_ID)
        return carry

    lax.fori_loop(1, DEVICES, signal_one, 0)


def wait_for_everyone():
    pl.semaphore_wait(pltpu.get_barrier_semaphore(), DEVICES - 1)


def neighbour(axis, offset):
    y, c, z, x = whereami()
    if axis == "y":
        return device_at(ring(y, offset), c, z, x)
    if axis == "z":
        return device_at(y, c, ring(z, offset), x)
    return device_at(y, c, z, ring(x, offset))


PART_ORDER = (("x", "y", "z"), ("y", "z", "x"), ("z", "x", "y"))


def part_view(ref, columns, done, axis, place, half):
    y, c, z, x = whereami()
    whole = slice(None)

    def index(name, own):
        if name == axis:
            return place
        return whole if name in done else own

    if axis == "x":
        pick_x = lax.rem(place, 2)
    else:
        pick_x = whole if "x" in done else lax.rem(x, 2)
    start, width = columns
    if half is not None:
        width = width // 2
        start = start + half * width
    return ref.at[pick_x, index("y", y), index("z", z), :, pl.ds(start, width)]


def ring_exists(axis, done, place):
    y, c, z, x = whereami()
    if axis == "x":
        return lax.div(place, 2) == c
    if "x" in done:
        return None
    return lax.div(x, 2) == c


def run_if(condition, action):
    if condition is None:
        action()
    else:
        pl.when(condition)(action)


class GatherLane:
    def __init__(self, ref, part, columns, send, recv, base, direct):
        self.ref, self.part, self.columns = ref, part, columns
        self.send, self.recv, self.base, self.direct = send, recv, base, direct

    def parts(self, phase):
        axis = PART_ORDER[self.part][phase]
        done = PART_ORDER[self.part][:phase]
        y, c, z, x = whereami()
        return axis, done, {"x": x, "y": y, "z": z}[axis], self.base + 4 * phase

    def copy(self, phase, slot, place, half, offset):
        axis, done, me, base = self.parts(phase)
        view = part_view(self.ref, self.columns, done, axis, place, half)
        return remote(
            view, view, self.send.at[base + slot], self.recv.at[base + slot], neighbour(axis, offset)
        )

    def first(self, phase):
        axis, done, me, base = self.parts(phase)

        def action():
            if phase in self.direct:
                for offset in (1, 2, 3):
                    self.copy(phase, offset - 1, me, None, offset).start()
            else:
                self.copy(phase, 0, me, None, 1).start()
                self.copy(phase, 1, me, None, 3).start()

        run_if(ring_exists(axis, done, me), action)

    def second(self, phase):
        axis, done, me, base = self.parts(phase)
        left, right = ring(me, 3), ring(me, 1)

        def from_left():
            self.copy(phase, 0, left, None, 1).wait_recv()
            self.copy(phase, 2, left, 0, 1).start()

        def from_right():
            self.copy(phase, 1, right, None, 1).wait_recv()
            self.copy(phase, 3, right, 1, 3).start()

        run_if(ring_exists(axis, done, left), from_left)
        run_if(ring_exists(axis, done, right), from_right)

    def third(self, phase):
        axis, done, me, base = self.parts(phase)
        far = ring(me, 2)

        def action():
            self.copy(phase, 2, far, 0, 1).wait_recv()
            self.copy(phase, 3, far, 1, 1).wait_recv()

        if phase in self.direct:
            for offset in (1, 2, 3):
                place = ring(me, 4 - offset)
                run_if(
                    ring_exists(axis, done, place),
                    lambda place=place, offset=offset: self.copy(
                        phase, offset - 1, place, None, 1
                    ).wait_recv(),
                )
        else:
            run_if(ring_exists(axis, done, far), action)

    def drain(self, phase):
        axis, done, me, base = self.parts(phase)
        left, right = ring(me, 3), ring(me, 1)

        def own():
            for slot in range(3 if phase in self.direct else 2):
                self.copy(phase, slot, me, None, 1).wait_send()

        run_if(ring_exists(axis, done, me), own)
        if phase not in self.direct:
            run_if(
                ring_exists(axis, done, left), lambda: self.copy(phase, 2, left, 0, 1).wait_send()
            )
            run_if(
                ring_exists(axis, done, right), lambda: self.copy(phase, 3, right, 1, 3).wait_send()
            )


class ReduceLane:
    def __init__(self, ref, boxes, part, columns, send, recv, base, direct, gives=None, takes=None):
        self.ref, self.boxes, self.part, self.columns = ref, boxes, part, columns
        self.send, self.recv, self.base, self.direct = send, recv, base, direct
        self.gives, self.takes = gives, takes

    def parts(self, phase):
        axis = PART_ORDER[self.part][2 - phase]
        done = PART_ORDER[self.part][: 2 - phase]
        y, c, z, x = whereami()
        return axis, done, {"x": x, "y": y, "z": z}[axis], self.base + 4 * phase

    def copy(self, phase, slot, place, half, offset):
        axis, done, me, base = self.parts(phase)
        view = part_view(self.ref, self.columns, done, axis, place, half)
        return remote(
            view,
            self.boxes[phase][slot],
            self.send.at[base + slot],
            self.recv.at[base + slot],
            neighbour(axis, offset),
        )

    def add(self, phase, place, half, boxes):
        axis, done, me, base = self.parts(phase)
        view = part_view(self.ref, self.columns, done, axis, place, half)
        lead = view.shape[:-2]

        def summed(where):
            terms = [view[where]] + [box[where] for box in boxes]
            while len(terms) > 1:
                terms = [
                    terms[i] + terms[i + 1] if i + 1 < len(terms) else terms[i]
                    for i in range(0, len(terms), 2)
                ]
            return terms[0]

        def add_one(index, carry):
            where = []
            for extent in reversed(lead):
                where.insert(0, lax.rem(index, extent))
                index = lax.div(index, extent)
            view[tuple(where)] = summed(tuple(where))
            return carry

        if len(lead) == 0:
            view[...] = summed(...)
        else:
            lax.fori_loop(0, math.prod(lead), add_one, 0)

    def first(self, phase):
        axis, done, me, base = self.parts(phase)
        far = ring(me, 2)

        def action():
            self.copy(phase, 0, far, 0, 1).start()
            self.copy(phase, 1, far, 1, 3).start()

        if phase in self.direct:
            for offset in (1, 2, 3):
                place = ring(me, offset)
                run_if(
                    ring_exists(axis, done, place),
                    lambda place=place, offset=offset: self.copy(
                        phase, offset - 1, place, None, offset
                    ).start(),
                )
        else:
            run_if(ring_exists(axis, done, far), action)

    def second(self, phase):
        axis, done, me, base = self.parts(phase)
        left, right = ring(me, 3), ring(me, 1)

        def to_right():
            self.copy(phase, 0, right, 0, 1).wait_recv()
            self.add(phase, right, 0, [self.boxes[phase][0]])
            if phase == 0 and self.takes is not None:
                pl.semaphore_wait(self.takes[0], 1)
            self.copy(phase, 2, right, None, 1).start()

        def to_left():
            self.copy(phase, 1, left, 1, 1).wait_recv()
            self.add(phase, left, 1, [self.boxes[phase][1]])
            if phase == 0 and self.takes is not None:
                pl.semaphore_wait(self.takes[1], 1)
            self.copy(phase, 3, left, None, 3).start()

        run_if(ring_exists(axis, done, right), to_right)
        run_if(ring_exists(axis, done, left), to_left)

    def third(self, phase):
        axis, done, me, base = self.parts(phase)

        def action():
            if phase in self.direct:
                slots = (0, 1, 2)
            else:
                slots = (2, 3)
            for slot in slots:
                self.copy(phase, slot, me, None, 1).wait_recv()
            self.add(phase, me, None, [self.boxes[phase][slot] for slot in slots])
            if phase == 0 and self.gives is not None:
                for sem, offset in zip(self.gives, (3, 1)):
                    pl.semaphore_signal(
                        sem, inc=1, device_id=neighbour(axis, offset), device_id_type=MESH_ID
                    )

        run_if(ring_exists(axis, done, me), action)

    def drain(self, phase):
        axis, done, me, base = self.parts(phase)
        far, left, right = ring(me, 2), ring(me, 3), ring(me, 1)

        def own():
            self.copy(phase, 0, far, 0, 1).wait_send()
            self.copy(phase, 1, far, 1, 3).wait_send()

        if phase in self.direct:
            for offset in (1, 2, 3):
                place = ring(me, offset)
                run_if(
                    ring_exists(axis, done, place),
                    lambda place=place, offset=offset: self.copy(
                        phase, offset - 1, place, None, offset
                    ).wait_send(),
                )
            return
        run_if(ring_exists(axis, done, far), own)
        run_if(ring_exists(axis, done, right), lambda: self.copy(phase, 2, right, None, 1).wait_send())
        run_if(ring_exists(axis, done, left), lambda: self.copy(phase, 3, left, None, 3).wait_send())


def box_shape(part, phase):
    order = PART_ORDER[part]
    axis, done = order[2 - phase], order[: 2 - phase]
    lead = []
    for name, extent in (("x", 2), ("y", 4), ("z", 4)):
        if name != axis and name in done:
            lead.append(extent)
    return tuple(lead)


def each(lanes, step, phase):
    for lane in lanes:
        getattr(lane, step)(phase)


HEADS_HERE = 6
TOKENS_HERE = 128
CHIP_TOKENS = 256
GROUP = 2048
Q_BLOCK = 256
K_BLOCK = 512
Q_BLOCKS = GROUP // Q_BLOCK
IN_COLS = 640
OUT_AT = 512
GATE_AT = 768
UP_AT = 1280
DOWN_AT = 1792
ASK_ROWS = 192
REPLY_ROWS = 64
SQUARE_COUNT = 8
WIDE_COUNT = 6
OWNERS = SQUARE_COUNT + WIDE_COUNT
bf16 = jnp.bfloat16
f32 = jnp.float32


def dot_nn(left, right):
    return jnp.dot(left, right, preferred_element_type=f32)


def dot_nt(left, right):
    return lax.dot_general(left, right, (((1,), (1,)), ((), ())), preferred_element_type=f32)


def dot_tn(left, right):
    return lax.dot_general(left, right, (((0,), (0,)), ((), ())), preferred_element_type=f32)


def sigmoid(value):
    return 1.0 / (1.0 + jnp.exp(-value))


def norm_scale(rows):
    return lax.rsqrt(jnp.mean(rows * rows, axis=-1, keepdims=True) + norm_eps)


def norm_back(rows, gain, grad):
    scale = norm_scale(rows)
    unit = rows * scale
    inner = grad * gain
    back = scale * (inner - unit * jnp.mean(inner * unit, axis=-1, keepdims=True))
    return back, jnp.sum(grad * unit, axis=0, keepdims=True)


def swap_halves(values):
    lower = lax.rem(lax.broadcasted_iota(jnp.int32, values.shape, 1), 64) < 32
    return jnp.where(lower, pltpu.roll(values, 96, 1), pltpu.roll(values, 32, 1))


def is_owner_here():
    y, c, z, x = whereami()
    return z < 3


def head_here():
    y, c, z, x = whereami()
    return 4 * z + x


def own_half(both):
    y, c, z, x = whereami()
    return jnp.where(c == 0, both[0:TOKENS_HERE], both[TOKENS_HERE:CHIP_TOKENS])


class Swap:
    def __init__(self, e, slot):
        self.send, self.recv = e.swap_send.at[slot], e.swap_recv.at[slot]

    def start(self, source, target):
        self.copy = remote(source, target, self.send, self.recv, sibling_here())
        self.copy.start()

    def wait(self):
        self.copy.wait_send()
        self.copy.wait_recv()


class HeadTraffic:
    def __init__(self, outbox, inbox, sems, recv_sem):
        self.outbox, self.inbox, self.sems, self.recv_sem = outbox, inbox, sems, recv_sem

    def owner_place(self, head):
        y, c, z, x = whereami()
        number = HEADS_HERE * c + head
        return lax.div(number, 4), lax.rem(number, 4)

    def owner_is_here(self, head, group):
        y, c, z, x = whereami()
        owner_z, owner_x = self.owner_place(head)
        return (owner_z == z) & (owner_x == x) & (c == group)

    def to_owner(self, head, group):
        y, c, z, x = whereami()
        owner_z, owner_x = self.owner_place(head)
        return remote(
            self.outbox.at[head, group],
            self.inbox.at[z * 4 + x],
            self.sems.at[head, group],
            self.recv_sem,
            device_at(y, group, owner_z, owner_x),
        )

    def send_to_owner(self, head, group):
        y, c, z, x = whereami()
        here = self.owner_is_here(head, group)

        @pl.when(here)
        def _():
            pltpu.make_async_copy(
                self.outbox.at[head, group], self.inbox.at[z * 4 + x], self.recv_sem
            ).start()

        @pl.when(jnp.logical_not(here))
        def _():
            self.to_owner(head, group).start()

    def drain_to_owner(self):
        for head in range(HEADS_HERE):
            for group in range(2):

                @pl.when(jnp.logical_not(self.owner_is_here(head, group)))
                def _(head=head, group=group):
                    self.to_owner(head, group).wait_send()

    def tokens_are_here(self, block):
        y, c, z, x = whereami()
        core = lax.div(head_here(), HEADS_HERE)
        return (lax.div(block, 4) == z) & (lax.rem(block, 4) == x) & (core == c)

    def to_tokens(self, block):
        y, c, z, x = whereami()
        core = lax.div(head_here(), HEADS_HERE)
        slot = head_here() - HEADS_HERE * core
        return remote(
            self.outbox.at[block],
            self.inbox.at[slot, c],
            self.sems.at[block],
            self.recv_sem,
            device_at(y, core, lax.div(block, 4), lax.rem(block, 4)),
        )

    def send_to_tokens(self, block):
        y, c, z, x = whereami()
        here = self.tokens_are_here(block)

        @pl.when(here)
        def _():
            slot = head_here() - HEADS_HERE * lax.div(head_here(), HEADS_HERE)
            pltpu.make_async_copy(
                self.outbox.at[block], self.inbox.at[slot, c], self.recv_sem
            ).start()

        @pl.when(jnp.logical_not(here))
        def _():
            self.to_tokens(block).start()

    def drain_to_tokens(self):
        def drain(block, carry):
            @pl.when(jnp.logical_not(self.tokens_are_here(block)))
            def _():
                self.to_tokens(block).wait_send()

            return carry

        lax.fori_loop(0, 16, drain, 0)

    def arrived(self):
        pltpu.make_async_copy(self.inbox, self.inbox, self.recv_sem).wait()


def block_mask(ends, query_at, key_at):
    query_row = query_at + lax.broadcasted_iota(jnp.int32, (Q_BLOCK, 1), 0)
    first, second = ends[0:1, 0:1], ends[1:2, 0:1]
    start = jnp.where(query_row >= second, second, jnp.where(query_row >= first, first, 0))
    shape = (Q_BLOCK, K_BLOCK)
    query = query_at + lax.broadcasted_iota(jnp.int32, shape, 0)
    key = key_at + lax.broadcasted_iota(jnp.int32, shape, 1)
    return (key <= query) & (key >= start)


def run_pumps(pumps, block):
    for number, action in sorted(pumps.items()):
        pl.when(block == number)(action)


def score_rows(step, lane):
    at = (step * (K_BLOCK // 128) + lane) * Q_BLOCK
    return pl.ds(pl.multiple_of(at, Q_BLOCK), Q_BLOCK)


def attend_forward(queries, keys_values, ends, score_box, kept_output, pumps, block_done):
    def one_block(block, carry):
        run_pumps(pumps, block)
        query_at = pl.multiple_of(block * Q_BLOCK, Q_BLOCK)
        rows = pl.ds(query_at, Q_BLOCK)
        query = queries[rows, :]
        key_blocks = lax.div(block, 2) + 1

        def scores(step, top):
            key_at = pl.multiple_of(step * K_BLOCK, K_BLOCK)
            raw = dot_nt(query, keys_values[pl.ds(key_at, K_BLOCK), :])
            masked = jnp.where(block_mask(ends, query_at, key_at), raw, mask_fill)
            for lane in range(K_BLOCK // 128):
                tile = masked[:, 128 * lane : 128 * lane + 128]
                score_box[score_rows(step, lane), :] = tile
                top = jnp.maximum(top, tile)
            return top

        top = lax.fori_loop(0, key_blocks, scores, jnp.full((Q_BLOCK, 128), mask_fill, f32))
        top = jnp.max(top, axis=1, keepdims=True)

        def collect(step, state):
            total, gathered = state
            key_at = pl.multiple_of(step * K_BLOCK, K_BLOCK)
            tiles = []
            for lane in range(K_BLOCK // 128):
                tile = jnp.exp(score_box[score_rows(step, lane), :] - top)
                total = total + tile
                tiles.append(tile.astype(bf16))
            return total, gathered + dot_nn(
                jnp.concatenate(tiles, axis=1), keys_values[pl.ds(key_at, K_BLOCK), :]
            )

        total, gathered = lax.fori_loop(
            0,
            key_blocks,
            collect,
            (jnp.zeros((Q_BLOCK, 128), f32), jnp.zeros((Q_BLOCK, 128), f32)),
        )
        total = jnp.sum(total, axis=1, keepdims=True)
        lane = lax.broadcasted_iota(jnp.int32, (Q_BLOCK, 128), 1)
        kept_output[rows, :] = jnp.where(
            lane < HEAD_DIM, top + jnp.log(total), gathered / total
        )
        block_done(block)
        return carry

    lax.fori_loop(0, Q_BLOCKS, one_block, 0)


def attend_backward(
    queries, keys_values, output_grad, kept_output, ends, query_grad, key_value_grad, pumps
):
    key_value_grad[...] = jnp.zeros_like(key_value_grad)

    def one_block(block, carry):
        run_pumps(pumps, block)
        query_at = pl.multiple_of(block * Q_BLOCK, Q_BLOCK)
        rows = pl.ds(query_at, Q_BLOCK)
        query = queries[rows, :]
        grad = output_grad[rows, :]
        kept = kept_output[rows, :]
        logs = kept[:, 0:1]
        inner = jnp.sum(grad.astype(f32) * kept, axis=1, keepdims=True)

        def one_key(step, total):
            key_at = pl.multiple_of(step * K_BLOCK, K_BLOCK)
            keys_here = pl.ds(key_at, K_BLOCK)
            both = keys_values[keys_here, :]
            masked = jnp.where(
                block_mask(ends, query_at, key_at), dot_nt(query, both), mask_fill
            )
            probability = jnp.exp(masked - logs)
            probability_grad = dot_nt(grad, both)
            score_grad = (probability * (probability_grad - inner)).astype(bf16)
            key_value_grad[keys_here, :] += dot_tn(score_grad, query) + dot_tn(
                probability.astype(bf16), grad
            )
            return total + dot_nn(score_grad, both)

        query_grad[rows, :] = lax.fori_loop(
            0, lax.div(block, 2) + 1, one_key, jnp.zeros((Q_BLOCK, 128), f32)
        )
        return carry

    lax.fori_loop(0, Q_BLOCKS, one_block, 0)


class Weights:
    def __init__(self, e):
        self.e = e
        self.ranges = {"attend": (0, GATE_AT, 0), "units": (GATE_AT, PACK_COLS - GATE_AT, 1)}

    def copy(self, layer, name):
        start, width, slot = self.ranges[name]
        columns = pl.ds(start, width)
        return pltpu.make_async_copy(
            self.e.full.at[layer, :, :, :, :, columns],
            self.e.weights.at[:, :, :, :, columns],
            self.e.load_sem.at[slot],
        )

    def load(self, layer, name):
        self.copy(layer, name).start()

    def wait(self, layer, name):
        self.copy(layer, name).wait()

    def keep_copy(self):
        return pltpu.make_async_copy(self.e.weights, self.e.full.at[0], self.e.load_sem.at[3])

    def keep(self):
        self.keep_copy().start()

    def keep_wait(self):
        self.keep_copy().wait()

    def units(self, step, start):
        side, at = lax.div(step, 2), start + 256 * lax.rem(step, 2)
        columns = pl.ds(pl.multiple_of(at, 128), 256)
        return self.e.weights[side, :, :, :, columns].reshape(D, 256)

    def get(self, side, start, stop):
        return self.e.weights[side, :, :, :, start:stop].reshape(D, stop - start)


def nothing():
    pass


def forward_pass(e, layer, rows_ref, rows_out, pump):
    y, c, z, x = whereami()
    weights = Weights(e)
    swaps = [Swap(e, 4 * layer + slot) for slot in range(4)]
    ask = HeadTraffic(e.ask_out, e.ask_in, e.ask_send, e.traffic_recv.at[4 * layer])
    answer = HeadTraffic(e.reply_out, e.reply_in, e.reply_send, e.traffic_recv.at[4 * layer + 1])
    theirs = pl.ds(pl.multiple_of((1 - c) * TOKENS_HERE, TOKENS_HERE), TOKENS_HERE)
    swaps[0].start(e.normed.at[layer, c], e.normed.at[layer, c])
    pump("start")
    if layer == 1:
        weights.wait(layer, "attend")
    swaps[0].wait()
    chip_normed = e.normed[layer].reshape(CHIP_TOKENS, D)
    cosine = e.tables[:, :, 0:128].reshape(CHIP_TOKENS, 128)
    sine = e.tables[:, :, 128:256].reshape(CHIP_TOKENS, 128)
    for side in range(2):
        mixed = dot_nn(chip_normed, weights.get(side, 0, IN_COLS))
        for inner in range(3):
            head = 3 * side + inner
            pair = mixed[:, 128 * inner : 128 * inner + 128]
            pair = (pair * cosine + swap_halves(pair) * sine).astype(bf16)
            value = mixed[:, 384 + 64 * inner : 448 + 64 * inner]
            for group in range(2):
                at = TOKENS_HERE * group
                e.ask_out[head, group, 0:128] = pair[at : at + 128]
                e.ask_out[head, group, 128:192] = jnp.concatenate(
                    [value[at : at + 64], value[at + 64 : at + 128]], axis=1
                ).astype(bf16)
                ask.send_to_owner(head, group)
    pump("asked")
    queries, keys_values = e.queries.at[layer], e.keys_values.at[layer]
    kept_output = e.kept_output.at[layer]

    @pl.when(is_owner_here())
    def _():
        ask.arrived()

        def place(block, carry):
            at = pl.multiple_of(block * TOKENS_HERE, TOKENS_HERE)
            pair = e.ask_in[block, 0:128].astype(f32)
            zeros = jnp.zeros((TOKENS_HERE, HEAD_DIM), f32)
            queries[pl.ds(at, 128), :] = jnp.concatenate(
                [pair[:, 0:64] * (1.0 / math.sqrt(HEAD_DIM)), zeros], axis=1
            ).astype(bf16)
            both = e.ask_in[block, 128:192].astype(f32)
            value = jnp.concatenate([both[:, 0:64], both[:, 64:128]], axis=0)
            keys_values[pl.ds(at, 128), :] = jnp.concatenate(
                [pair[:, 64:128], value], axis=1
            ).astype(bf16)
            return carry

        lax.fori_loop(0, 16, place, 0)

        def send_rows(block):
            for half in range(2):
                at = pl.multiple_of(block * Q_BLOCK + half * 128, 128)
                first = kept_output[pl.ds(at, 64), :]
                second = kept_output[pl.ds(at + 64, 64), :]
                e.reply_out[2 * block + half] = jnp.concatenate(
                    [first[:, HEAD_DIM:], second[:, HEAD_DIM:]], axis=1
                ).astype(bf16)
                answer.send_to_tokens(2 * block + half)

        attend_forward(
            queries, keys_values, e.ends, e.score_box, kept_output, pump.blocks(), send_rows
        )

    @pl.when(jnp.logical_not(is_owner_here()))
    def _():
        for number, action in sorted(pump.blocks().items()):
            action()

    pump("attended")
    answer.arrived()
    pump("answered")
    partial = None
    for side in range(2):
        columns = [jnp.zeros((CHIP_TOKENS, 64), f32)]
        for inner in range(3):
            pieces = []
            for group in range(2):
                both = e.reply_in[3 * side + inner, group].astype(f32)
                pieces += [both[:, 0:64], both[:, 64:128]]
            columns.append(jnp.concatenate(pieces, axis=0))
        e.attended[layer, side] = jnp.concatenate(columns, axis=1).astype(bf16)
        term = dot_nt(e.attended[layer, side], weights.get(side, OUT_AT, GATE_AT))
        partial = term if partial is None else partial + term
    e.partial_out[...] = partial.astype(bf16)
    swaps[1].start(e.partial_out.at[theirs], e.partial_in.at[0])
    own_part = own_half(partial)
    swaps[1].wait()
    middle = rows_ref[...] + (own_part + e.partial_in[0].astype(f32))
    e.mid_rows[layer] = middle
    e.normed_mid[layer, c] = (middle * norm_scale(middle) * e.gains[layer, 1:2, :]).astype(bf16)
    swaps[2].start(e.normed_mid.at[layer, c], e.normed_mid.at[layer, c])
    if layer == 1:
        weights.wait(layer, "units")
    swaps[2].wait()
    e.partial[...] = jnp.zeros_like(e.partial)

    def some_units(step, carry):
        chip_mid = e.normed_mid[layer].reshape(CHIP_TOKENS, D)
        gate = dot_nn(chip_mid, weights.units(step, GATE_AT))
        up = dot_nn(chip_mid, weights.units(step, UP_AT))
        active = (gate * sigmoid(gate) * up).astype(bf16)
        e.partial[...] += dot_nt(active, weights.units(step, DOWN_AT))
        return carry

    lax.fori_loop(0, 4, some_units, 0)
    partial = e.partial[...]
    e.partial_out[...] = partial.astype(bf16)
    swaps[3].start(e.partial_out.at[theirs], e.partial_in.at[1])
    own_part = own_half(partial)
    pump("units")
    swaps[3].wait()
    rows_out[...] = e.mid_rows[layer] + (own_part + e.partial_in[1].astype(f32))
    ask.drain_to_owner()
    pl.when(is_owner_here())(answer.drain_to_tokens)
    pump("end")


def backward_pass(e, layer, grad_ref, rows_ref, grad_out, pump, next_layer):
    y, c, z, x = whereami()
    weights = Weights(e)
    swaps = [Swap(e, 8 + 4 * layer + slot) for slot in range(4)]
    ask = HeadTraffic(e.back_ask_out, e.back_ask_in, e.ask_send, e.traffic_recv.at[4 * layer + 2])
    answer = HeadTraffic(
        e.back_reply_out, e.back_reply_in, e.reply_send, e.traffic_recv.at[4 * layer + 3]
    )
    theirs = pl.ds(pl.multiple_of((1 - c) * TOKENS_HERE, TOKENS_HERE), TOKENS_HERE)

    def transpose_rows(which, value):
        e.left_t[which] = value.T.reshape(4, D // 4, CHIP_TOKENS)

    def weight_grad(side, start, width, which, right):
        columns = pl.ds(pl.multiple_of(start, 128), width)
        for block in range(4):
            e.grads[layer, side, block, :, :, columns] = (
                dot_nn(e.left_t[which, block], right).astype(bf16).reshape(4, PAIR_ROWS, width)
            )

    e.grad_swap[0, c] = grad_ref[...].astype(bf16)
    swaps[0].start(e.grad_swap.at[0, c], e.grad_swap.at[0, c])
    pump("start")
    if next_layer is None:
        weights.wait(layer, "units")
    swaps[0].wait()
    transpose_rows(0, e.grad_swap[0].reshape(CHIP_TOKENS, D))
    transpose_rows(1, e.normed_mid[layer].reshape(CHIP_TOKENS, D))
    e.partial[...] = jnp.zeros_like(e.partial)

    def some_units(step, carry):
        down = e.grad_swap[0].reshape(CHIP_TOKENS, D)
        chip_mid = e.normed_mid[layer].reshape(CHIP_TOKENS, D)
        gate = dot_nn(chip_mid, weights.units(step, GATE_AT))
        up = dot_nn(chip_mid, weights.units(step, UP_AT))
        active_grad = dot_nn(down, weights.units(step, DOWN_AT))
        sigma = sigmoid(gate)
        active = gate * sigma
        gate_grad = (active_grad * up * sigma * (1.0 + gate * (1.0 - sigma))).astype(bf16)
        up_grad = (active_grad * active).astype(bf16)
        side, at = lax.div(step, 2), 256 * lax.rem(step, 2)
        weight_grad(side, DOWN_AT + at, 256, 0, (active * up).astype(bf16))
        weight_grad(side, GATE_AT + at, 256, 1, gate_grad)
        weight_grad(side, UP_AT + at, 256, 1, up_grad)
        e.partial[...] += dot_nt(gate_grad, weights.units(step, GATE_AT)) + dot_nt(
            up_grad, weights.units(step, UP_AT)
        )
        return carry

    lax.fori_loop(0, 4, some_units, 0)
    partial = e.partial[...]
    e.partial_out[...] = partial.astype(bf16)
    swaps[1].start(e.partial_out.at[theirs], e.partial_in.at[0])
    own_part = own_half(partial)
    if next_layer is not None:
        weights.load(next_layer, "units")
    pump("units")
    swaps[1].wait()
    back, gain_grad = norm_back(
        e.mid_rows[layer], e.gains[layer, 1:2, :], own_part + e.partial_in[0].astype(f32)
    )
    e.mid_grad[...] = grad_ref[...] + back
    e.gain_total[2 * layer + 1 : 2 * layer + 2, :] = gain_grad
    e.grad_swap[1, c] = e.mid_grad[...].astype(bf16)
    swaps[2].start(e.grad_swap.at[1, c], e.grad_swap.at[1, c])
    if next_layer is None:
        weights.wait(layer, "attend")
    swaps[2].wait()
    branch = e.grad_swap[1].reshape(CHIP_TOKENS, D)
    for side in range(2):
        heads_grad = dot_nn(branch, weights.get(side, OUT_AT, GATE_AT))
        for inner in range(3):
            head = 3 * side + inner
            piece = heads_grad[:, 64 + 64 * inner : 128 + 64 * inner]
            for group in range(2):
                at = TOKENS_HERE * group
                e.back_ask_out[head, group] = jnp.concatenate(
                    [piece[at : at + 64], piece[at + 64 : at + 128]], axis=1
                ).astype(bf16)
                ask.send_to_owner(head, group)
    transpose_rows(0, branch)
    for side in range(2):
        weight_grad(side, OUT_AT, GATE_AT - OUT_AT, 0, e.attended[layer, side])
    pump("asked")

    @pl.when(is_owner_here())
    def _():
        ask.arrived()

        def place(block, carry):
            at = pl.multiple_of(block * TOKENS_HERE, TOKENS_HERE)
            both = e.back_ask_in[block].astype(f32)
            grad = jnp.concatenate([both[:, 0:64], both[:, 64:128]], axis=0)
            e.output_grad[pl.ds(at, 128), :] = jnp.concatenate(
                [jnp.zeros((TOKENS_HERE, HEAD_DIM), f32), grad], axis=1
            ).astype(bf16)
            return carry

        lax.fori_loop(0, 16, place, 0)
        attend_backward(
            e.queries.at[layer],
            e.keys_values.at[layer],
            e.output_grad,
            e.kept_output.at[layer],
            e.ends,
            e.query_grad,
            e.key_value_grad,
            pump.blocks(),
        )

        def give(block, carry):
            at = pl.multiple_of(block * TOKENS_HERE, TOKENS_HERE)
            e.back_reply_out[block, 0:128] = jnp.concatenate(
                [
                    e.query_grad[pl.ds(at, 128), 0:64] * (1.0 / math.sqrt(HEAD_DIM)),
                    e.key_value_grad[pl.ds(at, 128), 0:64],
                ],
                axis=1,
            ).astype(bf16)
            e.back_reply_out[block, 128:192] = jnp.concatenate(
                [
                    e.key_value_grad[pl.ds(at, 64), 64:128],
                    e.key_value_grad[pl.ds(at + 64, 64), 64:128],
                ],
                axis=1,
            ).astype(bf16)
            answer.send_to_tokens(block)
            return carry

        lax.fori_loop(0, 16, give, 0)

    @pl.when(jnp.logical_not(is_owner_here()))
    def _():
        for number, action in sorted(pump.blocks().items()):
            action()

    pump("attended")
    answer.arrived()
    cosine = e.tables[:, :, 0:128].reshape(CHIP_TOKENS, 128)
    sine = e.tables[:, :, 128:256].reshape(CHIP_TOKENS, 128)
    transpose_rows(1, e.normed[layer].reshape(CHIP_TOKENS, D))
    partial = None
    for side in range(2):
        pieces = []
        for inner in range(3):
            head = 3 * side + inner
            pair = jnp.concatenate(
                [e.back_reply_in[head, 0, 0:128], e.back_reply_in[head, 1, 0:128]], axis=0
            ).astype(f32)
            pair = pair * cosine - swap_halves(pair) * sine
            e.mixed_grad[side, :, 128 * inner : 128 * inner + 128] = pair.astype(bf16)
            rows = []
            for group in range(2):
                both = e.back_reply_in[head, group, 128:192].astype(f32)
                rows += [both[:, 0:64], both[:, 64:128]]
            pieces.append(jnp.concatenate(rows, axis=0))
        pieces.append(jnp.zeros((CHIP_TOKENS, 64), f32))
        e.mixed_grad[side, :, 384:IN_COLS] = jnp.concatenate(pieces, axis=1).astype(bf16)
        weight_grad(side, 0, OUT_AT, 1, e.mixed_grad[side, :, 0:OUT_AT])
        last = dot_nn(e.left_t[1].reshape(D, CHIP_TOKENS), e.mixed_grad[side, :, OUT_AT:IN_COLS])
        here = e.grads[layer, side, :, :, :, OUT_AT:IN_COLS].reshape(D, IN_COLS - OUT_AT)
        e.grads[layer, side, :, :, :, OUT_AT:IN_COLS] = (
            (here.astype(f32) + last).astype(bf16).reshape(4, 4, PAIR_ROWS, IN_COLS - OUT_AT)
        )
    pump("mixed")
    for side in range(2):
        term = dot_nt(e.mixed_grad[side], weights.get(side, 0, IN_COLS))
        partial = term if partial is None else partial + term
    e.partial_out[...] = partial.astype(bf16)
    swaps[3].start(e.partial_out.at[theirs], e.partial_in.at[1])
    own_part = own_half(partial)
    if next_layer is not None:
        weights.load(next_layer, "attend")
    swaps[3].wait()
    back, gain_grad = norm_back(
        rows_ref[...], e.gains[layer, 0:1, :], own_part + e.partial_in[1].astype(f32)
    )
    e.gain_total[2 * layer : 2 * layer + 1, :] = gain_grad
    grad_out[...] = e.mid_grad[...] + back
    ask.drain_to_owner()
    pl.when(is_owner_here())(answer.drain_to_tokens)
    pump("end")


class Pump:
    def __init__(self, actions=None):
        self.actions = actions or {}

    def __call__(self, point):
        for action in self.actions.get(point, []):
            action()

    def blocks(self):
        def run(actions):
            def action():
                for one in actions:
                    one()

            return action

        return {key: run(value) for key, value in self.actions.items() if isinstance(key, int)}


def owner_place(matrix):
    return (matrix // 4, 0, (matrix // 4 + matrix % 4) % 4, matrix % 4)


def square_columns(kind):
    if kind < 2:
        return [(128 * head + 64 * kind, 64) for head in range(3)]
    return [(384 + 192 * (kind - 2), 192)]


def ns_step(source, target, gram, columns):
    blocks = 4
    rows = D // blocks

    def gram_rows(block, carry):
        part = source[block, :, :, 0:columns].reshape(rows, columns)
        gram[block, :, :, 0:D] = (
            dot_nt(part, source[:, :, :, 0:columns].reshape(D, columns))
            .astype(bf16)
            .reshape(4, PAIR_ROWS, D)
        )
        return carry

    lax.fori_loop(0, blocks, gram_rows, 0)

    def update_rows(block, carry):
        gram_block = gram[block, :, :, 0:D].reshape(rows, D)
        polynomial = (
            quintic_two * gram_block.astype(f32)
            + quintic_three * dot_nn(gram_block, gram[:, :, :, 0:D].reshape(D, D))
        ).astype(bf16)
        for start in range(0, columns, 512):
            stop = start + 512
            target[block, :, :, start:stop] = (
                (
                    quintic_one * source[block, :, :, start:stop].reshape(rows, 512).astype(f32)
                    + dot_nn(polynomial, source[:, :, :, start:stop].reshape(D, 512))
                )
                .astype(bf16)
                .reshape(4, PAIR_ROWS, 512)
            )
        return carry

    lax.fori_loop(0, blocks, update_rows, 0)


def orthogonal_owner(slots, front, back, gram, wide, send_back):
    columns = FF if wide else 1024
    slot_rows = PAIR_ROWS if wide else 32

    def add_squares(index, carry):
        value = slots[index, 0:slot_rows, :].astype(f32)
        return carry + jnp.sum(value * value, axis=0, keepdims=True)

    squares = lax.fori_loop(0, DEVICES, add_squares, jnp.zeros((1, 256), f32))
    scale = 1.0 / (jnp.sqrt(jnp.sum(squares, axis=1, keepdims=True)) + ortho_eps)

    def assemble(pair, carry):
        outer, inner = lax.div(pair, 4), lax.rem(pair, 4)
        for part in range(4):
            first = slots[pair * 8 + part, 0:slot_rows, :].astype(f32) * scale
            second = slots[pair * 8 + 4 + part, 0:slot_rows, :].astype(f32) * scale
            joined = jnp.concatenate([first[0:24], second[0:24]], axis=0).astype(bf16)
            if wide:
                front[outer, inner, :, part * 512 : part * 512 + 256] = joined
                front[outer, inner, :, part * 512 + 256 : part * 512 + 512] = jnp.concatenate(
                    [first[24:48], second[24:48]], axis=0
                ).astype(bf16)
            else:
                front[outer, inner, :, part * 256 : part * 256 + 256] = joined
        return carry

    lax.fori_loop(0, 16, assemble, 0)

    def two_steps(index, carry):
        ns_step(front, back, gram, columns)
        ns_step(back, front, gram, columns)
        return carry

    lax.fori_loop(0, NS_STEPS // 2, two_steps, 0)

    def take_apart(pair, carry):
        outer, inner = lax.div(pair, 4), lax.rem(pair, 4)
        for part in range(4):
            if wide:
                left = front[outer, inner, :, part * 512 : part * 512 + 256].astype(f32)
                right = front[outer, inner, :, part * 512 + 256 : part * 512 + 512].astype(f32)
                slots[pair * 8 + part] = jnp.concatenate([left[0:24], right[0:24]], axis=0).astype(
                    bf16
                )
                slots[pair * 8 + 4 + part] = jnp.concatenate(
                    [left[24:48], right[24:48]], axis=0
                ).astype(bf16)
            else:
                left = front[outer, inner, :, part * 256 : part * 256 + 256].astype(f32)
                slots[pair * 8 + part, 0:32] = left[0:32].astype(bf16)
                slots[pair * 8 + 4 + part, 0:32] = jnp.concatenate(
                    [left[24:48], left[0:8]], axis=0
                ).astype(bf16)
        for part in range(8):
            send_back(pair * 8 + part)
        return carry

    lax.fori_loop(0, 16, take_apart, 0)


class Muon:
    def __init__(self, e):
        self.e = e
        self.places = [owner_place(m) for m in range(OWNERS)]
        self.indices = [(p[0] * 2 + p[1]) * 16 + p[2] * 4 + p[3] for p in self.places]

    def tile(self, m):
        return self.e.square.at[m] if m < SQUARE_COUNT else self.e.wide.at[m - SQUARE_COUNT]

    def returned(self, m):
        return self.e.square_new.at[m] if m < SQUARE_COUNT else self.e.wide_new.at[m - SQUARE_COUNT]

    def slot(self, m):
        if m < SQUARE_COUNT:
            return self.e.slots.at[index_here(), pl.ds(0, 32)]
        return self.e.slots.at[index_here()]

    def outbound(self, m):
        return remote(
            self.tile(m),
            self.slot(m),
            self.e.tile_send.at[m],
            self.e.slot_recv.at[0],
            device_at(*self.places[m]),
        )

    def update_moment(self, layer, start, stop):
        e = self.e
        rows = slice(ROW_SHARD * layer, ROW_SHARD * layer + ROW_SHARD)
        e.moment_new[rows, start:stop] = (
            moment_decay * e.moment[rows, start:stop] + e.total[rows, start:stop]
        )

    def send(self, m):
        e = self.e
        if m < SQUARE_COUNT:
            layer, kind = m // 4, m % 4
            rows = slice(ROW_SHARD * layer, ROW_SHARD * layer + ROW_SHARD)
            pieces = [e.moment_new[rows, at : at + width] for at, width in square_columns(kind)]
            tile = jnp.concatenate(pieces + [jnp.zeros((ROW_SHARD, 64), f32)], axis=1)
            e.square[m] = jnp.concatenate([tile, jnp.zeros((8, 256), f32)], axis=0).astype(bf16)
        else:
            layer, kind = (m - SQUARE_COUNT) // 3, (m - SQUARE_COUNT) % 3
            rows = slice(ROW_SHARD * layer, ROW_SHARD * layer + ROW_SHARD)
            at = GATE_AT + 512 * kind
            e.wide[m - SQUARE_COUNT] = jnp.concatenate(
                [e.moment_new[rows, at : at + 256], e.moment_new[rows, at + 256 : at + 512]], axis=0
            ).astype(bf16)

        @pl.when(index_here() != self.indices[m])
        def _():
            self.outbound(m).start()

        @pl.when(index_here() == self.indices[m])
        def _():
            copy = pltpu.make_async_copy(self.tile(m), self.slot(m), self.e.tile_send.at[m])
            copy.start()
            copy.wait()

    def serve(self, is_wide):
        e = self.e
        y, c, z, x = whereami()
        slot_rows = PAIR_ROWS if is_wide else 32
        whole = e.slots.at[pl.ds(0, DEVICES - 1), pl.ds(0, slot_rows)]
        pltpu.make_async_copy(whole, whole, e.slot_recv.at[0]).wait()
        matrix = y * 4 + x
        mine = index_here()

        def send_back(index):
            if is_wide:
                source, target = e.slots.at[index], e.wide_new.at[matrix - SQUARE_COUNT]
            else:
                source, target = e.slots.at[index, pl.ds(0, 32)], e.square_new.at[matrix]

            @pl.when(index != mine)
            def _():
                remote(
                    source, target, e.slot_recv.at[1], e.tile_recv.at[matrix], device_of_index(index)
                ).start()

            @pl.when(index == mine)
            def _():
                copy = pltpu.make_async_copy(source, target, e.tile_recv.at[matrix])
                copy.start()

        orthogonal_owner(
            e.slots, e.weights.at[0], e.weights.at[1], e.grads.at[1, 0], is_wide, send_back
        )
        pltpu.make_async_copy(whole, whole, e.slot_recv.at[1]).wait()

    def serve_all(self):
        y, c, z, x = whereami()
        placed = (c == 0) & (z == ring(x, y))
        square_owner = placed & (y < 2)
        wide_owner = placed & ((y == 2) | ((y == 3) & (x < 2)))
        pl.when(square_owner)(lambda: self.serve(False))
        pl.when(wide_owner)(lambda: self.serve(True))

    def finish(self):
        e = self.e
        for m in range(OWNERS):
            tile = self.returned(m)
            pltpu.make_async_copy(tile, tile, e.tile_recv.at[m]).wait()
            if m < SQUARE_COUNT:
                layer, kind = m // 4, m % 4
                rate = project_rate if kind == 3 else matrix_rate
                factor = 0.2 * math.sqrt(D)
                value = e.square_new[m].astype(f32)[0:ROW_SHARD]
                places = square_columns(kind)
            else:
                layer, kind = (m - SQUARE_COUNT) // 3, (m - SQUARE_COUNT) % 3
                rate, factor = matrix_rate, 0.2 * math.sqrt(FF)
                value = e.wide_new[m - SQUARE_COUNT].astype(f32)
                value = jnp.concatenate([value[0:ROW_SHARD], value[ROW_SHARD:PAIR_ROWS]], axis=1)
                places = [(GATE_AT + 512 * kind, 512)]
            rows = slice(ROW_SHARD * layer, ROW_SHARD * layer + ROW_SHARD)
            offset = 0
            for at, width in places:
                weight = e.weights_own[rows, at : at + width]
                e.weights_new[rows, at : at + width] = weight - rate * (
                    factor * value[:, offset : offset + width] + matrix_decay * weight
                )
                offset += width

            @pl.when(index_here() != self.indices[m])
            def _(m=m):
                self.outbound(m).wait_send()


def finish_sum(e, layer, start, stop, slot):
    y, c, z, x = whereami()
    rows = slice(ROW_SHARD * layer, ROW_SHARD * layer + ROW_SHARD)
    source, target = e.pair.at[rows, start:stop], e.total.at[rows, start:stop]
    copy = lambda: remote(source, target, e.pair_send.at[slot], e.pair_recv.at[slot], sibling_here())

    @pl.when(c == lax.div(x, 2))
    def _():
        whole = e.grads[layer, lax.rem(x, 2), y, z, :, start:stop].astype(f32)
        first, second = whole[0:ROW_SHARD], whole[ROW_SHARD:PAIR_ROWS]
        e.total[rows, start:stop] = jnp.where(c == 0, first, second)
        e.pair[rows, start:stop] = jnp.where(c == 0, second, first)
        copy().start()
        copy().wait_send()

    @pl.when(c != lax.div(x, 2))
    def _():
        copy().wait_recv()


def gain_copies(e, hop):
    if hop == 0:
        devices = [sibling_here()]
    else:
        devices = [neighbour("xyz"[hop - 1], offset) for offset in (1, 2, 3)]
    base = 3 * hop
    return [
        remote(
            e.gain_total,
            e.gain_box.at[base + i],
            e.gain_send.at[base + i],
            e.gain_recv.at[base + i],
            device,
        )
        for i, device in enumerate(devices)
    ]


def gain_start(e, hop):
    for copy in gain_copies(e, hop):
        copy.start()


def gain_finish(e, hop):
    copies = gain_copies(e, hop)
    for copy in copies:
        copy.wait_send()
        copy.wait_recv()
    for i in range(len(copies)):
        e.gain_total[...] += e.gain_box[3 * hop + i]


BOX_SHAPES = {}
for _part in range(3):
    for _phase in range(3):
        _lead = box_shape(_part, _phase) + (PAIR_ROWS,)
        if _phase == 0:
            BOX_SHAPES[f"late_half_{_part}"] = (2,) + _lead + (256,)
            BOX_SHAPES[f"early_half_{_part}"] = (2,) + _lead + (256,)
            BOX_SHAPES[f"both_block_{_part}"] = (2,) + _lead + (512,)
            BOX_SHAPES[f"late_last_{_part}"] = (3,) + _lead + (256,)
            BOX_SHAPES[f"early_last_{_part}"] = (3,) + _lead + (256,)
        else:
            BOX_SHAPES[f"late_{_part}{_phase}"] = (3,) + _lead + (768,)
            BOX_SHAPES[f"early_{_part}{_phase}"] = (3,) + _lead + (768,)


def boxes_of(e, layer, kind, part):
    name = "late" if layer == 1 else "early"
    start, width = {"units": (0, 512), "attend": (512, 256)}[kind]
    found = []
    for phase in range(3):
        if phase == 0 and kind == "attend":
            boxes = getattr(e, f"{name}_last_{part}")
            found.append([boxes.at[i] for i in range(3)])
        elif phase == 0:
            blocks = getattr(e, f"both_block_{part}")
            halves = getattr(e, f"{name}_half_{part}")
            found.append([halves.at[0], halves.at[1], blocks.at[0], blocks.at[1]])
        else:
            cut = (slice(None),) * (len(box_shape(part, phase)) + 1) + (pl.ds(start, width),)
            boxes = getattr(e, f"{name}_{part}{phase}")
            found.append([boxes.at[(i,) + cut] for i in range(3)])
    return found


def step_kernel(*refs):
    e = types.SimpleNamespace(**dict(zip(REF_NAMES, refs)))
    e.query_grad = e.score_box.at[pl.ds(0, GROUP)]
    e.key_value_grad = e.score_box.at[pl.ds(GROUP, GROUP)]
    e.pair, e.total = e.moment_new, e.weights_new
    e.back_ask_out, e.back_reply_out, e.back_reply_in = e.reply_in, e.ask_in, e.ask_out
    y, c, z, x = whereami()
    holder = lax.div(x, 2)
    signal_everyone()
    e.own[...] = e.weights_own[...].astype(bf16)
    e.tables[c] = e.table[...]
    rows = e.rows_in[...]
    e.normed[0, c] = (rows * norm_scale(rows) * e.gains[0, 0:1, :]).astype(bf16)
    e.gain_total[...] = jnp.zeros_like(e.gain_total)
    wait_for_everyone()

    hand_over = lambda: remote(e.own, e.twin, e.pair_send.at[3], e.pair_recv.at[3], sibling_here())
    pl.when(c != holder)(lambda: hand_over().start())
    table_swap = remote(
        e.table, e.tables.at[c], e.pair_send.at[4], e.pair_recv.at[4], sibling_here()
    )
    table_swap.start()

    @pl.when(c == holder)
    def _():
        hand_over().wait_recv()
        mine = e.own[...].astype(f32)
        theirs = e.twin[...].astype(f32)
        first = jnp.where(c == 0, mine, theirs)
        second = jnp.where(c == 0, theirs, mine)
        for layer in range(LAYERS):
            part = slice(layer * ROW_SHARD, layer * ROW_SHARD + ROW_SHARD)
            joined = jnp.concatenate([first[part], second[part]], axis=0).astype(bf16)
            if layer == 0:
                e.weights[lax.rem(x, 2), y, z] = joined
            else:
                e.piece[...] = joined
                keep = pltpu.make_async_copy(
                    e.piece, e.full.at[1, lax.rem(x, 2), y, z], e.load_sem.at[2]
                )
                keep.start()
                keep.wait()

    def gather_lanes(ref, at, width, base, direct):
        return [
            GatherLane(
                ref,
                part,
                (at + part * width, width),
                e.gather_send,
                e.gather_recv,
                base + 12 * part,
                direct,
            )
            for part in range(3)
        ]

    ga = gather_lanes(e.weights, 0, 256, 0, (0, 1, 2))
    gb = gather_lanes(e.weights, GATE_AT, 512, 36, (0, 1))
    gc = gather_lanes(e.full.at[1], 0, 256, 72, (0, 1))
    gd = gather_lanes(e.full.at[1], GATE_AT, 512, 108, (0, 1))
    do = lambda lanes, step, phase: lambda: each(lanes, step, phase)
    weights = Weights(e)
    each(ga, "first", 0)
    each(gb, "first", 0)
    for lanes in (ga, gb):
        each(lanes, "third", 0)
        each(lanes, "first", 1)
    for lanes in (ga, gb):
        each(lanes, "third", 1)
        each(lanes, "first", 2)
    each(gc, "first", 0)
    each(gd, "first", 0)
    table_swap.wait_send()
    remote(
        e.table, e.tables.at[1 - c], e.pair_send.at[4], e.pair_recv.at[4], sibling_here()
    ).wait_recv()
    each(ga, "third", 2)

    def turn_to_layer_1():
        each(gc, "third", 2)
        for phase in range(3):
            each(ga, "drain", phase)
            each(gb, "drain", phase)
        weights.keep_wait()
        weights.load(1, "attend")

    def units_of_layer_1():
        each(gd, "third", 2)
        weights.load(1, "units")

    forward_pass(
        e,
        0,
        e.rows_in,
        e.rows_mid,
        Pump(
            {
                "asked": [
                    do(gb, "second", 2),
                    do(gc, "third", 0),
                    do(gc, "first", 1),
                    do(gd, "third", 0),
                    do(gd, "first", 1),
                ],
                6: [do(gc, "third", 1), do(gc, "first", 2)],
                "attended": [do(gb, "third", 2), weights.keep],
                "answered": [do(gc, "second", 2), do(gd, "third", 1), do(gd, "first", 2)],
                "end": [turn_to_layer_1],
            }
        ),
    )
    rows = e.rows_mid[...]
    e.normed[1, c] = (rows * norm_scale(rows) * e.gains[1, 0:1, :]).astype(bf16)
    forward_pass(e, 1, e.rows_mid, e.rows_out, Pump({"asked": [do(gd, "second", 2)], "attended": [units_of_layer_1]}))
    def reduce_lanes(layer, kind, base):
        at, width = {"units": (GATE_AT, 512), "attend": (0, 256)}[kind]
        lanes = []
        for part in range(3):
            credits = [e.credit.at[part, side] for side in range(2)]
            lanes.append(
                ReduceLane(
                    e.grads.at[layer],
                    boxes_of(e, layer, kind, part),
                    part,
                    (at + part * width, width),
                    e.reduce_send,
                    e.reduce_recv,
                    base + 12 * part,
                    (1, 2) if kind == "units" else (0, 1, 2),
                    gives=credits if kind == "units" and layer == 1 else None,
                    takes=credits if kind == "units" and layer == 0 else None,
                )
            )
        return lanes

    lu = reduce_lanes(1, "units", 0)
    la = reduce_lanes(1, "attend", 36)
    ru = reduce_lanes(0, "units", 72)
    ra = reduce_lanes(0, "attend", 108)
    muon = Muon(e)
    backward_pass(
        e,
        1,
        e.grad_in,
        e.rows_mid,
        e.grad_mid,
        Pump(
            {
                "asked": [do(lu, "first", 0)],
                4: [do(lu, "second", 0)],
                "mixed": [do(la, "first", 0), do(lu, "third", 0), do(lu, "first", 1)],
            }
        ),
        0,
    )

    def late_done():
        finish_sum(e, 1, 0, PACK_COLS, 0)
        muon.update_moment(1, 0, PACK_COLS)
        for m in (4, 5, 6, 7, 11, 12, 13):
            muon.send(m)

    def units_done():
        finish_sum(e, 0, GATE_AT, PACK_COLS, 1)
        muon.update_moment(0, GATE_AT, PACK_COLS)
        for m in (8, 9, 10):
            muon.send(m)

    backward_pass(
        e,
        0,
        e.grad_mid,
        e.rows_in,
        e.grad_out,
        Pump(
            {
                "units": [
                    do(la, "third", 0),
                    do(la, "first", 1),
                    do(lu, "third", 1),
                    do(lu, "first", 2),
                ],
                "asked": [
                    do(ru, "first", 0),
                    do(la, "third", 1),
                    do(la, "first", 2),
                    do(lu, "third", 2),
                ],
                3: [do(la, "third", 2), late_done],
                5: [do(ru, "second", 0)],
                "mixed": [do(ra, "first", 0), do(ru, "third", 0), do(ru, "first", 1)],
            }
        ),
        None,
    )
    gain_start(e, 0)
    each(ra, "third", 0)
    each(ra, "first", 1)
    gain_finish(e, 0)
    gain_start(e, 1)
    each(ru, "third", 1)
    each(ru, "first", 2)
    each(ra, "third", 1)
    each(ra, "first", 2)
    each(ru, "third", 2)
    units_done()
    gain_finish(e, 1)
    gain_start(e, 2)
    each(ra, "third", 2)
    finish_sum(e, 0, 0, GATE_AT, 2)
    muon.update_moment(0, 0, GATE_AT)
    for m in range(4):
        muon.send(m)
    gain_finish(e, 2)
    gain_start(e, 3)
    for lanes in (gc, gd, lu, la, ru, ra):
        for phase in range(3):
            each(lanes, "drain", phase)
    muon.serve_all()
    gain_finish(e, 3)
    pl.when(c != holder)(lambda: hand_over().wait_send())
    muon.finish()


REF_TABLE = [
    ("rows_in", "in", (TOKENS_HERE, D), f32),
    ("grad_in", "in", (TOKENS_HERE, D), f32),
    ("weights_own", "in", (LAYERS * ROW_SHARD, PACK_COLS), f32),
    ("moment", "in", (LAYERS * ROW_SHARD, PACK_COLS), f32),
    ("table", "in", (TOKENS_HERE, 256), f32),
    ("ends", "in", (8, 128), jnp.int32),
    ("gains", "in", (LAYERS, 8, D), f32),
    ("rows_out", "out", (TOKENS_HERE, D), f32),
    ("grad_out", "out", (TOKENS_HERE, D), f32),
    ("gain_total", "out", (8, D), f32),
    ("moment_new", "out", (LAYERS * ROW_SHARD, PACK_COLS), f32),
    ("weights_new", "out", (LAYERS * ROW_SHARD, PACK_COLS), f32),
    ("full", "hbm", (LAYERS, 2, 4, 4, PAIR_ROWS, PACK_COLS), bf16),
    ("weights", "vmem", (2, 4, 4, PAIR_ROWS, PACK_COLS), bf16),
    ("grads", "vmem", (LAYERS, 2, 4, 4, PAIR_ROWS, PACK_COLS), bf16),
    ("own", "vmem", (LAYERS * ROW_SHARD, PACK_COLS), bf16),
    ("twin", "vmem", (LAYERS * ROW_SHARD, PACK_COLS), bf16),
    ("piece", "vmem", (PAIR_ROWS, PACK_COLS), bf16),
    ("tables", "vmem", (2, TOKENS_HERE, 256), f32),
    ("rows_mid", "vmem", (TOKENS_HERE, D), f32),
    ("grad_mid", "vmem", (TOKENS_HERE, D), f32),
    ("mid_grad", "vmem", (TOKENS_HERE, D), f32),
    ("mid_rows", "vmem", (LAYERS, TOKENS_HERE, D), f32),
    ("normed", "vmem", (LAYERS, 2, TOKENS_HERE, D), bf16),
    ("normed_mid", "vmem", (LAYERS, 2, TOKENS_HERE, D), bf16),
    ("attended", "vmem", (LAYERS, 2, CHIP_TOKENS, 256), bf16),
    ("queries", "vmem", (LAYERS, GROUP, 128), bf16),
    ("keys_values", "vmem", (LAYERS, GROUP, 128), bf16),
    ("kept_output", "vmem", (LAYERS, GROUP, 2 * HEAD_DIM), f32),
    ("score_box", "vmem", (2 * GROUP, 128), f32),
    ("output_grad", "vmem", (GROUP, 128), bf16),
    ("partial", "vmem", (CHIP_TOKENS, D), f32),
    ("partial_out", "vmem", (CHIP_TOKENS, D), bf16),
    ("left_t", "vmem", (2, 4, D // 4, CHIP_TOKENS), bf16),
    ("partial_in", "vmem", (2, TOKENS_HERE, D), bf16),
    ("grad_swap", "vmem", (2, 2, TOKENS_HERE, D), bf16),
    ("mixed_grad", "vmem", (2, CHIP_TOKENS, IN_COLS), bf16),
    ("ask_out", "vmem", (HEADS_HERE, 2, ASK_ROWS, 128), bf16),
    ("ask_in", "vmem", (16, ASK_ROWS, 128), bf16),
    ("reply_out", "vmem", (16, REPLY_ROWS, 128), bf16),
    ("reply_in", "vmem", (HEADS_HERE, 2, REPLY_ROWS, 128), bf16),
    ("back_ask_in", "vmem", (16, REPLY_ROWS, 128), bf16),
    ("gain_box", "vmem", (12, 8, D), f32),
    ("square", "vmem", (SQUARE_COUNT, 32, 256), bf16),
    ("wide", "vmem", (WIDE_COUNT, PAIR_ROWS, 256), bf16),
    ("square_new", "vmem", (SQUARE_COUNT, 32, 256), bf16),
    ("wide_new", "vmem", (WIDE_COUNT, PAIR_ROWS, 256), bf16),
    ("slots", "vmem", (DEVICES, PAIR_ROWS, 256), bf16),
]
REF_TABLE += [(name, "vmem", shape, bf16) for name, shape in BOX_SHAPES.items()]
REF_TABLE += [
    ("gather_send", "dma", (144,), None),
    ("gather_recv", "dma", (144,), None),
    ("reduce_send", "dma", (144,), None),
    ("reduce_recv", "dma", (144,), None),
    ("load_sem", "dma", (4,), None),
    ("swap_send", "dma", (16,), None),
    ("swap_recv", "dma", (16,), None),
    ("ask_send", "dma", (HEADS_HERE, 2), None),
    ("reply_send", "dma", (16,), None),
    ("traffic_recv", "dma", (8,), None),
    ("pair_send", "dma", (5,), None),
    ("pair_recv", "dma", (5,), None),
    ("gain_send", "dma", (12,), None),
    ("gain_recv", "dma", (12,), None),
    ("tile_send", "dma", (OWNERS,), None),
    ("tile_recv", "dma", (OWNERS,), None),
    ("slot_recv", "dma", (2,), None),
    ("credit", "regular", (3, 2), None),
]
REF_NAMES = [row[0] for row in REF_TABLE]


def train_step(*inputs):
    scratch = []
    for name, where, shape, dtype in REF_TABLE:
        if where == "vmem":
            scratch.append(pltpu.VMEM(shape, dtype))
        elif where == "dma":
            scratch.append(pltpu.SemaphoreType.DMA(shape))
        elif where == "regular":
            scratch.append(pltpu.SemaphoreType.REGULAR(shape))
    outs = [row for row in REF_TABLE if row[1] in ("out", "hbm")]
    return pl.pallas_call(
        step_kernel,
        out_shape=[jax.ShapeDtypeStruct(shape, dtype) for _, _, shape, dtype in outs],
        in_specs=[pl.BlockSpec(memory_space=pltpu.VMEM)] * len(inputs),
        out_specs=[
            pl.BlockSpec(memory_space=pltpu.HBM if where == "hbm" else pltpu.VMEM)
            for _, where, _, _ in outs
        ],
        scratch_shapes=scratch,
        compiler_params=pltpu.CompilerParams(
            collective_id=0, has_side_effects=True, vmem_limit_bytes=63 * MIB
        ),
        name="train_step",
    )(*inputs)


def pack_layers(attend_in, attend_out, expand, shrink):
    query_key = jnp.stack(
        [attend_in[:, k].reshape(LAYERS, ROW_SHARD, 3, HEAD_DIM) for k in range(2)], axis=3
    )
    return jnp.concatenate(
        [
            query_key.reshape(LAYERS, ROW_SHARD, 384),
            attend_in[:, 2],
            jnp.swapaxes(attend_out, 1, 2),
            expand[:, 0],
            expand[:, 1],
            jnp.swapaxes(shrink, 1, 2),
        ],
        axis=2,
    )


def four_squares(packed):
    query_key = packed[:, :, 0:384].reshape(LAYERS, ROW_SHARD, 3, 2, HEAD_DIM)
    return [
        query_key[:, :, :, 0].reshape(LAYERS, ROW_SHARD, 192),
        query_key[:, :, :, 1].reshape(LAYERS, ROW_SHARD, 192),
        packed[:, :, 384:576],
        packed[:, :, 576:768],
    ]


def unpack_layers(packed):
    query, key, value, out = four_squares(packed)
    return (
        jnp.stack([query, key, value], axis=1),
        jnp.swapaxes(out, 1, 2),
        jnp.stack([packed[:, :, 768:1280], packed[:, :, 1280:1792]], axis=1),
        jnp.swapaxes(packed[:, :, 1792:2304], 1, 2),
    )


def to_chip_order(values):
    split = values.reshape(values.shape[:-1] + (4, 2, 4, ROW_SHARD))
    return jnp.swapaxes(split, -3, -2).reshape(values.shape)


def from_chip_order(values):
    split = values.reshape(values.shape[:-1] + (4, 4, 2, ROW_SHARD))
    return jnp.swapaxes(split, -3, -2).reshape(values.shape)


def rope_table(positions):
    frequency = rope_base ** (-jnp.arange(HEAD_DIM // 2, dtype=jnp.float32) * 2.0 / HEAD_DIM)
    angles = positions.astype(jnp.float32)[:, None] * frequency[None, :]
    cosine, sine_part = jnp.cos(angles), jnp.sin(angles)
    return jnp.concatenate(
        [cosine, cosine, cosine, cosine, -sine_part, sine_part, -sine_part, sine_part], axis=1
    )


def body(
    hidden_in,
    out_grad,
    seq_lengths,
    norm_gains,
    gain_first,
    gain_second,
    attend_in,
    attend_out,
    expand,
    shrink,
    attend_in_moment,
    attend_out_moment,
    expand_moment,
    shrink_moment,
):
    document, position, places = doc_layout(seq_lengths[0], GROUP)
    doc_ends = jnp.cumsum(seq_lengths[0])
    ends = jnp.pad(
        jnp.broadcast_to(doc_ends[0:2, None], (2, 128)).astype(jnp.int32), ((0, 6), (0, 0))
    )
    token_block = lax.axis_index("ctx") * 4 + lax.axis_index("tp")
    table = rope_table(
        lax.dynamic_slice_in_dim(position, token_block * TOKENS_HERE, TOKENS_HERE)
    )
    weights_packed = pack_layers(attend_in, attend_out, expand, shrink)
    moment_packed = pack_layers(attend_in_moment, attend_out_moment, expand_moment, shrink_moment)
    gains = jnp.pad(to_chip_order(norm_gains), ((0, 0), (0, 6), (0, 0)))
    flat = (LAYERS * ROW_SHARD, PACK_COLS)
    rows, rows_grad, gain_total, moment_new, weights_new, _ = train_step(
        to_chip_order(hidden_in).astype(jnp.float32),
        to_chip_order(out_grad).astype(jnp.float32),
        weights_packed.reshape(flat),
        moment_packed.reshape(flat),
        table,
        ends,
        gains,
    )
    moment_new = moment_new.reshape(LAYERS, ROW_SHARD, PACK_COLS)
    weights_new = weights_new.reshape(LAYERS, ROW_SHARD, PACK_COLS)
    gain_grad = from_chip_order(gain_total[0:4]).reshape(LAYERS, 2, D)
    gain_first_new = first_decay * gain_first + (1.0 - first_decay) * gain_grad
    gain_second_new = second_decay * gain_second + (1.0 - second_decay) * gain_grad * gain_grad
    norm_gains_new = norm_gains - gain_rate * (gain_first_new / (1.0 - first_decay**STEP)) / (
        jnp.sqrt(gain_second_new / (1.0 - second_decay**STEP)) + adam_eps
    )
    return (
        from_chip_order(rows),
        from_chip_order(rows_grad),
        gain_first_new,
        gain_second_new,
        norm_gains_new,
        *unpack_layers(moment_new),
        *unpack_layers(weights_new),
    )


def solution(mesh):
    placed = (
        P(("fsdp", "ctx", "tp"), None),
        P(("fsdp", "ctx", "tp"), None),
        P("fsdp", None),
        P(),
        P(),
        P(),
        P(None, None, ("fsdp", "ctx"), "tp"),
        P(None, "tp", ("fsdp", "ctx")),
        P(None, None, ("fsdp", "ctx"), "tp"),
        P(None, "tp", ("fsdp", "ctx")),
        P(None, None, ("fsdp", "ctx"), "tp"),
        P(None, "tp", ("fsdp", "ctx")),
        P(None, None, ("fsdp", "ctx"), "tp"),
        P(None, "tp", ("fsdp", "ctx")),
    )
    return jax.shard_map(
        body,
        mesh=mesh,
        in_specs=placed,
        out_specs=(
            P(("fsdp", "ctx", "tp"), None),
            P(("fsdp", "ctx", "tp"), None),
            P(),
            P(),
            P(),
            P(None, None, ("fsdp", "ctx"), "tp"),
            P(None, "tp", ("fsdp", "ctx")),
            P(None, None, ("fsdp", "ctx"), "tp"),
            P(None, "tp", ("fsdp", "ctx")),
            P(None, None, ("fsdp", "ctx"), "tp"),
            P(None, "tp", ("fsdp", "ctx")),
            P(None, None, ("fsdp", "ctx"), "tp"),
            P(None, "tp", ("fsdp", "ctx")),
        ),
        check_vma=False,
    )
```

```python
import math
import types

import jax
import jax.numpy as jnp
from jax import lax
from jax.experimental import pallas as pl
from jax.experimental.pallas import tpu as pltpu
from jax.sharding import PartitionSpec as P

D = 768
HEAD_DIM = 64
FF = 2048
NS_STEPS = 4
STEP = 5


norm_eps = 1e-05
rope_base = 10000.0
mask_fill = -1e30
quintic_one = 3.4445
quintic_two = -4.775
quintic_three = 2.0315
moment_decay = 0.95
matrix_rate = 0.1
project_rate = 0.8
matrix_decay = 0.1
gain_rate = 0.8
first_decay = 0.9
second_decay = 0.95
adam_eps = 1e-08
ortho_eps = 1e-07


MESH_ID = pl.DeviceIdType.MESH
ROW_SHARD = 24
PAIR_ROWS = 2 * ROW_SHARD
PACK_COLS = 2304
LAYERS = 2
MIB = 1024 * 1024
DEVICES = 128


def whereami():
    fsdp_index = lax.axis_index("fsdp")
    return (lax.div(fsdp_index, 2), lax.rem(fsdp_index, 2), lax.axis_index("ctx"), lax.axis_index("tp"))


def device_at(y, c, z, x):
    return (y * 2 + c, z, x)


def device_of_index(index):
    return (lax.div(index, 16), lax.rem(lax.div(index, 4), 4), lax.rem(index, 4))


def index_here():
    y, c, z, x = whereami()
    return (y * 2 + c) * 16 + z * 4 + x


def sibling_here():
    y, c, z, x = whereami()
    return device_at(y, 1 - c, z, x)


def ring(index, offset):
    return lax.rem(index + offset, 4)


def remote(source, target, send_sem, recv_sem, device):
    return pltpu.make_async_remote_copy(
        src_ref=source,
        dst_ref=target,
        send_sem=send_sem,
        recv_sem=recv_sem,
        device_id=device,
        device_id_type=MESH_ID,
    )


def signal_everyone():
    barrier = pltpu.get_barrier_semaphore()
    mine = index_here()

    def signal_one(offset, carry):
        device = device_of_index(lax.rem(mine + offset, DEVICES))
        pl.semaphore_signal(barrier, inc=1, device_id=device, device_id_type=MESH_ID)
        return carry

    lax.fori_loop(1, DEVICES, signal_one, 0)


def wait_for_everyone():
    pl.semaphore_wait(pltpu.get_barrier_semaphore(), DEVICES - 1)


def neighbour(axis, offset):
    y, c, z, x = whereami()
    if axis == "y":
        return device_at(ring(y, offset), c, z, x)
    if axis == "z":
        return device_at(y, c, ring(z, offset), x)
    return device_at(y, c, z, ring(x, offset))


PART_ORDER = (("x", "y", "z"), ("y", "z", "x"), ("z", "x", "y"))


def row_place(z):
    return 2 * lax.rem(z, 2) + lax.div(z, 2)


def part_view(ref, columns, done, axis, place, half):
    y, c, z, x = whereami()
    whole = slice(None)

    def index(name, own):
        if name != axis and name in done:
            return whole
        value = place if name == axis else own
        return row_place(value) if name == "z" else value

    if axis == "x":
        pick_x = lax.rem(place, 2)
    else:
        pick_x = whole if "x" in done else lax.rem(x, 2)
    start, width = columns
    if half is not None:
        width = width // 2
        start = start + half * width
    return ref.at[pick_x, index("y", y), index("z", z), :, pl.ds(start, width)]


def ring_exists(axis, done, place):
    y, c, z, x = whereami()
    if axis == "x":
        return lax.div(place, 2) == c
    if "x" in done:
        return None
    return lax.div(x, 2) == c


def run_if(condition, action):
    if condition is None:
        action()
    else:
        pl.when(condition)(action)


class GatherLane:
    def __init__(self, ref, part, columns, send, recv, base, direct):
        self.ref, self.part, self.columns = ref, part, columns
        self.send, self.recv, self.base, self.direct = send, recv, base, direct

    def parts(self, phase):
        axis = PART_ORDER[self.part][phase]
        done = PART_ORDER[self.part][:phase]
        y, c, z, x = whereami()
        return axis, done, {"x": x, "y": y, "z": z}[axis], self.base + 4 * phase

    def copy(self, phase, slot, place, half, offset):
        axis, done, me, base = self.parts(phase)
        view = part_view(self.ref, self.columns, done, axis, place, half)
        return remote(
            view, view, self.send.at[base + slot], self.recv.at[base + slot], neighbour(axis, offset)
        )

    def first(self, phase):
        axis, done, me, base = self.parts(phase)

        def action():
            if phase in self.direct:
                for offset in (1, 2, 3):
                    self.copy(phase, offset - 1, me, None, offset).start()
            else:
                self.copy(phase, 0, me, None, 1).start()
                self.copy(phase, 1, me, None, 3).start()

        run_if(ring_exists(axis, done, me), action)

    def second(self, phase):
        axis, done, me, base = self.parts(phase)
        left, right = ring(me, 3), ring(me, 1)

        def from_left():
            self.copy(phase, 0, left, None, 1).wait_recv()
            self.copy(phase, 2, left, 0, 1).start()

        def from_right():
            self.copy(phase, 1, right, None, 1).wait_recv()
            self.copy(phase, 3, right, 1, 3).start()

        run_if(ring_exists(axis, done, left), from_left)
        run_if(ring_exists(axis, done, right), from_right)

    def third(self, phase):
        axis, done, me, base = self.parts(phase)
        far = ring(me, 2)

        def action():
            self.copy(phase, 2, far, 0, 1).wait_recv()
            self.copy(phase, 3, far, 1, 1).wait_recv()

        if phase in self.direct:
            for offset in (1, 2, 3):
                place = ring(me, 4 - offset)
                run_if(
                    ring_exists(axis, done, place),
                    lambda place=place, offset=offset: self.copy(
                        phase, offset - 1, place, None, 1
                    ).wait_recv(),
                )
        else:
            run_if(ring_exists(axis, done, far), action)

    def drain(self, phase):
        axis, done, me, base = self.parts(phase)
        left, right = ring(me, 3), ring(me, 1)

        def own():
            for slot in range(3 if phase in self.direct else 2):
                self.copy(phase, slot, me, None, 1).wait_send()

        run_if(ring_exists(axis, done, me), own)
        if phase not in self.direct:
            run_if(
                ring_exists(axis, done, left), lambda: self.copy(phase, 2, left, 0, 1).wait_send()
            )
            run_if(
                ring_exists(axis, done, right), lambda: self.copy(phase, 3, right, 1, 3).wait_send()
            )


class ReduceLane:
    def __init__(self, ref, boxes, part, columns, send, recv, base, direct, gives=None, takes=None):
        self.ref, self.boxes, self.part, self.columns = ref, boxes, part, columns
        self.send, self.recv, self.base, self.direct = send, recv, base, direct
        self.gives, self.takes = gives, takes

    def parts(self, phase):
        axis = PART_ORDER[self.part][2 - phase]
        done = PART_ORDER[self.part][: 2 - phase]
        y, c, z, x = whereami()
        return axis, done, {"x": x, "y": y, "z": z}[axis], self.base + 4 * phase

    def copy(self, phase, slot, place, half, offset):
        axis, done, me, base = self.parts(phase)
        view = part_view(self.ref, self.columns, done, axis, place, half)
        return remote(
            view,
            self.boxes[phase][slot],
            self.send.at[base + slot],
            self.recv.at[base + slot],
            neighbour(axis, offset),
        )

    def add(self, phase, place, half, boxes):
        axis, done, me, base = self.parts(phase)
        view = part_view(self.ref, self.columns, done, axis, place, half)
        lead = view.shape[:-2]

        def summed(where):
            terms = [view[where]] + [box[where] for box in boxes]
            while len(terms) > 1:
                terms = [
                    terms[i] + terms[i + 1] if i + 1 < len(terms) else terms[i]
                    for i in range(0, len(terms), 2)
                ]
            return terms[0]

        def add_one(index, carry):
            where = []
            for extent in reversed(lead):
                where.insert(0, lax.rem(index, extent))
                index = lax.div(index, extent)
            view[tuple(where)] = summed(tuple(where))
            return carry

        if len(lead) == 0:
            view[...] = summed(...)
        else:
            lax.fori_loop(0, math.prod(lead), add_one, 0)

    def first(self, phase):
        axis, done, me, base = self.parts(phase)
        far = ring(me, 2)

        def action():
            self.copy(phase, 0, far, 0, 1).start()
            self.copy(phase, 1, far, 1, 3).start()

        if phase in self.direct:
            for offset in (1, 2, 3):
                place = ring(me, offset)
                run_if(
                    ring_exists(axis, done, place),
                    lambda place=place, offset=offset: self.copy(
                        phase, offset - 1, place, None, offset
                    ).start(),
                )
        else:
            run_if(ring_exists(axis, done, far), action)

    def second(self, phase):
        axis, done, me, base = self.parts(phase)
        left, right = ring(me, 3), ring(me, 1)

        def to_right():
            self.copy(phase, 0, right, 0, 1).wait_recv()
            self.add(phase, right, 0, [self.boxes[phase][0]])
            if phase == 0 and self.takes is not None:
                pl.semaphore_wait(self.takes[0], 1)
            self.copy(phase, 2, right, None, 1).start()

        def to_left():
            self.copy(phase, 1, left, 1, 1).wait_recv()
            self.add(phase, left, 1, [self.boxes[phase][1]])
            if phase == 0 and self.takes is not None:
                pl.semaphore_wait(self.takes[1], 1)
            self.copy(phase, 3, left, None, 3).start()

        run_if(ring_exists(axis, done, right), to_right)
        run_if(ring_exists(axis, done, left), to_left)

    def third(self, phase):
        axis, done, me, base = self.parts(phase)

        def action():
            if phase in self.direct:
                slots = (0, 1, 2)
            else:
                slots = (2, 3)
            for slot in slots:
                self.copy(phase, slot, me, None, 1).wait_recv()
            self.add(phase, me, None, [self.boxes[phase][slot] for slot in slots])
            if phase == 0 and self.gives is not None:
                for sem, offset in zip(self.gives, (3, 1)):
                    pl.semaphore_signal(
                        sem, inc=1, device_id=neighbour(axis, offset), device_id_type=MESH_ID
                    )

        run_if(ring_exists(axis, done, me), action)

    def drain(self, phase):
        axis, done, me, base = self.parts(phase)
        far, left, right = ring(me, 2), ring(me, 3), ring(me, 1)

        def own():
            self.copy(phase, 0, far, 0, 1).wait_send()
            self.copy(phase, 1, far, 1, 3).wait_send()

        if phase in self.direct:
            for offset in (1, 2, 3):
                place = ring(me, offset)
                run_if(
                    ring_exists(axis, done, place),
                    lambda place=place, offset=offset: self.copy(
                        phase, offset - 1, place, None, offset
                    ).wait_send(),
                )
            return
        run_if(ring_exists(axis, done, far), own)
        run_if(ring_exists(axis, done, right), lambda: self.copy(phase, 2, right, None, 1).wait_send())
        run_if(ring_exists(axis, done, left), lambda: self.copy(phase, 3, left, None, 3).wait_send())


def box_shape(part, phase):
    order = PART_ORDER[part]
    axis, done = order[2 - phase], order[: 2 - phase]
    lead = []
    for name, extent in (("x", 2), ("y", 4), ("z", 4)):
        if name != axis and name in done:
            lead.append(extent)
    return tuple(lead)


def each(lanes, step, phase):
    for lane in lanes:
        getattr(lane, step)(phase)


HEADS_HERE = 6
TOKENS_HERE = 128
CHIP_TOKENS = 256
GROUP = 2048
Q_BLOCK = 256
K_BLOCK = 512
Q_BLOCKS = GROUP // Q_BLOCK
IN_COLS = 640
OUT_AT = 512
GATE_AT = 768
UP_AT = 1280
DOWN_AT = 1792
ASK_ROWS = 192
REPLY_ROWS = 64
SQUARE_COUNT = 8
WIDE_COUNT = 6
OWNERS = SQUARE_COUNT + WIDE_COUNT
bf16 = jnp.bfloat16
f32 = jnp.float32


def dot_nn(left, right):
    return jnp.dot(left, right, preferred_element_type=f32)


def dot_nt(left, right):
    return lax.dot_general(left, right, (((1,), (1,)), ((), ())), preferred_element_type=f32)


def dot_tn(left, right):
    return lax.dot_general(left, right, (((0,), (0,)), ((), ())), preferred_element_type=f32)


def sigmoid(value):
    return 1.0 / (1.0 + jnp.exp(-value))


def norm_scale(rows):
    return lax.rsqrt(jnp.mean(rows * rows, axis=-1, keepdims=True) + norm_eps)


def normalized(rows, gain):
    return (rows * norm_scale(rows) * gain).astype(bf16)


def rope_table(lengths):
    y, c, z, x = whereami()
    shape = (TOKENS_HERE, 128)
    place = (z * 4 + x) * TOKENS_HERE + lax.broadcasted_iota(jnp.int32, shape, 0)
    lane = lax.broadcasted_iota(jnp.int32, shape, 1)
    position = place - document_start(lengths, place)
    frequency = jnp.exp(lax.rem(lane, 32).astype(f32) * (-2.0 / HEAD_DIM * math.log(rope_base)))
    angle = position.astype(f32) * frequency
    sine = jnp.sin(angle)
    sine = jnp.where(lax.rem(lane, 64) < 32, -sine, sine)
    return jnp.concatenate([jnp.cos(angle), sine], axis=1)


def document_start(lengths, place):
    first = lengths[0:1, 0:1]
    second = first + lengths[0:1, 1:2]
    return jnp.where(place >= second, second, jnp.where(place >= first, first, 0))


def norm_back(rows, gain, grad):
    scale = norm_scale(rows)
    unit = rows * scale
    inner = grad * gain
    back = scale * (inner - unit * jnp.mean(inner * unit, axis=-1, keepdims=True))
    return back, jnp.sum(grad * unit, axis=0, keepdims=True)


def swap_halves(values):
    lower = lax.rem(lax.broadcasted_iota(jnp.int32, values.shape, 1), 64) < 32
    return jnp.where(lower, pltpu.roll(values, 96, 1), pltpu.roll(values, 32, 1))


def is_owner_here():
    y, c, z, x = whereami()
    return z < 3


def head_here():
    y, c, z, x = whereami()
    return 4 * z + x


def own_half(both):
    y, c, z, x = whereami()
    return jnp.where(c == 0, both[0:TOKENS_HERE], both[TOKENS_HERE:CHIP_TOKENS])


class Swap:
    def __init__(self, e, slot):
        self.send, self.recv = e.swap_send.at[slot], e.swap_recv.at[slot]

    def start(self, source, target):
        self.copy = remote(source, target, self.send, self.recv, sibling_here())
        self.copy.start()

    def wait(self):
        self.copy.wait_send()
        self.copy.wait_recv()


class HeadTraffic:
    def __init__(self, outbox, inbox, sems, recv_sem):
        self.outbox, self.inbox, self.sems, self.recv_sem = outbox, inbox, sems, recv_sem

    def owner_place(self, head):
        y, c, z, x = whereami()
        number = HEADS_HERE * c + head
        return lax.div(number, 4), lax.rem(number, 4)

    def owner_is_here(self, head, group):
        y, c, z, x = whereami()
        owner_z, owner_x = self.owner_place(head)
        return (owner_z == z) & (owner_x == x) & (c == group)

    def to_owner(self, head, group):
        y, c, z, x = whereami()
        owner_z, owner_x = self.owner_place(head)
        return remote(
            self.outbox.at[head, group],
            self.inbox.at[z * 4 + x],
            self.sems.at[head, group],
            self.recv_sem,
            device_at(y, group, owner_z, owner_x),
        )

    def send_to_owner(self, head, group):
        y, c, z, x = whereami()
        here = self.owner_is_here(head, group)

        @pl.when(here)
        def _():
            pltpu.make_async_copy(
                self.outbox.at[head, group], self.inbox.at[z * 4 + x], self.recv_sem
            ).start()

        @pl.when(jnp.logical_not(here))
        def _():
            self.to_owner(head, group).start()

    def drain_to_owner(self):
        for head in range(HEADS_HERE):
            for group in range(2):

                @pl.when(jnp.logical_not(self.owner_is_here(head, group)))
                def _(head=head, group=group):
                    self.to_owner(head, group).wait_send()

    def tokens_are_here(self, block):
        y, c, z, x = whereami()
        core = lax.div(head_here(), HEADS_HERE)
        return (lax.div(block, 4) == z) & (lax.rem(block, 4) == x) & (core == c)

    def to_tokens(self, block):
        y, c, z, x = whereami()
        core = lax.div(head_here(), HEADS_HERE)
        slot = head_here() - HEADS_HERE * core
        return remote(
            self.outbox.at[block],
            self.inbox.at[slot, c],
            self.sems.at[block],
            self.recv_sem,
            device_at(y, core, lax.div(block, 4), lax.rem(block, 4)),
        )

    def send_to_tokens(self, block):
        y, c, z, x = whereami()
        here = self.tokens_are_here(block)

        @pl.when(here)
        def _():
            slot = head_here() - HEADS_HERE * lax.div(head_here(), HEADS_HERE)
            pltpu.make_async_copy(
                self.outbox.at[block], self.inbox.at[slot, c], self.recv_sem
            ).start()

        @pl.when(jnp.logical_not(here))
        def _():
            self.to_tokens(block).start()

    def drain_to_tokens(self):
        def drain(block, carry):
            @pl.when(jnp.logical_not(self.tokens_are_here(block)))
            def _():
                self.to_tokens(block).wait_send()

            return carry

        lax.fori_loop(0, 16, drain, 0)

    def arrived(self):
        pltpu.make_async_copy(self.inbox, self.inbox, self.recv_sem).wait()


def block_mask(ends, query_at, key_at):
    query_row = query_at + lax.broadcasted_iota(jnp.int32, (Q_BLOCK, 1), 0)
    start = document_start(ends, query_row)
    shape = (Q_BLOCK, K_BLOCK)
    query = query_at + lax.broadcasted_iota(jnp.int32, shape, 0)
    key = key_at + lax.broadcasted_iota(jnp.int32, shape, 1)
    return (key <= query) & (key >= start)


def run_pumps(pumps, block):
    for number, action in sorted(pumps.items()):
        pl.when(block == number)(action)


def score_rows(step, lane):
    at = (step * (K_BLOCK // 128) + lane) * Q_BLOCK
    return pl.ds(pl.multiple_of(at, Q_BLOCK), Q_BLOCK)


def attend_forward(queries, keys_values, ends, score_box, kept_output, pumps, block_done):
    def one_block(block, carry):
        run_pumps(pumps, block)
        query_at = pl.multiple_of(block * Q_BLOCK, Q_BLOCK)
        rows = pl.ds(query_at, Q_BLOCK)
        query = queries[rows, :]
        key_blocks = lax.div(block, 2) + 1

        def scores(step, top):
            key_at = pl.multiple_of(step * K_BLOCK, K_BLOCK)
            raw = dot_nt(query, keys_values[pl.ds(key_at, K_BLOCK), :])
            masked = jnp.where(block_mask(ends, query_at, key_at), raw, mask_fill)
            for lane in range(K_BLOCK // 128):
                tile = masked[:, 128 * lane : 128 * lane + 128]
                score_box[score_rows(step, lane), :] = tile
                top = jnp.maximum(top, tile)
            return top

        top = lax.fori_loop(0, key_blocks, scores, jnp.full((Q_BLOCK, 128), mask_fill, f32))
        top = jnp.max(top, axis=1, keepdims=True)

        def collect(step, state):
            total, gathered = state
            key_at = pl.multiple_of(step * K_BLOCK, K_BLOCK)
            tiles = []
            for lane in range(K_BLOCK // 128):
                tile = jnp.exp(score_box[score_rows(step, lane), :] - top)
                total = total + tile
                tiles.append(tile.astype(bf16))
            return total, gathered + dot_nn(
                jnp.concatenate(tiles, axis=1), keys_values[pl.ds(key_at, K_BLOCK), :]
            )

        total, gathered = lax.fori_loop(
            0,
            key_blocks,
            collect,
            (jnp.zeros((Q_BLOCK, 128), f32), jnp.zeros((Q_BLOCK, 128), f32)),
        )
        total = jnp.sum(total, axis=1, keepdims=True)
        lane = lax.broadcasted_iota(jnp.int32, (Q_BLOCK, 128), 1)
        kept_output[rows, :] = jnp.where(
            lane < HEAD_DIM, top + jnp.log(total), gathered / total
        )
        block_done(block)
        return carry

    lax.fori_loop(0, Q_BLOCKS, one_block, 0)


def attend_backward(
    queries, keys_values, output_grad, kept_output, ends, query_grad, key_value_grad, pumps
):
    key_value_grad[...] = jnp.zeros_like(key_value_grad)

    def one_block(block, carry):
        run_pumps(pumps, block)
        query_at = pl.multiple_of(block * Q_BLOCK, Q_BLOCK)
        rows = pl.ds(query_at, Q_BLOCK)
        query = queries[rows, :]
        grad = output_grad[rows, :]
        kept = kept_output[rows, :]
        logs = kept[:, 0:1]
        inner = jnp.sum(grad.astype(f32) * kept, axis=1, keepdims=True)

        def one_key(step, total):
            key_at = pl.multiple_of(step * K_BLOCK, K_BLOCK)
            keys_here = pl.ds(key_at, K_BLOCK)
            both = keys_values[keys_here, :]
            masked = jnp.where(
                block_mask(ends, query_at, key_at), dot_nt(query, both), mask_fill
            )
            probability = jnp.exp(masked - logs)
            probability_grad = dot_nt(grad, both)
            score_grad = (probability * (probability_grad - inner)).astype(bf16)
            key_value_grad[keys_here, :] += dot_tn(score_grad, query) + dot_tn(
                probability.astype(bf16), grad
            )
            return total + dot_nn(score_grad, both)

        query_grad[rows, :] = lax.fori_loop(
            0, lax.div(block, 2) + 1, one_key, jnp.zeros((Q_BLOCK, 128), f32)
        )
        return carry

    lax.fori_loop(0, Q_BLOCKS, one_block, 0)


class Weights:
    def __init__(self, e):
        self.e = e
        self.ranges = {"attend": (0, GATE_AT, 0), "units": (GATE_AT, PACK_COLS - GATE_AT, 1)}

    def copy(self, layer, name):
        start, width, slot = self.ranges[name]
        columns = pl.ds(start, width)
        return pltpu.make_async_copy(
            self.e.full.at[layer, :, :, :, :, columns],
            self.e.weights.at[:, :, :, :, columns],
            self.e.load_sem.at[slot],
        )

    def load(self, layer, name):
        self.copy(layer, name).start()

    def wait(self, layer, name):
        self.copy(layer, name).wait()

    def keep_copy(self):
        return pltpu.make_async_copy(self.e.weights, self.e.full.at[0], self.e.load_sem.at[3])

    def keep(self):
        self.keep_copy().start()

    def keep_wait(self):
        self.keep_copy().wait()

    def units(self, step, start):
        side, at = lax.div(step, 2), start + 256 * lax.rem(step, 2)
        columns = pl.ds(pl.multiple_of(at, 128), 256)
        return self.e.weights[side, :, :, :, columns].reshape(D, 256)

    def get(self, side, start, stop):
        return self.e.weights[side, :, :, :, start:stop].reshape(D, stop - start)


def nothing():
    pass


def forward_pass(e, layer, rows_ref, rows_out, pump):
    y, c, z, x = whereami()
    weights = Weights(e)
    swaps = [Swap(e, 4 * layer + slot) for slot in range(4)]
    ask = HeadTraffic(e.ask_out, e.ask_in, e.ask_send, e.traffic_recv.at[4 * layer])
    answer = HeadTraffic(e.reply_out, e.reply_in, e.reply_send, e.traffic_recv.at[4 * layer + 1])
    theirs = pl.ds(pl.multiple_of((1 - c) * TOKENS_HERE, TOKENS_HERE), TOKENS_HERE)
    swaps[0].start(e.normed.at[layer, c], e.normed.at[layer, c])
    pump("start")
    if layer == 1:
        weights.wait(layer, "attend")
    swaps[0].wait()
    chip_normed = e.normed[layer].reshape(CHIP_TOKENS, D)
    cosine = e.tables[:, :, 0:128].reshape(CHIP_TOKENS, 128)
    sine = e.tables[:, :, 128:256].reshape(CHIP_TOKENS, 128)
    for side in range(2):
        mixed = dot_nn(chip_normed, weights.get(side, 0, IN_COLS))
        for inner in range(3):
            head = 3 * side + inner
            pair = mixed[:, 128 * inner : 128 * inner + 128]
            pair = (pair * cosine + swap_halves(pair) * sine).astype(bf16)
            value = mixed[:, 384 + 64 * inner : 448 + 64 * inner]
            for group in range(2):
                at = TOKENS_HERE * group
                e.ask_out[head, group, 0:128] = pair[at : at + 128]
                e.ask_out[head, group, 128:192] = jnp.concatenate(
                    [value[at : at + 64], value[at + 64 : at + 128]], axis=1
                ).astype(bf16)
                ask.send_to_owner(head, group)
    pump("asked")
    queries, keys_values = e.queries.at[layer], e.keys_values.at[layer]
    kept_output = e.kept_output.at[layer]

    @pl.when(is_owner_here())
    def _():
        ask.arrived()

        def place(block, carry):
            at = pl.multiple_of(block * TOKENS_HERE, TOKENS_HERE)
            pair = e.ask_in[block, 0:128].astype(f32)
            zeros = jnp.zeros((TOKENS_HERE, HEAD_DIM), f32)
            queries[pl.ds(at, 128), :] = jnp.concatenate(
                [pair[:, 0:64] * (1.0 / math.sqrt(HEAD_DIM)), zeros], axis=1
            ).astype(bf16)
            both = e.ask_in[block, 128:192].astype(f32)
            value = jnp.concatenate([both[:, 0:64], both[:, 64:128]], axis=0)
            keys_values[pl.ds(at, 128), :] = jnp.concatenate(
                [pair[:, 64:128], value], axis=1
            ).astype(bf16)
            return carry

        lax.fori_loop(0, 16, place, 0)

        def send_rows(block):
            for half in range(2):
                at = pl.multiple_of(block * Q_BLOCK + half * 128, 128)
                first = kept_output[pl.ds(at, 64), :]
                second = kept_output[pl.ds(at + 64, 64), :]
                e.reply_out[2 * block + half] = jnp.concatenate(
                    [first[:, HEAD_DIM:], second[:, HEAD_DIM:]], axis=1
                ).astype(bf16)
                answer.send_to_tokens(2 * block + half)

        attend_forward(
            queries, keys_values, e.lengths, e.score_box, kept_output, pump.blocks(), send_rows
        )

    @pl.when(jnp.logical_not(is_owner_here()))
    def _():
        for number, action in sorted(pump.blocks().items()):
            action()

    pump("attended")
    answer.arrived()
    pump("answered")
    partial = None
    for side in range(2):
        columns = [jnp.zeros((CHIP_TOKENS, 64), f32)]
        for inner in range(3):
            pieces = []
            for group in range(2):
                both = e.reply_in[3 * side + inner, group].astype(f32)
                pieces += [both[:, 0:64], both[:, 64:128]]
            columns.append(jnp.concatenate(pieces, axis=0))
        e.attended[layer, side] = jnp.concatenate(columns, axis=1).astype(bf16)
        term = dot_nt(e.attended[layer, side], weights.get(side, OUT_AT, GATE_AT))
        partial = term if partial is None else partial + term
    e.partial_out[...] = partial.astype(bf16)
    swaps[1].start(e.partial_out.at[theirs], e.partial_in.at[0])
    own_part = own_half(partial)
    swaps[1].wait()
    middle = rows_ref[...].astype(f32) + (own_part + e.partial_in[0].astype(f32))
    e.mid_rows[layer] = middle
    e.normed_mid[layer, c] = (middle * norm_scale(middle) * e.gains[layer, 1:2, :]).astype(bf16)
    swaps[2].start(e.normed_mid.at[layer, c], e.normed_mid.at[layer, c])
    pump("before units")
    if layer == 1:
        weights.wait(layer, "units")
    swaps[2].wait()
    e.partial[...] = jnp.zeros_like(e.partial)

    def some_units(step, carry):
        chip_mid = e.normed_mid[layer].reshape(CHIP_TOKENS, D)
        gate = dot_nn(chip_mid, weights.units(step, GATE_AT))
        up = dot_nn(chip_mid, weights.units(step, UP_AT))
        active = (gate * sigmoid(gate) * up).astype(bf16)
        e.partial[...] += dot_nt(active, weights.units(step, DOWN_AT))
        return carry

    lax.fori_loop(0, 4, some_units, 0)
    partial = e.partial[...]
    e.partial_out[...] = partial.astype(bf16)
    swaps[3].start(e.partial_out.at[theirs], e.partial_in.at[1])
    own_part = own_half(partial)
    pump("units")
    swaps[3].wait()
    branch = own_part + e.partial_in[1].astype(f32)
    if layer == 1:
        rows_out[0] = e.mid_rows[layer]
        rows_out[1] = branch
    else:
        rows_out[...] = e.mid_rows[layer] + branch
    ask.drain_to_owner()
    pl.when(is_owner_here())(answer.drain_to_tokens)
    pump("end")


def backward_pass(e, layer, grad_ref, rows_ref, grad_out, pump, next_layer):
    y, c, z, x = whereami()
    weights = Weights(e)
    swaps = [Swap(e, 8 + 4 * layer + slot) for slot in range(4)]
    ask = HeadTraffic(e.back_ask_out, e.back_ask_in, e.ask_send, e.traffic_recv.at[4 * layer + 2])
    answer = HeadTraffic(
        e.back_reply_out, e.back_reply_in, e.reply_send, e.traffic_recv.at[4 * layer + 3]
    )
    theirs = pl.ds(pl.multiple_of((1 - c) * TOKENS_HERE, TOKENS_HERE), TOKENS_HERE)

    def transpose_rows(which, value):
        e.left_t[which] = value.T.reshape(4, D // 4, CHIP_TOKENS)

    def weight_grad(side, start, width, which, right):
        columns = pl.ds(pl.multiple_of(start, 128), width)
        for block in range(4):
            e.grads[layer, side, block, :, :, columns] = (
                dot_nn(e.left_t[which, block], right).astype(bf16).reshape(4, PAIR_ROWS, width)
            )

    e.grad_swap[0, c] = grad_ref[...].astype(bf16)
    swaps[0].start(e.grad_swap.at[0, c], e.grad_swap.at[0, c])
    pump("start")
    if next_layer is None:
        weights.wait(layer, "units")
    swaps[0].wait()
    transpose_rows(0, e.grad_swap[0].reshape(CHIP_TOKENS, D))
    transpose_rows(1, e.normed_mid[layer].reshape(CHIP_TOKENS, D))
    e.partial[...] = jnp.zeros_like(e.partial)

    def some_units(step, carry):
        down = e.grad_swap[0].reshape(CHIP_TOKENS, D)
        chip_mid = e.normed_mid[layer].reshape(CHIP_TOKENS, D)
        gate = dot_nn(chip_mid, weights.units(step, GATE_AT))
        up = dot_nn(chip_mid, weights.units(step, UP_AT))
        active_grad = dot_nn(down, weights.units(step, DOWN_AT))
        sigma = sigmoid(gate)
        active = gate * sigma
        gate_grad = (active_grad * up * sigma * (1.0 + gate * (1.0 - sigma))).astype(bf16)
        up_grad = (active_grad * active).astype(bf16)
        side, at = lax.div(step, 2), 256 * lax.rem(step, 2)
        weight_grad(side, DOWN_AT + at, 256, 0, (active * up).astype(bf16))
        weight_grad(side, GATE_AT + at, 256, 1, gate_grad)
        weight_grad(side, UP_AT + at, 256, 1, up_grad)
        e.partial[...] += dot_nt(gate_grad, weights.units(step, GATE_AT)) + dot_nt(
            up_grad, weights.units(step, UP_AT)
        )
        return carry

    lax.fori_loop(0, 4, some_units, 0)
    partial = e.partial[...]
    e.partial_out[...] = partial.astype(bf16)
    swaps[1].start(e.partial_out.at[theirs], e.partial_in.at[0])
    own_part = own_half(partial)
    if next_layer is not None:
        weights.load(next_layer, "units")
    pump("units")
    swaps[1].wait()
    back, gain_grad = norm_back(
        e.mid_rows[layer], e.gains[layer, 1:2, :], own_part + e.partial_in[0].astype(f32)
    )
    e.mid_grad[...] = grad_ref[...].astype(f32) + back
    e.gain_total[2 * layer + 1 : 2 * layer + 2, :] = gain_grad
    e.grad_swap[1, c] = e.mid_grad[...].astype(bf16)
    swaps[2].start(e.grad_swap.at[1, c], e.grad_swap.at[1, c])
    if next_layer is None:
        weights.wait(layer, "attend")
    swaps[2].wait()
    branch = e.grad_swap[1].reshape(CHIP_TOKENS, D)
    for side in range(2):
        heads_grad = dot_nn(branch, weights.get(side, OUT_AT, GATE_AT))
        for inner in range(3):
            head = 3 * side + inner
            piece = heads_grad[:, 64 + 64 * inner : 128 + 64 * inner]
            for group in range(2):
                at = TOKENS_HERE * group
                e.back_ask_out[head, group] = jnp.concatenate(
                    [piece[at : at + 64], piece[at + 64 : at + 128]], axis=1
                ).astype(bf16)
                ask.send_to_owner(head, group)
    transpose_rows(0, branch)
    for side in range(2):
        weight_grad(side, OUT_AT, GATE_AT - OUT_AT, 0, e.attended[layer, side])
    pump("asked")

    @pl.when(is_owner_here())
    def _():
        ask.arrived()

        def place(block, carry):
            at = pl.multiple_of(block * TOKENS_HERE, TOKENS_HERE)
            both = e.back_ask_in[block].astype(f32)
            grad = jnp.concatenate([both[:, 0:64], both[:, 64:128]], axis=0)
            e.output_grad[pl.ds(at, 128), :] = jnp.concatenate(
                [jnp.zeros((TOKENS_HERE, HEAD_DIM), f32), grad], axis=1
            ).astype(bf16)
            return carry

        lax.fori_loop(0, 16, place, 0)
        attend_backward(
            e.queries.at[layer],
            e.keys_values.at[layer],
            e.output_grad,
            e.kept_output.at[layer],
            e.lengths,
            e.query_grad,
            e.key_value_grad,
            pump.blocks(),
        )

        def give(block, carry):
            at = pl.multiple_of(block * TOKENS_HERE, TOKENS_HERE)
            e.back_reply_out[block, 0:128] = jnp.concatenate(
                [
                    e.query_grad[pl.ds(at, 128), 0:64] * (1.0 / math.sqrt(HEAD_DIM)),
                    e.key_value_grad[pl.ds(at, 128), 0:64],
                ],
                axis=1,
            ).astype(bf16)
            e.back_reply_out[block, 128:192] = jnp.concatenate(
                [
                    e.key_value_grad[pl.ds(at, 64), 64:128],
                    e.key_value_grad[pl.ds(at + 64, 64), 64:128],
                ],
                axis=1,
            ).astype(bf16)
            answer.send_to_tokens(block)
            return carry

        lax.fori_loop(0, 16, give, 0)

    @pl.when(jnp.logical_not(is_owner_here()))
    def _():
        for number, action in sorted(pump.blocks().items()):
            action()

    pump("attended")
    answer.arrived()
    cosine = e.tables[:, :, 0:128].reshape(CHIP_TOKENS, 128)
    sine = e.tables[:, :, 128:256].reshape(CHIP_TOKENS, 128)
    transpose_rows(1, e.normed[layer].reshape(CHIP_TOKENS, D))
    partial = None
    for side in range(2):
        pieces = []
        for inner in range(3):
            head = 3 * side + inner
            pair = jnp.concatenate(
                [e.back_reply_in[head, 0, 0:128], e.back_reply_in[head, 1, 0:128]], axis=0
            ).astype(f32)
            pair = pair * cosine - swap_halves(pair) * sine
            e.mixed_grad[side, :, 128 * inner : 128 * inner + 128] = pair.astype(bf16)
            rows = []
            for group in range(2):
                both = e.back_reply_in[head, group, 128:192].astype(f32)
                rows += [both[:, 0:64], both[:, 64:128]]
            pieces.append(jnp.concatenate(rows, axis=0))
        pieces.append(jnp.zeros((CHIP_TOKENS, 64), f32))
        e.mixed_grad[side, :, 384:IN_COLS] = jnp.concatenate(pieces, axis=1).astype(bf16)
        weight_grad(side, 0, OUT_AT, 1, e.mixed_grad[side, :, 0:OUT_AT])
        last = dot_nn(e.left_t[1].reshape(D, CHIP_TOKENS), e.mixed_grad[side, :, OUT_AT:IN_COLS])
        here = e.grads[layer, side, :, :, :, OUT_AT:IN_COLS].reshape(D, IN_COLS - OUT_AT)
        e.grads[layer, side, :, :, :, OUT_AT:IN_COLS] = (
            (here.astype(f32) + last).astype(bf16).reshape(4, 4, PAIR_ROWS, IN_COLS - OUT_AT)
        )
    pump("mixed")
    for side in range(2):
        term = dot_nt(e.mixed_grad[side], weights.get(side, 0, IN_COLS))
        partial = term if partial is None else partial + term
    e.partial_out[...] = partial.astype(bf16)
    swaps[3].start(e.partial_out.at[theirs], e.partial_in.at[1])
    own_part = own_half(partial)
    if next_layer is not None:
        weights.load(next_layer, "attend")
    pump("swapped")
    swaps[3].wait()
    back, gain_grad = norm_back(
        rows_ref[...].astype(f32), e.gains[layer, 0:1, :], own_part + e.partial_in[1].astype(f32)
    )
    e.gain_total[2 * layer : 2 * layer + 1, :] = gain_grad
    if layer == 0:
        grad_out[0] = e.mid_grad[...]
        grad_out[1] = back
    else:
        grad_out[...] = e.mid_grad[...] + back
    ask.drain_to_owner()
    pl.when(is_owner_here())(answer.drain_to_tokens)
    pump("end")


class Pump:
    def __init__(self, actions=None):
        self.actions = actions or {}

    def __call__(self, point):
        for action in self.actions.get(point, []):
            action()

    def blocks(self):
        def run(actions):
            def action():
                for one in actions:
                    one()

            return action

        return {key: run(value) for key, value in self.actions.items() if isinstance(key, int)}


COPIES = 2


def owner_place(matrix, copy):
    return (matrix // 4, 0, (matrix // 4 + matrix % 4 + 2 * copy) % 4, matrix % 4)


def square_columns(kind):
    if kind < 2:
        return [(128 * head + 64 * kind, 64) for head in range(3)]
    return [(384 + 192 * (kind - 2), 192)]


def ns_step(source, target, gram, polynomial, columns, pumps, tick):
    rows = D // 2

    def gram_rows(block, carry):
        run_pumps(pumps, tick + block)
        here = pl.ds(2 * block, 2)
        part = source[here, :, :, 0:columns].reshape(rows, columns)
        gram[here, :, :, 0:D] = (
            dot_nt(part, source[:, :, :, 0:columns].reshape(D, columns))
            .astype(bf16)
            .reshape(2, 4, PAIR_ROWS, D)
        )
        return carry

    lax.fori_loop(0, 2, gram_rows, 0)

    def polynomial_columns(block, carry):
        run_pumps(pumps, tick + 2 + block)
        here = pl.ds(pl.multiple_of(block * 256, 256), 256)
        part = gram[:, :, :, here].reshape(D, 256)
        polynomial[:, :, :, here] = (
            (
                quintic_two * part.astype(f32)
                + quintic_three * dot_nn(gram[:, :, :, 0:D].reshape(D, D), part)
            )
            .astype(bf16)
            .reshape(4, 4, PAIR_ROWS, 256)
        )
        return carry

    lax.fori_loop(0, 3, polynomial_columns, 0)

    def update_columns(block, carry):
        run_pumps(pumps, tick + 5 + block)
        here = pl.ds(pl.multiple_of(block * 256, 256), 256)
        part = source[:, :, :, here].reshape(D, 256)
        target[:, :, :, here] = (
            (
                quintic_one * part.astype(f32)
                + dot_nn(polynomial[:, :, :, 0:D].reshape(D, D), part)
            )
            .astype(bf16)
            .reshape(4, 4, PAIR_ROWS, 256)
        )
        return carry

    lax.fori_loop(0, columns // 256, update_columns, 0)


def orthogonal_owner(slots, front, back, gram, polynomial, wide, send_back, pumps):
    columns = FF if wide else D
    slot_rows = PAIR_ROWS if wide else 32

    def add_squares(index, carry):
        value = slots[index, 0:slot_rows, :].astype(f32)
        return carry + jnp.sum(value * value, axis=0, keepdims=True)

    squares = lax.fori_loop(0, DEVICES, add_squares, jnp.zeros((1, 256), f32))
    scale = 1.0 / (jnp.sqrt(jnp.sum(squares, axis=1, keepdims=True)) + ortho_eps)

    def assemble(pair, carry):
        outer, inner = lax.div(pair, 4), lax.rem(pair, 4)
        narrow = []
        for part in range(4):
            first = slots[pair * 8 + part, 0:slot_rows, :].astype(f32) * scale
            second = slots[pair * 8 + 4 + part, 0:slot_rows, :].astype(f32) * scale
            joined = jnp.concatenate([first[0:24], second[0:24]], axis=0)
            if wide:
                front[outer, inner, :, part * 512 : part * 512 + 256] = joined.astype(bf16)
                front[outer, inner, :, part * 512 + 256 : part * 512 + 512] = jnp.concatenate(
                    [first[24:48], second[24:48]], axis=0
                ).astype(bf16)
            else:
                narrow.append(joined[:, 0:192])
        if not wide:
            front[outer, inner, :, 0:D] = jnp.concatenate(narrow, axis=1).astype(bf16)
        return carry

    lax.fori_loop(0, 16, assemble, 0)
    ticks = 5 + columns // 256

    def two_steps(index, carry):
        ns_step(front, back, gram, polynomial, columns, pumps, 2 * ticks * index)
        ns_step(back, front, gram, polynomial, columns, pumps, 2 * ticks * index + ticks)
        return carry

    lax.fori_loop(0, NS_STEPS // 2, two_steps, 0)

    def take_apart(pair, carry):
        outer, inner = lax.div(pair, 4), lax.rem(pair, 4)
        if not wide:
            whole = front[outer, inner, :, 0:D].astype(f32)
        for part in range(4):
            if wide:
                left = front[outer, inner, :, part * 512 : part * 512 + 256].astype(f32)
                right = front[outer, inner, :, part * 512 + 256 : part * 512 + 512].astype(f32)
                slots[pair * 8 + part] = jnp.concatenate([left[0:24], right[0:24]], axis=0).astype(
                    bf16
                )
                slots[pair * 8 + 4 + part] = jnp.concatenate(
                    [left[24:48], right[24:48]], axis=0
                ).astype(bf16)
            else:
                left = jnp.concatenate(
                    [whole[:, 192 * part : 192 * part + 192], jnp.zeros((PAIR_ROWS, 64), f32)], axis=1
                )
                slots[pair * 8 + part, 0:32] = left[0:32].astype(bf16)
                slots[pair * 8 + 4 + part, 0:32] = jnp.concatenate(
                    [left[24:48], left[0:8]], axis=0
                ).astype(bf16)
        for part in range(8):
            send_back(pair * 8 + part)
        return carry

    lax.fori_loop(0, 16, take_apart, 0)


class Muon:
    def __init__(self, e):
        self.e = e
        self.places = [[owner_place(m, copy) for copy in range(COPIES)] for m in range(OWNERS)]

    def is_owner(self, m, copy):
        y, c, z, x = whereami()
        place = self.places[m][copy]
        return (y == place[0]) & (c == place[1]) & (z == place[2]) & (x == place[3])

    def tile(self, m):
        return self.e.square.at[m] if m < SQUARE_COUNT else self.e.wide.at[m - SQUARE_COUNT]

    def returned(self, m):
        return self.e.square_new.at[m] if m < SQUARE_COUNT else self.e.wide_new.at[m - SQUARE_COUNT]

    def slot(self, m):
        if m < SQUARE_COUNT:
            return self.e.slots.at[index_here(), pl.ds(0, 32)]
        return self.e.slots.at[index_here()]

    def outbound(self, m, copy):
        return remote(
            self.tile(m),
            self.slot(m),
            self.e.tile_send.at[copy, m],
            self.e.slot_recv.at[0],
            device_at(*self.places[m][copy]),
        )

    def update_moment(self, layer, start, stop):
        e = self.e
        rows = slice(ROW_SHARD * layer, ROW_SHARD * layer + ROW_SHARD)
        e.moment_new[rows, start:stop] = (
            moment_decay * e.moment[rows, start:stop] + e.total[rows, start:stop]
        )

    def send(self, m):
        e = self.e
        if m < SQUARE_COUNT:
            layer, kind = m // 4, m % 4
            rows = slice(ROW_SHARD * layer, ROW_SHARD * layer + ROW_SHARD)
            pieces = [e.moment_new[rows, at : at + width] for at, width in square_columns(kind)]
            tile = jnp.concatenate(pieces + [jnp.zeros((ROW_SHARD, 64), f32)], axis=1)
            e.square[m] = jnp.concatenate([tile, jnp.zeros((8, 256), f32)], axis=0).astype(bf16)
        else:
            layer, kind = (m - SQUARE_COUNT) // 3, (m - SQUARE_COUNT) % 3
            rows = slice(ROW_SHARD * layer, ROW_SHARD * layer + ROW_SHARD)
            at = GATE_AT + 512 * kind
            e.wide[m - SQUARE_COUNT] = jnp.concatenate(
                [e.moment_new[rows, at : at + 256], e.moment_new[rows, at + 256 : at + 512]], axis=0
            ).astype(bf16)

        for copy in range(COPIES):

            @pl.when(jnp.logical_not(self.is_owner(m, copy)))
            def _(copy=copy):
                self.outbound(m, copy).start()

            @pl.when(self.is_owner(m, copy))
            def _(copy=copy):
                keep = pltpu.make_async_copy(
                    self.tile(m), self.slot(m), self.e.tile_send.at[copy, m]
                )
                keep.start()
                keep.wait()

    def serve(self, is_wide, pumps):
        e = self.e
        y, c, z, x = whereami()
        slot_rows = PAIR_ROWS if is_wide else 32
        whole = e.slots.at[pl.ds(0, DEVICES - 1), pl.ds(0, slot_rows)]
        pltpu.make_async_copy(whole, whole, e.slot_recv.at[0]).wait()
        matrix = y * 4 + x
        mine = index_here()

        def send_back(index):
            if is_wide:
                source, target = e.slots.at[index], e.wide_new.at[matrix - SQUARE_COUNT]
            else:
                source, target = e.slots.at[index, pl.ds(0, 32)], e.square_new.at[matrix]

            ahead = lax.rem(lax.rem(lax.div(index, 4), 4) - z + 4, 4)

            @pl.when((index != mine) & (ahead < 2))
            def _():
                remote(
                    source, target, e.slot_recv.at[1], e.tile_recv.at[matrix], device_of_index(index)
                ).start()

            @pl.when(index == mine)
            def _():
                copy = pltpu.make_async_copy(source, target, e.tile_recv.at[matrix])
                copy.start()

        orthogonal_owner(
            e.slots,
            e.weights.at[0],
            e.weights.at[1],
            e.grads.at[1, 0],
            e.grads.at[1, 1],
            is_wide,
            send_back,
            pumps,
        )
        sent = e.slots.at[pl.ds(0, DEVICES // COPIES - 1), pl.ds(0, slot_rows)]
        pltpu.make_async_copy(sent, sent, e.slot_recv.at[1]).wait()

    def serve_all(self, last_steps):
        y, c, z, x = whereami()
        placed = (c == 0) & (lax.rem(lax.rem(z - x - y + 8, 4), 2) == 0)
        square_owner = placed & (y < 2)
        wide_owner = placed & ((y == 2) | ((y == 3) & (x < 2)))

        @pl.when(wide_owner)
        def _():
            self.serve(True, dict(zip((1, 4, 8), last_steps)))

        @pl.when(jnp.logical_not(wide_owner))
        def _():
            for step in last_steps:
                step()

        pl.when(square_owner)(lambda: self.serve(False, {}))

    def finish(self):
        e = self.e
        for m in range(OWNERS):
            tile = self.returned(m)
            pltpu.make_async_copy(tile, tile, e.tile_recv.at[m]).wait()
            if m < SQUARE_COUNT:
                layer, kind = m // 4, m % 4
                rate = project_rate if kind == 3 else matrix_rate
                factor = 0.2 * math.sqrt(D)
                value = e.square_new[m].astype(f32)[0:ROW_SHARD]
                places = square_columns(kind)
            else:
                layer, kind = (m - SQUARE_COUNT) // 3, (m - SQUARE_COUNT) % 3
                rate, factor = matrix_rate, 0.2 * math.sqrt(FF)
                value = e.wide_new[m - SQUARE_COUNT].astype(f32)
                value = jnp.concatenate([value[0:ROW_SHARD], value[ROW_SHARD:PAIR_ROWS]], axis=1)
                places = [(GATE_AT + 512 * kind, 512)]
            rows = slice(ROW_SHARD * layer, ROW_SHARD * layer + ROW_SHARD)
            offset = 0
            for at, width in places:
                weight = e.weights_own[rows, at : at + width]
                e.weights_new[rows, at : at + width] = weight - rate * (
                    factor * value[:, offset : offset + width] + matrix_decay * weight
                )
                offset += width

            for copy in range(COPIES):

                @pl.when(jnp.logical_not(self.is_owner(m, copy)))
                def _(m=m, copy=copy):
                    self.outbound(m, copy).wait_send()


def finish_sum(e, layer, start, stop, slot, sending):
    y, c, z, x = whereami()
    holder, odd, low = lax.div(x, 2), lax.rem(z, 2), 2 * lax.div(z, 2)
    rows = slice(ROW_SHARD * layer, ROW_SHARD * layer + ROW_SHARD)
    target = e.total.at[rows, start:stop]
    sources = [e.pair.at[rows, start:stop], e.pair_more.at[:, start:stop]]

    def copy(i):
        return remote(
            sources[i],
            target,
            e.pair_send.at[2 * slot + i],
            e.pair_recv.at[slot],
            device_at(y, odd, low + i, x),
        )

    def send():
        for i in range(2):
            here = (c == odd) & (odd == i)
            part = slice(ROW_SHARD * i, ROW_SHARD * i + ROW_SHARD)

            def half():
                whole = e.grads[layer, lax.rem(x, 2), y, row_place(z), :, start:stop]
                return whole.astype(f32)[part]

            @pl.when(here)
            def _():
                target[...] = half()

            @pl.when(jnp.logical_not(here))
            def _():
                sources[i][...] = half()
                copy(i).start()

    def sent():
        for i in range(2):
            pl.when(jnp.logical_not((c == odd) & (odd == i)))(lambda i=i: copy(i).wait_send())

    if sending:
        pl.when(c == holder)(send)
    else:
        pl.when(c == holder)(sent)
        pl.when(jnp.logical_not((c == holder) & (low + c == z)))(lambda: copy(0).wait_recv())


def gain_copies(e, hop):
    if hop == 0:
        devices = [sibling_here()]
    else:
        devices = [neighbour("xyz"[hop - 1], offset) for offset in (1, 2, 3)]
    base = 3 * hop
    return [
        remote(
            e.gain_total,
            e.gain_box.at[base + i],
            e.gain_send.at[base + i],
            e.gain_recv.at[base + i],
            device,
        )
        for i, device in enumerate(devices)
    ]


def gain_start(e, hop):
    for copy in gain_copies(e, hop):
        copy.start()


def gain_finish(e, hop):
    copies = gain_copies(e, hop)
    for copy in copies:
        copy.wait_send()
        copy.wait_recv()
    for i in range(len(copies)):
        e.gain_total[...] += e.gain_box[3 * hop + i]


BOX_SHAPES = {}
for _part in range(3):
    for _phase in range(3):
        _lead = box_shape(_part, _phase) + (PAIR_ROWS,)
        if _phase == 0:
            BOX_SHAPES[f"late_half_{_part}"] = (2,) + _lead + (256,)
            BOX_SHAPES[f"early_half_{_part}"] = (2,) + _lead + (256,)
            BOX_SHAPES[f"both_block_{_part}"] = (2,) + _lead + (512,)
            BOX_SHAPES[f"late_last_{_part}"] = (3,) + _lead + (256,)
            BOX_SHAPES[f"early_last_{_part}"] = (3,) + _lead + (256,)
        else:
            BOX_SHAPES[f"late_{_part}{_phase}"] = (3,) + _lead + (768,)
            BOX_SHAPES[f"early_{_part}{_phase}"] = (3,) + _lead + (768,)


def boxes_of(e, layer, kind, part):
    name = "late" if layer == 1 else "early"
    start, width = {"units": (0, 512), "attend": (512, 256)}[kind]
    found = []
    for phase in range(3):
        if phase == 0 and kind == "attend":
            boxes = getattr(e, f"{name}_last_{part}")
            found.append([boxes.at[i] for i in range(3)])
        elif phase == 0:
            blocks = getattr(e, f"both_block_{part}")
            halves = getattr(e, f"{name}_half_{part}")
            found.append([halves.at[0], halves.at[1], blocks.at[0], blocks.at[1]])
        else:
            cut = (slice(None),) * (len(box_shape(part, phase)) + 1) + (pl.ds(start, width),)
            boxes = getattr(e, f"{name}_{part}{phase}")
            found.append([boxes.at[(i,) + cut] for i in range(3)])
    return found


def step_kernel(*refs):
    e = types.SimpleNamespace(**dict(zip(REF_NAMES, refs)))
    e.query_grad = e.score_box.at[pl.ds(0, GROUP)]
    e.key_value_grad = e.score_box.at[pl.ds(GROUP, GROUP)]
    e.pair, e.total = e.moment_new, e.weights_new
    e.back_ask_out, e.back_reply_out, e.back_reply_in = e.reply_in, e.ask_in, e.ask_out
    y, c, z, x = whereami()
    holder = lax.div(x, 2)
    signal_everyone()
    e.own[...] = e.weights_own[...].astype(bf16)
    e.tables[c] = rope_table(e.lengths)
    e.normed[0, c] = normalized(e.rows_in[...].astype(f32), e.gains[0, 0:1, :])
    e.gain_total[...] = jnp.zeros_like(e.gain_total)
    wait_for_everyone()

    odd, low = lax.rem(z, 2), 2 * lax.div(z, 2)
    table_swap = remote(
        e.tables.at[c], e.tables.at[c], e.pair_send.at[6], e.pair_recv.at[5], sibling_here()
    )
    table_swap.start()

    def hand_over(i):
        return remote(
            e.own, e.twin.at[i], e.pair_send.at[7], e.pair_recv.at[3 + i], device_at(y, holder, low + c, x)
        )

    own_stays = (c == holder) & (low + c == z)
    for i in range(2):
        pl.when(jnp.logical_not(own_stays) & (odd == i))(lambda i=i: hand_over(i).start())

    @pl.when(c == holder)
    def _():
        for i in range(2):
            mine = (c == odd) & (odd == i)

            @pl.when(mine)
            def _(i=i):
                e.twin[i] = e.own[...]

            pl.when(jnp.logical_not(mine))(lambda i=i: hand_over(i).wait_recv())
        first, second = e.twin[0].astype(f32), e.twin[1].astype(f32)
        for layer in range(LAYERS):
            part = slice(layer * ROW_SHARD, layer * ROW_SHARD + ROW_SHARD)
            joined = jnp.concatenate([first[part], second[part]], axis=0).astype(bf16)
            if layer == 0:
                e.weights[lax.rem(x, 2), y, row_place(z)] = joined
            else:
                e.piece[...] = joined
                keep = pltpu.make_async_copy(
                    e.piece, e.full.at[1, lax.rem(x, 2), y, row_place(z)], e.load_sem.at[2]
                )
                keep.start()
                keep.wait()

    def gather_lanes(ref, at, width, base, direct):
        return [
            GatherLane(
                ref,
                part,
                (at + part * width, width),
                e.gather_send,
                e.gather_recv,
                base + 12 * part,
                direct,
            )
            for part in range(3)
        ]

    ga = gather_lanes(e.weights, 0, 256, 0, (0, 1, 2))
    gb = gather_lanes(e.weights, GATE_AT, 512, 36, (0, 1))
    gc = gather_lanes(e.full.at[1], 0, 256, 72, (0, 1))
    gd = gather_lanes(e.full.at[1], GATE_AT, 512, 108, (0, 1))
    do = lambda lanes, step, phase: lambda: each(lanes, step, phase)
    weights = Weights(e)
    each(ga, "first", 0)
    each(gb, "first", 0)
    for lanes in (ga, gb):
        each(lanes, "third", 0)
        each(lanes, "first", 1)
    for lanes in (ga, gb):
        each(lanes, "third", 1)
        each(lanes, "first", 2)
    each(gc, "first", 0)
    each(gd, "first", 0)
    table_swap.wait_send()
    remote(
        e.tables.at[c], e.tables.at[1 - c], e.pair_send.at[6], e.pair_recv.at[5], sibling_here()
    ).wait_recv()
    each(ga, "third", 2)

    def turn_to_layer_1():
        each(gc, "third", 2)
        for phase in range(3):
            each(ga, "drain", phase)
            each(gb, "drain", phase)
        weights.keep_wait()
        weights.load(1, "attend")

    def units_of_layer_1():
        each(gd, "third", 2)
        weights.load(1, "units")

    forward_pass(
        e,
        0,
        e.rows_in,
        e.rows_mid,
        Pump(
            {
                "asked": [do(gb, "second", 2)],
                3: [
                    do(gc, "third", 0),
                    do(gc, "first", 1),
                    do(gd, "third", 0),
                    do(gd, "first", 1),
                ],
                7: [do(gc, "third", 1), do(gc, "first", 2)],
                "answered": [do(gd, "third", 1), do(gd, "first", 2)],
                "before units": [do(gb, "third", 2), weights.keep, do(gc, "second", 2)],
                "end": [turn_to_layer_1],
            }
        ),
    )
    e.normed[1, c] = normalized(e.rows_mid[...], e.gains[1, 0:1, :])
    forward_pass(e, 1, e.rows_mid, e.rows_out, Pump({"asked": [do(gd, "second", 2)], "answered": [units_of_layer_1]}))
    def reduce_lanes(layer, kind, base):
        at, width = {"units": (GATE_AT, 512), "attend": (0, 256)}[kind]
        lanes = []
        for part in range(3):
            credits = [e.credit.at[part, side] for side in range(2)]
            lanes.append(
                ReduceLane(
                    e.grads.at[layer],
                    boxes_of(e, layer, kind, part),
                    part,
                    (at + part * width, width),
                    e.reduce_send,
                    e.reduce_recv,
                    base + 12 * part,
                    (1, 2) if kind == "units" else (0, 1, 2),
                    gives=credits if kind == "units" and layer == 1 else None,
                    takes=credits if kind == "units" and layer == 0 else None,
                )
            )
        return lanes

    lu = reduce_lanes(1, "units", 0)
    la = reduce_lanes(1, "attend", 36)
    ru = reduce_lanes(0, "units", 72)
    ra = reduce_lanes(0, "attend", 108)
    muon = Muon(e)
    backward_pass(
        e,
        1,
        e.grad_in,
        e.rows_mid,
        e.grad_mid,
        Pump(
            {
                "asked": [do(lu, "first", 0)],
                4: [do(lu, "second", 0)],
                "mixed": [do(la, "first", 0), do(lu, "third", 0), do(lu, "first", 1)],
            }
        ),
        0,
    )

    def late_done():
        finish_sum(e, 1, 0, PACK_COLS, 0, False)
        muon.update_moment(1, 0, PACK_COLS)
        for m in (4, 5, 6, 7, 11, 12, 13):
            muon.send(m)

    def units_done():
        finish_sum(e, 0, GATE_AT, PACK_COLS, 1, False)
        muon.update_moment(0, GATE_AT, PACK_COLS)
        for m in (8, 9, 10):
            muon.send(m)

    backward_pass(
        e,
        0,
        e.grad_mid,
        e.rows_in,
        e.grad_out,
        Pump(
            {
                "units": [
                    do(la, "third", 0),
                    do(la, "first", 1),
                    do(lu, "third", 1),
                    do(lu, "first", 2),
                ],
                "asked": [
                    do(ru, "first", 0),
                    do(la, "third", 1),
                    do(la, "first", 2),
                    do(lu, "third", 2),
                ],
                3: [do(la, "third", 2), lambda: finish_sum(e, 1, 0, PACK_COLS, 0, True)],
                5: [do(ru, "second", 0)],
                "attended": [
                    late_done,
                    do(ru, "third", 0),
                    do(ru, "first", 1),
                    do(ru, "third", 1),
                    do(ru, "first", 2),
                ],
                "mixed": [
                    do(ra, "first", 0),
                    do(ru, "third", 2),
                    lambda: finish_sum(e, 0, GATE_AT, PACK_COLS, 1, True),
                ],
                "swapped": [units_done],
            }
        ),
        None,
    )
    gain_start(e, 0)

    def sum_step_one():
        gain_finish(e, 0)
        gain_start(e, 1)
        each(ra, "third", 0)
        each(ra, "first", 1)

    def sum_step_two():
        gain_finish(e, 1)
        gain_start(e, 2)
        each(ra, "third", 1)
        each(ra, "first", 2)

    def sum_step_three():
        each(ra, "third", 2)
        finish_sum(e, 0, 0, GATE_AT, 2, True)
        finish_sum(e, 0, 0, GATE_AT, 2, False)
        muon.update_moment(0, 0, GATE_AT)
        for m in range(4):
            muon.send(m)
        gain_finish(e, 2)
        gain_start(e, 3)

    for lanes in (gc, gd, lu, la):
        for phase in range(3):
            each(lanes, "drain", phase)
    muon.serve_all([sum_step_one, sum_step_two, sum_step_three])
    for lanes in (ru, ra):
        for phase in range(3):
            each(lanes, "drain", phase)
    gain_finish(e, 3)
    pl.when(jnp.logical_not(own_stays))(lambda: hand_over(0).wait_send())
    muon.finish()


REF_TABLE = [
    ("rows_in", "in", (TOKENS_HERE, D), bf16),
    ("grad_in", "in", (TOKENS_HERE, D), bf16),
    ("lengths", "in", (1, 3), jnp.int32),
    ("weights_own", "in", (LAYERS * ROW_SHARD, PACK_COLS), f32),
    ("moment", "in", (LAYERS * ROW_SHARD, PACK_COLS), f32),
    ("gains", "in", (LAYERS, 2, D), f32),
    ("rows_out", "out", (2, TOKENS_HERE, D), f32),
    ("grad_out", "out", (2, TOKENS_HERE, D), f32),
    ("gain_total", "out", (8, D), f32),
    ("moment_new", "out", (LAYERS * ROW_SHARD, PACK_COLS), f32),
    ("weights_new", "out", (LAYERS * ROW_SHARD, PACK_COLS), f32),
    ("full", "hbm", (LAYERS, 2, 4, 4, PAIR_ROWS, PACK_COLS), bf16),
    ("weights", "vmem", (2, 4, 4, PAIR_ROWS, PACK_COLS), bf16),
    ("grads", "vmem", (LAYERS, 2, 4, 4, PAIR_ROWS, PACK_COLS), bf16),
    ("own", "vmem", (LAYERS * ROW_SHARD, PACK_COLS), bf16),
    ("twin", "vmem", (2, LAYERS * ROW_SHARD, PACK_COLS), bf16),
    ("pair_more", "vmem", (ROW_SHARD, PACK_COLS), f32),

    ("piece", "vmem", (PAIR_ROWS, PACK_COLS), bf16),
    ("tables", "vmem", (2, TOKENS_HERE, 256), f32),
    ("rows_mid", "vmem", (TOKENS_HERE, D), f32),
    ("grad_mid", "vmem", (TOKENS_HERE, D), f32),
    ("mid_grad", "vmem", (TOKENS_HERE, D), f32),
    ("mid_rows", "vmem", (LAYERS, TOKENS_HERE, D), f32),
    ("normed", "vmem", (LAYERS, 2, TOKENS_HERE, D), bf16),
    ("normed_mid", "vmem", (LAYERS, 2, TOKENS_HERE, D), bf16),
    ("attended", "vmem", (LAYERS, 2, CHIP_TOKENS, 256), bf16),
    ("queries", "vmem", (LAYERS, GROUP, 128), bf16),
    ("keys_values", "vmem", (LAYERS, GROUP, 128), bf16),
    ("kept_output", "vmem", (LAYERS, GROUP, 2 * HEAD_DIM), f32),
    ("score_box", "vmem", (2 * GROUP, 128), f32),
    ("output_grad", "vmem", (GROUP, 128), bf16),
    ("partial", "vmem", (CHIP_TOKENS, D), f32),
    ("partial_out", "vmem", (CHIP_TOKENS, D), bf16),
    ("left_t", "vmem", (2, 4, D // 4, CHIP_TOKENS), bf16),
    ("partial_in", "vmem", (2, TOKENS_HERE, D), bf16),
    ("grad_swap", "vmem", (2, 2, TOKENS_HERE, D), bf16),
    ("mixed_grad", "vmem", (2, CHIP_TOKENS, IN_COLS), bf16),
    ("ask_out", "vmem", (HEADS_HERE, 2, ASK_ROWS, 128), bf16),
    ("ask_in", "vmem", (16, ASK_ROWS, 128), bf16),
    ("reply_out", "vmem", (16, REPLY_ROWS, 128), bf16),
    ("reply_in", "vmem", (HEADS_HERE, 2, REPLY_ROWS, 128), bf16),
    ("back_ask_in", "vmem", (16, REPLY_ROWS, 128), bf16),
    ("gain_box", "vmem", (12, 8, D), f32),
    ("square", "vmem", (SQUARE_COUNT, 32, 256), bf16),
    ("wide", "vmem", (WIDE_COUNT, PAIR_ROWS, 256), bf16),
    ("square_new", "vmem", (SQUARE_COUNT, 32, 256), bf16),
    ("wide_new", "vmem", (WIDE_COUNT, PAIR_ROWS, 256), bf16),
    ("slots", "vmem", (DEVICES, PAIR_ROWS, 256), bf16),
]
REF_TABLE += [(name, "vmem", shape, bf16) for name, shape in BOX_SHAPES.items()]
REF_TABLE += [
    ("gather_send", "dma", (144,), None),
    ("gather_recv", "dma", (144,), None),
    ("reduce_send", "dma", (144,), None),
    ("reduce_recv", "dma", (144,), None),
    ("load_sem", "dma", (4,), None),
    ("swap_send", "dma", (16,), None),
    ("swap_recv", "dma", (16,), None),
    ("ask_send", "dma", (HEADS_HERE, 2), None),
    ("reply_send", "dma", (16,), None),
    ("traffic_recv", "dma", (8,), None),
    ("pair_send", "dma", (8,), None),
    ("pair_recv", "dma", (6,), None),
    ("gain_send", "dma", (12,), None),
    ("gain_recv", "dma", (12,), None),
    ("tile_send", "dma", (COPIES, OWNERS), None),
    ("tile_recv", "dma", (OWNERS,), None),
    ("slot_recv", "dma", (2,), None),
    ("credit", "regular", (3, 2), None),
]
REF_NAMES = [row[0] for row in REF_TABLE]


def train_step(*inputs):
    scratch = []
    for name, where, shape, dtype in REF_TABLE:
        if where == "vmem":
            scratch.append(pltpu.VMEM(shape, dtype))
        elif where == "dma":
            scratch.append(pltpu.SemaphoreType.DMA(shape))
        elif where == "regular":
            scratch.append(pltpu.SemaphoreType.REGULAR(shape))
    outs = [row for row in REF_TABLE if row[1] in ("out", "hbm")]
    return pl.pallas_call(
        step_kernel,
        out_shape=[jax.ShapeDtypeStruct(shape, dtype) for _, _, shape, dtype in outs],
        in_specs=[pl.BlockSpec(memory_space=pltpu.VMEM)] * len(inputs),
        out_specs=[
            pl.BlockSpec(memory_space=pltpu.HBM if where == "hbm" else pltpu.VMEM)
            for _, where, _, _ in outs
        ],
        scratch_shapes=scratch,
        compiler_params=pltpu.CompilerParams(
            collective_id=0, has_side_effects=True, vmem_limit_bytes=63 * MIB + MIB // 2
        ),
        name="train_step",
    )(*inputs)


def pack_layers(attend_in, attend_out, expand, shrink):
    query_key = jnp.stack(
        [attend_in[:, k].reshape(LAYERS, ROW_SHARD, 3, HEAD_DIM) for k in range(2)], axis=3
    )
    return jnp.concatenate(
        [
            query_key.reshape(LAYERS, ROW_SHARD, 384),
            attend_in[:, 2],
            jnp.swapaxes(attend_out, 1, 2),
            expand[:, 0],
            expand[:, 1],
            jnp.swapaxes(shrink, 1, 2),
        ],
        axis=2,
    )


def four_squares(packed):
    query_key = packed[:, :, 0:384].reshape(LAYERS, ROW_SHARD, 3, 2, HEAD_DIM)
    return [
        query_key[:, :, :, 0].reshape(LAYERS, ROW_SHARD, 192),
        query_key[:, :, :, 1].reshape(LAYERS, ROW_SHARD, 192),
        packed[:, :, 384:576],
        packed[:, :, 576:768],
    ]


def unpack_layers(packed):
    query, key, value, out = four_squares(packed)
    return (
        jnp.stack([query, key, value], axis=1),
        jnp.swapaxes(out, 1, 2),
        jnp.stack([packed[:, :, 768:1280], packed[:, :, 1280:1792]], axis=1),
        jnp.swapaxes(packed[:, :, 1792:2304], 1, 2),
    )


def body(
    hidden_in,
    out_grad,
    seq_lengths,
    norm_gains,
    gain_first,
    gain_second,
    attend_in,
    attend_out,
    expand,
    shrink,
    attend_in_moment,
    attend_out_moment,
    expand_moment,
    shrink_moment,
):
    flat = (LAYERS * ROW_SHARD, PACK_COLS)
    rows, rows_grad, gain_total, moment_new, weights_new, _ = train_step(
        hidden_in,
        out_grad,
        seq_lengths,
        pack_layers(attend_in, attend_out, expand, shrink).reshape(flat),
        pack_layers(attend_in_moment, attend_out_moment, expand_moment, shrink_moment).reshape(flat),
        norm_gains,
    )
    split = (LAYERS, ROW_SHARD, PACK_COLS)
    gain_grad = gain_total[0:4].reshape(LAYERS, 2, D)
    gain_first_new = first_decay * gain_first + (1.0 - first_decay) * gain_grad
    gain_second_new = second_decay * gain_second + (1.0 - second_decay) * gain_grad * gain_grad
    gains_new = norm_gains - gain_rate * (gain_first_new / (1.0 - first_decay**STEP)) / (
        jnp.sqrt(gain_second_new / (1.0 - second_decay**STEP)) + adam_eps
    )
    return (
        rows[0] + rows[1],
        rows_grad[0] + rows_grad[1],
        gain_first_new,
        gain_second_new,
        gains_new,
        *unpack_layers(moment_new.reshape(split)),
        *unpack_layers(weights_new.reshape(split)),
    )


def solution(mesh):
    placed = (
        P(("fsdp", "ctx", "tp"), None),
        P(("fsdp", "ctx", "tp"), None),
        P("fsdp", None),
        P(),
        P(),
        P(),
        P(None, None, ("fsdp", "ctx"), "tp"),
        P(None, "tp", ("fsdp", "ctx")),
        P(None, None, ("fsdp", "ctx"), "tp"),
        P(None, "tp", ("fsdp", "ctx")),
        P(None, None, ("fsdp", "ctx"), "tp"),
        P(None, "tp", ("fsdp", "ctx")),
        P(None, None, ("fsdp", "ctx"), "tp"),
        P(None, "tp", ("fsdp", "ctx")),
    )
    return jax.shard_map(
        body,
        mesh=mesh,
        in_specs=placed,
        out_specs=(
            P(("fsdp", "ctx", "tp"), None),
            P(("fsdp", "ctx", "tp"), None),
            P(),
            P(),
            P(),
            P(None, None, ("fsdp", "ctx"), "tp"),
            P(None, "tp", ("fsdp", "ctx")),
            P(None, None, ("fsdp", "ctx"), "tp"),
            P(None, "tp", ("fsdp", "ctx")),
            P(None, None, ("fsdp", "ctx"), "tp"),
            P(None, "tp", ("fsdp", "ctx")),
            P(None, None, ("fsdp", "ctx"), "tp"),
            P(None, "tp", ("fsdp", "ctx")),
        ),
        check_vma=False,
    )
```

```python
import math
import types

import jax
import jax.numpy as jnp
from jax import lax
from jax.experimental import pallas as pl
from jax.experimental.pallas import tpu as pltpu
from jax.sharding import PartitionSpec as P

D = 768
HEAD_DIM = 64
FF = 2048
NS_STEPS = 4
STEP = 5


norm_eps = 1e-05
rope_base = 10000.0
mask_fill = -1e30
quintic_one = 3.4445
quintic_two = -4.775
quintic_three = 2.0315
moment_decay = 0.95
matrix_rate = 0.1
project_rate = 0.8
matrix_decay = 0.1
gain_rate = 0.8
first_decay = 0.9
second_decay = 0.95
adam_eps = 1e-08
ortho_eps = 1e-07


MESH_ID = pl.DeviceIdType.MESH
ROW_SHARD = 24
PAIR_ROWS = 2 * ROW_SHARD
PACK_COLS = 2304
LAYERS = 2
MIB = 1024 * 1024
DEVICES = 128


def whereami():
    fsdp_index = lax.axis_index("fsdp")
    return (lax.div(fsdp_index, 2), lax.rem(fsdp_index, 2), lax.axis_index("ctx"), lax.axis_index("tp"))


def device_at(y, c, z, x):
    return (y * 2 + c, z, x)


def device_of_index(index):
    return (lax.div(index, 16), lax.rem(lax.div(index, 4), 4), lax.rem(index, 4))


def index_here():
    y, c, z, x = whereami()
    return (y * 2 + c) * 16 + z * 4 + x


def sibling_here():
    y, c, z, x = whereami()
    return device_at(y, 1 - c, z, x)


def ring(index, offset):
    return lax.rem(index + offset, 4)


def remote(source, target, send_sem, recv_sem, device):
    return pltpu.make_async_remote_copy(
        src_ref=source,
        dst_ref=target,
        send_sem=send_sem,
        recv_sem=recv_sem,
        device_id=device,
        device_id_type=MESH_ID,
    )


def signal_everyone():
    barrier = pltpu.get_barrier_semaphore()
    mine = index_here()

    def signal_one(offset, carry):
        device = device_of_index(lax.rem(mine + offset, DEVICES))
        pl.semaphore_signal(barrier, inc=1, device_id=device, device_id_type=MESH_ID)
        return carry

    lax.fori_loop(1, DEVICES, signal_one, 0)


def wait_for_everyone():
    pl.semaphore_wait(pltpu.get_barrier_semaphore(), DEVICES - 1)


def neighbour(axis, offset):
    y, c, z, x = whereami()
    if axis == "y":
        return device_at(ring(y, offset), c, z, x)
    if axis == "z":
        return device_at(y, c, ring(z, offset), x)
    return device_at(y, c, z, ring(x, offset))


PART_ORDER = (("x", "y", "z"), ("y", "z", "x"), ("z", "x", "y"))


def row_place(z):
    return 2 * lax.rem(z, 2) + lax.div(z, 2)


def part_view(ref, columns, done, axis, place, half):
    y, c, z, x = whereami()
    whole = slice(None)

    def index(name, own):
        if name != axis and name in done:
            return whole
        value = place if name == axis else own
        return row_place(value) if name == "z" else value

    if axis == "x":
        pick_x = lax.rem(place, 2)
    else:
        pick_x = whole if "x" in done else lax.rem(x, 2)
    start, width = columns
    if half is not None:
        width = width // 2
        start = start + half * width
    return ref.at[pick_x, index("y", y), index("z", z), :, pl.ds(start, width)]


def ring_exists(axis, done, place):
    y, c, z, x = whereami()
    if axis == "x":
        return lax.div(place, 2) == c
    if "x" in done:
        return None
    return lax.div(x, 2) == c


def run_if(condition, action):
    if condition is None:
        action()
    else:
        pl.when(condition)(action)


class GatherLane:
    def __init__(self, ref, part, columns, send, recv, base, direct):
        self.ref, self.part, self.columns = ref, part, columns
        self.send, self.recv, self.base, self.direct = send, recv, base, direct

    def parts(self, phase):
        axis = PART_ORDER[self.part][phase]
        done = PART_ORDER[self.part][:phase]
        y, c, z, x = whereami()
        return axis, done, {"x": x, "y": y, "z": z}[axis], self.base + 4 * phase

    def copy(self, phase, slot, place, half, offset):
        axis, done, me, base = self.parts(phase)
        view = part_view(self.ref, self.columns, done, axis, place, half)
        return remote(
            view, view, self.send.at[base + slot], self.recv.at[base + slot], neighbour(axis, offset)
        )

    def first(self, phase):
        axis, done, me, base = self.parts(phase)

        def action():
            if phase in self.direct:
                for offset in (1, 2, 3):
                    self.copy(phase, offset - 1, me, None, offset).start()
            else:
                self.copy(phase, 0, me, None, 1).start()
                self.copy(phase, 1, me, None, 3).start()

        run_if(ring_exists(axis, done, me), action)

    def second(self, phase):
        axis, done, me, base = self.parts(phase)
        left, right = ring(me, 3), ring(me, 1)

        def from_left():
            self.copy(phase, 0, left, None, 1).wait_recv()
            self.copy(phase, 2, left, 0, 1).start()

        def from_right():
            self.copy(phase, 1, right, None, 1).wait_recv()
            self.copy(phase, 3, right, 1, 3).start()

        run_if(ring_exists(axis, done, left), from_left)
        run_if(ring_exists(axis, done, right), from_right)

    def third(self, phase):
        axis, done, me, base = self.parts(phase)
        far = ring(me, 2)

        def action():
            self.copy(phase, 2, far, 0, 1).wait_recv()
            self.copy(phase, 3, far, 1, 1).wait_recv()

        if phase in self.direct:
            for offset in (1, 2, 3):
                place = ring(me, 4 - offset)
                run_if(
                    ring_exists(axis, done, place),
                    lambda place=place, offset=offset: self.copy(
                        phase, offset - 1, place, None, 1
                    ).wait_recv(),
                )
        else:
            run_if(ring_exists(axis, done, far), action)

    def drain(self, phase):
        axis, done, me, base = self.parts(phase)
        left, right = ring(me, 3), ring(me, 1)

        def own():
            for slot in range(3 if phase in self.direct else 2):
                self.copy(phase, slot, me, None, 1).wait_send()

        run_if(ring_exists(axis, done, me), own)
        if phase not in self.direct:
            run_if(
                ring_exists(axis, done, left), lambda: self.copy(phase, 2, left, 0, 1).wait_send()
            )
            run_if(
                ring_exists(axis, done, right), lambda: self.copy(phase, 3, right, 1, 3).wait_send()
            )


class ReduceLane:
    def __init__(self, ref, boxes, part, columns, send, recv, base, direct, gives=None, takes=None):
        self.ref, self.boxes, self.part, self.columns = ref, boxes, part, columns
        self.send, self.recv, self.base, self.direct = send, recv, base, direct
        self.gives, self.takes = gives, takes

    def parts(self, phase):
        axis = PART_ORDER[self.part][2 - phase]
        done = PART_ORDER[self.part][: 2 - phase]
        y, c, z, x = whereami()
        return axis, done, {"x": x, "y": y, "z": z}[axis], self.base + 4 * phase

    def copy(self, phase, slot, place, half, offset):
        axis, done, me, base = self.parts(phase)
        view = part_view(self.ref, self.columns, done, axis, place, half)
        return remote(
            view,
            self.boxes[phase][slot],
            self.send.at[base + slot],
            self.recv.at[base + slot],
            neighbour(axis, offset),
        )

    def add(self, phase, place, half, boxes):
        axis, done, me, base = self.parts(phase)
        view = part_view(self.ref, self.columns, done, axis, place, half)
        lead = view.shape[:-2]

        def summed(where):
            terms = [view[where]] + [box[where] for box in boxes]
            while len(terms) > 1:
                terms = [
                    terms[i] + terms[i + 1] if i + 1 < len(terms) else terms[i]
                    for i in range(0, len(terms), 2)
                ]
            return terms[0]

        def add_one(index, carry):
            where = []
            for extent in reversed(lead):
                where.insert(0, lax.rem(index, extent))
                index = lax.div(index, extent)
            view[tuple(where)] = summed(tuple(where))
            return carry

        if len(lead) == 0:
            view[...] = summed(...)
        else:
            lax.fori_loop(0, math.prod(lead), add_one, 0)

    def first(self, phase):
        axis, done, me, base = self.parts(phase)
        far = ring(me, 2)

        def action():
            self.copy(phase, 0, far, 0, 1).start()
            self.copy(phase, 1, far, 1, 3).start()

        if phase in self.direct:
            for offset in (1, 2, 3):
                place = ring(me, offset)
                run_if(
                    ring_exists(axis, done, place),
                    lambda place=place, offset=offset: self.copy(
                        phase, offset - 1, place, None, offset
                    ).start(),
                )
        else:
            run_if(ring_exists(axis, done, far), action)

    def second(self, phase):
        axis, done, me, base = self.parts(phase)
        left, right = ring(me, 3), ring(me, 1)

        def to_right():
            self.copy(phase, 0, right, 0, 1).wait_recv()
            self.add(phase, right, 0, [self.boxes[phase][0]])
            if phase == 0 and self.takes is not None:
                pl.semaphore_wait(self.takes[0], 1)
            self.copy(phase, 2, right, None, 1).start()

        def to_left():
            self.copy(phase, 1, left, 1, 1).wait_recv()
            self.add(phase, left, 1, [self.boxes[phase][1]])
            if phase == 0 and self.takes is not None:
                pl.semaphore_wait(self.takes[1], 1)
            self.copy(phase, 3, left, None, 3).start()

        run_if(ring_exists(axis, done, right), to_right)
        run_if(ring_exists(axis, done, left), to_left)

    def third(self, phase):
        axis, done, me, base = self.parts(phase)

        def action():
            if phase in self.direct:
                slots = (0, 1, 2)
            else:
                slots = (2, 3)
            for slot in slots:
                self.copy(phase, slot, me, None, 1).wait_recv()
            self.add(phase, me, None, [self.boxes[phase][slot] for slot in slots])
            if phase == 0 and self.gives is not None:
                for sem, offset in zip(self.gives, (3, 1)):
                    pl.semaphore_signal(
                        sem, inc=1, device_id=neighbour(axis, offset), device_id_type=MESH_ID
                    )

        run_if(ring_exists(axis, done, me), action)

    def drain(self, phase):
        axis, done, me, base = self.parts(phase)
        far, left, right = ring(me, 2), ring(me, 3), ring(me, 1)

        def own():
            self.copy(phase, 0, far, 0, 1).wait_send()
            self.copy(phase, 1, far, 1, 3).wait_send()

        if phase in self.direct:
            for offset in (1, 2, 3):
                place = ring(me, offset)
                run_if(
                    ring_exists(axis, done, place),
                    lambda place=place, offset=offset: self.copy(
                        phase, offset - 1, place, None, offset
                    ).wait_send(),
                )
            return
        run_if(ring_exists(axis, done, far), own)
        run_if(ring_exists(axis, done, right), lambda: self.copy(phase, 2, right, None, 1).wait_send())
        run_if(ring_exists(axis, done, left), lambda: self.copy(phase, 3, left, None, 3).wait_send())


def box_shape(part, phase):
    order = PART_ORDER[part]
    axis, done = order[2 - phase], order[: 2 - phase]
    lead = []
    for name, extent in (("x", 2), ("y", 4), ("z", 4)):
        if name != axis and name in done:
            lead.append(extent)
    return tuple(lead)


def each(lanes, step, phase):
    for lane in lanes:
        getattr(lane, step)(phase)


HEADS_HERE = 6
TOKENS_HERE = 128
CHIP_TOKENS = 256
GROUP = 2048
Q_BLOCK = 256
K_BLOCK = 512
Q_BLOCKS = GROUP // Q_BLOCK
IN_COLS = 640
OUT_AT = 512
GATE_AT = 768
UP_AT = 1280
DOWN_AT = 1792
ASK_ROWS = 192
REPLY_ROWS = 64
SQUARE_COUNT = 8
WIDE_COUNT = 6
OWNERS = SQUARE_COUNT + WIDE_COUNT
bf16 = jnp.bfloat16
f32 = jnp.float32


def dot_nn(left, right):
    return jnp.dot(left, right, preferred_element_type=f32)


def dot_nt(left, right):
    return lax.dot_general(left, right, (((1,), (1,)), ((), ())), preferred_element_type=f32)


def dot_tn(left, right):
    return lax.dot_general(left, right, (((0,), (0,)), ((), ())), preferred_element_type=f32)


def sigmoid(value):
    return 1.0 / (1.0 + jnp.exp(-value))


def norm_scale(rows):
    return lax.rsqrt(jnp.mean(rows * rows, axis=-1, keepdims=True) + norm_eps)


def normalized(rows, gain):
    return (rows * norm_scale(rows) * gain).astype(bf16)


def rope_table(lengths):
    y, c, z, x = whereami()
    shape = (TOKENS_HERE, 128)
    place = (z * 4 + x) * TOKENS_HERE + lax.broadcasted_iota(jnp.int32, shape, 0)
    lane = lax.broadcasted_iota(jnp.int32, shape, 1)
    position = place - document_start(lengths, place)
    frequency = jnp.exp(lax.rem(lane, 32).astype(f32) * (-2.0 / HEAD_DIM * math.log(rope_base)))
    angle = position.astype(f32) * frequency
    sine = jnp.sin(angle)
    sine = jnp.where(lax.rem(lane, 64) < 32, -sine, sine)
    return jnp.concatenate([jnp.cos(angle), sine], axis=1)


def document_start(lengths, place):
    first = lengths[0:1, 0:1]
    second = first + lengths[0:1, 1:2]
    return jnp.where(place >= second, second, jnp.where(place >= first, first, 0))


def norm_back(rows, gain, grad):
    scale = norm_scale(rows)
    unit = rows * scale
    inner = grad * gain
    back = scale * (inner - unit * jnp.mean(inner * unit, axis=-1, keepdims=True))
    return back, jnp.sum(grad * unit, axis=0, keepdims=True)


def swap_halves(values):
    lower = lax.rem(lax.broadcasted_iota(jnp.int32, values.shape, 1), 64) < 32
    return jnp.where(lower, pltpu.roll(values, 96, 1), pltpu.roll(values, 32, 1))


def is_owner_here():
    y, c, z, x = whereami()
    return z < 3


def head_here():
    y, c, z, x = whereami()
    return 4 * z + x


def own_half(both):
    y, c, z, x = whereami()
    return jnp.where(c == 0, both[0:TOKENS_HERE], both[TOKENS_HERE:CHIP_TOKENS])


class Swap:
    def __init__(self, e, slot):
        self.send, self.recv = e.swap_send.at[slot], e.swap_recv.at[slot]

    def start(self, source, target):
        self.copy = remote(source, target, self.send, self.recv, sibling_here())
        self.copy.start()

    def wait(self):
        self.copy.wait_send()
        self.copy.wait_recv()


class HeadTraffic:
    def __init__(self, outbox, inbox, sems, recv_sem):
        self.outbox, self.inbox, self.sems, self.recv_sem = outbox, inbox, sems, recv_sem

    def owner_place(self, head):
        y, c, z, x = whereami()
        number = HEADS_HERE * c + head
        return lax.div(number, 4), lax.rem(number, 4)

    def owner_is_here(self, head, group):
        y, c, z, x = whereami()
        owner_z, owner_x = self.owner_place(head)
        return (owner_z == z) & (owner_x == x) & (c == group)

    def to_owner(self, head, group):
        y, c, z, x = whereami()
        owner_z, owner_x = self.owner_place(head)
        return remote(
            self.outbox.at[head, group],
            self.inbox.at[z * 4 + x],
            self.sems.at[head, group],
            self.recv_sem,
            device_at(y, group, owner_z, owner_x),
        )

    def send_to_owner(self, head, group):
        y, c, z, x = whereami()
        here = self.owner_is_here(head, group)

        @pl.when(here)
        def _():
            pltpu.make_async_copy(
                self.outbox.at[head, group], self.inbox.at[z * 4 + x], self.recv_sem
            ).start()

        @pl.when(jnp.logical_not(here))
        def _():
            self.to_owner(head, group).start()

    def drain_to_owner(self):
        for head in range(HEADS_HERE):
            for group in range(2):

                @pl.when(jnp.logical_not(self.owner_is_here(head, group)))
                def _(head=head, group=group):
                    self.to_owner(head, group).wait_send()

    def tokens_are_here(self, block):
        y, c, z, x = whereami()
        core = lax.div(head_here(), HEADS_HERE)
        return (lax.div(block, 4) == z) & (lax.rem(block, 4) == x) & (core == c)

    def to_tokens(self, block):
        y, c, z, x = whereami()
        core = lax.div(head_here(), HEADS_HERE)
        slot = head_here() - HEADS_HERE * core
        return remote(
            self.outbox.at[block],
            self.inbox.at[slot, c],
            self.sems.at[block],
            self.recv_sem,
            device_at(y, core, lax.div(block, 4), lax.rem(block, 4)),
        )

    def send_to_tokens(self, block):
        y, c, z, x = whereami()
        here = self.tokens_are_here(block)

        @pl.when(here)
        def _():
            slot = head_here() - HEADS_HERE * lax.div(head_here(), HEADS_HERE)
            pltpu.make_async_copy(
                self.outbox.at[block], self.inbox.at[slot, c], self.recv_sem
            ).start()

        @pl.when(jnp.logical_not(here))
        def _():
            self.to_tokens(block).start()

    def drain_to_tokens(self):
        def drain(block, carry):
            @pl.when(jnp.logical_not(self.tokens_are_here(block)))
            def _():
                self.to_tokens(block).wait_send()

            return carry

        lax.fori_loop(0, 16, drain, 0)

    def arrived(self):
        pltpu.make_async_copy(self.inbox, self.inbox, self.recv_sem).wait()


def block_mask(ends, query_at, key_at):
    query_row = query_at + lax.broadcasted_iota(jnp.int32, (Q_BLOCK, 1), 0)
    start = document_start(ends, query_row)
    shape = (Q_BLOCK, K_BLOCK)
    query = query_at + lax.broadcasted_iota(jnp.int32, shape, 0)
    key = key_at + lax.broadcasted_iota(jnp.int32, shape, 1)
    return (key <= query) & (key >= start)


def run_pumps(pumps, block):
    for number, action in sorted(pumps.items()):
        pl.when(block == number)(action)


def score_rows(step, lane):
    at = (step * (K_BLOCK // 128) + lane) * Q_BLOCK
    return pl.ds(pl.multiple_of(at, Q_BLOCK), Q_BLOCK)


def attend_forward(queries, keys_values, ends, score_box, kept_output, pumps, block_done):
    def one_block(block, carry):
        run_pumps(pumps, block)
        query_at = pl.multiple_of(block * Q_BLOCK, Q_BLOCK)
        rows = pl.ds(query_at, Q_BLOCK)
        query = queries[rows, :]
        key_blocks = lax.div(block, 2) + 1

        def scores(step, top):
            key_at = pl.multiple_of(step * K_BLOCK, K_BLOCK)
            raw = dot_nt(query, keys_values[pl.ds(key_at, K_BLOCK), :])
            masked = jnp.where(block_mask(ends, query_at, key_at), raw, mask_fill)
            for lane in range(K_BLOCK // 128):
                tile = masked[:, 128 * lane : 128 * lane + 128]
                score_box[score_rows(step, lane), :] = tile
                top = jnp.maximum(top, tile)
            return top

        top = lax.fori_loop(0, key_blocks, scores, jnp.full((Q_BLOCK, 128), mask_fill, f32))
        top = jnp.max(top, axis=1, keepdims=True)

        def collect(step, state):
            total, gathered = state
            key_at = pl.multiple_of(step * K_BLOCK, K_BLOCK)
            tiles = []
            for lane in range(K_BLOCK // 128):
                tile = jnp.exp(score_box[score_rows(step, lane), :] - top)
                total = total + tile
                tiles.append(tile.astype(bf16))
            return total, gathered + dot_nn(
                jnp.concatenate(tiles, axis=1), keys_values[pl.ds(key_at, K_BLOCK), :]
            )

        total, gathered = lax.fori_loop(
            0,
            key_blocks,
            collect,
            (jnp.zeros((Q_BLOCK, 128), f32), jnp.zeros((Q_BLOCK, 128), f32)),
        )
        total = jnp.sum(total, axis=1, keepdims=True)
        lane = lax.broadcasted_iota(jnp.int32, (Q_BLOCK, 128), 1)
        kept_output[rows, :] = jnp.where(
            lane < HEAD_DIM, top + jnp.log(total), gathered / total
        )
        block_done(block)
        return carry

    lax.fori_loop(0, Q_BLOCKS, one_block, 0)


def attend_backward(
    queries, keys_values, output_grad, kept_output, ends, query_grad, key_value_grad, pumps
):
    key_value_grad[...] = jnp.zeros_like(key_value_grad)

    def one_block(block, carry):
        run_pumps(pumps, block)
        query_at = pl.multiple_of(block * Q_BLOCK, Q_BLOCK)
        rows = pl.ds(query_at, Q_BLOCK)
        query = queries[rows, :]
        grad = output_grad[rows, :]
        kept = kept_output[rows, :]
        logs = kept[:, 0:1]
        inner = jnp.sum(grad.astype(f32) * kept, axis=1, keepdims=True)

        def one_key(step, total):
            key_at = pl.multiple_of(step * K_BLOCK, K_BLOCK)
            keys_here = pl.ds(key_at, K_BLOCK)
            both = keys_values[keys_here, :]
            masked = jnp.where(
                block_mask(ends, query_at, key_at), dot_nt(query, both), mask_fill
            )
            probability = jnp.exp(masked - logs)
            probability_grad = dot_nt(grad, both)
            score_grad = (probability * (probability_grad - inner)).astype(bf16)
            key_value_grad[keys_here, :] += dot_tn(score_grad, query) + dot_tn(
                probability.astype(bf16), grad
            )
            return total + dot_nn(score_grad, both)

        query_grad[rows, :] = lax.fori_loop(
            0, lax.div(block, 2) + 1, one_key, jnp.zeros((Q_BLOCK, 128), f32)
        )
        return carry

    lax.fori_loop(0, Q_BLOCKS, one_block, 0)


class Weights:
    def __init__(self, e):
        self.e = e
        self.ranges = {"attend": (0, GATE_AT, 0), "units": (GATE_AT, PACK_COLS - GATE_AT, 1)}

    def copy(self, layer, name):
        start, width, slot = self.ranges[name]
        columns = pl.ds(start, width)
        return pltpu.make_async_copy(
            self.e.full.at[layer, :, :, :, :, columns],
            self.e.weights.at[:, :, :, :, columns],
            self.e.load_sem.at[slot],
        )

    def load(self, layer, name):
        self.copy(layer, name).start()

    def wait(self, layer, name):
        self.copy(layer, name).wait()

    def keep_copy(self):
        return pltpu.make_async_copy(self.e.weights, self.e.full.at[0], self.e.load_sem.at[3])

    def keep(self):
        self.keep_copy().start()

    def keep_wait(self):
        self.keep_copy().wait()

    def units(self, step, start):
        side, at = lax.div(step, 2), start + 256 * lax.rem(step, 2)
        columns = pl.ds(pl.multiple_of(at, 128), 256)
        return self.e.weights[side, :, :, :, columns].reshape(D, 256)

    def get(self, side, start, stop):
        return self.e.weights[side, :, :, :, start:stop].reshape(D, stop - start)


def nothing():
    pass


def forward_pass(e, layer, rows_ref, rows_out, pump):
    y, c, z, x = whereami()
    weights = Weights(e)
    swaps = [Swap(e, 4 * layer + slot) for slot in range(4)]
    ask = HeadTraffic(e.ask_out, e.ask_in, e.ask_send, e.traffic_recv.at[4 * layer])
    answer = HeadTraffic(e.reply_out, e.reply_in, e.reply_send, e.traffic_recv.at[4 * layer + 1])
    theirs = pl.ds(pl.multiple_of((1 - c) * TOKENS_HERE, TOKENS_HERE), TOKENS_HERE)
    swaps[0].start(e.normed.at[layer, c], e.normed.at[layer, c])
    pump("start")
    if layer == 1:
        weights.wait(layer, "attend")
    swaps[0].wait()
    chip_normed = e.normed[layer].reshape(CHIP_TOKENS, D)
    cosine = e.tables[:, :, 0:128].reshape(CHIP_TOKENS, 128)
    sine = e.tables[:, :, 128:256].reshape(CHIP_TOKENS, 128)
    for side in range(2):
        mixed = dot_nn(chip_normed, weights.get(side, 0, IN_COLS))
        for inner in range(3):
            head = 3 * side + inner
            pair = mixed[:, 128 * inner : 128 * inner + 128]
            pair = (pair * cosine + swap_halves(pair) * sine).astype(bf16)
            value = mixed[:, 384 + 64 * inner : 448 + 64 * inner]
            for group in range(2):
                at = TOKENS_HERE * group
                e.ask_out[head, group, 0:128] = pair[at : at + 128]
                e.ask_out[head, group, 128:192] = jnp.concatenate(
                    [value[at : at + 64], value[at + 64 : at + 128]], axis=1
                ).astype(bf16)
                ask.send_to_owner(head, group)
    pump("asked")
    queries, keys_values = e.queries.at[layer], e.keys_values.at[layer]
    kept_output = e.kept_output.at[layer]

    @pl.when(is_owner_here())
    def _():
        ask.arrived()

        def place(block, carry):
            at = pl.multiple_of(block * TOKENS_HERE, TOKENS_HERE)
            pair = e.ask_in[block, 0:128].astype(f32)
            zeros = jnp.zeros((TOKENS_HERE, HEAD_DIM), f32)
            queries[pl.ds(at, 128), :] = jnp.concatenate(
                [pair[:, 0:64] * (1.0 / math.sqrt(HEAD_DIM)), zeros], axis=1
            ).astype(bf16)
            both = e.ask_in[block, 128:192].astype(f32)
            value = jnp.concatenate([both[:, 0:64], both[:, 64:128]], axis=0)
            keys_values[pl.ds(at, 128), :] = jnp.concatenate(
                [pair[:, 64:128], value], axis=1
            ).astype(bf16)
            return carry

        lax.fori_loop(0, 16, place, 0)

        def send_rows(block):
            for half in range(2):
                at = pl.multiple_of(block * Q_BLOCK + half * 128, 128)
                first = kept_output[pl.ds(at, 64), :]
                second = kept_output[pl.ds(at + 64, 64), :]
                e.reply_out[2 * block + half] = jnp.concatenate(
                    [first[:, HEAD_DIM:], second[:, HEAD_DIM:]], axis=1
                ).astype(bf16)
                answer.send_to_tokens(2 * block + half)

        attend_forward(
            queries, keys_values, e.lengths, e.score_box, kept_output, pump.blocks(), send_rows
        )

    @pl.when(jnp.logical_not(is_owner_here()))
    def _():
        for number, action in sorted(pump.blocks().items()):
            action()

    pump("attended")
    answer.arrived()
    pump("answered")
    partial = None
    for side in range(2):
        columns = [jnp.zeros((CHIP_TOKENS, 64), f32)]
        for inner in range(3):
            pieces = []
            for group in range(2):
                both = e.reply_in[3 * side + inner, group].astype(f32)
                pieces += [both[:, 0:64], both[:, 64:128]]
            columns.append(jnp.concatenate(pieces, axis=0))
        e.attended[layer, side] = jnp.concatenate(columns, axis=1).astype(bf16)
        term = dot_nt(e.attended[layer, side], weights.get(side, OUT_AT, GATE_AT))
        partial = term if partial is None else partial + term
    e.partial_out[...] = partial.astype(bf16)
    swaps[1].start(e.partial_out.at[theirs], e.partial_in.at[0])
    own_part = own_half(partial)
    swaps[1].wait()
    middle = rows_ref[...].astype(f32) + (own_part + e.partial_in[0].astype(f32))
    e.mid_rows[layer] = middle
    e.normed_mid[layer, c] = (middle * norm_scale(middle) * e.gains[layer, 1:2, :]).astype(bf16)
    swaps[2].start(e.normed_mid.at[layer, c], e.normed_mid.at[layer, c])
    pump("before units")
    if layer == 1:
        weights.wait(layer, "units")
    swaps[2].wait()
    e.partial[...] = jnp.zeros_like(e.partial)

    def some_units(step, carry):
        chip_mid = e.normed_mid[layer].reshape(CHIP_TOKENS, D)
        gate = dot_nn(chip_mid, weights.units(step, GATE_AT))
        up = dot_nn(chip_mid, weights.units(step, UP_AT))
        active = (gate * sigmoid(gate) * up).astype(bf16)
        e.partial[...] += dot_nt(active, weights.units(step, DOWN_AT))
        return carry

    lax.fori_loop(0, 4, some_units, 0)
    partial = e.partial[...]
    e.partial_out[...] = partial.astype(bf16)
    swaps[3].start(e.partial_out.at[theirs], e.partial_in.at[1])
    own_part = own_half(partial)
    pump("units")
    swaps[3].wait()
    branch = own_part + e.partial_in[1].astype(f32)
    if layer == 1:
        rows_out[0] = e.mid_rows[layer]
        rows_out[1] = branch
    else:
        rows_out[...] = e.mid_rows[layer] + branch
    ask.drain_to_owner()
    pl.when(is_owner_here())(answer.drain_to_tokens)
    pump("end")


def backward_pass(e, layer, grad_ref, rows_ref, grad_out, pump, next_layer):
    y, c, z, x = whereami()
    weights = Weights(e)
    swaps = [Swap(e, 8 + 4 * layer + slot) for slot in range(4)]
    ask = HeadTraffic(e.back_ask_out, e.back_ask_in, e.ask_send, e.traffic_recv.at[4 * layer + 2])
    answer = HeadTraffic(
        e.back_reply_out, e.back_reply_in, e.reply_send, e.traffic_recv.at[4 * layer + 3]
    )
    theirs = pl.ds(pl.multiple_of((1 - c) * TOKENS_HERE, TOKENS_HERE), TOKENS_HERE)

    def transpose_rows(which, value):
        e.left_t[which] = value.T.reshape(4, D // 4, CHIP_TOKENS)

    def weight_grad(side, start, width, which, right):
        columns = pl.ds(pl.multiple_of(start, 128), width)
        for block in range(4):
            e.grads[layer, side, block, :, :, columns] = (
                dot_nn(e.left_t[which, block], right).astype(bf16).reshape(4, PAIR_ROWS, width)
            )

    e.grad_swap[0, c] = grad_ref[...].astype(bf16)
    swaps[0].start(e.grad_swap.at[0, c], e.grad_swap.at[0, c])
    pump("start")
    if next_layer is None:
        weights.wait(layer, "units")
    swaps[0].wait()
    transpose_rows(0, e.grad_swap[0].reshape(CHIP_TOKENS, D))
    transpose_rows(1, e.normed_mid[layer].reshape(CHIP_TOKENS, D))
    e.partial[...] = jnp.zeros_like(e.partial)

    def some_units(step, carry):
        down = e.grad_swap[0].reshape(CHIP_TOKENS, D)
        chip_mid = e.normed_mid[layer].reshape(CHIP_TOKENS, D)
        gate = dot_nn(chip_mid, weights.units(step, GATE_AT))
        up = dot_nn(chip_mid, weights.units(step, UP_AT))
        active_grad = dot_nn(down, weights.units(step, DOWN_AT))
        sigma = sigmoid(gate)
        active = gate * sigma
        gate_grad = (active_grad * up * sigma * (1.0 + gate * (1.0 - sigma))).astype(bf16)
        up_grad = (active_grad * active).astype(bf16)
        side, at = lax.div(step, 2), 256 * lax.rem(step, 2)
        weight_grad(side, DOWN_AT + at, 256, 0, (active * up).astype(bf16))
        weight_grad(side, GATE_AT + at, 256, 1, gate_grad)
        weight_grad(side, UP_AT + at, 256, 1, up_grad)
        e.partial[...] += dot_nt(gate_grad, weights.units(step, GATE_AT)) + dot_nt(
            up_grad, weights.units(step, UP_AT)
        )
        return carry

    lax.fori_loop(0, 4, some_units, 0)
    partial = e.partial[...]
    e.partial_out[...] = partial.astype(bf16)
    swaps[1].start(e.partial_out.at[theirs], e.partial_in.at[0])
    own_part = own_half(partial)
    if next_layer is not None:
        weights.load(next_layer, "units")
    pump("units")
    swaps[1].wait()
    back, gain_grad = norm_back(
        e.mid_rows[layer], e.gains[layer, 1:2, :], own_part + e.partial_in[0].astype(f32)
    )
    e.mid_grad[...] = grad_ref[...].astype(f32) + back
    e.gain_total[2 * layer + 1 : 2 * layer + 2, :] = gain_grad
    e.grad_swap[1, c] = e.mid_grad[...].astype(bf16)
    swaps[2].start(e.grad_swap.at[1, c], e.grad_swap.at[1, c])
    if next_layer is None:
        weights.wait(layer, "attend")
    swaps[2].wait()
    branch = e.grad_swap[1].reshape(CHIP_TOKENS, D)
    for side in range(2):
        heads_grad = dot_nn(branch, weights.get(side, OUT_AT, GATE_AT))
        for inner in range(3):
            head = 3 * side + inner
            piece = heads_grad[:, 64 + 64 * inner : 128 + 64 * inner]
            for group in range(2):
                at = TOKENS_HERE * group
                e.back_ask_out[head, group] = jnp.concatenate(
                    [piece[at : at + 64], piece[at + 64 : at + 128]], axis=1
                ).astype(bf16)
                ask.send_to_owner(head, group)
    transpose_rows(0, branch)
    for side in range(2):
        weight_grad(side, OUT_AT, GATE_AT - OUT_AT, 0, e.attended[layer, side])
    pump("asked")

    @pl.when(is_owner_here())
    def _():
        ask.arrived()

        def place(block, carry):
            at = pl.multiple_of(block * TOKENS_HERE, TOKENS_HERE)
            both = e.back_ask_in[block].astype(f32)
            grad = jnp.concatenate([both[:, 0:64], both[:, 64:128]], axis=0)
            e.output_grad[pl.ds(at, 128), :] = jnp.concatenate(
                [jnp.zeros((TOKENS_HERE, HEAD_DIM), f32), grad], axis=1
            ).astype(bf16)
            return carry

        lax.fori_loop(0, 16, place, 0)
        attend_backward(
            e.queries.at[layer],
            e.keys_values.at[layer],
            e.output_grad,
            e.kept_output.at[layer],
            e.lengths,
            e.query_grad,
            e.key_value_grad,
            pump.blocks(),
        )

        def give(block, carry):
            at = pl.multiple_of(block * TOKENS_HERE, TOKENS_HERE)
            e.back_reply_out[block, 0:128] = jnp.concatenate(
                [
                    e.query_grad[pl.ds(at, 128), 0:64] * (1.0 / math.sqrt(HEAD_DIM)),
                    e.key_value_grad[pl.ds(at, 128), 0:64],
                ],
                axis=1,
            ).astype(bf16)
            e.back_reply_out[block, 128:192] = jnp.concatenate(
                [
                    e.key_value_grad[pl.ds(at, 64), 64:128],
                    e.key_value_grad[pl.ds(at + 64, 64), 64:128],
                ],
                axis=1,
            ).astype(bf16)
            answer.send_to_tokens(block)
            return carry

        lax.fori_loop(0, 16, give, 0)

    @pl.when(jnp.logical_not(is_owner_here()))
    def _():
        for number, action in sorted(pump.blocks().items()):
            action()

    pump("attended")
    answer.arrived()
    cosine = e.tables[:, :, 0:128].reshape(CHIP_TOKENS, 128)
    sine = e.tables[:, :, 128:256].reshape(CHIP_TOKENS, 128)
    transpose_rows(1, e.normed[layer].reshape(CHIP_TOKENS, D))
    partial = None
    for side in range(2):
        pieces = []
        for inner in range(3):
            head = 3 * side + inner
            pair = jnp.concatenate(
                [e.back_reply_in[head, 0, 0:128], e.back_reply_in[head, 1, 0:128]], axis=0
            ).astype(f32)
            pair = pair * cosine - swap_halves(pair) * sine
            e.mixed_grad[side, :, 128 * inner : 128 * inner + 128] = pair.astype(bf16)
            rows = []
            for group in range(2):
                both = e.back_reply_in[head, group, 128:192].astype(f32)
                rows += [both[:, 0:64], both[:, 64:128]]
            pieces.append(jnp.concatenate(rows, axis=0))
        pieces.append(jnp.zeros((CHIP_TOKENS, 64), f32))
        e.mixed_grad[side, :, 384:IN_COLS] = jnp.concatenate(pieces, axis=1).astype(bf16)
        weight_grad(side, 0, OUT_AT, 1, e.mixed_grad[side, :, 0:OUT_AT])
        last = dot_nn(e.left_t[1].reshape(D, CHIP_TOKENS), e.mixed_grad[side, :, OUT_AT:IN_COLS])
        here = e.grads[layer, side, :, :, :, OUT_AT:IN_COLS].reshape(D, IN_COLS - OUT_AT)
        e.grads[layer, side, :, :, :, OUT_AT:IN_COLS] = (
            (here.astype(f32) + last).astype(bf16).reshape(4, 4, PAIR_ROWS, IN_COLS - OUT_AT)
        )
    pump("mixed")
    for side in range(2):
        term = dot_nt(e.mixed_grad[side], weights.get(side, 0, IN_COLS))
        partial = term if partial is None else partial + term
    e.partial_out[...] = partial.astype(bf16)
    swaps[3].start(e.partial_out.at[theirs], e.partial_in.at[1])
    own_part = own_half(partial)
    if next_layer is not None:
        weights.load(next_layer, "attend")
    swaps[3].wait()
    back, gain_grad = norm_back(
        rows_ref[...].astype(f32), e.gains[layer, 0:1, :], own_part + e.partial_in[1].astype(f32)
    )
    e.gain_total[2 * layer : 2 * layer + 1, :] = gain_grad
    if layer == 0:
        grad_out[0] = e.mid_grad[...]
        grad_out[1] = back
    else:
        grad_out[...] = e.mid_grad[...] + back
    ask.drain_to_owner()
    pl.when(is_owner_here())(answer.drain_to_tokens)
    pump("end")


class Pump:
    def __init__(self, actions=None):
        self.actions = actions or {}

    def __call__(self, point):
        for action in self.actions.get(point, []):
            action()

    def blocks(self):
        def run(actions):
            def action():
                for one in actions:
                    one()

            return action

        return {key: run(value) for key, value in self.actions.items() if isinstance(key, int)}


COPIES = 2


def owner_place(matrix, copy):
    return (matrix // 4, 0, (matrix // 4 + matrix % 4 + 2 * copy) % 4, matrix % 4)


def square_columns(kind):
    if kind < 2:
        return [(128 * head + 64 * kind, 64) for head in range(3)]
    return [(384 + 192 * (kind - 2), 192)]


def ns_step(source, target, gram, polynomial, columns, pumps, tick):
    rows = D // 2

    def gram_rows(block, carry):
        run_pumps(pumps, tick + block)
        here = pl.ds(2 * block, 2)
        part = source[here, :, :, 0:columns].reshape(rows, columns)
        gram[here, :, :, 0:D] = (
            dot_nt(part, source[:, :, :, 0:columns].reshape(D, columns))
            .astype(bf16)
            .reshape(2, 4, PAIR_ROWS, D)
        )
        return carry

    lax.fori_loop(0, 2, gram_rows, 0)

    def polynomial_columns(block, carry):
        run_pumps(pumps, tick + 2 + block)
        here = pl.ds(pl.multiple_of(block * 256, 256), 256)
        part = gram[:, :, :, here].reshape(D, 256)
        polynomial[:, :, :, here] = (
            (
                quintic_two * part.astype(f32)
                + quintic_three * dot_nn(gram[:, :, :, 0:D].reshape(D, D), part)
            )
            .astype(bf16)
            .reshape(4, 4, PAIR_ROWS, 256)
        )
        return carry

    lax.fori_loop(0, 3, polynomial_columns, 0)

    def update_columns(block, carry):
        run_pumps(pumps, tick + 5 + block)
        here = pl.ds(pl.multiple_of(block * 256, 256), 256)
        part = source[:, :, :, here].reshape(D, 256)
        target[:, :, :, here] = (
            (
                quintic_one * part.astype(f32)
                + dot_nn(polynomial[:, :, :, 0:D].reshape(D, D), part)
            )
            .astype(bf16)
            .reshape(4, 4, PAIR_ROWS, 256)
        )
        return carry

    lax.fori_loop(0, columns // 256, update_columns, 0)


def orthogonal_owner(slots, front, back, gram, polynomial, wide, send_back, pumps):
    columns = FF if wide else D
    slot_rows = PAIR_ROWS if wide else 32

    def add_squares(index, carry):
        value = slots[index, 0:slot_rows, :].astype(f32)
        return carry + jnp.sum(value * value, axis=0, keepdims=True)

    squares = lax.fori_loop(0, DEVICES, add_squares, jnp.zeros((1, 256), f32))
    scale = 1.0 / (jnp.sqrt(jnp.sum(squares, axis=1, keepdims=True)) + ortho_eps)

    def assemble(pair, carry):
        outer, inner = lax.div(pair, 4), lax.rem(pair, 4)
        narrow = []
        for part in range(4):
            first = slots[pair * 8 + part, 0:slot_rows, :].astype(f32) * scale
            second = slots[pair * 8 + 4 + part, 0:slot_rows, :].astype(f32) * scale
            joined = jnp.concatenate([first[0:24], second[0:24]], axis=0)
            if wide:
                front[outer, inner, :, part * 512 : part * 512 + 256] = joined.astype(bf16)
                front[outer, inner, :, part * 512 + 256 : part * 512 + 512] = jnp.concatenate(
                    [first[24:48], second[24:48]], axis=0
                ).astype(bf16)
            else:
                narrow.append(joined[:, 0:192])
        if not wide:
            front[outer, inner, :, 0:D] = jnp.concatenate(narrow, axis=1).astype(bf16)
        return carry

    lax.fori_loop(0, 16, assemble, 0)
    ticks = 5 + columns // 256

    def two_steps(index, carry):
        ns_step(front, back, gram, polynomial, columns, pumps, 2 * ticks * index)
        ns_step(back, front, gram, polynomial, columns, pumps, 2 * ticks * index + ticks)
        return carry

    lax.fori_loop(0, NS_STEPS // 2, two_steps, 0)

    def take_apart(pair, carry):
        outer, inner = lax.div(pair, 4), lax.rem(pair, 4)
        if not wide:
            whole = front[outer, inner, :, 0:D].astype(f32)
        for part in range(4):
            if wide:
                left = front[outer, inner, :, part * 512 : part * 512 + 256].astype(f32)
                right = front[outer, inner, :, part * 512 + 256 : part * 512 + 512].astype(f32)
                slots[pair * 8 + part] = jnp.concatenate([left[0:24], right[0:24]], axis=0).astype(
                    bf16
                )
                slots[pair * 8 + 4 + part] = jnp.concatenate(
                    [left[24:48], right[24:48]], axis=0
                ).astype(bf16)
            else:
                left = jnp.concatenate(
                    [whole[:, 192 * part : 192 * part + 192], jnp.zeros((PAIR_ROWS, 64), f32)], axis=1
                )
                slots[pair * 8 + part, 0:32] = left[0:32].astype(bf16)
                slots[pair * 8 + 4 + part, 0:32] = jnp.concatenate(
                    [left[24:48], left[0:8]], axis=0
                ).astype(bf16)
        for part in range(8):
            send_back(pair * 8 + part)
        return carry

    lax.fori_loop(0, 16, take_apart, 0)


class Muon:
    def __init__(self, e):
        self.e = e
        self.places = [[owner_place(m, copy) for copy in range(COPIES)] for m in range(OWNERS)]

    def is_owner(self, m, copy):
        y, c, z, x = whereami()
        place = self.places[m][copy]
        return (y == place[0]) & (c == place[1]) & (z == place[2]) & (x == place[3])

    def tile(self, m):
        return self.e.square.at[m] if m < SQUARE_COUNT else self.e.wide.at[m - SQUARE_COUNT]

    def returned(self, m):
        return self.e.square_new.at[m] if m < SQUARE_COUNT else self.e.wide_new.at[m - SQUARE_COUNT]

    def slot(self, m):
        if m < SQUARE_COUNT:
            return self.e.slots.at[index_here(), pl.ds(0, 32)]
        return self.e.slots.at[index_here()]

    def outbound(self, m, copy):
        return remote(
            self.tile(m),
            self.slot(m),
            self.e.tile_send.at[copy, m],
            self.e.slot_recv.at[0],
            device_at(*self.places[m][copy]),
        )

    def update_moment(self, layer, start, stop):
        e = self.e
        rows = slice(ROW_SHARD * layer, ROW_SHARD * layer + ROW_SHARD)
        e.moment_new[rows, start:stop] = (
            moment_decay * e.moment[rows, start:stop] + e.total[rows, start:stop]
        )

    def send(self, m):
        e = self.e
        if m < SQUARE_COUNT:
            layer, kind = m // 4, m % 4
            rows = slice(ROW_SHARD * layer, ROW_SHARD * layer + ROW_SHARD)
            pieces = [e.moment_new[rows, at : at + width] for at, width in square_columns(kind)]
            tile = jnp.concatenate(pieces + [jnp.zeros((ROW_SHARD, 64), f32)], axis=1)
            e.square[m] = jnp.concatenate([tile, jnp.zeros((8, 256), f32)], axis=0).astype(bf16)
        else:
            layer, kind = (m - SQUARE_COUNT) // 3, (m - SQUARE_COUNT) % 3
            rows = slice(ROW_SHARD * layer, ROW_SHARD * layer + ROW_SHARD)
            at = GATE_AT + 512 * kind
            e.wide[m - SQUARE_COUNT] = jnp.concatenate(
                [e.moment_new[rows, at : at + 256], e.moment_new[rows, at + 256 : at + 512]], axis=0
            ).astype(bf16)

        for copy in range(COPIES):

            @pl.when(jnp.logical_not(self.is_owner(m, copy)))
            def _(copy=copy):
                self.outbound(m, copy).start()

            @pl.when(self.is_owner(m, copy))
            def _(copy=copy):
                keep = pltpu.make_async_copy(
                    self.tile(m), self.slot(m), self.e.tile_send.at[copy, m]
                )
                keep.start()
                keep.wait()

    def serve(self, is_wide, pumps):
        e = self.e
        y, c, z, x = whereami()
        slot_rows = PAIR_ROWS if is_wide else 32
        whole = e.slots.at[pl.ds(0, DEVICES - 1), pl.ds(0, slot_rows)]
        pltpu.make_async_copy(whole, whole, e.slot_recv.at[0]).wait()
        matrix = y * 4 + x
        mine = index_here()

        def send_back(index):
            if is_wide:
                source, target = e.slots.at[index], e.wide_new.at[matrix - SQUARE_COUNT]
            else:
                source, target = e.slots.at[index, pl.ds(0, 32)], e.square_new.at[matrix]

            ahead = lax.rem(lax.rem(lax.div(index, 4), 4) - z + 4, 4)

            @pl.when((index != mine) & (ahead < 2))
            def _():
                remote(
                    source, target, e.slot_recv.at[1], e.tile_recv.at[matrix], device_of_index(index)
                ).start()

            @pl.when(index == mine)
            def _():
                copy = pltpu.make_async_copy(source, target, e.tile_recv.at[matrix])
                copy.start()

        orthogonal_owner(
            e.slots,
            e.weights.at[0],
            e.weights.at[1],
            e.grads.at[1, 0],
            e.grads.at[1, 1],
            is_wide,
            send_back,
            pumps,
        )
        sent = e.slots.at[pl.ds(0, DEVICES // COPIES - 1), pl.ds(0, slot_rows)]
        pltpu.make_async_copy(sent, sent, e.slot_recv.at[1]).wait()

    def serve_all(self, last_steps):
        y, c, z, x = whereami()
        placed = (c == 0) & (lax.rem(lax.rem(z - x - y + 8, 4), 2) == 0)
        square_owner = placed & (y < 2)
        wide_owner = placed & ((y == 2) | ((y == 3) & (x < 2)))

        pl.when(wide_owner)(lambda: self.serve(True, dict(zip((0, 4), last_steps))))

        @pl.when(jnp.logical_not(wide_owner))
        def _():
            for step in last_steps:
                step()

        pl.when(square_owner)(lambda: self.serve(False, {}))

    def finish(self):
        e = self.e
        for m in range(OWNERS):
            tile = self.returned(m)
            pltpu.make_async_copy(tile, tile, e.tile_recv.at[m]).wait()
            if m < SQUARE_COUNT:
                layer, kind = m // 4, m % 4
                rate = project_rate if kind == 3 else matrix_rate
                factor = 0.2 * math.sqrt(D)
                value = e.square_new[m].astype(f32)[0:ROW_SHARD]
                places = square_columns(kind)
            else:
                layer, kind = (m - SQUARE_COUNT) // 3, (m - SQUARE_COUNT) % 3
                rate, factor = matrix_rate, 0.2 * math.sqrt(FF)
                value = e.wide_new[m - SQUARE_COUNT].astype(f32)
                value = jnp.concatenate([value[0:ROW_SHARD], value[ROW_SHARD:PAIR_ROWS]], axis=1)
                places = [(GATE_AT + 512 * kind, 512)]
            rows = slice(ROW_SHARD * layer, ROW_SHARD * layer + ROW_SHARD)
            offset = 0
            for at, width in places:
                weight = e.weights_own[rows, at : at + width]
                e.weights_new[rows, at : at + width] = weight - rate * (
                    factor * value[:, offset : offset + width] + matrix_decay * weight
                )
                offset += width

            for copy in range(COPIES):

                @pl.when(jnp.logical_not(self.is_owner(m, copy)))
                def _(m=m, copy=copy):
                    self.outbound(m, copy).wait_send()


def finish_sum(e, layer, start, stop, slot, sending):
    y, c, z, x = whereami()
    holder, odd, low = lax.div(x, 2), lax.rem(z, 2), 2 * lax.div(z, 2)
    rows = slice(ROW_SHARD * layer, ROW_SHARD * layer + ROW_SHARD)
    target = e.total.at[rows, start:stop]
    sources = [e.pair.at[rows, start:stop], e.pair_more.at[:, start:stop]]

    def copy(i):
        return remote(
            sources[i],
            target,
            e.pair_send.at[2 * slot + i],
            e.pair_recv.at[slot],
            device_at(y, odd, low + i, x),
        )

    def send():
        for i in range(2):
            here = (c == odd) & (odd == i)
            part = slice(ROW_SHARD * i, ROW_SHARD * i + ROW_SHARD)

            def half():
                whole = e.grads[layer, lax.rem(x, 2), y, row_place(z), :, start:stop]
                return whole.astype(f32)[part]

            @pl.when(here)
            def _():
                target[...] = half()

            @pl.when(jnp.logical_not(here))
            def _():
                sources[i][...] = half()
                copy(i).start()

    def sent():
        for i in range(2):
            pl.when(jnp.logical_not((c == odd) & (odd == i)))(lambda i=i: copy(i).wait_send())

    if sending:
        pl.when(c == holder)(send)
    else:
        pl.when(c == holder)(sent)
        pl.when(jnp.logical_not((c == holder) & (low + c == z)))(lambda: copy(0).wait_recv())


def gain_copies(e, hop):
    if hop == 0:
        devices = [sibling_here()]
    else:
        devices = [neighbour("xyz"[hop - 1], offset) for offset in (1, 2, 3)]
    base = 3 * hop
    return [
        remote(
            e.gain_total,
            e.gain_box.at[base + i],
            e.gain_send.at[base + i],
            e.gain_recv.at[base + i],
            device,
        )
        for i, device in enumerate(devices)
    ]


def gain_start(e, hop):
    for copy in gain_copies(e, hop):
        copy.start()


def gain_finish(e, hop):
    copies = gain_copies(e, hop)
    for copy in copies:
        copy.wait_send()
        copy.wait_recv()
    for i in range(len(copies)):
        e.gain_total[...] += e.gain_box[3 * hop + i]


BOX_SHAPES = {}
for _part in range(3):
    for _phase in range(3):
        _lead = box_shape(_part, _phase) + (PAIR_ROWS,)
        if _phase == 0:
            BOX_SHAPES[f"late_half_{_part}"] = (2,) + _lead + (256,)
            BOX_SHAPES[f"early_half_{_part}"] = (2,) + _lead + (256,)
            BOX_SHAPES[f"both_block_{_part}"] = (2,) + _lead + (512,)
            BOX_SHAPES[f"late_last_{_part}"] = (3,) + _lead + (256,)
            BOX_SHAPES[f"early_last_{_part}"] = (3,) + _lead + (256,)
        else:
            BOX_SHAPES[f"late_{_part}{_phase}"] = (3,) + _lead + (768,)
            BOX_SHAPES[f"early_{_part}{_phase}"] = (3,) + _lead + (768,)


def boxes_of(e, layer, kind, part):
    name = "late" if layer == 1 else "early"
    start, width = {"units": (0, 512), "attend": (512, 256)}[kind]
    found = []
    for phase in range(3):
        if phase == 0 and kind == "attend":
            boxes = getattr(e, f"{name}_last_{part}")
            found.append([boxes.at[i] for i in range(3)])
        elif phase == 0:
            blocks = getattr(e, f"both_block_{part}")
            halves = getattr(e, f"{name}_half_{part}")
            found.append([halves.at[0], halves.at[1], blocks.at[0], blocks.at[1]])
        else:
            cut = (slice(None),) * (len(box_shape(part, phase)) + 1) + (pl.ds(start, width),)
            boxes = getattr(e, f"{name}_{part}{phase}")
            found.append([boxes.at[(i,) + cut] for i in range(3)])
    return found


def step_kernel(*refs):
    e = types.SimpleNamespace(**dict(zip(REF_NAMES, refs)))
    e.query_grad = e.score_box.at[pl.ds(0, GROUP)]
    e.key_value_grad = e.score_box.at[pl.ds(GROUP, GROUP)]
    e.pair, e.total = e.moment_new, e.weights_new
    e.back_ask_out, e.back_reply_out, e.back_reply_in = e.reply_in, e.ask_in, e.ask_out
    y, c, z, x = whereami()
    holder = lax.div(x, 2)
    signal_everyone()
    e.own[...] = e.weights_own[...].astype(bf16)
    e.tables[c] = rope_table(e.lengths)
    e.normed[0, c] = normalized(e.rows_in[...].astype(f32), e.gains[0, 0:1, :])
    e.gain_total[...] = jnp.zeros_like(e.gain_total)
    wait_for_everyone()

    odd, low = lax.rem(z, 2), 2 * lax.div(z, 2)
    table_swap = remote(
        e.tables.at[c], e.tables.at[c], e.pair_send.at[6], e.pair_recv.at[5], sibling_here()
    )
    table_swap.start()

    def hand_over(i):
        return remote(
            e.own, e.twin.at[i], e.pair_send.at[7], e.pair_recv.at[3 + i], device_at(y, holder, low + c, x)
        )

    own_stays = (c == holder) & (low + c == z)
    for i in range(2):
        pl.when(jnp.logical_not(own_stays) & (odd == i))(lambda i=i: hand_over(i).start())

    @pl.when(c == holder)
    def _():
        for i in range(2):
            mine = (c == odd) & (odd == i)

            @pl.when(mine)
            def _(i=i):
                e.twin[i] = e.own[...]

            pl.when(jnp.logical_not(mine))(lambda i=i: hand_over(i).wait_recv())
        first, second = e.twin[0].astype(f32), e.twin[1].astype(f32)
        for layer in range(LAYERS):
            part = slice(layer * ROW_SHARD, layer * ROW_SHARD + ROW_SHARD)
            joined = jnp.concatenate([first[part], second[part]], axis=0).astype(bf16)
            if layer == 0:
                e.weights[lax.rem(x, 2), y, row_place(z)] = joined
            else:
                e.piece[...] = joined
                keep = pltpu.make_async_copy(
                    e.piece, e.full.at[1, lax.rem(x, 2), y, row_place(z)], e.load_sem.at[2]
                )
                keep.start()
                keep.wait()

    def gather_lanes(ref, at, width, base, direct):
        return [
            GatherLane(
                ref,
                part,
                (at + part * width, width),
                e.gather_send,
                e.gather_recv,
                base + 12 * part,
                direct,
            )
            for part in range(3)
        ]

    ga = gather_lanes(e.weights, 0, 256, 0, (0, 1, 2))
    gb = gather_lanes(e.weights, GATE_AT, 512, 36, (0, 1))
    gc = gather_lanes(e.full.at[1], 0, 256, 72, (0, 1))
    gd = gather_lanes(e.full.at[1], GATE_AT, 512, 108, (0, 1))
    do = lambda lanes, step, phase: lambda: each(lanes, step, phase)
    weights = Weights(e)
    each(ga, "first", 0)
    each(gb, "first", 0)
    for lanes in (ga, gb):
        each(lanes, "third", 0)
        each(lanes, "first", 1)
    for lanes in (ga, gb):
        each(lanes, "third", 1)
        each(lanes, "first", 2)
    each(gc, "first", 0)
    each(gd, "first", 0)
    table_swap.wait_send()
    remote(
        e.tables.at[c], e.tables.at[1 - c], e.pair_send.at[6], e.pair_recv.at[5], sibling_here()
    ).wait_recv()
    each(ga, "third", 2)

    def turn_to_layer_1():
        each(gc, "third", 2)
        for phase in range(3):
            each(ga, "drain", phase)
            each(gb, "drain", phase)
        weights.keep_wait()
        weights.load(1, "attend")

    def units_of_layer_1():
        each(gd, "third", 2)
        weights.load(1, "units")

    forward_pass(
        e,
        0,
        e.rows_in,
        e.rows_mid,
        Pump(
            {
                "asked": [do(gb, "second", 2)],
                3: [
                    do(gc, "third", 0),
                    do(gc, "first", 1),
                    do(gd, "third", 0),
                    do(gd, "first", 1),
                ],
                7: [do(gc, "third", 1), do(gc, "first", 2)],
                "answered": [do(gd, "third", 1), do(gd, "first", 2)],
                "before units": [do(gb, "third", 2), weights.keep, do(gc, "second", 2)],
                "end": [turn_to_layer_1],
            }
        ),
    )
    e.normed[1, c] = normalized(e.rows_mid[...], e.gains[1, 0:1, :])
    forward_pass(e, 1, e.rows_mid, e.rows_out, Pump({"asked": [do(gd, "second", 2)], "answered": [units_of_layer_1]}))
    def reduce_lanes(layer, kind, base):
        at, width = {"units": (GATE_AT, 512), "attend": (0, 256)}[kind]
        lanes = []
        for part in range(3):
            credits = [e.credit.at[part, side] for side in range(2)]
            lanes.append(
                ReduceLane(
                    e.grads.at[layer],
                    boxes_of(e, layer, kind, part),
                    part,
                    (at + part * width, width),
                    e.reduce_send,
                    e.reduce_recv,
                    base + 12 * part,
                    (1, 2) if kind == "units" else (0, 1, 2),
                    gives=credits if kind == "units" and layer == 1 else None,
                    takes=credits if kind == "units" and layer == 0 else None,
                )
            )
        return lanes

    lu = reduce_lanes(1, "units", 0)
    la = reduce_lanes(1, "attend", 36)
    ru = reduce_lanes(0, "units", 72)
    ra = reduce_lanes(0, "attend", 108)
    muon = Muon(e)
    backward_pass(
        e,
        1,
        e.grad_in,
        e.rows_mid,
        e.grad_mid,
        Pump(
            {
                "asked": [do(lu, "first", 0)],
                4: [do(lu, "second", 0)],
                "mixed": [do(la, "first", 0), do(lu, "third", 0), do(lu, "first", 1)],
            }
        ),
        0,
    )

    def late_done():
        finish_sum(e, 1, 0, PACK_COLS, 0, False)
        muon.update_moment(1, 0, PACK_COLS)
        for m in (4, 5, 6, 7, 11, 12, 13):
            muon.send(m)

    def units_done():
        finish_sum(e, 0, GATE_AT, PACK_COLS, 1, False)
        muon.update_moment(0, GATE_AT, PACK_COLS)
        for m in (8, 9, 10):
            muon.send(m)

    backward_pass(
        e,
        0,
        e.grad_mid,
        e.rows_in,
        e.grad_out,
        Pump(
            {
                "units": [
                    do(ru, "first", 0),
                    do(la, "third", 0),
                    do(la, "first", 1),
                    do(lu, "third", 1),
                    do(lu, "first", 2),
                ],
                "asked": [
                    do(la, "third", 1),
                    do(la, "first", 2),
                    do(lu, "third", 2),
                ],
                2: [do(ru, "second", 0)],
                4: [do(la, "third", 2), lambda: finish_sum(e, 1, 0, PACK_COLS, 0, True)],
                6: [do(ru, "third", 0), do(ru, "first", 1)],
                "attended": [
                    do(ru, "third", 1),
                    do(ru, "first", 2),
                    late_done,
                    do(ru, "third", 2),
                    lambda: finish_sum(e, 0, GATE_AT, PACK_COLS, 1, True),
                ],
                "mixed": [do(ra, "first", 0), units_done],
            }
        ),
        None,
    )
    gain_start(e, 0)

    def sum_step_one():
        gain_finish(e, 0)
        gain_start(e, 1)
        each(ra, "third", 0)
        each(ra, "first", 1)

    def sum_step_two():
        gain_finish(e, 1)
        gain_start(e, 2)
        each(ra, "third", 1)
        each(ra, "first", 2)

    def sum_step_three():
        each(ra, "third", 2)
        finish_sum(e, 0, 0, GATE_AT, 2, True)
        finish_sum(e, 0, 0, GATE_AT, 2, False)
        muon.update_moment(0, 0, GATE_AT)
        for m in range(4):
            muon.send(m)
        gain_finish(e, 2)
        gain_start(e, 3)

    sum_step_one()
    for lanes in (gc, gd, lu, la):
        for phase in range(3):
            each(lanes, "drain", phase)
    muon.serve_all([sum_step_two, sum_step_three])
    for lanes in (ru, ra):
        for phase in range(3):
            each(lanes, "drain", phase)
    gain_finish(e, 3)
    pl.when(jnp.logical_not(own_stays))(lambda: hand_over(0).wait_send())
    muon.finish()


REF_TABLE = [
    ("rows_in", "in", (TOKENS_HERE, D), bf16),
    ("grad_in", "in", (TOKENS_HERE, D), bf16),
    ("lengths", "in", (1, 3), jnp.int32),
    ("weights_own", "in", (LAYERS * ROW_SHARD, PACK_COLS), f32),
    ("moment", "in", (LAYERS * ROW_SHARD, PACK_COLS), f32),
    ("gains", "in", (LAYERS, 2, D), f32),
    ("rows_out", "out", (2, TOKENS_HERE, D), f32),
    ("grad_out", "out", (2, TOKENS_HERE, D), f32),
    ("gain_total", "out", (8, D), f32),
    ("moment_new", "out", (LAYERS * ROW_SHARD, PACK_COLS), f32),
    ("weights_new", "out", (LAYERS * ROW_SHARD, PACK_COLS), f32),
    ("full", "hbm", (LAYERS, 2, 4, 4, PAIR_ROWS, PACK_COLS), bf16),
    ("weights", "vmem", (2, 4, 4, PAIR_ROWS, PACK_COLS), bf16),
    ("grads", "vmem", (LAYERS, 2, 4, 4, PAIR_ROWS, PACK_COLS), bf16),
    ("own", "vmem", (LAYERS * ROW_SHARD, PACK_COLS), bf16),
    ("twin", "vmem", (2, LAYERS * ROW_SHARD, PACK_COLS), bf16),
    ("pair_more", "vmem", (ROW_SHARD, PACK_COLS), f32),

    ("piece", "vmem", (PAIR_ROWS, PACK_COLS), bf16),
    ("tables", "vmem", (2, TOKENS_HERE, 256), f32),
    ("rows_mid", "vmem", (TOKENS_HERE, D), f32),
    ("grad_mid", "vmem", (TOKENS_HERE, D), f32),
    ("mid_grad", "vmem", (TOKENS_HERE, D), f32),
    ("mid_rows", "vmem", (LAYERS, TOKENS_HERE, D), f32),
    ("normed", "vmem", (LAYERS, 2, TOKENS_HERE, D), bf16),
    ("normed_mid", "vmem", (LAYERS, 2, TOKENS_HERE, D), bf16),
    ("attended", "vmem", (LAYERS, 2, CHIP_TOKENS, 256), bf16),
    ("queries", "vmem", (LAYERS, GROUP, 128), bf16),
    ("keys_values", "vmem", (LAYERS, GROUP, 128), bf16),
    ("kept_output", "vmem", (LAYERS, GROUP, 2 * HEAD_DIM), f32),
    ("score_box", "vmem", (2 * GROUP, 128), f32),
    ("output_grad", "vmem", (GROUP, 128), bf16),
    ("partial", "vmem", (CHIP_TOKENS, D), f32),
    ("partial_out", "vmem", (CHIP_TOKENS, D), bf16),
    ("left_t", "vmem", (2, 4, D // 4, CHIP_TOKENS), bf16),
    ("partial_in", "vmem", (2, TOKENS_HERE, D), bf16),
    ("grad_swap", "vmem", (2, 2, TOKENS_HERE, D), bf16),
    ("mixed_grad", "vmem", (2, CHIP_TOKENS, IN_COLS), bf16),
    ("ask_out", "vmem", (HEADS_HERE, 2, ASK_ROWS, 128), bf16),
    ("ask_in", "vmem", (16, ASK_ROWS, 128), bf16),
    ("reply_out", "vmem", (16, REPLY_ROWS, 128), bf16),
    ("reply_in", "vmem", (HEADS_HERE, 2, REPLY_ROWS, 128), bf16),
    ("back_ask_in", "vmem", (16, REPLY_ROWS, 128), bf16),
    ("gain_box", "vmem", (12, 8, D), f32),
    ("square", "vmem", (SQUARE_COUNT, 32, 256), bf16),
    ("wide", "vmem", (WIDE_COUNT, PAIR_ROWS, 256), bf16),
    ("square_new", "vmem", (SQUARE_COUNT, 32, 256), bf16),
    ("wide_new", "vmem", (WIDE_COUNT, PAIR_ROWS, 256), bf16),
    ("slots", "vmem", (DEVICES, PAIR_ROWS, 256), bf16),
]
REF_TABLE += [(name, "vmem", shape, bf16) for name, shape in BOX_SHAPES.items()]
REF_TABLE += [
    ("gather_send", "dma", (144,), None),
    ("gather_recv", "dma", (144,), None),
    ("reduce_send", "dma", (144,), None),
    ("reduce_recv", "dma", (144,), None),
    ("load_sem", "dma", (4,), None),
    ("swap_send", "dma", (16,), None),
    ("swap_recv", "dma", (16,), None),
    ("ask_send", "dma", (HEADS_HERE, 2), None),
    ("reply_send", "dma", (16,), None),
    ("traffic_recv", "dma", (8,), None),
    ("pair_send", "dma", (8,), None),
    ("pair_recv", "dma", (6,), None),
    ("gain_send", "dma", (12,), None),
    ("gain_recv", "dma", (12,), None),
    ("tile_send", "dma", (COPIES, OWNERS), None),
    ("tile_recv", "dma", (OWNERS,), None),
    ("slot_recv", "dma", (2,), None),
    ("credit", "regular", (3, 2), None),
]
REF_NAMES = [row[0] for row in REF_TABLE]


def train_step(*inputs):
    scratch = []
    for name, where, shape, dtype in REF_TABLE:
        if where == "vmem":
            scratch.append(pltpu.VMEM(shape, dtype))
        elif where == "dma":
            scratch.append(pltpu.SemaphoreType.DMA(shape))
        elif where == "regular":
            scratch.append(pltpu.SemaphoreType.REGULAR(shape))
    outs = [row for row in REF_TABLE if row[1] in ("out", "hbm")]
    return pl.pallas_call(
        step_kernel,
        out_shape=[jax.ShapeDtypeStruct(shape, dtype) for _, _, shape, dtype in outs],
        in_specs=[pl.BlockSpec(memory_space=pltpu.VMEM)] * len(inputs),
        out_specs=[
            pl.BlockSpec(memory_space=pltpu.HBM if where == "hbm" else pltpu.VMEM)
            for _, where, _, _ in outs
        ],
        scratch_shapes=scratch,
        compiler_params=pltpu.CompilerParams(
            collective_id=0, has_side_effects=True, vmem_limit_bytes=63 * MIB + MIB // 2
        ),
        name="train_step",
    )(*inputs)


def pack_layers(attend_in, attend_out, expand, shrink):
    query_key = jnp.stack(
        [attend_in[:, k].reshape(LAYERS, ROW_SHARD, 3, HEAD_DIM) for k in range(2)], axis=3
    )
    return jnp.concatenate(
        [
            query_key.reshape(LAYERS, ROW_SHARD, 384),
            attend_in[:, 2],
            jnp.swapaxes(attend_out, 1, 2),
            expand[:, 0],
            expand[:, 1],
            jnp.swapaxes(shrink, 1, 2),
        ],
        axis=2,
    )


def four_squares(packed):
    query_key = packed[:, :, 0:384].reshape(LAYERS, ROW_SHARD, 3, 2, HEAD_DIM)
    return [
        query_key[:, :, :, 0].reshape(LAYERS, ROW_SHARD, 192),
        query_key[:, :, :, 1].reshape(LAYERS, ROW_SHARD, 192),
        packed[:, :, 384:576],
        packed[:, :, 576:768],
    ]


def unpack_layers(packed):
    query, key, value, out = four_squares(packed)
    return (
        jnp.stack([query, key, value], axis=1),
        jnp.swapaxes(out, 1, 2),
        jnp.stack([packed[:, :, 768:1280], packed[:, :, 1280:1792]], axis=1),
        jnp.swapaxes(packed[:, :, 1792:2304], 1, 2),
    )


def body(
    hidden_in,
    out_grad,
    seq_lengths,
    norm_gains,
    gain_first,
    gain_second,
    attend_in,
    attend_out,
    expand,
    shrink,
    attend_in_moment,
    attend_out_moment,
    expand_moment,
    shrink_moment,
):
    flat = (LAYERS * ROW_SHARD, PACK_COLS)
    rows, rows_grad, gain_total, moment_new, weights_new, _ = train_step(
        hidden_in,
        out_grad,
        seq_lengths,
        pack_layers(attend_in, attend_out, expand, shrink).reshape(flat),
        pack_layers(attend_in_moment, attend_out_moment, expand_moment, shrink_moment).reshape(flat),
        norm_gains,
    )
    split = (LAYERS, ROW_SHARD, PACK_COLS)
    gain_grad = gain_total[0:4].reshape(LAYERS, 2, D)
    gain_first_new = first_decay * gain_first + (1.0 - first_decay) * gain_grad
    gain_second_new = second_decay * gain_second + (1.0 - second_decay) * gain_grad * gain_grad
    gains_new = norm_gains - gain_rate * (gain_first_new / (1.0 - first_decay**STEP)) / (
        jnp.sqrt(gain_second_new / (1.0 - second_decay**STEP)) + adam_eps
    )
    return (
        rows[0] + rows[1],
        rows_grad[0] + rows_grad[1],
        gain_first_new,
        gain_second_new,
        gains_new,
        *unpack_layers(moment_new.reshape(split)),
        *unpack_layers(weights_new.reshape(split)),
    )


def solution(mesh):
    placed = (
        P(("fsdp", "ctx", "tp"), None),
        P(("fsdp", "ctx", "tp"), None),
        P("fsdp", None),
        P(),
        P(),
        P(),
        P(None, None, ("fsdp", "ctx"), "tp"),
        P(None, "tp", ("fsdp", "ctx")),
        P(None, None, ("fsdp", "ctx"), "tp"),
        P(None, "tp", ("fsdp", "ctx")),
        P(None, None, ("fsdp", "ctx"), "tp"),
        P(None, "tp", ("fsdp", "ctx")),
        P(None, None, ("fsdp", "ctx"), "tp"),
        P(None, "tp", ("fsdp", "ctx")),
    )
    return jax.shard_map(
        body,
        mesh=mesh,
        in_specs=placed,
        out_specs=(
            P(("fsdp", "ctx", "tp"), None),
            P(("fsdp", "ctx", "tp"), None),
            P(),
            P(),
            P(),
            P(None, None, ("fsdp", "ctx"), "tp"),
            P(None, "tp", ("fsdp", "ctx")),
            P(None, None, ("fsdp", "ctx"), "tp"),
            P(None, "tp", ("fsdp", "ctx")),
            P(None, None, ("fsdp", "ctx"), "tp"),
            P(None, "tp", ("fsdp", "ctx")),
            P(None, None, ("fsdp", "ctx"), "tp"),
            P(None, "tp", ("fsdp", "ctx")),
        ),
        check_vma=False,
    )
```

```python
import math
import types

import jax
import jax.numpy as jnp
from jax import lax
from jax.experimental import pallas as pl
from jax.experimental.pallas import tpu as pltpu
from jax.sharding import PartitionSpec as P

D = 768
HEAD_DIM = 64
FF = 2048
NS_STEPS = 4
STEP = 5


norm_eps = 1e-05
rope_base = 10000.0
mask_fill = -1e30
quintic_one = 3.4445
quintic_two = -4.775
quintic_three = 2.0315
moment_decay = 0.95
matrix_rate = 0.1
project_rate = 0.8
matrix_decay = 0.1
gain_rate = 0.8
first_decay = 0.9
second_decay = 0.95
adam_eps = 1e-08
ortho_eps = 1e-07


MESH_ID = pl.DeviceIdType.MESH
ROW_SHARD = 24
PAIR_ROWS = 2 * ROW_SHARD
PACK_COLS = 2304
LAYERS = 2
MIB = 1024 * 1024
DEVICES = 128


def whereami():
    fsdp_index = lax.axis_index("fsdp")
    return (lax.div(fsdp_index, 2), lax.rem(fsdp_index, 2), lax.axis_index("ctx"), lax.axis_index("tp"))


def device_at(y, c, z, x):
    return (y * 2 + c, z, x)


def device_of_index(index):
    return (lax.div(index, 16), lax.rem(lax.div(index, 4), 4), lax.rem(index, 4))


def index_here():
    y, c, z, x = whereami()
    return (y * 2 + c) * 16 + z * 4 + x


def sibling_here():
    y, c, z, x = whereami()
    return device_at(y, 1 - c, z, x)


def ring(index, offset):
    return lax.rem(index + offset, 4)


def remote(source, target, send_sem, recv_sem, device):
    return pltpu.make_async_remote_copy(
        src_ref=source,
        dst_ref=target,
        send_sem=send_sem,
        recv_sem=recv_sem,
        device_id=device,
        device_id_type=MESH_ID,
    )


def signal_everyone():
    barrier = pltpu.get_barrier_semaphore()
    mine = index_here()

    def signal_one(offset, carry):
        device = device_of_index(lax.rem(mine + offset, DEVICES))
        pl.semaphore_signal(barrier, inc=1, device_id=device, device_id_type=MESH_ID)
        return carry

    lax.fori_loop(1, DEVICES, signal_one, 0)


def wait_for_everyone():
    pl.semaphore_wait(pltpu.get_barrier_semaphore(), DEVICES - 1)


def neighbour(axis, offset):
    y, c, z, x = whereami()
    if axis == "y":
        return device_at(ring(y, offset), c, z, x)
    if axis == "z":
        return device_at(y, c, ring(z, offset), x)
    return device_at(y, c, z, ring(x, offset))


PART_ORDER = (("x", "y", "z"), ("y", "z", "x"), ("z", "x", "y"))


def row_place(z):
    return 2 * lax.rem(z, 2) + lax.div(z, 2)


def part_view(ref, columns, done, axis, place, half):
    y, c, z, x = whereami()
    whole = slice(None)

    def index(name, own):
        if name != axis and name in done:
            return whole
        value = place if name == axis else own
        return row_place(value) if name == "z" else value

    if axis == "x":
        pick_x = lax.rem(place, 2)
    else:
        pick_x = whole if "x" in done else lax.rem(x, 2)
    start, width = columns
    if half is not None:
        width = width // 2
        start = start + half * width
    return ref.at[pick_x, index("y", y), index("z", z), :, pl.ds(start, width)]


def ring_exists(axis, done, place):
    y, c, z, x = whereami()
    if axis == "x":
        return lax.div(place, 2) == c
    if "x" in done:
        return None
    return lax.div(x, 2) == c


def run_if(condition, action):
    if condition is None:
        action()
    else:
        pl.when(condition)(action)


class GatherLane:
    def __init__(self, ref, part, columns, send, recv, base, direct):
        self.ref, self.part, self.columns = ref, part, columns
        self.send, self.recv, self.base, self.direct = send, recv, base, direct

    def parts(self, phase):
        axis = PART_ORDER[self.part][phase]
        done = PART_ORDER[self.part][:phase]
        y, c, z, x = whereami()
        return axis, done, {"x": x, "y": y, "z": z}[axis], self.base + 4 * phase

    def copy(self, phase, slot, place, half, offset):
        axis, done, me, base = self.parts(phase)
        view = part_view(self.ref, self.columns, done, axis, place, half)
        return remote(
            view, view, self.send.at[base + slot], self.recv.at[base + slot], neighbour(axis, offset)
        )

    def first(self, phase):
        axis, done, me, base = self.parts(phase)

        def action():
            if phase in self.direct:
                for offset in (1, 2, 3):
                    self.copy(phase, offset - 1, me, None, offset).start()
            else:
                self.copy(phase, 0, me, None, 1).start()
                self.copy(phase, 1, me, None, 3).start()

        run_if(ring_exists(axis, done, me), action)

    def second(self, phase):
        axis, done, me, base = self.parts(phase)
        left, right = ring(me, 3), ring(me, 1)

        def from_left():
            self.copy(phase, 0, left, None, 1).wait_recv()
            self.copy(phase, 2, left, 0, 1).start()

        def from_right():
            self.copy(phase, 1, right, None, 1).wait_recv()
            self.copy(phase, 3, right, 1, 3).start()

        run_if(ring_exists(axis, done, left), from_left)
        run_if(ring_exists(axis, done, right), from_right)

    def third(self, phase):
        axis, done, me, base = self.parts(phase)
        far = ring(me, 2)

        def action():
            self.copy(phase, 2, far, 0, 1).wait_recv()
            self.copy(phase, 3, far, 1, 1).wait_recv()

        if phase in self.direct:
            for offset in (1, 2, 3):
                place = ring(me, 4 - offset)
                run_if(
                    ring_exists(axis, done, place),
                    lambda place=place, offset=offset: self.copy(
                        phase, offset - 1, place, None, 1
                    ).wait_recv(),
                )
        else:
            run_if(ring_exists(axis, done, far), action)

    def drain(self, phase):
        axis, done, me, base = self.parts(phase)
        left, right = ring(me, 3), ring(me, 1)

        def own():
            for slot in range(3 if phase in self.direct else 2):
                self.copy(phase, slot, me, None, 1).wait_send()

        run_if(ring_exists(axis, done, me), own)
        if phase not in self.direct:
            run_if(
                ring_exists(axis, done, left), lambda: self.copy(phase, 2, left, 0, 1).wait_send()
            )
            run_if(
                ring_exists(axis, done, right), lambda: self.copy(phase, 3, right, 1, 3).wait_send()
            )


class ReduceLane:
    def __init__(self, ref, boxes, part, columns, send, recv, base, direct, gives=None, takes=None):
        self.ref, self.boxes, self.part, self.columns = ref, boxes, part, columns
        self.send, self.recv, self.base, self.direct = send, recv, base, direct
        self.gives, self.takes = gives, takes

    def parts(self, phase):
        axis = PART_ORDER[self.part][2 - phase]
        done = PART_ORDER[self.part][: 2 - phase]
        y, c, z, x = whereami()
        return axis, done, {"x": x, "y": y, "z": z}[axis], self.base + 4 * phase

    def copy(self, phase, slot, place, half, offset):
        axis, done, me, base = self.parts(phase)
        view = part_view(self.ref, self.columns, done, axis, place, half)
        return remote(
            view,
            self.boxes[phase][slot],
            self.send.at[base + slot],
            self.recv.at[base + slot],
            neighbour(axis, offset),
        )

    def add(self, phase, place, half, boxes):
        axis, done, me, base = self.parts(phase)
        view = part_view(self.ref, self.columns, done, axis, place, half)
        lead = view.shape[:-2]

        def summed(where):
            terms = [view[where]] + [box[where] for box in boxes]
            while len(terms) > 1:
                terms = [
                    terms[i] + terms[i + 1] if i + 1 < len(terms) else terms[i]
                    for i in range(0, len(terms), 2)
                ]
            return terms[0]

        def add_one(index, carry):
            where = []
            for extent in reversed(lead):
                where.insert(0, lax.rem(index, extent))
                index = lax.div(index, extent)
            view[tuple(where)] = summed(tuple(where))
            return carry

        if len(lead) == 0:
            view[...] = summed(...)
        else:
            lax.fori_loop(0, math.prod(lead), add_one, 0)

    def first(self, phase):
        axis, done, me, base = self.parts(phase)
        far = ring(me, 2)

        def action():
            self.copy(phase, 0, far, 0, 1).start()
            self.copy(phase, 1, far, 1, 3).start()

        if phase in self.direct:
            for offset in (1, 2, 3):
                place = ring(me, offset)
                run_if(
                    ring_exists(axis, done, place),
                    lambda place=place, offset=offset: self.copy(
                        phase, offset - 1, place, None, offset
                    ).start(),
                )
        else:
            run_if(ring_exists(axis, done, far), action)

    def second(self, phase):
        axis, done, me, base = self.parts(phase)
        left, right = ring(me, 3), ring(me, 1)

        def to_right():
            self.copy(phase, 0, right, 0, 1).wait_recv()
            self.add(phase, right, 0, [self.boxes[phase][0]])
            if phase == 0 and self.takes is not None:
                pl.semaphore_wait(self.takes[0], 1)
            self.copy(phase, 2, right, None, 1).start()

        def to_left():
            self.copy(phase, 1, left, 1, 1).wait_recv()
            self.add(phase, left, 1, [self.boxes[phase][1]])
            if phase == 0 and self.takes is not None:
                pl.semaphore_wait(self.takes[1], 1)
            self.copy(phase, 3, left, None, 3).start()

        run_if(ring_exists(axis, done, right), to_right)
        run_if(ring_exists(axis, done, left), to_left)

    def third(self, phase):
        axis, done, me, base = self.parts(phase)

        def action():
            if phase in self.direct:
                slots = (0, 1, 2)
            else:
                slots = (2, 3)
            for slot in slots:
                self.copy(phase, slot, me, None, 1).wait_recv()
            self.add(phase, me, None, [self.boxes[phase][slot] for slot in slots])
            if phase == 0 and self.gives is not None:
                for sem, offset in zip(self.gives, (3, 1)):
                    pl.semaphore_signal(
                        sem, inc=1, device_id=neighbour(axis, offset), device_id_type=MESH_ID
                    )

        run_if(ring_exists(axis, done, me), action)

    def drain(self, phase):
        axis, done, me, base = self.parts(phase)
        far, left, right = ring(me, 2), ring(me, 3), ring(me, 1)

        def own():
            self.copy(phase, 0, far, 0, 1).wait_send()
            self.copy(phase, 1, far, 1, 3).wait_send()

        if phase in self.direct:
            for offset in (1, 2, 3):
                place = ring(me, offset)
                run_if(
                    ring_exists(axis, done, place),
                    lambda place=place, offset=offset: self.copy(
                        phase, offset - 1, place, None, offset
                    ).wait_send(),
                )
            return
        run_if(ring_exists(axis, done, far), own)
        run_if(ring_exists(axis, done, right), lambda: self.copy(phase, 2, right, None, 1).wait_send())
        run_if(ring_exists(axis, done, left), lambda: self.copy(phase, 3, left, None, 3).wait_send())


def box_shape(part, phase):
    order = PART_ORDER[part]
    axis, done = order[2 - phase], order[: 2 - phase]
    lead = []
    for name, extent in (("x", 2), ("y", 4), ("z", 4)):
        if name != axis and name in done:
            lead.append(extent)
    return tuple(lead)


def each(lanes, step, phase):
    for lane in lanes:
        getattr(lane, step)(phase)


HEADS_HERE = 6
TOKENS_HERE = 128
CHIP_TOKENS = 256
GROUP = 2048
Q_BLOCK = 256
K_BLOCK = 512
Q_BLOCKS = GROUP // Q_BLOCK
IN_COLS = 640
OUT_AT = 512
GATE_AT = 768
UP_AT = 1280
DOWN_AT = 1792
ASK_ROWS = 192
REPLY_ROWS = 64
SQUARE_COUNT = 8
WIDE_COUNT = 6
OWNERS = SQUARE_COUNT + WIDE_COUNT
bf16 = jnp.bfloat16
f32 = jnp.float32


def dot_nn(left, right):
    return jnp.dot(left, right, preferred_element_type=f32)


def dot_nt(left, right):
    return lax.dot_general(left, right, (((1,), (1,)), ((), ())), preferred_element_type=f32)


def dot_tn(left, right):
    return lax.dot_general(left, right, (((0,), (0,)), ((), ())), preferred_element_type=f32)


def sigmoid(value):
    return 1.0 / (1.0 + jnp.exp(-value))


def norm_scale(rows):
    return lax.rsqrt(jnp.mean(rows * rows, axis=-1, keepdims=True) + norm_eps)


def normalized(rows, gain):
    return (rows * norm_scale(rows) * gain).astype(bf16)


def rope_table(lengths):
    y, c, z, x = whereami()
    shape = (TOKENS_HERE, 128)
    place = (z * 4 + x) * TOKENS_HERE + lax.broadcasted_iota(jnp.int32, shape, 0)
    lane = lax.broadcasted_iota(jnp.int32, shape, 1)
    position = place - document_start(lengths, place)
    frequency = jnp.exp(lax.rem(lane, 32).astype(f32) * (-2.0 / HEAD_DIM * math.log(rope_base)))
    angle = position.astype(f32) * frequency
    sine = jnp.sin(angle)
    sine = jnp.where(lax.rem(lane, 64) < 32, -sine, sine)
    return jnp.concatenate([jnp.cos(angle), sine], axis=1)


def document_start(lengths, place):
    first = lengths[0:1, 0:1]
    second = first + lengths[0:1, 1:2]
    return jnp.where(place >= second, second, jnp.where(place >= first, first, 0))


def norm_back(rows, gain, grad):
    scale = norm_scale(rows)
    unit = rows * scale
    inner = grad * gain
    back = scale * (inner - unit * jnp.mean(inner * unit, axis=-1, keepdims=True))
    return back, jnp.sum(grad * unit, axis=0, keepdims=True)


def swap_halves(values):
    lower = lax.rem(lax.broadcasted_iota(jnp.int32, values.shape, 1), 64) < 32
    return jnp.where(lower, pltpu.roll(values, 96, 1), pltpu.roll(values, 32, 1))


def is_owner_here():
    y, c, z, x = whereami()
    return z < 3


def head_here():
    y, c, z, x = whereami()
    return 4 * z + x


def own_half(both):
    y, c, z, x = whereami()
    return jnp.where(c == 0, both[0:TOKENS_HERE], both[TOKENS_HERE:CHIP_TOKENS])


class Swap:
    def __init__(self, e, slot):
        self.send, self.recv = e.swap_send.at[slot], e.swap_recv.at[slot]

    def start(self, source, target):
        self.copy = remote(source, target, self.send, self.recv, sibling_here())
        self.copy.start()

    def wait(self):
        self.copy.wait_send()
        self.copy.wait_recv()


class HeadTraffic:
    def __init__(self, outbox, inbox, sems, recv_sem):
        self.outbox, self.inbox, self.sems, self.recv_sem = outbox, inbox, sems, recv_sem

    def owner_place(self, head):
        y, c, z, x = whereami()
        number = HEADS_HERE * c + head
        return lax.div(number, 4), lax.rem(number, 4)

    def owner_is_here(self, head, group):
        y, c, z, x = whereami()
        owner_z, owner_x = self.owner_place(head)
        return (owner_z == z) & (owner_x == x) & (c == group)

    def to_owner(self, head, group):
        y, c, z, x = whereami()
        owner_z, owner_x = self.owner_place(head)
        return remote(
            self.outbox.at[head, group],
            self.inbox.at[z * 4 + x],
            self.sems.at[head, group],
            self.recv_sem,
            device_at(y, group, owner_z, owner_x),
        )

    def send_to_owner(self, head, group):
        y, c, z, x = whereami()
        here = self.owner_is_here(head, group)

        @pl.when(here)
        def _():
            pltpu.make_async_copy(
                self.outbox.at[head, group], self.inbox.at[z * 4 + x], self.recv_sem
            ).start()

        @pl.when(jnp.logical_not(here))
        def _():
            self.to_owner(head, group).start()

    def drain_to_owner(self):
        for head in range(HEADS_HERE):
            for group in range(2):

                @pl.when(jnp.logical_not(self.owner_is_here(head, group)))
                def _(head=head, group=group):
                    self.to_owner(head, group).wait_send()

    def tokens_are_here(self, block):
        y, c, z, x = whereami()
        core = lax.div(head_here(), HEADS_HERE)
        return (lax.div(block, 4) == z) & (lax.rem(block, 4) == x) & (core == c)

    def to_tokens(self, block):
        y, c, z, x = whereami()
        core = lax.div(head_here(), HEADS_HERE)
        slot = head_here() - HEADS_HERE * core
        return remote(
            self.outbox.at[block],
            self.inbox.at[slot, c],
            self.sems.at[block],
            self.recv_sem,
            device_at(y, core, lax.div(block, 4), lax.rem(block, 4)),
        )

    def send_to_tokens(self, block):
        y, c, z, x = whereami()
        here = self.tokens_are_here(block)

        @pl.when(here)
        def _():
            slot = head_here() - HEADS_HERE * lax.div(head_here(), HEADS_HERE)
            pltpu.make_async_copy(
                self.outbox.at[block], self.inbox.at[slot, c], self.recv_sem
            ).start()

        @pl.when(jnp.logical_not(here))
        def _():
            self.to_tokens(block).start()

    def drain_to_tokens(self):
        def drain(block, carry):
            @pl.when(jnp.logical_not(self.tokens_are_here(block)))
            def _():
                self.to_tokens(block).wait_send()

            return carry

        lax.fori_loop(0, 16, drain, 0)

    def arrived(self):
        pltpu.make_async_copy(self.inbox, self.inbox, self.recv_sem).wait()


def block_mask(ends, query_at, key_at):
    query_row = query_at + lax.broadcasted_iota(jnp.int32, (Q_BLOCK, 1), 0)
    start = document_start(ends, query_row)
    shape = (Q_BLOCK, K_BLOCK)
    query = query_at + lax.broadcasted_iota(jnp.int32, shape, 0)
    key = key_at + lax.broadcasted_iota(jnp.int32, shape, 1)
    return (key <= query) & (key >= start)


def run_pumps(pumps, block):
    for number, action in sorted(pumps.items()):
        pl.when(block == number)(action)


def score_rows(step, lane):
    at = (step * (K_BLOCK // 128) + lane) * Q_BLOCK
    return pl.ds(pl.multiple_of(at, Q_BLOCK), Q_BLOCK)


def attend_forward(queries, keys_values, ends, score_box, kept_output, pumps, block_done):
    def one_block(block, carry):
        run_pumps(pumps, block)
        query_at = pl.multiple_of(block * Q_BLOCK, Q_BLOCK)
        rows = pl.ds(query_at, Q_BLOCK)
        query = queries[rows, :]
        key_blocks = lax.div(block, 2) + 1

        def scores(step, top):
            key_at = pl.multiple_of(step * K_BLOCK, K_BLOCK)
            raw = dot_nt(query, keys_values[pl.ds(key_at, K_BLOCK), :])
            masked = jnp.where(block_mask(ends, query_at, key_at), raw, mask_fill)
            for lane in range(K_BLOCK // 128):
                tile = masked[:, 128 * lane : 128 * lane + 128]
                score_box[score_rows(step, lane), :] = tile
                top = jnp.maximum(top, tile)
            return top

        top = lax.fori_loop(0, key_blocks, scores, jnp.full((Q_BLOCK, 128), mask_fill, f32))
        top = jnp.max(top, axis=1, keepdims=True)

        def collect(step, state):
            total, gathered = state
            key_at = pl.multiple_of(step * K_BLOCK, K_BLOCK)
            tiles = []
            for lane in range(K_BLOCK // 128):
                tile = jnp.exp(score_box[score_rows(step, lane), :] - top)
                total = total + tile
                tiles.append(tile.astype(bf16))
            return total, gathered + dot_nn(
                jnp.concatenate(tiles, axis=1), keys_values[pl.ds(key_at, K_BLOCK), :]
            )

        total, gathered = lax.fori_loop(
            0,
            key_blocks,
            collect,
            (jnp.zeros((Q_BLOCK, 128), f32), jnp.zeros((Q_BLOCK, 128), f32)),
        )
        total = jnp.sum(total, axis=1, keepdims=True)
        lane = lax.broadcasted_iota(jnp.int32, (Q_BLOCK, 128), 1)
        kept_output[rows, :] = jnp.where(
            lane < HEAD_DIM, top + jnp.log(total), gathered / total
        )
        block_done(block)
        return carry

    lax.fori_loop(0, Q_BLOCKS, one_block, 0)


def attend_backward(
    queries, keys_values, output_grad, kept_output, ends, query_grad, key_value_grad, pumps
):
    key_value_grad[...] = jnp.zeros_like(key_value_grad)

    def one_block(block, carry):
        run_pumps(pumps, block)
        query_at = pl.multiple_of(block * Q_BLOCK, Q_BLOCK)
        rows = pl.ds(query_at, Q_BLOCK)
        query = queries[rows, :]
        grad = output_grad[rows, :]
        kept = kept_output[rows, :]
        logs = kept[:, 0:1]
        inner = jnp.sum(grad.astype(f32) * kept, axis=1, keepdims=True)

        def one_key(step, total):
            key_at = pl.multiple_of(step * K_BLOCK, K_BLOCK)
            keys_here = pl.ds(key_at, K_BLOCK)
            both = keys_values[keys_here, :]
            masked = jnp.where(
                block_mask(ends, query_at, key_at), dot_nt(query, both), mask_fill
            )
            probability = jnp.exp(masked - logs)
            probability_grad = dot_nt(grad, both)
            score_grad = (probability * (probability_grad - inner)).astype(bf16)
            key_value_grad[keys_here, :] += dot_tn(score_grad, query) + dot_tn(
                probability.astype(bf16), grad
            )
            return total + dot_nn(score_grad, both)

        query_grad[rows, :] = lax.fori_loop(
            0, lax.div(block, 2) + 1, one_key, jnp.zeros((Q_BLOCK, 128), f32)
        )
        return carry

    lax.fori_loop(0, Q_BLOCKS, one_block, 0)


class Weights:
    def __init__(self, e):
        self.e = e
        self.ranges = {"attend": (0, GATE_AT, 0), "units": (GATE_AT, PACK_COLS - GATE_AT, 1)}

    def copy(self, layer, name):
        start, width, slot = self.ranges[name]
        columns = pl.ds(start, width)
        return pltpu.make_async_copy(
            self.e.full.at[layer, :, :, :, :, columns],
            self.e.weights.at[:, :, :, :, columns],
            self.e.load_sem.at[slot],
        )

    def load(self, layer, name):
        self.copy(layer, name).start()

    def wait(self, layer, name):
        self.copy(layer, name).wait()

    def keep_copy(self):
        return pltpu.make_async_copy(self.e.weights, self.e.full.at[0], self.e.load_sem.at[3])

    def keep(self):
        self.keep_copy().start()

    def keep_wait(self):
        self.keep_copy().wait()

    def units(self, step, start):
        side, at = lax.div(step, 2), start + 256 * lax.rem(step, 2)
        columns = pl.ds(pl.multiple_of(at, 128), 256)
        return self.e.weights[side, :, :, :, columns].reshape(D, 256)

    def get(self, side, start, stop):
        return self.e.weights[side, :, :, :, start:stop].reshape(D, stop - start)


def nothing():
    pass


def forward_pass(e, layer, rows_ref, rows_out, pump):
    y, c, z, x = whereami()
    weights = Weights(e)
    swaps = [Swap(e, 4 * layer + slot) for slot in range(4)]
    ask = HeadTraffic(e.ask_out, e.ask_in, e.ask_send, e.traffic_recv.at[4 * layer])
    answer = HeadTraffic(e.reply_out, e.reply_in, e.reply_send, e.traffic_recv.at[4 * layer + 1])
    theirs = pl.ds(pl.multiple_of((1 - c) * TOKENS_HERE, TOKENS_HERE), TOKENS_HERE)
    swaps[0].start(e.normed.at[layer, c], e.normed.at[layer, c])
    pump("start")
    if layer == 1:
        weights.wait(layer, "attend")
    swaps[0].wait()
    chip_normed = e.normed[layer].reshape(CHIP_TOKENS, D)
    cosine = e.tables[:, :, 0:128].reshape(CHIP_TOKENS, 128)
    sine = e.tables[:, :, 128:256].reshape(CHIP_TOKENS, 128)
    for side in range(2):
        mixed = dot_nn(chip_normed, weights.get(side, 0, IN_COLS))
        for inner in range(3):
            head = 3 * side + inner
            pair = mixed[:, 128 * inner : 128 * inner + 128]
            pair = (pair * cosine + swap_halves(pair) * sine).astype(bf16)
            value = mixed[:, 384 + 64 * inner : 448 + 64 * inner]
            for group in range(2):
                at = TOKENS_HERE * group
                e.ask_out[head, group, 0:128] = pair[at : at + 128]
                e.ask_out[head, group, 128:192] = jnp.concatenate(
                    [value[at : at + 64], value[at + 64 : at + 128]], axis=1
                ).astype(bf16)
                ask.send_to_owner(head, group)
    pump("asked")
    queries, keys_values = e.queries.at[layer], e.keys_values.at[layer]
    kept_output = e.kept_output.at[layer]

    @pl.when(is_owner_here())
    def _():
        ask.arrived()

        def place(block, carry):
            at = pl.multiple_of(block * TOKENS_HERE, TOKENS_HERE)
            pair = e.ask_in[block, 0:128].astype(f32)
            zeros = jnp.zeros((TOKENS_HERE, HEAD_DIM), f32)
            queries[pl.ds(at, 128), :] = jnp.concatenate(
                [pair[:, 0:64] * (1.0 / math.sqrt(HEAD_DIM)), zeros], axis=1
            ).astype(bf16)
            both = e.ask_in[block, 128:192].astype(f32)
            value = jnp.concatenate([both[:, 0:64], both[:, 64:128]], axis=0)
            keys_values[pl.ds(at, 128), :] = jnp.concatenate(
                [pair[:, 64:128], value], axis=1
            ).astype(bf16)
            return carry

        lax.fori_loop(0, 16, place, 0)

        def send_rows(block):
            for half in range(2):
                at = pl.multiple_of(block * Q_BLOCK + half * 128, 128)
                first = kept_output[pl.ds(at, 64), :]
                second = kept_output[pl.ds(at + 64, 64), :]
                e.reply_out[2 * block + half] = jnp.concatenate(
                    [first[:, HEAD_DIM:], second[:, HEAD_DIM:]], axis=1
                ).astype(bf16)
                answer.send_to_tokens(2 * block + half)

        attend_forward(
            queries, keys_values, e.lengths, e.score_box, kept_output, pump.blocks(), send_rows
        )

    @pl.when(jnp.logical_not(is_owner_here()))
    def _():
        for number, action in sorted(pump.blocks().items()):
            action()

    pump("attended")
    answer.arrived()
    pump("answered")
    partial = None
    for side in range(2):
        columns = [jnp.zeros((CHIP_TOKENS, 64), f32)]
        for inner in range(3):
            pieces = []
            for group in range(2):
                both = e.reply_in[3 * side + inner, group].astype(f32)
                pieces += [both[:, 0:64], both[:, 64:128]]
            columns.append(jnp.concatenate(pieces, axis=0))
        e.attended[layer, side] = jnp.concatenate(columns, axis=1).astype(bf16)
        term = dot_nt(e.attended[layer, side], weights.get(side, OUT_AT, GATE_AT))
        partial = term if partial is None else partial + term
    e.partial_out[...] = partial.astype(bf16)
    swaps[1].start(e.partial_out.at[theirs], e.partial_in.at[0])
    own_part = own_half(partial)
    swaps[1].wait()
    middle = rows_ref[...].astype(f32) + (own_part + e.partial_in[0].astype(f32))
    e.mid_rows[layer] = middle
    e.normed_mid[layer, c] = (middle * norm_scale(middle) * e.gains[layer, 1:2, :]).astype(bf16)
    swaps[2].start(e.normed_mid.at[layer, c], e.normed_mid.at[layer, c])
    pump("before units")
    if layer == 1:
        weights.wait(layer, "units")
    swaps[2].wait()
    e.partial[...] = jnp.zeros_like(e.partial)

    def some_units(step, carry):
        chip_mid = e.normed_mid[layer].reshape(CHIP_TOKENS, D)
        gate = dot_nn(chip_mid, weights.units(step, GATE_AT))
        up = dot_nn(chip_mid, weights.units(step, UP_AT))
        active = (gate * sigmoid(gate) * up).astype(bf16)
        e.partial[...] += dot_nt(active, weights.units(step, DOWN_AT))
        return carry

    lax.fori_loop(0, 4, some_units, 0)
    partial = e.partial[...]
    e.partial_out[...] = partial.astype(bf16)
    swaps[3].start(e.partial_out.at[theirs], e.partial_in.at[1])
    own_part = own_half(partial)
    pump("units")
    swaps[3].wait()
    branch = own_part + e.partial_in[1].astype(f32)
    if layer == 1:
        rows_out[0] = e.mid_rows[layer]
        rows_out[1] = branch
    else:
        rows_out[...] = e.mid_rows[layer] + branch
    ask.drain_to_owner()
    pl.when(is_owner_here())(answer.drain_to_tokens)
    pump("end")


def backward_pass(e, layer, grad_ref, rows_ref, grad_out, pump, next_layer):
    y, c, z, x = whereami()
    weights = Weights(e)
    swaps = [Swap(e, 8 + 4 * layer + slot) for slot in range(4)]
    ask = HeadTraffic(e.back_ask_out, e.back_ask_in, e.ask_send, e.traffic_recv.at[4 * layer + 2])
    answer = HeadTraffic(
        e.back_reply_out, e.back_reply_in, e.reply_send, e.traffic_recv.at[4 * layer + 3]
    )
    theirs = pl.ds(pl.multiple_of((1 - c) * TOKENS_HERE, TOKENS_HERE), TOKENS_HERE)

    def transpose_rows(which, value):
        e.left_t[which] = value.T.reshape(4, D // 4, CHIP_TOKENS)

    def weight_grad(side, start, width, which, right):
        columns = pl.ds(pl.multiple_of(start, 128), width)
        for block in range(4):
            e.grads[layer, side, block, :, :, columns] = (
                dot_nn(e.left_t[which, block], right).astype(bf16).reshape(4, PAIR_ROWS, width)
            )

    e.grad_swap[0, c] = grad_ref[...].astype(bf16)
    swaps[0].start(e.grad_swap.at[0, c], e.grad_swap.at[0, c])
    pump("start")
    if next_layer is None:
        weights.wait(layer, "units")
    swaps[0].wait()
    transpose_rows(0, e.grad_swap[0].reshape(CHIP_TOKENS, D))
    transpose_rows(1, e.normed_mid[layer].reshape(CHIP_TOKENS, D))
    e.partial[...] = jnp.zeros_like(e.partial)

    def some_units(step, carry):
        down = e.grad_swap[0].reshape(CHIP_TOKENS, D)
        chip_mid = e.normed_mid[layer].reshape(CHIP_TOKENS, D)
        gate = dot_nn(chip_mid, weights.units(step, GATE_AT))
        up = dot_nn(chip_mid, weights.units(step, UP_AT))
        active_grad = dot_nn(down, weights.units(step, DOWN_AT))
        sigma = sigmoid(gate)
        active = gate * sigma
        gate_grad = (active_grad * up * sigma * (1.0 + gate * (1.0 - sigma))).astype(bf16)
        up_grad = (active_grad * active).astype(bf16)
        side, at = lax.div(step, 2), 256 * lax.rem(step, 2)
        weight_grad(side, DOWN_AT + at, 256, 0, (active * up).astype(bf16))
        weight_grad(side, GATE_AT + at, 256, 1, gate_grad)
        weight_grad(side, UP_AT + at, 256, 1, up_grad)
        e.partial[...] += dot_nt(gate_grad, weights.units(step, GATE_AT)) + dot_nt(
            up_grad, weights.units(step, UP_AT)
        )
        return carry

    lax.fori_loop(0, 4, some_units, 0)
    partial = e.partial[...]
    e.partial_out[...] = partial.astype(bf16)
    swaps[1].start(e.partial_out.at[theirs], e.partial_in.at[0])
    own_part = own_half(partial)
    if next_layer is not None:
        weights.load(next_layer, "units")
    pump("units")
    swaps[1].wait()
    back, gain_grad = norm_back(
        e.mid_rows[layer], e.gains[layer, 1:2, :], own_part + e.partial_in[0].astype(f32)
    )
    e.mid_grad[...] = grad_ref[...].astype(f32) + back
    e.gain_total[2 * layer + 1 : 2 * layer + 2, :] = gain_grad
    e.grad_swap[1, c] = e.mid_grad[...].astype(bf16)
    swaps[2].start(e.grad_swap.at[1, c], e.grad_swap.at[1, c])
    if next_layer is None:
        weights.wait(layer, "attend")
    swaps[2].wait()
    branch = e.grad_swap[1].reshape(CHIP_TOKENS, D)
    for side in range(2):
        heads_grad = dot_nn(branch, weights.get(side, OUT_AT, GATE_AT))
        for inner in range(3):
            head = 3 * side + inner
            piece = heads_grad[:, 64 + 64 * inner : 128 + 64 * inner]
            for group in range(2):
                at = TOKENS_HERE * group
                e.back_ask_out[head, group] = jnp.concatenate(
                    [piece[at : at + 64], piece[at + 64 : at + 128]], axis=1
                ).astype(bf16)
                ask.send_to_owner(head, group)
    transpose_rows(0, branch)
    for side in range(2):
        weight_grad(side, OUT_AT, GATE_AT - OUT_AT, 0, e.attended[layer, side])
    pump("asked")

    @pl.when(is_owner_here())
    def _():
        ask.arrived()

        def place(block, carry):
            at = pl.multiple_of(block * TOKENS_HERE, TOKENS_HERE)
            both = e.back_ask_in[block].astype(f32)
            grad = jnp.concatenate([both[:, 0:64], both[:, 64:128]], axis=0)
            e.output_grad[pl.ds(at, 128), :] = jnp.concatenate(
                [jnp.zeros((TOKENS_HERE, HEAD_DIM), f32), grad], axis=1
            ).astype(bf16)
            return carry

        lax.fori_loop(0, 16, place, 0)
        attend_backward(
            e.queries.at[layer],
            e.keys_values.at[layer],
            e.output_grad,
            e.kept_output.at[layer],
            e.lengths,
            e.query_grad,
            e.key_value_grad,
            pump.blocks(),
        )

        def give(block, carry):
            at = pl.multiple_of(block * TOKENS_HERE, TOKENS_HERE)
            e.back_reply_out[block, 0:128] = jnp.concatenate(
                [
                    e.query_grad[pl.ds(at, 128), 0:64] * (1.0 / math.sqrt(HEAD_DIM)),
                    e.key_value_grad[pl.ds(at, 128), 0:64],
                ],
                axis=1,
            ).astype(bf16)
            e.back_reply_out[block, 128:192] = jnp.concatenate(
                [
                    e.key_value_grad[pl.ds(at, 64), 64:128],
                    e.key_value_grad[pl.ds(at + 64, 64), 64:128],
                ],
                axis=1,
            ).astype(bf16)
            answer.send_to_tokens(block)
            return carry

        lax.fori_loop(0, 16, give, 0)

    @pl.when(jnp.logical_not(is_owner_here()))
    def _():
        for number, action in sorted(pump.blocks().items()):
            action()

    pump("attended")
    answer.arrived()
    cosine = e.tables[:, :, 0:128].reshape(CHIP_TOKENS, 128)
    sine = e.tables[:, :, 128:256].reshape(CHIP_TOKENS, 128)
    transpose_rows(1, e.normed[layer].reshape(CHIP_TOKENS, D))
    partial = None
    for side in range(2):
        pieces = []
        for inner in range(3):
            head = 3 * side + inner
            pair = jnp.concatenate(
                [e.back_reply_in[head, 0, 0:128], e.back_reply_in[head, 1, 0:128]], axis=0
            ).astype(f32)
            pair = pair * cosine - swap_halves(pair) * sine
            e.mixed_grad[side, :, 128 * inner : 128 * inner + 128] = pair.astype(bf16)
            rows = []
            for group in range(2):
                both = e.back_reply_in[head, group, 128:192].astype(f32)
                rows += [both[:, 0:64], both[:, 64:128]]
            pieces.append(jnp.concatenate(rows, axis=0))
        pieces.append(jnp.zeros((CHIP_TOKENS, 64), f32))
        e.mixed_grad[side, :, 384:IN_COLS] = jnp.concatenate(pieces, axis=1).astype(bf16)
        weight_grad(side, 0, OUT_AT, 1, e.mixed_grad[side, :, 0:OUT_AT])
        last = dot_nn(e.left_t[1].reshape(D, CHIP_TOKENS), e.mixed_grad[side, :, OUT_AT:IN_COLS])
        here = e.grads[layer, side, :, :, :, OUT_AT:IN_COLS].reshape(D, IN_COLS - OUT_AT)
        e.grads[layer, side, :, :, :, OUT_AT:IN_COLS] = (
            (here.astype(f32) + last).astype(bf16).reshape(4, 4, PAIR_ROWS, IN_COLS - OUT_AT)
        )
    pump("mixed")
    for side in range(2):
        term = dot_nt(e.mixed_grad[side], weights.get(side, 0, IN_COLS))
        partial = term if partial is None else partial + term
    e.partial_out[...] = partial.astype(bf16)
    swaps[3].start(e.partial_out.at[theirs], e.partial_in.at[1])
    own_part = own_half(partial)
    if next_layer is not None:
        weights.load(next_layer, "attend")
    pump("swapped")
    swaps[3].wait()
    back, gain_grad = norm_back(
        rows_ref[...].astype(f32), e.gains[layer, 0:1, :], own_part + e.partial_in[1].astype(f32)
    )
    e.gain_total[2 * layer : 2 * layer + 1, :] = gain_grad
    if layer == 0:
        grad_out[0] = e.mid_grad[...]
        grad_out[1] = back
    else:
        grad_out[...] = e.mid_grad[...] + back
    ask.drain_to_owner()
    pl.when(is_owner_here())(answer.drain_to_tokens)
    pump("end")


class Pump:
    def __init__(self, actions=None):
        self.actions = actions or {}

    def __call__(self, point):
        for action in self.actions.get(point, []):
            action()

    def blocks(self):
        def run(actions):
            def action():
                for one in actions:
                    one()

            return action

        return {key: run(value) for key, value in self.actions.items() if isinstance(key, int)}


COPIES = 2


def owner_place(matrix, copy):
    return (matrix // 4, 0, (matrix // 4 + matrix % 4 + 2 * copy) % 4, matrix % 4)


def square_columns(kind):
    if kind < 2:
        return [(128 * head + 64 * kind, 64) for head in range(3)]
    return [(384 + 192 * (kind - 2), 192)]


def ns_step(source, target, gram, polynomial, columns, pumps, tick):
    rows = D // 2

    def gram_rows(block, carry):
        run_pumps(pumps, tick + block)
        here = pl.ds(2 * block, 2)
        part = source[here, :, :, 0:columns].reshape(rows, columns)
        gram[here, :, :, 0:D] = (
            dot_nt(part, source[:, :, :, 0:columns].reshape(D, columns))
            .astype(bf16)
            .reshape(2, 4, PAIR_ROWS, D)
        )
        return carry

    lax.fori_loop(0, 2, gram_rows, 0)

    def polynomial_columns(block, carry):
        run_pumps(pumps, tick + 2 + block)
        here = pl.ds(pl.multiple_of(block * 256, 256), 256)
        part = gram[:, :, :, here].reshape(D, 256)
        polynomial[:, :, :, here] = (
            (
                quintic_two * part.astype(f32)
                + quintic_three * dot_nn(gram[:, :, :, 0:D].reshape(D, D), part)
            )
            .astype(bf16)
            .reshape(4, 4, PAIR_ROWS, 256)
        )
        return carry

    lax.fori_loop(0, 3, polynomial_columns, 0)

    def update_columns(block, carry):
        run_pumps(pumps, tick + 5 + block)
        here = pl.ds(pl.multiple_of(block * 256, 256), 256)
        part = source[:, :, :, here].reshape(D, 256)
        target[:, :, :, here] = (
            (
                quintic_one * part.astype(f32)
                + dot_nn(polynomial[:, :, :, 0:D].reshape(D, D), part)
            )
            .astype(bf16)
            .reshape(4, 4, PAIR_ROWS, 256)
        )
        return carry

    lax.fori_loop(0, columns // 256, update_columns, 0)


def orthogonal_owner(slots, front, back, gram, polynomial, wide, send_back, pumps):
    columns = FF if wide else D
    slot_rows = PAIR_ROWS if wide else 32

    def add_squares(index, carry):
        for slot in range(4):
            value = slots[4 * index + slot, 0:slot_rows, :].astype(f32)
            carry = carry + jnp.sum((value * value).reshape(slot_rows // 8, 8, 256), axis=0)
        return carry

    squares = lax.fori_loop(0, DEVICES // 4, add_squares, jnp.zeros((8, 256), f32))
    squares = jnp.sum(jnp.sum(squares, axis=0, keepdims=True), axis=1, keepdims=True)
    scale = 1.0 / (jnp.sqrt(squares) + ortho_eps)

    def assemble(pair, carry):
        outer, inner = lax.div(pair, 4), lax.rem(pair, 4)
        narrow = []
        for part in range(4):
            first = slots[pair * 8 + part, 0:slot_rows, :].astype(f32) * scale
            second = slots[pair * 8 + 4 + part, 0:slot_rows, :].astype(f32) * scale
            joined = jnp.concatenate([first[0:24], second[0:24]], axis=0)
            if wide:
                front[outer, inner, :, part * 512 : part * 512 + 256] = joined.astype(bf16)
                front[outer, inner, :, part * 512 + 256 : part * 512 + 512] = jnp.concatenate(
                    [first[24:48], second[24:48]], axis=0
                ).astype(bf16)
            else:
                narrow.append(joined[:, 0:192])
        if not wide:
            front[outer, inner, :, 0:D] = jnp.concatenate(narrow, axis=1).astype(bf16)
        return carry

    lax.fori_loop(0, 16, assemble, 0)
    ticks = 5 + columns // 256

    def two_steps(index, carry):
        ns_step(front, back, gram, polynomial, columns, pumps, 2 * ticks * index)
        ns_step(back, front, gram, polynomial, columns, pumps, 2 * ticks * index + ticks)
        return carry

    lax.fori_loop(0, NS_STEPS // 2, two_steps, 0)

    def take_apart(pair, carry):
        outer, inner = lax.div(pair, 4), lax.rem(pair, 4)
        if not wide:
            whole = front[outer, inner, :, 0:D].astype(f32)
        for part in range(4):
            if wide:
                left = front[outer, inner, :, part * 512 : part * 512 + 256].astype(f32)
                right = front[outer, inner, :, part * 512 + 256 : part * 512 + 512].astype(f32)
                slots[pair * 8 + part] = jnp.concatenate([left[0:24], right[0:24]], axis=0).astype(
                    bf16
                )
                slots[pair * 8 + 4 + part] = jnp.concatenate(
                    [left[24:48], right[24:48]], axis=0
                ).astype(bf16)
            else:
                left = jnp.concatenate(
                    [whole[:, 192 * part : 192 * part + 192], jnp.zeros((PAIR_ROWS, 64), f32)], axis=1
                )
                slots[pair * 8 + part, 0:32] = left[0:32].astype(bf16)
                slots[pair * 8 + 4 + part, 0:32] = jnp.concatenate(
                    [left[24:48], left[0:8]], axis=0
                ).astype(bf16)
        for part in range(8):
            send_back(pair * 8 + part)
        return carry

    lax.fori_loop(0, 16, take_apart, 0)


class Muon:
    def __init__(self, e):
        self.e = e
        self.places = [[owner_place(m, copy) for copy in range(COPIES)] for m in range(OWNERS)]

    def is_owner(self, m, copy):
        y, c, z, x = whereami()
        place = self.places[m][copy]
        return (y == place[0]) & (c == place[1]) & (z == place[2]) & (x == place[3])

    def tile(self, m):
        return self.e.square.at[m] if m < SQUARE_COUNT else self.e.wide.at[m - SQUARE_COUNT]

    def returned(self, m):
        return self.e.square_new.at[m] if m < SQUARE_COUNT else self.e.wide_new.at[m - SQUARE_COUNT]

    def slot(self, m):
        if m < SQUARE_COUNT:
            return self.e.slots.at[index_here(), pl.ds(0, 32)]
        return self.e.slots.at[index_here()]

    def outbound(self, m, copy):
        return remote(
            self.tile(m),
            self.slot(m),
            self.e.tile_send.at[copy, m],
            self.e.slot_recv.at[0],
            device_at(*self.places[m][copy]),
        )

    def update_moment(self, layer, start, stop):
        e = self.e
        rows = slice(ROW_SHARD * layer, ROW_SHARD * layer + ROW_SHARD)
        e.moment_new[rows, start:stop] = (
            moment_decay * e.moment[rows, start:stop] + e.total[rows, start:stop]
        )

    def send(self, m):
        e = self.e
        if m < SQUARE_COUNT:
            layer, kind = m // 4, m % 4
            rows = slice(ROW_SHARD * layer, ROW_SHARD * layer + ROW_SHARD)
            pieces = [e.moment_new[rows, at : at + width] for at, width in square_columns(kind)]
            tile = jnp.concatenate(pieces + [jnp.zeros((ROW_SHARD, 64), f32)], axis=1)
            e.square[m] = jnp.concatenate([tile, jnp.zeros((8, 256), f32)], axis=0).astype(bf16)
        else:
            layer, kind = (m - SQUARE_COUNT) // 3, (m - SQUARE_COUNT) % 3
            rows = slice(ROW_SHARD * layer, ROW_SHARD * layer + ROW_SHARD)
            at = GATE_AT + 512 * kind
            e.wide[m - SQUARE_COUNT] = jnp.concatenate(
                [e.moment_new[rows, at : at + 256], e.moment_new[rows, at + 256 : at + 512]], axis=0
            ).astype(bf16)

        for copy in range(COPIES):

            @pl.when(jnp.logical_not(self.is_owner(m, copy)))
            def _(copy=copy):
                self.outbound(m, copy).start()

            @pl.when(self.is_owner(m, copy))
            def _(copy=copy):
                keep = pltpu.make_async_copy(
                    self.tile(m), self.slot(m), self.e.tile_send.at[copy, m]
                )
                keep.start()
                keep.wait()

    def serve(self, is_wide, pumps):
        e = self.e
        y, c, z, x = whereami()
        slot_rows = PAIR_ROWS if is_wide else 32
        whole = e.slots.at[pl.ds(0, DEVICES - 1), pl.ds(0, slot_rows)]
        pltpu.make_async_copy(whole, whole, e.slot_recv.at[0]).wait()
        matrix = y * 4 + x
        mine = index_here()

        def send_back(index):
            if is_wide:
                source, target = e.slots.at[index], e.wide_new.at[matrix - SQUARE_COUNT]
            else:
                source, target = e.slots.at[index, pl.ds(0, 32)], e.square_new.at[matrix]

            ahead = lax.rem(lax.rem(lax.div(index, 4), 4) - z + 4, 4)

            @pl.when((index != mine) & (ahead < 2))
            def _():
                remote(
                    source, target, e.slot_recv.at[1], e.tile_recv.at[matrix], device_of_index(index)
                ).start()

            @pl.when(index == mine)
            def _():
                copy = pltpu.make_async_copy(source, target, e.tile_recv.at[matrix])
                copy.start()

        orthogonal_owner(
            e.slots,
            e.weights.at[0],
            e.weights.at[1],
            e.grads.at[1, 0],
            e.grads.at[1, 1],
            is_wide,
            send_back,
            pumps,
        )
        sent = e.slots.at[pl.ds(0, DEVICES // COPIES - 1), pl.ds(0, slot_rows)]
        pltpu.make_async_copy(sent, sent, e.slot_recv.at[1]).wait()

    def serve_all(self, last_steps):
        y, c, z, x = whereami()
        placed = (c == 0) & (lax.rem(lax.rem(z - x - y + 8, 4), 2) == 0)
        square_owner = placed & (y < 2)
        wide_owner = placed & ((y == 2) | ((y == 3) & (x < 2)))

        pl.when(wide_owner)(lambda: self.serve(True, dict(zip((0, 4), last_steps))))

        @pl.when(jnp.logical_not(wide_owner))
        def _():
            for step in last_steps:
                step()

        pl.when(square_owner)(lambda: self.serve(False, {}))

    def finish(self):
        e = self.e
        for m in range(OWNERS):
            tile = self.returned(m)
            pltpu.make_async_copy(tile, tile, e.tile_recv.at[m]).wait()
            if m < SQUARE_COUNT:
                layer, kind = m // 4, m % 4
                rate = project_rate if kind == 3 else matrix_rate
                factor = 0.2 * math.sqrt(D)
                value = e.square_new[m].astype(f32)[0:ROW_SHARD]
                places = square_columns(kind)
            else:
                layer, kind = (m - SQUARE_COUNT) // 3, (m - SQUARE_COUNT) % 3
                rate, factor = matrix_rate, 0.2 * math.sqrt(FF)
                value = e.wide_new[m - SQUARE_COUNT].astype(f32)
                value = jnp.concatenate([value[0:ROW_SHARD], value[ROW_SHARD:PAIR_ROWS]], axis=1)
                places = [(GATE_AT + 512 * kind, 512)]
            rows = slice(ROW_SHARD * layer, ROW_SHARD * layer + ROW_SHARD)
            offset = 0
            for at, width in places:
                weight = e.weights_own[rows, at : at + width]
                e.weights_new[rows, at : at + width] = weight - rate * (
                    factor * value[:, offset : offset + width] + matrix_decay * weight
                )
                offset += width

            for copy in range(COPIES):

                @pl.when(jnp.logical_not(self.is_owner(m, copy)))
                def _(m=m, copy=copy):
                    self.outbound(m, copy).wait_send()


def finish_sum(e, layer, start, stop, slot, sending):
    y, c, z, x = whereami()
    holder, odd, low = lax.div(x, 2), lax.rem(z, 2), 2 * lax.div(z, 2)
    rows = slice(ROW_SHARD * layer, ROW_SHARD * layer + ROW_SHARD)
    target = e.total.at[rows, start:stop]
    sources = [e.pair.at[rows, start:stop], e.pair_more.at[:, start:stop]]

    def copy(i):
        return remote(
            sources[i],
            target,
            e.pair_send.at[2 * slot + i],
            e.pair_recv.at[slot],
            device_at(y, odd, low + i, x),
        )

    def send():
        for i in range(2):
            here = (c == odd) & (odd == i)
            part = slice(ROW_SHARD * i, ROW_SHARD * i + ROW_SHARD)

            def half():
                whole = e.grads[layer, lax.rem(x, 2), y, row_place(z), :, start:stop]
                return whole.astype(f32)[part]

            @pl.when(here)
            def _():
                target[...] = half()

            @pl.when(jnp.logical_not(here))
            def _():
                sources[i][...] = half()
                copy(i).start()

    def sent():
        for i in range(2):
            pl.when(jnp.logical_not((c == odd) & (odd == i)))(lambda i=i: copy(i).wait_send())

    if sending:
        pl.when(c == holder)(send)
    else:
        pl.when(c == holder)(sent)
        pl.when(jnp.logical_not((c == holder) & (low + c == z)))(lambda: copy(0).wait_recv())


def gain_copies(e, hop):
    if hop == 0:
        devices = [sibling_here()]
    else:
        devices = [neighbour("xyz"[hop - 1], offset) for offset in (1, 2, 3)]
    base = 3 * hop
    return [
        remote(
            e.gain_total,
            e.gain_box.at[base + i],
            e.gain_send.at[base + i],
            e.gain_recv.at[base + i],
            device,
        )
        for i, device in enumerate(devices)
    ]


def gain_start(e, hop):
    for copy in gain_copies(e, hop):
        copy.start()


def gain_finish(e, hop):
    copies = gain_copies(e, hop)
    for copy in copies:
        copy.wait_send()
        copy.wait_recv()
    for i in range(len(copies)):
        e.gain_total[...] += e.gain_box[3 * hop + i]


BOX_SHAPES = {}
for _part in range(3):
    for _phase in range(3):
        _lead = box_shape(_part, _phase) + (PAIR_ROWS,)
        if _phase == 0:
            BOX_SHAPES[f"late_half_{_part}"] = (2,) + _lead + (256,)
            BOX_SHAPES[f"early_half_{_part}"] = (2,) + _lead + (256,)
            BOX_SHAPES[f"both_block_{_part}"] = (2,) + _lead + (512,)
            BOX_SHAPES[f"late_last_{_part}"] = (3,) + _lead + (256,)
            BOX_SHAPES[f"early_last_{_part}"] = (3,) + _lead + (256,)
        else:
            BOX_SHAPES[f"late_{_part}{_phase}"] = (3,) + _lead + (768,)
            BOX_SHAPES[f"early_{_part}{_phase}"] = (3,) + _lead + (768,)


def boxes_of(e, layer, kind, part):
    name = "late" if layer == 1 else "early"
    start, width = {"units": (0, 512), "attend": (512, 256)}[kind]
    found = []
    for phase in range(3):
        if phase == 0 and kind == "attend":
            boxes = getattr(e, f"{name}_last_{part}")
            found.append([boxes.at[i] for i in range(3)])
        elif phase == 0:
            blocks = getattr(e, f"both_block_{part}")
            halves = getattr(e, f"{name}_half_{part}")
            found.append([halves.at[0], halves.at[1], blocks.at[0], blocks.at[1]])
        else:
            cut = (slice(None),) * (len(box_shape(part, phase)) + 1) + (pl.ds(start, width),)
            boxes = getattr(e, f"{name}_{part}{phase}")
            found.append([boxes.at[(i,) + cut] for i in range(3)])
    return found


def step_kernel(*refs):
    e = types.SimpleNamespace(**dict(zip(REF_NAMES, refs)))
    e.query_grad = e.score_box.at[pl.ds(0, GROUP)]
    e.key_value_grad = e.score_box.at[pl.ds(GROUP, GROUP)]
    e.pair, e.total = e.moment_new, e.weights_new
    e.back_ask_out, e.back_reply_out, e.back_reply_in = e.reply_in, e.ask_in, e.ask_out
    y, c, z, x = whereami()
    holder = lax.div(x, 2)
    signal_everyone()
    e.own[...] = e.weights_own[...].astype(bf16)
    e.tables[c] = rope_table(e.lengths)
    e.normed[0, c] = normalized(e.rows_in[...].astype(f32), e.gains[0, 0:1, :])
    e.gain_total[...] = jnp.zeros_like(e.gain_total)
    wait_for_everyone()

    odd, low = lax.rem(z, 2), 2 * lax.div(z, 2)
    table_swap = remote(
        e.tables.at[c], e.tables.at[c], e.pair_send.at[6], e.pair_recv.at[5], sibling_here()
    )
    table_swap.start()

    def hand_over(i):
        return remote(
            e.own, e.twin.at[i], e.pair_send.at[7], e.pair_recv.at[3 + i], device_at(y, holder, low + c, x)
        )

    own_stays = (c == holder) & (low + c == z)
    for i in range(2):
        pl.when(jnp.logical_not(own_stays) & (odd == i))(lambda i=i: hand_over(i).start())

    @pl.when(c == holder)
    def _():
        for i in range(2):
            mine = (c == odd) & (odd == i)

            @pl.when(mine)
            def _(i=i):
                e.twin[i] = e.own[...]

            pl.when(jnp.logical_not(mine))(lambda i=i: hand_over(i).wait_recv())
        first, second = e.twin[0].astype(f32), e.twin[1].astype(f32)
        for layer in range(LAYERS):
            part = slice(layer * ROW_SHARD, layer * ROW_SHARD + ROW_SHARD)
            joined = jnp.concatenate([first[part], second[part]], axis=0).astype(bf16)
            if layer == 0:
                e.weights[lax.rem(x, 2), y, row_place(z)] = joined
            else:
                e.piece[...] = joined
                keep = pltpu.make_async_copy(
                    e.piece, e.full.at[1, lax.rem(x, 2), y, row_place(z)], e.load_sem.at[2]
                )
                keep.start()
                keep.wait()

    def gather_lanes(ref, at, width, base, direct):
        return [
            GatherLane(
                ref,
                part,
                (at + part * width, width),
                e.gather_send,
                e.gather_recv,
                base + 12 * part,
                direct,
            )
            for part in range(3)
        ]

    ga = gather_lanes(e.weights, 0, 256, 0, (0, 1, 2))
    gb = gather_lanes(e.weights, GATE_AT, 512, 36, (0, 1))
    gc = gather_lanes(e.full.at[1], 0, 256, 72, (0, 1))
    gd = gather_lanes(e.full.at[1], GATE_AT, 512, 108, (0, 1))
    do = lambda lanes, step, phase: lambda: each(lanes, step, phase)
    weights = Weights(e)
    each(ga, "first", 0)
    each(gb, "first", 0)
    for lanes in (ga, gb):
        each(lanes, "third", 0)
        each(lanes, "first", 1)
    for lanes in (ga, gb):
        each(lanes, "third", 1)
        each(lanes, "first", 2)
    each(gc, "first", 0)
    each(gd, "first", 0)
    table_swap.wait_send()
    remote(
        e.tables.at[c], e.tables.at[1 - c], e.pair_send.at[6], e.pair_recv.at[5], sibling_here()
    ).wait_recv()
    each(ga, "third", 2)

    def turn_to_layer_1():
        each(gc, "third", 2)
        each(gb, "drain", 2)
        weights.keep_wait()
        weights.load(1, "attend")

    def units_of_layer_1():
        each(gd, "third", 2)
        weights.load(1, "units")

    forward_pass(
        e,
        0,
        e.rows_in,
        e.rows_mid,
        Pump(
            {
                "asked": [do(gb, "second", 2)],
                3: [
                    do(gc, "third", 0),
                    do(gc, "first", 1),
                    do(gd, "third", 0),
                    do(gd, "first", 1),
                ],
                7: [do(gc, "third", 1), do(gc, "first", 2)],
                "attended": [do(lanes, "drain", phase) for phase in range(2) for lanes in (ga, gb)]
                + [do(ga, "drain", 2)],
                "answered": [do(gd, "third", 1), do(gd, "first", 2)],
                "before units": [do(gb, "third", 2), weights.keep, do(gc, "second", 2)],
                "end": [turn_to_layer_1],
            }
        ),
    )
    e.normed[1, c] = normalized(e.rows_mid[...], e.gains[1, 0:1, :])
    forward_pass(e, 1, e.rows_mid, e.rows_out, Pump({"asked": [do(gd, "second", 2)], "answered": [units_of_layer_1]}))
    def reduce_lanes(layer, kind, base):
        at, width = {"units": (GATE_AT, 512), "attend": (0, 256)}[kind]
        lanes = []
        for part in range(3):
            credits = [e.credit.at[part, side] for side in range(2)]
            lanes.append(
                ReduceLane(
                    e.grads.at[layer],
                    boxes_of(e, layer, kind, part),
                    part,
                    (at + part * width, width),
                    e.reduce_send,
                    e.reduce_recv,
                    base + 12 * part,
                    (1, 2) if kind == "units" else (0, 1, 2),
                    gives=credits if kind == "units" and layer == 1 else None,
                    takes=credits if kind == "units" and layer == 0 else None,
                )
            )
        return lanes

    lu = reduce_lanes(1, "units", 0)
    la = reduce_lanes(1, "attend", 36)
    ru = reduce_lanes(0, "units", 72)
    ra = reduce_lanes(0, "attend", 108)
    muon = Muon(e)
    backward_pass(
        e,
        1,
        e.grad_in,
        e.rows_mid,
        e.grad_mid,
        Pump(
            {
                "asked": [do(lu, "first", 0)],
                4: [do(lu, "second", 0)],
                "attended": [do(lanes, "drain", phase) for phase in range(3) for lanes in (gc, gd)],
                "mixed": [do(la, "first", 0), do(lu, "third", 0), do(lu, "first", 1)],
            }
        ),
        0,
    )

    def late_done():
        finish_sum(e, 1, 0, PACK_COLS, 0, False)
        muon.update_moment(1, 0, PACK_COLS)
        for m in (4, 5, 6, 7, 11, 12, 13):
            muon.send(m)

    def units_done():
        finish_sum(e, 0, GATE_AT, PACK_COLS, 1, False)
        muon.update_moment(0, GATE_AT, PACK_COLS)
        for m in (8, 9, 10):
            muon.send(m)

    backward_pass(
        e,
        0,
        e.grad_mid,
        e.rows_in,
        e.grad_out,
        Pump(
            {
                "units": [
                    do(ru, "first", 0),
                    do(la, "third", 0),
                    do(la, "first", 1),
                    do(lu, "third", 1),
                    do(lu, "first", 2),
                ],
                "asked": [
                    do(la, "third", 1),
                    do(la, "first", 2),
                    do(lu, "third", 2),
                    do(lu, "drain", 0),
                    do(lu, "drain", 1),
                    do(la, "drain", 0),
                ],
                2: [do(ru, "second", 0)],
                4: [do(la, "third", 2), lambda: finish_sum(e, 1, 0, PACK_COLS, 0, True)],
                6: [do(ru, "third", 0), do(ru, "first", 1)],
                "attended": [
                    do(ru, "third", 1),
                    do(ru, "first", 2),
                    late_done,
                    do(ru, "third", 2),
                    lambda: finish_sum(e, 0, GATE_AT, PACK_COLS, 1, True),
                ],
                "mixed": [do(ra, "first", 0)],
                "swapped": [units_done],
            }
        ),
        None,
    )
    gain_start(e, 0)

    def sum_step_one():
        gain_finish(e, 0)
        gain_start(e, 1)
        each(ra, "third", 0)
        each(ra, "first", 1)

    def sum_step_two():
        gain_finish(e, 1)
        gain_start(e, 2)
        each(ra, "third", 1)
        each(ra, "first", 2)

    def sum_step_three():
        each(ra, "third", 2)
        finish_sum(e, 0, 0, GATE_AT, 2, True)
        finish_sum(e, 0, 0, GATE_AT, 2, False)
        muon.update_moment(0, 0, GATE_AT)
        for m in range(4):
            muon.send(m)
        gain_finish(e, 2)
        gain_start(e, 3)

    sum_step_one()
    each(lu, "drain", 2)
    each(la, "drain", 1)
    each(la, "drain", 2)
    muon.serve_all([sum_step_two, sum_step_three])
    for lanes in (ru, ra):
        for phase in range(3):
            each(lanes, "drain", phase)
    gain_finish(e, 3)
    pl.when(jnp.logical_not(own_stays))(lambda: hand_over(0).wait_send())
    muon.finish()


REF_TABLE = [
    ("rows_in", "in", (TOKENS_HERE, D), bf16),
    ("grad_in", "in", (TOKENS_HERE, D), bf16),
    ("lengths", "in", (1, 3), jnp.int32),
    ("weights_own", "in", (LAYERS * ROW_SHARD, PACK_COLS), f32),
    ("moment", "in", (LAYERS * ROW_SHARD, PACK_COLS), f32),
    ("gains", "in", (LAYERS, 2, D), f32),
    ("rows_out", "out", (2, TOKENS_HERE, D), f32),
    ("grad_out", "out", (2, TOKENS_HERE, D), f32),
    ("gain_total", "out", (8, D), f32),
    ("moment_new", "out", (LAYERS * ROW_SHARD, PACK_COLS), f32),
    ("weights_new", "out", (LAYERS * ROW_SHARD, PACK_COLS), f32),
    ("full", "hbm", (LAYERS, 2, 4, 4, PAIR_ROWS, PACK_COLS), bf16),
    ("weights", "vmem", (2, 4, 4, PAIR_ROWS, PACK_COLS), bf16),
    ("grads", "vmem", (LAYERS, 2, 4, 4, PAIR_ROWS, PACK_COLS), bf16),
    ("own", "vmem", (LAYERS * ROW_SHARD, PACK_COLS), bf16),
    ("twin", "vmem", (2, LAYERS * ROW_SHARD, PACK_COLS), bf16),
    ("pair_more", "vmem", (ROW_SHARD, PACK_COLS), f32),

    ("piece", "vmem", (PAIR_ROWS, PACK_COLS), bf16),
    ("tables", "vmem", (2, TOKENS_HERE, 256), f32),
    ("rows_mid", "vmem", (TOKENS_HERE, D), f32),
    ("grad_mid", "vmem", (TOKENS_HERE, D), f32),
    ("mid_grad", "vmem", (TOKENS_HERE, D), f32),
    ("mid_rows", "vmem", (LAYERS, TOKENS_HERE, D), f32),
    ("normed", "vmem", (LAYERS, 2, TOKENS_HERE, D), bf16),
    ("normed_mid", "vmem", (LAYERS, 2, TOKENS_HERE, D), bf16),
    ("attended", "vmem", (LAYERS, 2, CHIP_TOKENS, 256), bf16),
    ("queries", "vmem", (LAYERS, GROUP, 128), bf16),
    ("keys_values", "vmem", (LAYERS, GROUP, 128), bf16),
    ("kept_output", "vmem", (LAYERS, GROUP, 2 * HEAD_DIM), f32),
    ("score_box", "vmem", (2 * GROUP, 128), f32),
    ("output_grad", "vmem", (GROUP, 128), bf16),
    ("partial", "vmem", (CHIP_TOKENS, D), f32),
    ("partial_out", "vmem", (CHIP_TOKENS, D), bf16),
    ("left_t", "vmem", (2, 4, D // 4, CHIP_TOKENS), bf16),
    ("partial_in", "vmem", (2, TOKENS_HERE, D), bf16),
    ("grad_swap", "vmem", (2, 2, TOKENS_HERE, D), bf16),
    ("mixed_grad", "vmem", (2, CHIP_TOKENS, IN_COLS), bf16),
    ("ask_out", "vmem", (HEADS_HERE, 2, ASK_ROWS, 128), bf16),
    ("ask_in", "vmem", (16, ASK_ROWS, 128), bf16),
    ("reply_out", "vmem", (16, REPLY_ROWS, 128), bf16),
    ("reply_in", "vmem", (HEADS_HERE, 2, REPLY_ROWS, 128), bf16),
    ("back_ask_in", "vmem", (16, REPLY_ROWS, 128), bf16),
    ("gain_box", "vmem", (12, 8, D), f32),
    ("square", "vmem", (SQUARE_COUNT, 32, 256), bf16),
    ("wide", "vmem", (WIDE_COUNT, PAIR_ROWS, 256), bf16),
    ("square_new", "vmem", (SQUARE_COUNT, 32, 256), bf16),
    ("wide_new", "vmem", (WIDE_COUNT, PAIR_ROWS, 256), bf16),
    ("slots", "vmem", (DEVICES, PAIR_ROWS, 256), bf16),
]
REF_TABLE += [(name, "vmem", shape, bf16) for name, shape in BOX_SHAPES.items()]
REF_TABLE += [
    ("gather_send", "dma", (144,), None),
    ("gather_recv", "dma", (144,), None),
    ("reduce_send", "dma", (144,), None),
    ("reduce_recv", "dma", (144,), None),
    ("load_sem", "dma", (4,), None),
    ("swap_send", "dma", (16,), None),
    ("swap_recv", "dma", (16,), None),
    ("ask_send", "dma", (HEADS_HERE, 2), None),
    ("reply_send", "dma", (16,), None),
    ("traffic_recv", "dma", (8,), None),
    ("pair_send", "dma", (8,), None),
    ("pair_recv", "dma", (6,), None),
    ("gain_send", "dma", (12,), None),
    ("gain_recv", "dma", (12,), None),
    ("tile_send", "dma", (COPIES, OWNERS), None),
    ("tile_recv", "dma", (OWNERS,), None),
    ("slot_recv", "dma", (2,), None),
    ("credit", "regular", (3, 2), None),
]
REF_NAMES = [row[0] for row in REF_TABLE]


def train_step(*inputs):
    scratch = []
    for name, where, shape, dtype in REF_TABLE:
        if where == "vmem":
            scratch.append(pltpu.VMEM(shape, dtype))
        elif where == "dma":
            scratch.append(pltpu.SemaphoreType.DMA(shape))
        elif where == "regular":
            scratch.append(pltpu.SemaphoreType.REGULAR(shape))
    outs = [row for row in REF_TABLE if row[1] in ("out", "hbm")]
    return pl.pallas_call(
        step_kernel,
        out_shape=[jax.ShapeDtypeStruct(shape, dtype) for _, _, shape, dtype in outs],
        in_specs=[pl.BlockSpec(memory_space=pltpu.VMEM)] * len(inputs),
        out_specs=[
            pl.BlockSpec(memory_space=pltpu.HBM if where == "hbm" else pltpu.VMEM)
            for _, where, _, _ in outs
        ],
        scratch_shapes=scratch,
        compiler_params=pltpu.CompilerParams(
            collective_id=0, has_side_effects=True, vmem_limit_bytes=63 * MIB + MIB // 2
        ),
        name="train_step",
    )(*inputs)


def pack_layers(attend_in, attend_out, expand, shrink):
    query_key = jnp.stack(
        [attend_in[:, k].reshape(LAYERS, ROW_SHARD, 3, HEAD_DIM) for k in range(2)], axis=3
    )
    return jnp.concatenate(
        [
            query_key.reshape(LAYERS, ROW_SHARD, 384),
            attend_in[:, 2],
            jnp.swapaxes(attend_out, 1, 2),
            expand[:, 0],
            expand[:, 1],
            jnp.swapaxes(shrink, 1, 2),
        ],
        axis=2,
    )


def four_squares(packed):
    query_key = packed[:, :, 0:384].reshape(LAYERS, ROW_SHARD, 3, 2, HEAD_DIM)
    return [
        query_key[:, :, :, 0].reshape(LAYERS, ROW_SHARD, 192),
        query_key[:, :, :, 1].reshape(LAYERS, ROW_SHARD, 192),
        packed[:, :, 384:576],
        packed[:, :, 576:768],
    ]


def unpack_layers(packed):
    query, key, value, out = four_squares(packed)
    return (
        jnp.stack([query, key, value], axis=1),
        jnp.swapaxes(out, 1, 2),
        jnp.stack([packed[:, :, 768:1280], packed[:, :, 1280:1792]], axis=1),
        jnp.swapaxes(packed[:, :, 1792:2304], 1, 2),
    )


def body(
    hidden_in,
    out_grad,
    seq_lengths,
    norm_gains,
    gain_first,
    gain_second,
    attend_in,
    attend_out,
    expand,
    shrink,
    attend_in_moment,
    attend_out_moment,
    expand_moment,
    shrink_moment,
):
    flat = (LAYERS * ROW_SHARD, PACK_COLS)
    rows, rows_grad, gain_total, moment_new, weights_new, _ = train_step(
        hidden_in,
        out_grad,
        seq_lengths,
        pack_layers(attend_in, attend_out, expand, shrink).reshape(flat),
        pack_layers(attend_in_moment, attend_out_moment, expand_moment, shrink_moment).reshape(flat),
        norm_gains,
    )
    split = (LAYERS, ROW_SHARD, PACK_COLS)
    gain_grad = gain_total[0:4].reshape(LAYERS, 2, D)
    gain_first_new = first_decay * gain_first + (1.0 - first_decay) * gain_grad
    gain_second_new = second_decay * gain_second + (1.0 - second_decay) * gain_grad * gain_grad
    gains_new = norm_gains - gain_rate * (gain_first_new / (1.0 - first_decay**STEP)) / (
        jnp.sqrt(gain_second_new / (1.0 - second_decay**STEP)) + adam_eps
    )
    return (
        rows[0] + rows[1],
        rows_grad[0] + rows_grad[1],
        gain_first_new,
        gain_second_new,
        gains_new,
        *unpack_layers(moment_new.reshape(split)),
        *unpack_layers(weights_new.reshape(split)),
    )


def solution(mesh):
    placed = (
        P(("fsdp", "ctx", "tp"), None),
        P(("fsdp", "ctx", "tp"), None),
        P("fsdp", None),
        P(),
        P(),
        P(),
        P(None, None, ("fsdp", "ctx"), "tp"),
        P(None, "tp", ("fsdp", "ctx")),
        P(None, None, ("fsdp", "ctx"), "tp"),
        P(None, "tp", ("fsdp", "ctx")),
        P(None, None, ("fsdp", "ctx"), "tp"),
        P(None, "tp", ("fsdp", "ctx")),
        P(None, None, ("fsdp", "ctx"), "tp"),
        P(None, "tp", ("fsdp", "ctx")),
    )
    return jax.shard_map(
        body,
        mesh=mesh,
        in_specs=placed,
        out_specs=(
            P(("fsdp", "ctx", "tp"), None),
            P(("fsdp", "ctx", "tp"), None),
            P(),
            P(),
            P(),
            P(None, None, ("fsdp", "ctx"), "tp"),
            P(None, "tp", ("fsdp", "ctx")),
            P(None, None, ("fsdp", "ctx"), "tp"),
            P(None, "tp", ("fsdp", "ctx")),
            P(None, None, ("fsdp", "ctx"), "tp"),
            P(None, "tp", ("fsdp", "ctx")),
            P(None, None, ("fsdp", "ctx"), "tp"),
            P(None, "tp", ("fsdp", "ctx")),
        ),
        check_vma=False,
    )
```

```python
import math
import types

import jax
import jax.numpy as jnp
from jax import lax
from jax.experimental import pallas as pl
from jax.experimental.pallas import tpu as pltpu
from jax.sharding import PartitionSpec as P

D = 768
HEAD_DIM = 64
FF = 2048
NS_STEPS = 4
STEP = 5


norm_eps = 1e-05
rope_base = 10000.0
mask_fill = -1e30
quintic_one = 3.4445
quintic_two = -4.775
quintic_three = 2.0315
moment_decay = 0.95
matrix_rate = 0.1
project_rate = 0.8
matrix_decay = 0.1
gain_rate = 0.8
first_decay = 0.9
second_decay = 0.95
adam_eps = 1e-08
ortho_eps = 1e-07


MESH_ID = pl.DeviceIdType.MESH
ROW_SHARD = 24
PAIR_ROWS = 2 * ROW_SHARD
PACK_COLS = 2304
LAYERS = 2
MIB = 1024 * 1024
DEVICES = 128


def whereami():
    fsdp_index = lax.axis_index("fsdp")
    return (lax.div(fsdp_index, 2), lax.rem(fsdp_index, 2), lax.axis_index("ctx"), lax.axis_index("tp"))


def device_at(y, c, z, x):
    return (y * 2 + c, z, x)


def device_of_index(index):
    return (lax.div(index, 16), lax.rem(lax.div(index, 4), 4), lax.rem(index, 4))


def index_here():
    y, c, z, x = whereami()
    return (y * 2 + c) * 16 + z * 4 + x


def sibling_here():
    y, c, z, x = whereami()
    return device_at(y, 1 - c, z, x)


def ring(index, offset):
    return lax.rem(index + offset, 4)


def remote(source, target, send_sem, recv_sem, device):
    return pltpu.make_async_remote_copy(
        src_ref=source,
        dst_ref=target,
        send_sem=send_sem,
        recv_sem=recv_sem,
        device_id=device,
        device_id_type=MESH_ID,
    )


def signal_everyone():
    barrier = pltpu.get_barrier_semaphore()
    mine = index_here()

    def signal_one(offset, carry):
        device = device_of_index(lax.rem(mine + offset, DEVICES))
        pl.semaphore_signal(barrier, inc=1, device_id=device, device_id_type=MESH_ID)
        return carry

    lax.fori_loop(1, DEVICES, signal_one, 0)


def wait_for_everyone():
    pl.semaphore_wait(pltpu.get_barrier_semaphore(), DEVICES - 1)


def neighbour(axis, offset):
    y, c, z, x = whereami()
    if axis == "y":
        return device_at(ring(y, offset), c, z, x)
    if axis == "z":
        return device_at(y, c, ring(z, offset), x)
    return device_at(y, c, z, ring(x, offset))


PART_ORDER = (("x", "y", "z"), ("y", "z", "x"), ("z", "x", "y"))


def row_place(z):
    return 2 * lax.rem(z, 2) + lax.div(z, 2)


def part_view(ref, columns, done, axis, place, half):
    y, c, z, x = whereami()
    whole = slice(None)

    def index(name, own):
        if name != axis and name in done:
            return whole
        value = place if name == axis else own
        return row_place(value) if name == "z" else value

    if axis == "x":
        pick_x = lax.rem(place, 2)
    else:
        pick_x = whole if "x" in done else lax.rem(x, 2)
    start, width = columns
    if half is not None:
        width = width // 2
        start = start + half * width
    return ref.at[pick_x, index("y", y), index("z", z), :, pl.ds(start, width)]


def ring_exists(axis, done, place):
    y, c, z, x = whereami()
    if axis == "x":
        return lax.div(place, 2) == c
    if "x" in done:
        return None
    return lax.div(x, 2) == c


def run_if(condition, action):
    if condition is None:
        action()
    else:
        pl.when(condition)(action)


class GatherLane:
    def __init__(self, ref, part, columns, send, recv, base, direct):
        self.ref, self.part, self.columns = ref, part, columns
        self.send, self.recv, self.base, self.direct = send, recv, base, direct

    def parts(self, phase):
        axis = PART_ORDER[self.part][phase]
        done = PART_ORDER[self.part][:phase]
        y, c, z, x = whereami()
        return axis, done, {"x": x, "y": y, "z": z}[axis], self.base + 4 * phase

    def copy(self, phase, slot, place, half, offset):
        axis, done, me, base = self.parts(phase)
        view = part_view(self.ref, self.columns, done, axis, place, half)
        return remote(
            view, view, self.send.at[base + slot], self.recv.at[base + slot], neighbour(axis, offset)
        )

    def first(self, phase):
        axis, done, me, base = self.parts(phase)

        def action():
            if phase in self.direct:
                for offset in (1, 2, 3):
                    self.copy(phase, offset - 1, me, None, offset).start()
            else:
                self.copy(phase, 0, me, None, 1).start()
                self.copy(phase, 1, me, None, 3).start()

        run_if(ring_exists(axis, done, me), action)

    def second(self, phase):
        axis, done, me, base = self.parts(phase)
        left, right = ring(me, 3), ring(me, 1)

        def from_left():
            self.copy(phase, 0, left, None, 1).wait_recv()
            self.copy(phase, 2, left, 0, 1).start()

        def from_right():
            self.copy(phase, 1, right, None, 1).wait_recv()
            self.copy(phase, 3, right, 1, 3).start()

        run_if(ring_exists(axis, done, left), from_left)
        run_if(ring_exists(axis, done, right), from_right)

    def third(self, phase):
        axis, done, me, base = self.parts(phase)
        far = ring(me, 2)

        def action():
            self.copy(phase, 2, far, 0, 1).wait_recv()
            self.copy(phase, 3, far, 1, 1).wait_recv()

        if phase in self.direct:
            for offset in (1, 2, 3):
                place = ring(me, 4 - offset)
                run_if(
                    ring_exists(axis, done, place),
                    lambda place=place, offset=offset: self.copy(
                        phase, offset - 1, place, None, 1
                    ).wait_recv(),
                )
        else:
            run_if(ring_exists(axis, done, far), action)

    def drain(self, phase):
        axis, done, me, base = self.parts(phase)
        left, right = ring(me, 3), ring(me, 1)

        def own():
            for slot in range(3 if phase in self.direct else 2):
                self.copy(phase, slot, me, None, 1).wait_send()

        run_if(ring_exists(axis, done, me), own)
        if phase not in self.direct:
            run_if(
                ring_exists(axis, done, left), lambda: self.copy(phase, 2, left, 0, 1).wait_send()
            )
            run_if(
                ring_exists(axis, done, right), lambda: self.copy(phase, 3, right, 1, 3).wait_send()
            )


class ReduceLane:
    def __init__(self, ref, boxes, part, columns, send, recv, base, direct, gives=None, takes=None):
        self.ref, self.boxes, self.part, self.columns = ref, boxes, part, columns
        self.send, self.recv, self.base, self.direct = send, recv, base, direct
        self.gives, self.takes = gives, takes

    def parts(self, phase):
        axis = PART_ORDER[self.part][2 - phase]
        done = PART_ORDER[self.part][: 2 - phase]
        y, c, z, x = whereami()
        return axis, done, {"x": x, "y": y, "z": z}[axis], self.base + 4 * phase

    def copy(self, phase, slot, place, half, offset):
        axis, done, me, base = self.parts(phase)
        view = part_view(self.ref, self.columns, done, axis, place, half)
        return remote(
            view,
            self.boxes[phase][slot],
            self.send.at[base + slot],
            self.recv.at[base + slot],
            neighbour(axis, offset),
        )

    def add(self, phase, place, half, boxes):
        axis, done, me, base = self.parts(phase)
        view = part_view(self.ref, self.columns, done, axis, place, half)
        lead = view.shape[:-2]

        def summed(where):
            terms = [view[where]] + [box[where] for box in boxes]
            while len(terms) > 1:
                terms = [
                    terms[i] + terms[i + 1] if i + 1 < len(terms) else terms[i]
                    for i in range(0, len(terms), 2)
                ]
            return terms[0]

        def add_one(index, carry):
            where = []
            for extent in reversed(lead):
                where.insert(0, lax.rem(index, extent))
                index = lax.div(index, extent)
            view[tuple(where)] = summed(tuple(where))
            return carry

        if len(lead) == 0:
            view[...] = summed(...)
        else:
            lax.fori_loop(0, math.prod(lead), add_one, 0)

    def first(self, phase):
        axis, done, me, base = self.parts(phase)
        far = ring(me, 2)

        def action():
            self.copy(phase, 0, far, 0, 1).start()
            self.copy(phase, 1, far, 1, 3).start()

        if phase in self.direct:
            for offset in (1, 2, 3):
                place = ring(me, offset)
                run_if(
                    ring_exists(axis, done, place),
                    lambda place=place, offset=offset: self.copy(
                        phase, offset - 1, place, None, offset
                    ).start(),
                )
        else:
            run_if(ring_exists(axis, done, far), action)

    def second(self, phase):
        axis, done, me, base = self.parts(phase)
        left, right = ring(me, 3), ring(me, 1)

        def to_right():
            self.copy(phase, 0, right, 0, 1).wait_recv()
            self.add(phase, right, 0, [self.boxes[phase][0]])
            if phase == 0 and self.takes is not None:
                pl.semaphore_wait(self.takes[0], 1)
            self.copy(phase, 2, right, None, 1).start()

        def to_left():
            self.copy(phase, 1, left, 1, 1).wait_recv()
            self.add(phase, left, 1, [self.boxes[phase][1]])
            if phase == 0 and self.takes is not None:
                pl.semaphore_wait(self.takes[1], 1)
            self.copy(phase, 3, left, None, 3).start()

        run_if(ring_exists(axis, done, right), to_right)
        run_if(ring_exists(axis, done, left), to_left)

    def third(self, phase):
        axis, done, me, base = self.parts(phase)

        def action():
            if phase in self.direct:
                slots = (0, 1, 2)
            else:
                slots = (2, 3)
            for slot in slots:
                self.copy(phase, slot, me, None, 1).wait_recv()
            self.add(phase, me, None, [self.boxes[phase][slot] for slot in slots])
            if phase == 0 and self.gives is not None:
                for sem, offset in zip(self.gives, (3, 1)):
                    pl.semaphore_signal(
                        sem, inc=1, device_id=neighbour(axis, offset), device_id_type=MESH_ID
                    )

        run_if(ring_exists(axis, done, me), action)

    def drain(self, phase):
        axis, done, me, base = self.parts(phase)
        far, left, right = ring(me, 2), ring(me, 3), ring(me, 1)

        def own():
            self.copy(phase, 0, far, 0, 1).wait_send()
            self.copy(phase, 1, far, 1, 3).wait_send()

        if phase in self.direct:
            for offset in (1, 2, 3):
                place = ring(me, offset)
                run_if(
                    ring_exists(axis, done, place),
                    lambda place=place, offset=offset: self.copy(
                        phase, offset - 1, place, None, offset
                    ).wait_send(),
                )
            return
        run_if(ring_exists(axis, done, far), own)
        run_if(ring_exists(axis, done, right), lambda: self.copy(phase, 2, right, None, 1).wait_send())
        run_if(ring_exists(axis, done, left), lambda: self.copy(phase, 3, left, None, 3).wait_send())


def box_shape(part, phase):
    order = PART_ORDER[part]
    axis, done = order[2 - phase], order[: 2 - phase]
    lead = []
    for name, extent in (("x", 2), ("y", 4), ("z", 4)):
        if name != axis and name in done:
            lead.append(extent)
    return tuple(lead)


def each(lanes, step, phase):
    for lane in lanes:
        getattr(lane, step)(phase)


HEADS_HERE = 6
TOKENS_HERE = 128
CHIP_TOKENS = 256
GROUP = 2048
Q_BLOCK = 256
K_BLOCK = 512
Q_BLOCKS = GROUP // Q_BLOCK
IN_COLS = 640
OUT_AT = 512
GATE_AT = 768
UP_AT = 1280
DOWN_AT = 1792
ASK_ROWS = 192
REPLY_ROWS = 64
SQUARE_COUNT = 8
WIDE_COUNT = 6
OWNERS = SQUARE_COUNT + WIDE_COUNT
bf16 = jnp.bfloat16
f32 = jnp.float32


def dot_nn(left, right):
    return jnp.dot(left, right, preferred_element_type=f32)


def dot_nt(left, right):
    return lax.dot_general(left, right, (((1,), (1,)), ((), ())), preferred_element_type=f32)


def dot_tn(left, right):
    return lax.dot_general(left, right, (((0,), (0,)), ((), ())), preferred_element_type=f32)


def sigmoid(value):
    return 1.0 / (1.0 + jnp.exp(-value))


def norm_scale(rows):
    return lax.rsqrt(jnp.mean(rows * rows, axis=-1, keepdims=True) + norm_eps)


def normalized(rows, gain):
    return (rows * norm_scale(rows) * gain).astype(bf16)


def rope_table(lengths):
    y, c, z, x = whereami()
    shape = (TOKENS_HERE, 128)
    place = (z * 4 + x) * TOKENS_HERE + lax.broadcasted_iota(jnp.int32, shape, 0)
    lane = lax.broadcasted_iota(jnp.int32, shape, 1)
    position = place - document_start(lengths, place)
    frequency = jnp.exp(lax.rem(lane, 32).astype(f32) * (-2.0 / HEAD_DIM * math.log(rope_base)))
    angle = position.astype(f32) * frequency
    sine = jnp.sin(angle)
    sine = jnp.where(lax.rem(lane, 64) < 32, -sine, sine)
    return jnp.concatenate([jnp.cos(angle), sine], axis=1)


def document_start(lengths, place):
    first = lengths[0:1, 0:1]
    second = first + lengths[0:1, 1:2]
    return jnp.where(place >= second, second, jnp.where(place >= first, first, 0))


def norm_back(rows, gain, grad):
    scale = norm_scale(rows)
    unit = rows * scale
    inner = grad * gain
    back = scale * (inner - unit * jnp.mean(inner * unit, axis=-1, keepdims=True))
    return back, jnp.sum(grad * unit, axis=0, keepdims=True)


def swap_halves(values):
    lower = lax.rem(lax.broadcasted_iota(jnp.int32, values.shape, 1), 64) < 32
    return jnp.where(lower, pltpu.roll(values, 96, 1), pltpu.roll(values, 32, 1))


def is_owner_here():
    y, c, z, x = whereami()
    return z < 3


def head_here():
    y, c, z, x = whereami()
    return 4 * z + x


def own_half(both):
    y, c, z, x = whereami()
    return jnp.where(c == 0, both[0:TOKENS_HERE], both[TOKENS_HERE:CHIP_TOKENS])


class Swap:
    def __init__(self, e, slot):
        self.send, self.recv = e.swap_send.at[slot], e.swap_recv.at[slot]

    def start(self, source, target):
        self.copy = remote(source, target, self.send, self.recv, sibling_here())
        self.copy.start()

    def wait(self):
        self.copy.wait_send()
        self.copy.wait_recv()


class HeadTraffic:
    def __init__(self, outbox, inbox, sems, recv_sem):
        self.outbox, self.inbox, self.sems, self.recv_sem = outbox, inbox, sems, recv_sem

    def owner_place(self, head):
        y, c, z, x = whereami()
        number = HEADS_HERE * c + head
        return lax.div(number, 4), lax.rem(number, 4)

    def owner_is_here(self, head, group):
        y, c, z, x = whereami()
        owner_z, owner_x = self.owner_place(head)
        return (owner_z == z) & (owner_x == x) & (c == group)

    def to_owner(self, head, group):
        y, c, z, x = whereami()
        owner_z, owner_x = self.owner_place(head)
        return remote(
            self.outbox.at[head, group],
            self.inbox.at[z * 4 + x],
            self.sems.at[head, group],
            self.recv_sem,
            device_at(y, group, owner_z, owner_x),
        )

    def send_to_owner(self, head, group):
        y, c, z, x = whereami()
        here = self.owner_is_here(head, group)

        @pl.when(here)
        def _():
            pltpu.make_async_copy(
                self.outbox.at[head, group], self.inbox.at[z * 4 + x], self.recv_sem
            ).start()

        @pl.when(jnp.logical_not(here))
        def _():
            self.to_owner(head, group).start()

    def drain_to_owner(self):
        for head in range(HEADS_HERE):
            for group in range(2):

                @pl.when(jnp.logical_not(self.owner_is_here(head, group)))
                def _(head=head, group=group):
                    self.to_owner(head, group).wait_send()

    def tokens_are_here(self, block):
        y, c, z, x = whereami()
        core = lax.div(head_here(), HEADS_HERE)
        return (lax.div(block, 4) == z) & (lax.rem(block, 4) == x) & (core == c)

    def to_tokens(self, block):
        y, c, z, x = whereami()
        core = lax.div(head_here(), HEADS_HERE)
        slot = head_here() - HEADS_HERE * core
        return remote(
            self.outbox.at[block],
            self.inbox.at[slot, c],
            self.sems.at[block],
            self.recv_sem,
            device_at(y, core, lax.div(block, 4), lax.rem(block, 4)),
        )

    def send_to_tokens(self, block):
        y, c, z, x = whereami()
        here = self.tokens_are_here(block)

        @pl.when(here)
        def _():
            slot = head_here() - HEADS_HERE * lax.div(head_here(), HEADS_HERE)
            pltpu.make_async_copy(
                self.outbox.at[block], self.inbox.at[slot, c], self.recv_sem
            ).start()

        @pl.when(jnp.logical_not(here))
        def _():
            self.to_tokens(block).start()

    def drain_to_tokens(self):
        def drain(block, carry):
            @pl.when(jnp.logical_not(self.tokens_are_here(block)))
            def _():
                self.to_tokens(block).wait_send()

            return carry

        lax.fori_loop(0, 16, drain, 0)

    def arrived(self):
        pltpu.make_async_copy(self.inbox, self.inbox, self.recv_sem).wait()


def row_starts(ends, query_at):
    query_row = query_at + lax.broadcasted_iota(jnp.int32, (Q_BLOCK, 128), 0)
    return document_start(ends, query_row)


def block_mask(starts, query_at, key_at):
    start = jnp.concatenate([starts] * (K_BLOCK // 128), axis=1)
    shape = (Q_BLOCK, K_BLOCK)
    query = (query_at - key_at) + lax.broadcasted_iota(jnp.int32, shape, 0)
    key = lax.broadcasted_iota(jnp.int32, shape, 1)
    return (key <= query) & (key + key_at >= start)


def run_pumps(pumps, block):
    for number, action in sorted(pumps.items()):
        pl.when(block == number)(action)


def score_rows(step, lane):
    at = (step * (K_BLOCK // 128) + lane) * Q_BLOCK
    return pl.ds(pl.multiple_of(at, Q_BLOCK), Q_BLOCK)


def attend_forward(queries, keys_values, ends, score_box, kept_output, pumps, block_done):
    def one_block(block, carry):
        run_pumps(pumps, block)
        query_at = pl.multiple_of(block * Q_BLOCK, Q_BLOCK)
        rows = pl.ds(query_at, Q_BLOCK)
        query = queries[rows, :]
        starts = row_starts(ends, query_at)
        key_blocks = lax.div(block, 2) + 1

        def scores(step, top):
            key_at = pl.multiple_of(step * K_BLOCK, K_BLOCK)
            raw = dot_nt(query, keys_values[pl.ds(key_at, K_BLOCK), :])
            masked = jnp.where(block_mask(starts, query_at, key_at), raw, mask_fill)
            for lane in range(K_BLOCK // 128):
                tile = masked[:, 128 * lane : 128 * lane + 128]
                score_box[score_rows(step, lane), :] = tile
                top = jnp.maximum(top, tile)
            return top

        top = lax.fori_loop(0, key_blocks, scores, jnp.full((Q_BLOCK, 128), mask_fill, f32))
        top = jnp.max(top, axis=1, keepdims=True)

        def collect(step, state):
            total, gathered = state
            key_at = pl.multiple_of(step * K_BLOCK, K_BLOCK)
            tiles = []
            for lane in range(K_BLOCK // 128):
                tile = jnp.exp(score_box[score_rows(step, lane), :] - top)
                total = total + tile
                tiles.append(tile.astype(bf16))
            return total, gathered + dot_nn(
                jnp.concatenate(tiles, axis=1), keys_values[pl.ds(key_at, K_BLOCK), :]
            )

        total, gathered = lax.fori_loop(
            0,
            key_blocks,
            collect,
            (jnp.zeros((Q_BLOCK, 128), f32), jnp.zeros((Q_BLOCK, 128), f32)),
        )
        total = jnp.sum(total, axis=1, keepdims=True)
        lane = lax.broadcasted_iota(jnp.int32, (Q_BLOCK, 128), 1)
        kept_output[rows, :] = jnp.where(
            lane < HEAD_DIM, top + jnp.log(total), gathered / total
        )
        block_done(block)
        return carry

    lax.fori_loop(0, Q_BLOCKS, one_block, 0)


def attend_backward(
    queries, keys_values, output_grad, kept_output, ends, query_grad, key_value_grad, pumps
):
    key_value_grad[...] = jnp.zeros_like(key_value_grad)

    def one_block(block, carry):
        run_pumps(pumps, block)
        query_at = pl.multiple_of(block * Q_BLOCK, Q_BLOCK)
        rows = pl.ds(query_at, Q_BLOCK)
        query = queries[rows, :]
        starts = row_starts(ends, query_at)
        grad = output_grad[rows, :]
        kept = kept_output[rows, :]
        logs = kept[:, 0:1]
        inner = jnp.sum(grad.astype(f32) * kept, axis=1, keepdims=True)

        def one_key(step, total):
            key_at = pl.multiple_of(step * K_BLOCK, K_BLOCK)
            keys_here = pl.ds(key_at, K_BLOCK)
            both = keys_values[keys_here, :]
            masked = jnp.where(
                block_mask(starts, query_at, key_at), dot_nt(query, both), mask_fill
            )
            probability = jnp.exp(masked - logs)
            probability_grad = dot_nt(grad, both)
            score_grad = (probability * (probability_grad - inner)).astype(bf16)
            key_value_grad[keys_here, :] += dot_tn(score_grad, query) + dot_tn(
                probability.astype(bf16), grad
            )
            return total + dot_nn(score_grad, both)

        query_grad[rows, :] = lax.fori_loop(
            0, lax.div(block, 2) + 1, one_key, jnp.zeros((Q_BLOCK, 128), f32)
        )
        return carry

    lax.fori_loop(0, Q_BLOCKS, one_block, 0)


class Weights:
    def __init__(self, e):
        self.e = e
        self.ranges = {"attend": (0, GATE_AT, 0), "units": (GATE_AT, PACK_COLS - GATE_AT, 1)}

    def copy(self, layer, name):
        start, width, slot = self.ranges[name]
        columns = pl.ds(start, width)
        return pltpu.make_async_copy(
            self.e.full.at[layer, :, :, :, :, columns],
            self.e.weights.at[:, :, :, :, columns],
            self.e.load_sem.at[slot],
        )

    def load(self, layer, name):
        self.copy(layer, name).start()

    def wait(self, layer, name):
        self.copy(layer, name).wait()

    def keep_copy(self):
        return pltpu.make_async_copy(self.e.weights, self.e.full.at[0], self.e.load_sem.at[3])

    def keep(self):
        self.keep_copy().start()

    def keep_wait(self):
        self.keep_copy().wait()

    def units(self, step, start):
        side, at = lax.div(step, 2), start + 256 * lax.rem(step, 2)
        columns = pl.ds(pl.multiple_of(at, 128), 256)
        return self.e.weights[side, :, :, :, columns].reshape(D, 256)

    def get(self, side, start, stop):
        return self.e.weights[side, :, :, :, start:stop].reshape(D, stop - start)


def nothing():
    pass


def forward_pass(e, layer, rows_ref, rows_out, pump):
    y, c, z, x = whereami()
    weights = Weights(e)
    swaps = [Swap(e, 4 * layer + slot) for slot in range(4)]
    ask = HeadTraffic(e.ask_out, e.ask_in, e.ask_send, e.traffic_recv.at[4 * layer])
    answer = HeadTraffic(e.reply_out, e.reply_in, e.reply_send, e.traffic_recv.at[4 * layer + 1])
    theirs = pl.ds(pl.multiple_of((1 - c) * TOKENS_HERE, TOKENS_HERE), TOKENS_HERE)
    swaps[0].start(e.normed.at[layer, c], e.normed.at[layer, c])
    pump("start")
    if layer == 1:
        weights.wait(layer, "attend")
    swaps[0].wait()
    chip_normed = e.normed[layer].reshape(CHIP_TOKENS, D)
    cosine = e.tables[:, :, 0:128].reshape(CHIP_TOKENS, 128)
    sine = e.tables[:, :, 128:256].reshape(CHIP_TOKENS, 128)
    for side in range(2):
        mixed = dot_nn(chip_normed, weights.get(side, 0, IN_COLS))
        for inner in range(3):
            head = 3 * side + inner
            pair = mixed[:, 128 * inner : 128 * inner + 128]
            pair = (pair * cosine + swap_halves(pair) * sine).astype(bf16)
            value = mixed[:, 384 + 64 * inner : 448 + 64 * inner]
            for group in range(2):
                at = TOKENS_HERE * group
                e.ask_out[head, group, 0:128] = pair[at : at + 128]
                e.ask_out[head, group, 128:192] = jnp.concatenate(
                    [value[at : at + 64], value[at + 64 : at + 128]], axis=1
                ).astype(bf16)
                ask.send_to_owner(head, group)
    pump("asked")
    queries, keys_values = e.queries.at[layer], e.keys_values.at[layer]
    kept_output = e.kept_output.at[layer]

    @pl.when(is_owner_here())
    def _():
        ask.arrived()

        def place(block, carry):
            at = pl.multiple_of(block * TOKENS_HERE, TOKENS_HERE)
            pair = e.ask_in[block, 0:128].astype(f32)
            zeros = jnp.zeros((TOKENS_HERE, HEAD_DIM), f32)
            queries[pl.ds(at, 128), :] = jnp.concatenate(
                [pair[:, 0:64] * (1.0 / math.sqrt(HEAD_DIM)), zeros], axis=1
            ).astype(bf16)
            both = e.ask_in[block, 128:192].astype(f32)
            value = jnp.concatenate([both[:, 0:64], both[:, 64:128]], axis=0)
            keys_values[pl.ds(at, 128), :] = jnp.concatenate(
                [pair[:, 64:128], value], axis=1
            ).astype(bf16)
            return carry

        lax.fori_loop(0, 16, place, 0)

        def send_rows(block):
            for half in range(2):
                at = pl.multiple_of(block * Q_BLOCK + half * 128, 128)
                first = kept_output[pl.ds(at, 64), :]
                second = kept_output[pl.ds(at + 64, 64), :]
                e.reply_out[2 * block + half] = jnp.concatenate(
                    [first[:, HEAD_DIM:], second[:, HEAD_DIM:]], axis=1
                ).astype(bf16)
                answer.send_to_tokens(2 * block + half)

        attend_forward(
            queries, keys_values, e.lengths, e.score_box, kept_output, pump.blocks(), send_rows
        )

    @pl.when(jnp.logical_not(is_owner_here()))
    def _():
        for number, action in sorted(pump.blocks().items()):
            action()

    pump("attended")
    answer.arrived()
    pump("answered")
    partial = None
    for side in range(2):
        columns = [jnp.zeros((CHIP_TOKENS, 64), f32)]
        for inner in range(3):
            pieces = []
            for group in range(2):
                both = e.reply_in[3 * side + inner, group].astype(f32)
                pieces += [both[:, 0:64], both[:, 64:128]]
            columns.append(jnp.concatenate(pieces, axis=0))
        e.attended[layer, side] = jnp.concatenate(columns, axis=1).astype(bf16)
        term = dot_nt(e.attended[layer, side], weights.get(side, OUT_AT, GATE_AT))
        partial = term if partial is None else partial + term
    e.partial_out[...] = partial.astype(bf16)
    swaps[1].start(e.partial_out.at[theirs], e.partial_in.at[0])
    own_part = own_half(partial)
    swaps[1].wait()
    middle = rows_ref[...].astype(f32) + (own_part + e.partial_in[0].astype(f32))
    e.mid_rows[layer] = middle
    e.normed_mid[layer, c] = (middle * norm_scale(middle) * e.gains[layer, 1:2, :]).astype(bf16)
    swaps[2].start(e.normed_mid.at[layer, c], e.normed_mid.at[layer, c])
    pump("before units")
    if layer == 1:
        weights.wait(layer, "units")
    swaps[2].wait()
    e.partial[...] = jnp.zeros_like(e.partial)

    def some_units(step, carry):
        chip_mid = e.normed_mid[layer].reshape(CHIP_TOKENS, D)
        gate = dot_nn(chip_mid, weights.units(step, GATE_AT))
        up = dot_nn(chip_mid, weights.units(step, UP_AT))
        active = (gate * sigmoid(gate) * up).astype(bf16)
        e.partial[...] += dot_nt(active, weights.units(step, DOWN_AT))
        return carry

    lax.fori_loop(0, 4, some_units, 0)
    partial = e.partial[...]
    e.partial_out[...] = partial.astype(bf16)
    swaps[3].start(e.partial_out.at[theirs], e.partial_in.at[1])
    own_part = own_half(partial)
    pump("units")
    swaps[3].wait()
    branch = own_part + e.partial_in[1].astype(f32)
    if layer == 1:
        rows_out[0] = e.mid_rows[layer]
        rows_out[1] = branch
    else:
        rows_out[...] = e.mid_rows[layer] + branch
    ask.drain_to_owner()
    pl.when(is_owner_here())(answer.drain_to_tokens)
    pump("end")


def backward_pass(e, layer, grad_ref, rows_ref, grad_out, pump, next_layer):
    y, c, z, x = whereami()
    weights = Weights(e)
    swaps = [Swap(e, 8 + 4 * layer + slot) for slot in range(4)]
    ask = HeadTraffic(e.back_ask_out, e.back_ask_in, e.ask_send, e.traffic_recv.at[4 * layer + 2])
    answer = HeadTraffic(
        e.back_reply_out, e.back_reply_in, e.reply_send, e.traffic_recv.at[4 * layer + 3]
    )
    theirs = pl.ds(pl.multiple_of((1 - c) * TOKENS_HERE, TOKENS_HERE), TOKENS_HERE)

    def transpose_rows(which, value):
        e.left_t[which] = value.T.reshape(4, D // 4, CHIP_TOKENS)

    def weight_grad(side, start, width, which, right):
        columns = pl.ds(pl.multiple_of(start, 128), width)
        for block in range(4):
            e.grads[layer, side, block, :, :, columns] = (
                dot_nn(e.left_t[which, block], right).astype(bf16).reshape(4, PAIR_ROWS, width)
            )

    e.grad_swap[0, c] = grad_ref[...].astype(bf16)
    swaps[0].start(e.grad_swap.at[0, c], e.grad_swap.at[0, c])
    pump("start")
    if next_layer is None:
        weights.wait(layer, "units")
    swaps[0].wait()
    transpose_rows(0, e.grad_swap[0].reshape(CHIP_TOKENS, D))
    transpose_rows(1, e.normed_mid[layer].reshape(CHIP_TOKENS, D))
    e.partial[...] = jnp.zeros_like(e.partial)

    def some_units(step, carry):
        down = e.grad_swap[0].reshape(CHIP_TOKENS, D)
        chip_mid = e.normed_mid[layer].reshape(CHIP_TOKENS, D)
        gate = dot_nn(chip_mid, weights.units(step, GATE_AT))
        up = dot_nn(chip_mid, weights.units(step, UP_AT))
        active_grad = dot_nn(down, weights.units(step, DOWN_AT))
        sigma = sigmoid(gate)
        active = gate * sigma
        gate_grad = (active_grad * up * sigma * (1.0 + gate * (1.0 - sigma))).astype(bf16)
        up_grad = (active_grad * active).astype(bf16)
        side, at = lax.div(step, 2), 256 * lax.rem(step, 2)
        weight_grad(side, DOWN_AT + at, 256, 0, (active * up).astype(bf16))
        weight_grad(side, GATE_AT + at, 256, 1, gate_grad)
        weight_grad(side, UP_AT + at, 256, 1, up_grad)
        e.partial[...] += dot_nt(gate_grad, weights.units(step, GATE_AT)) + dot_nt(
            up_grad, weights.units(step, UP_AT)
        )
        return carry

    lax.fori_loop(0, 4, some_units, 0)
    partial = e.partial[...]
    e.partial_out[...] = partial.astype(bf16)
    swaps[1].start(e.partial_out.at[theirs], e.partial_in.at[0])
    own_part = own_half(partial)
    if next_layer is not None:
        weights.load(next_layer, "units")
    pump("units")
    swaps[1].wait()
    back, gain_grad = norm_back(
        e.mid_rows[layer], e.gains[layer, 1:2, :], own_part + e.partial_in[0].astype(f32)
    )
    e.mid_grad[...] = grad_ref[...].astype(f32) + back
    e.gain_total[2 * layer + 1 : 2 * layer + 2, :] = gain_grad
    e.grad_swap[1, c] = e.mid_grad[...].astype(bf16)
    swaps[2].start(e.grad_swap.at[1, c], e.grad_swap.at[1, c])
    if next_layer is None:
        weights.wait(layer, "attend")
    swaps[2].wait()
    branch = e.grad_swap[1].reshape(CHIP_TOKENS, D)
    for side in range(2):
        heads_grad = dot_nn(branch, weights.get(side, OUT_AT, GATE_AT))
        for inner in range(3):
            head = 3 * side + inner
            piece = heads_grad[:, 64 + 64 * inner : 128 + 64 * inner]
            for group in range(2):
                at = TOKENS_HERE * group
                e.back_ask_out[head, group] = jnp.concatenate(
                    [piece[at : at + 64], piece[at + 64 : at + 128]], axis=1
                ).astype(bf16)
                ask.send_to_owner(head, group)
    transpose_rows(0, branch)
    for side in range(2):
        weight_grad(side, OUT_AT, GATE_AT - OUT_AT, 0, e.attended[layer, side])
    pump("asked")

    @pl.when(is_owner_here())
    def _():
        ask.arrived()

        def place(block, carry):
            at = pl.multiple_of(block * TOKENS_HERE, TOKENS_HERE)
            both = e.back_ask_in[block].astype(f32)
            grad = jnp.concatenate([both[:, 0:64], both[:, 64:128]], axis=0)
            e.output_grad[pl.ds(at, 128), :] = jnp.concatenate(
                [jnp.zeros((TOKENS_HERE, HEAD_DIM), f32), grad], axis=1
            ).astype(bf16)
            return carry

        lax.fori_loop(0, 16, place, 0)
        attend_backward(
            e.queries.at[layer],
            e.keys_values.at[layer],
            e.output_grad,
            e.kept_output.at[layer],
            e.lengths,
            e.query_grad,
            e.key_value_grad,
            pump.blocks(),
        )

        def give(block, carry):
            at = pl.multiple_of(block * TOKENS_HERE, TOKENS_HERE)
            e.back_reply_out[block, 0:128] = jnp.concatenate(
                [
                    e.query_grad[pl.ds(at, 128), 0:64] * (1.0 / math.sqrt(HEAD_DIM)),
                    e.key_value_grad[pl.ds(at, 128), 0:64],
                ],
                axis=1,
            ).astype(bf16)
            e.back_reply_out[block, 128:192] = jnp.concatenate(
                [
                    e.key_value_grad[pl.ds(at, 64), 64:128],
                    e.key_value_grad[pl.ds(at + 64, 64), 64:128],
                ],
                axis=1,
            ).astype(bf16)
            answer.send_to_tokens(block)
            return carry

        lax.fori_loop(0, 16, give, 0)

    @pl.when(jnp.logical_not(is_owner_here()))
    def _():
        for number, action in sorted(pump.blocks().items()):
            action()

    pump("attended")
    answer.arrived()
    cosine = e.tables[:, :, 0:128].reshape(CHIP_TOKENS, 128)
    sine = e.tables[:, :, 128:256].reshape(CHIP_TOKENS, 128)
    transpose_rows(1, e.normed[layer].reshape(CHIP_TOKENS, D))
    partial = None
    for side in range(2):
        pieces = []
        for inner in range(3):
            head = 3 * side + inner
            pair = jnp.concatenate(
                [e.back_reply_in[head, 0, 0:128], e.back_reply_in[head, 1, 0:128]], axis=0
            ).astype(f32)
            pair = pair * cosine - swap_halves(pair) * sine
            e.mixed_grad[side, :, 128 * inner : 128 * inner + 128] = pair.astype(bf16)
            rows = []
            for group in range(2):
                both = e.back_reply_in[head, group, 128:192].astype(f32)
                rows += [both[:, 0:64], both[:, 64:128]]
            pieces.append(jnp.concatenate(rows, axis=0))
        pieces.append(jnp.zeros((CHIP_TOKENS, 64), f32))
        e.mixed_grad[side, :, 384:IN_COLS] = jnp.concatenate(pieces, axis=1).astype(bf16)
        weight_grad(side, 0, OUT_AT, 1, e.mixed_grad[side, :, 0:OUT_AT])
        last = dot_nn(e.left_t[1].reshape(D, CHIP_TOKENS), e.mixed_grad[side, :, OUT_AT:IN_COLS])
        here = e.grads[layer, side, :, :, :, OUT_AT:IN_COLS].reshape(D, IN_COLS - OUT_AT)
        e.grads[layer, side, :, :, :, OUT_AT:IN_COLS] = (
            (here.astype(f32) + last).astype(bf16).reshape(4, 4, PAIR_ROWS, IN_COLS - OUT_AT)
        )
    pump("mixed")
    for side in range(2):
        term = dot_nt(e.mixed_grad[side], weights.get(side, 0, IN_COLS))
        partial = term if partial is None else partial + term
    e.partial_out[...] = partial.astype(bf16)
    swaps[3].start(e.partial_out.at[theirs], e.partial_in.at[1])
    own_part = own_half(partial)
    if next_layer is not None:
        weights.load(next_layer, "attend")
    pump("swapped")
    swaps[3].wait()
    back, gain_grad = norm_back(
        rows_ref[...].astype(f32), e.gains[layer, 0:1, :], own_part + e.partial_in[1].astype(f32)
    )
    e.gain_total[2 * layer : 2 * layer + 1, :] = gain_grad
    if layer == 0:
        grad_out[0] = e.mid_grad[...]
        grad_out[1] = back
    else:
        grad_out[...] = e.mid_grad[...] + back
    ask.drain_to_owner()
    pl.when(is_owner_here())(answer.drain_to_tokens)
    pump("end")


class Pump:
    def __init__(self, actions=None):
        self.actions = actions or {}

    def __call__(self, point):
        for action in self.actions.get(point, []):
            action()

    def blocks(self):
        def run(actions):
            def action():
                for one in actions:
                    one()

            return action

        return {key: run(value) for key, value in self.actions.items() if isinstance(key, int)}


COPIES = 2


def owner_place(matrix, copy):
    return (matrix // 4, 0, (matrix // 4 + matrix % 4 + 2 * copy) % 4, matrix % 4)


def square_columns(kind):
    if kind < 2:
        return [(128 * head + 64 * kind, 64) for head in range(3)]
    return [(384 + 192 * (kind - 2), 192)]


def ns_step(source, target, gram, polynomial, columns, pumps, tick):
    rows = D // 2

    def gram_rows(block, carry):
        run_pumps(pumps, tick + block)
        here = pl.ds(2 * block, 2)
        part = source[here, :, :, 0:columns].reshape(rows, columns)
        gram[here, :, :, 0:D] = (
            dot_nt(part, source[:, :, :, 0:columns].reshape(D, columns))
            .astype(bf16)
            .reshape(2, 4, PAIR_ROWS, D)
        )
        return carry

    lax.fori_loop(0, 2, gram_rows, 0)

    def polynomial_columns(block, carry):
        run_pumps(pumps, tick + 2 + block)
        here = pl.ds(pl.multiple_of(block * 256, 256), 256)
        part = gram[:, :, :, here].reshape(D, 256)
        polynomial[:, :, :, here] = (
            (
                quintic_two * part.astype(f32)
                + quintic_three * dot_nn(gram[:, :, :, 0:D].reshape(D, D), part)
            )
            .astype(bf16)
            .reshape(4, 4, PAIR_ROWS, 256)
        )
        return carry

    lax.fori_loop(0, 3, polynomial_columns, 0)

    def update_columns(block, carry):
        run_pumps(pumps, tick + 5 + block)
        here = pl.ds(pl.multiple_of(block * 256, 256), 256)
        part = source[:, :, :, here].reshape(D, 256)
        target[:, :, :, here] = (
            (
                quintic_one * part.astype(f32)
                + dot_nn(polynomial[:, :, :, 0:D].reshape(D, D), part)
            )
            .astype(bf16)
            .reshape(4, 4, PAIR_ROWS, 256)
        )
        return carry

    lax.fori_loop(0, columns // 256, update_columns, 0)


def orthogonal_owner(slots, front, back, gram, polynomial, wide, send_back, pumps):
    columns = FF if wide else D
    slot_rows = PAIR_ROWS if wide else 32

    def add_squares(index, carry):
        for slot in range(4):
            value = slots[4 * index + slot, 0:slot_rows, :].astype(f32)
            carry = carry + jnp.sum((value * value).reshape(slot_rows // 8, 8, 256), axis=0)
        return carry

    squares = lax.fori_loop(0, DEVICES // 4, add_squares, jnp.zeros((8, 256), f32))
    squares = jnp.sum(jnp.sum(squares, axis=0, keepdims=True), axis=1, keepdims=True)
    scale = 1.0 / (jnp.sqrt(squares) + ortho_eps)

    def assemble(pair, carry):
        outer, inner = lax.div(pair, 4), lax.rem(pair, 4)
        narrow = []
        for part in range(4):
            first = slots[pair * 8 + part, 0:slot_rows, :].astype(f32) * scale
            second = slots[pair * 8 + 4 + part, 0:slot_rows, :].astype(f32) * scale
            joined = jnp.concatenate([first[0:24], second[0:24]], axis=0)
            if wide:
                front[outer, inner, :, part * 512 : part * 512 + 256] = joined.astype(bf16)
                front[outer, inner, :, part * 512 + 256 : part * 512 + 512] = jnp.concatenate(
                    [first[24:48], second[24:48]], axis=0
                ).astype(bf16)
            else:
                narrow.append(joined[:, 0:192])
        if not wide:
            front[outer, inner, :, 0:D] = jnp.concatenate(narrow, axis=1).astype(bf16)
        return carry

    lax.fori_loop(0, 16, assemble, 0)
    ticks = 5 + columns // 256

    def two_steps(index, carry):
        ns_step(front, back, gram, polynomial, columns, pumps, 2 * ticks * index)
        ns_step(back, front, gram, polynomial, columns, pumps, 2 * ticks * index + ticks)
        return carry

    lax.fori_loop(0, NS_STEPS // 2, two_steps, 0)

    def take_apart(pair, carry):
        outer, inner = lax.div(pair, 4), lax.rem(pair, 4)
        if not wide:
            whole = front[outer, inner, :, 0:D].astype(f32)
        for part in range(4):
            if wide:
                left = front[outer, inner, :, part * 512 : part * 512 + 256].astype(f32)
                right = front[outer, inner, :, part * 512 + 256 : part * 512 + 512].astype(f32)
                slots[pair * 8 + part] = jnp.concatenate([left[0:24], right[0:24]], axis=0).astype(
                    bf16
                )
                slots[pair * 8 + 4 + part] = jnp.concatenate(
                    [left[24:48], right[24:48]], axis=0
                ).astype(bf16)
            else:
                left = jnp.concatenate(
                    [whole[:, 192 * part : 192 * part + 192], jnp.zeros((PAIR_ROWS, 64), f32)], axis=1
                )
                slots[pair * 8 + part, 0:32] = left[0:32].astype(bf16)
                slots[pair * 8 + 4 + part, 0:32] = jnp.concatenate(
                    [left[24:48], left[0:8]], axis=0
                ).astype(bf16)
        for part in range(8):
            send_back(pair * 8 + part)
        return carry

    lax.fori_loop(0, 16, take_apart, 0)


class Muon:
    def __init__(self, e):
        self.e = e
        self.places = [[owner_place(m, copy) for copy in range(COPIES)] for m in range(OWNERS)]

    def is_owner(self, m, copy):
        y, c, z, x = whereami()
        place = self.places[m][copy]
        return (y == place[0]) & (c == place[1]) & (z == place[2]) & (x == place[3])

    def tile(self, m):
        return self.e.square.at[m] if m < SQUARE_COUNT else self.e.wide.at[m - SQUARE_COUNT]

    def returned(self, m):
        return self.e.square_new.at[m] if m < SQUARE_COUNT else self.e.wide_new.at[m - SQUARE_COUNT]

    def slot(self, m):
        if m < SQUARE_COUNT:
            return self.e.slots.at[index_here(), pl.ds(0, 32)]
        return self.e.slots.at[index_here()]

    def outbound(self, m, copy):
        return remote(
            self.tile(m),
            self.slot(m),
            self.e.tile_send.at[copy, m],
            self.e.slot_recv.at[0],
            device_at(*self.places[m][copy]),
        )

    def update_moment(self, layer, start, stop):
        e = self.e
        rows = slice(ROW_SHARD * layer, ROW_SHARD * layer + ROW_SHARD)
        e.moment_new[rows, start:stop] = (
            moment_decay * e.moment[rows, start:stop] + e.total[rows, start:stop]
        )

    def send(self, m):
        e = self.e
        if m < SQUARE_COUNT:
            layer, kind = m // 4, m % 4
            rows = slice(ROW_SHARD * layer, ROW_SHARD * layer + ROW_SHARD)
            pieces = [e.moment_new[rows, at : at + width] for at, width in square_columns(kind)]
            tile = jnp.concatenate(pieces + [jnp.zeros((ROW_SHARD, 64), f32)], axis=1)
            e.square[m] = jnp.concatenate([tile, jnp.zeros((8, 256), f32)], axis=0).astype(bf16)
        else:
            layer, kind = (m - SQUARE_COUNT) // 3, (m - SQUARE_COUNT) % 3
            rows = slice(ROW_SHARD * layer, ROW_SHARD * layer + ROW_SHARD)
            at = GATE_AT + 512 * kind
            e.wide[m - SQUARE_COUNT] = jnp.concatenate(
                [e.moment_new[rows, at : at + 256], e.moment_new[rows, at + 256 : at + 512]], axis=0
            ).astype(bf16)

        for copy in range(COPIES):

            @pl.when(jnp.logical_not(self.is_owner(m, copy)))
            def _(copy=copy):
                self.outbound(m, copy).start()

            @pl.when(self.is_owner(m, copy))
            def _(copy=copy):
                keep = pltpu.make_async_copy(
                    self.tile(m), self.slot(m), self.e.tile_send.at[copy, m]
                )
                keep.start()
                keep.wait()

    def serve(self, is_wide, pumps):
        e = self.e
        y, c, z, x = whereami()
        slot_rows = PAIR_ROWS if is_wide else 32
        whole = e.slots.at[pl.ds(0, DEVICES - 1), pl.ds(0, slot_rows)]
        pltpu.make_async_copy(whole, whole, e.slot_recv.at[0]).wait()
        matrix = y * 4 + x
        mine = index_here()

        def send_back(index):
            if is_wide:
                source, target = e.slots.at[index], e.wide_new.at[matrix - SQUARE_COUNT]
            else:
                source, target = e.slots.at[index, pl.ds(0, 32)], e.square_new.at[matrix]

            ahead = lax.rem(lax.rem(lax.div(index, 4), 4) - z + 4, 4)

            @pl.when((index != mine) & (ahead < 2))
            def _():
                remote(
                    source, target, e.slot_recv.at[1], e.tile_recv.at[matrix], device_of_index(index)
                ).start()

            @pl.when(index == mine)
            def _():
                copy = pltpu.make_async_copy(source, target, e.tile_recv.at[matrix])
                copy.start()

        orthogonal_owner(
            e.slots,
            e.weights.at[0],
            e.weights.at[1],
            e.grads.at[1, 0],
            e.grads.at[1, 1],
            is_wide,
            send_back,
            pumps,
        )
        sent = e.slots.at[pl.ds(0, DEVICES // COPIES - 1), pl.ds(0, slot_rows)]
        pltpu.make_async_copy(sent, sent, e.slot_recv.at[1]).wait()

    def serve_all(self, last_steps):
        y, c, z, x = whereami()
        placed = (c == 0) & (lax.rem(lax.rem(z - x - y + 8, 4), 2) == 0)
        square_owner = placed & (y < 2)
        wide_owner = placed & ((y == 2) | ((y == 3) & (x < 2)))

        pl.when(wide_owner)(lambda: self.serve(True, dict(zip((0, 4), last_steps))))

        @pl.when(jnp.logical_not(wide_owner))
        def _():
            for step in last_steps:
                step()

        pl.when(square_owner)(lambda: self.serve(False, {}))

    def finish(self):
        e = self.e
        for m in range(OWNERS):
            tile = self.returned(m)
            pltpu.make_async_copy(tile, tile, e.tile_recv.at[m]).wait()
            if m < SQUARE_COUNT:
                layer, kind = m // 4, m % 4
                rate = project_rate if kind == 3 else matrix_rate
                factor = 0.2 * math.sqrt(D)
                value = e.square_new[m].astype(f32)[0:ROW_SHARD]
                places = square_columns(kind)
            else:
                layer, kind = (m - SQUARE_COUNT) // 3, (m - SQUARE_COUNT) % 3
                rate, factor = matrix_rate, 0.2 * math.sqrt(FF)
                value = e.wide_new[m - SQUARE_COUNT].astype(f32)
                value = jnp.concatenate([value[0:ROW_SHARD], value[ROW_SHARD:PAIR_ROWS]], axis=1)
                places = [(GATE_AT + 512 * kind, 512)]
            rows = slice(ROW_SHARD * layer, ROW_SHARD * layer + ROW_SHARD)
            offset = 0
            for at, width in places:
                weight = e.weights_own[rows, at : at + width]
                e.weights_new[rows, at : at + width] = weight - rate * (
                    factor * value[:, offset : offset + width] + matrix_decay * weight
                )
                offset += width

            for copy in range(COPIES):

                @pl.when(jnp.logical_not(self.is_owner(m, copy)))
                def _(m=m, copy=copy):
                    self.outbound(m, copy).wait_send()


def finish_sum(e, layer, start, stop, slot, sending):
    y, c, z, x = whereami()
    holder, odd, low = lax.div(x, 2), lax.rem(z, 2), 2 * lax.div(z, 2)
    rows = slice(ROW_SHARD * layer, ROW_SHARD * layer + ROW_SHARD)
    target = e.total.at[rows, start:stop]
    sources = [e.pair.at[rows, start:stop], e.pair_more.at[:, start:stop]]

    def copy(i):
        return remote(
            sources[i],
            target,
            e.pair_send.at[2 * slot + i],
            e.pair_recv.at[slot],
            device_at(y, odd, low + i, x),
        )

    def send():
        for i in range(2):
            here = (c == odd) & (odd == i)
            part = slice(ROW_SHARD * i, ROW_SHARD * i + ROW_SHARD)

            def half():
                whole = e.grads[layer, lax.rem(x, 2), y, row_place(z), :, start:stop]
                return whole.astype(f32)[part]

            @pl.when(here)
            def _():
                target[...] = half()

            @pl.when(jnp.logical_not(here))
            def _():
                sources[i][...] = half()
                copy(i).start()

    def sent():
        for i in range(2):
            pl.when(jnp.logical_not((c == odd) & (odd == i)))(lambda i=i: copy(i).wait_send())

    if sending:
        pl.when(c == holder)(send)
    else:
        pl.when(c == holder)(sent)
        pl.when(jnp.logical_not((c == holder) & (low + c == z)))(lambda: copy(0).wait_recv())


def gain_copies(e, hop):
    if hop == 0:
        devices = [sibling_here()]
    else:
        devices = [neighbour("xyz"[hop - 1], offset) for offset in (1, 2, 3)]
    base = 3 * hop
    return [
        remote(
            e.gain_total,
            e.gain_box.at[base + i],
            e.gain_send.at[base + i],
            e.gain_recv.at[base + i],
            device,
        )
        for i, device in enumerate(devices)
    ]


def gain_start(e, hop):
    for copy in gain_copies(e, hop):
        copy.start()


def gain_finish(e, hop):
    copies = gain_copies(e, hop)
    for copy in copies:
        copy.wait_send()
        copy.wait_recv()
    for i in range(len(copies)):
        e.gain_total[...] += e.gain_box[3 * hop + i]


BOX_SHAPES = {}
for _part in range(3):
    for _phase in range(3):
        _lead = box_shape(_part, _phase) + (PAIR_ROWS,)
        if _phase == 0:
            BOX_SHAPES[f"late_half_{_part}"] = (2,) + _lead + (256,)
            BOX_SHAPES[f"early_half_{_part}"] = (2,) + _lead + (256,)
            BOX_SHAPES[f"both_block_{_part}"] = (2,) + _lead + (512,)
            BOX_SHAPES[f"late_last_{_part}"] = (3,) + _lead + (256,)
            BOX_SHAPES[f"early_last_{_part}"] = (3,) + _lead + (256,)
        else:
            BOX_SHAPES[f"late_{_part}{_phase}"] = (3,) + _lead + (768,)
            BOX_SHAPES[f"early_{_part}{_phase}"] = (3,) + _lead + (768,)


def boxes_of(e, layer, kind, part):
    name = "late" if layer == 1 else "early"
    start, width = {"units": (0, 512), "attend": (512, 256)}[kind]
    found = []
    for phase in range(3):
        if phase == 0 and kind == "attend":
            boxes = getattr(e, f"{name}_last_{part}")
            found.append([boxes.at[i] for i in range(3)])
        elif phase == 0:
            blocks = getattr(e, f"both_block_{part}")
            halves = getattr(e, f"{name}_half_{part}")
            found.append([halves.at[0], halves.at[1], blocks.at[0], blocks.at[1]])
        else:
            cut = (slice(None),) * (len(box_shape(part, phase)) + 1) + (pl.ds(start, width),)
            boxes = getattr(e, f"{name}_{part}{phase}")
            found.append([boxes.at[(i,) + cut] for i in range(3)])
    return found


def step_kernel(*refs):
    e = types.SimpleNamespace(**dict(zip(REF_NAMES, refs)))
    e.query_grad = e.score_box.at[pl.ds(0, GROUP)]
    e.key_value_grad = e.score_box.at[pl.ds(GROUP, GROUP)]
    e.pair, e.total = e.moment_new, e.weights_new
    e.back_ask_out, e.back_reply_out, e.back_reply_in = e.reply_in, e.ask_in, e.ask_out
    y, c, z, x = whereami()
    holder = lax.div(x, 2)
    signal_everyone()
    e.own[...] = e.weights_own[...].astype(bf16)
    e.tables[c] = rope_table(e.lengths)
    e.normed[0, c] = normalized(e.rows_in[...].astype(f32), e.gains[0, 0:1, :])
    e.gain_total[...] = jnp.zeros_like(e.gain_total)
    wait_for_everyone()

    odd, low = lax.rem(z, 2), 2 * lax.div(z, 2)
    table_swap = remote(
        e.tables.at[c], e.tables.at[c], e.pair_send.at[6], e.pair_recv.at[5], sibling_here()
    )
    table_swap.start()

    def hand_over(i):
        return remote(
            e.own, e.twin.at[i], e.pair_send.at[7], e.pair_recv.at[3 + i], device_at(y, holder, low + c, x)
        )

    own_stays = (c == holder) & (low + c == z)
    for i in range(2):
        pl.when(jnp.logical_not(own_stays) & (odd == i))(lambda i=i: hand_over(i).start())

    @pl.when(c == holder)
    def _():
        for i in range(2):
            mine = (c == odd) & (odd == i)

            @pl.when(mine)
            def _(i=i):
                e.twin[i] = e.own[...]

            pl.when(jnp.logical_not(mine))(lambda i=i: hand_over(i).wait_recv())
        first, second = e.twin[0].astype(f32), e.twin[1].astype(f32)
        for layer in range(LAYERS):
            part = slice(layer * ROW_SHARD, layer * ROW_SHARD + ROW_SHARD)
            joined = jnp.concatenate([first[part], second[part]], axis=0).astype(bf16)
            if layer == 0:
                e.weights[lax.rem(x, 2), y, row_place(z)] = joined
            else:
                e.piece[...] = joined
                keep = pltpu.make_async_copy(
                    e.piece, e.full.at[1, lax.rem(x, 2), y, row_place(z)], e.load_sem.at[2]
                )
                keep.start()
                keep.wait()

    def gather_lanes(ref, at, width, base, direct):
        return [
            GatherLane(
                ref,
                part,
                (at + part * width, width),
                e.gather_send,
                e.gather_recv,
                base + 12 * part,
                direct,
            )
            for part in range(3)
        ]

    ga = gather_lanes(e.weights, 0, 256, 0, (0, 1, 2))
    gb = gather_lanes(e.weights, GATE_AT, 512, 36, (0, 1))
    gc = gather_lanes(e.full.at[1], 0, 256, 72, (0, 1))
    gd = gather_lanes(e.full.at[1], GATE_AT, 512, 108, (0, 1))
    do = lambda lanes, step, phase: lambda: each(lanes, step, phase)
    weights = Weights(e)
    each(ga, "first", 0)
    each(gb, "first", 0)
    for lanes in (ga, gb):
        each(lanes, "third", 0)
        each(lanes, "first", 1)
    for lanes in (ga, gb):
        each(lanes, "third", 1)
        each(lanes, "first", 2)
    each(gc, "first", 0)
    each(gd, "first", 0)
    table_swap.wait_send()
    remote(
        e.tables.at[c], e.tables.at[1 - c], e.pair_send.at[6], e.pair_recv.at[5], sibling_here()
    ).wait_recv()
    each(ga, "third", 2)

    def turn_to_layer_1():
        each(gc, "third", 2)
        each(gb, "drain", 2)
        weights.keep_wait()
        weights.load(1, "attend")

    def units_of_layer_1():
        each(gd, "third", 2)
        weights.load(1, "units")

    forward_pass(
        e,
        0,
        e.rows_in,
        e.rows_mid,
        Pump(
            {
                "asked": [do(gb, "second", 2)],
                3: [
                    do(gc, "third", 0),
                    do(gc, "first", 1),
                    do(gd, "third", 0),
                    do(gd, "first", 1),
                ],
                7: [do(gc, "third", 1), do(gc, "first", 2)],
                "attended": [do(lanes, "drain", phase) for phase in range(2) for lanes in (ga, gb)]
                + [do(ga, "drain", 2)],
                "answered": [do(gd, "third", 1), do(gd, "first", 2)],
                "before units": [do(gb, "third", 2), weights.keep, do(gc, "second", 2)],
                "end": [turn_to_layer_1],
            }
        ),
    )
    e.normed[1, c] = normalized(e.rows_mid[...], e.gains[1, 0:1, :])
    forward_pass(e, 1, e.rows_mid, e.rows_out, Pump({"asked": [do(gd, "second", 2)], "answered": [units_of_layer_1]}))
    def reduce_lanes(layer, kind, base):
        at, width = {"units": (GATE_AT, 512), "attend": (0, 256)}[kind]
        lanes = []
        for part in range(3):
            credits = [e.credit.at[part, side] for side in range(2)]
            lanes.append(
                ReduceLane(
                    e.grads.at[layer],
                    boxes_of(e, layer, kind, part),
                    part,
                    (at + part * width, width),
                    e.reduce_send,
                    e.reduce_recv,
                    base + 12 * part,
                    (1, 2) if kind == "units" else (0, 1, 2),
                    gives=credits if kind == "units" and layer == 1 else None,
                    takes=credits if kind == "units" and layer == 0 else None,
                )
            )
        return lanes

    lu = reduce_lanes(1, "units", 0)
    la = reduce_lanes(1, "attend", 36)
    ru = reduce_lanes(0, "units", 72)
    ra = reduce_lanes(0, "attend", 108)
    muon = Muon(e)
    backward_pass(
        e,
        1,
        e.grad_in,
        e.rows_mid,
        e.grad_mid,
        Pump(
            {
                "asked": [do(lu, "first", 0)],
                4: [do(lu, "second", 0)],
                "attended": [do(lanes, "drain", phase) for phase in range(3) for lanes in (gc, gd)],
                "mixed": [do(la, "first", 0), do(lu, "third", 0), do(lu, "first", 1)],
            }
        ),
        0,
    )

    def late_done():
        finish_sum(e, 1, 0, PACK_COLS, 0, False)
        muon.update_moment(1, 0, PACK_COLS)
        for m in (4, 5, 6, 7, 11, 12, 13):
            muon.send(m)

    def units_done():
        finish_sum(e, 0, GATE_AT, PACK_COLS, 1, False)
        muon.update_moment(0, GATE_AT, PACK_COLS)
        for m in (8, 9, 10):
            muon.send(m)

    backward_pass(
        e,
        0,
        e.grad_mid,
        e.rows_in,
        e.grad_out,
        Pump(
            {
                "units": [
                    do(ru, "first", 0),
                    do(la, "third", 0),
                    do(la, "first", 1),
                    do(lu, "third", 1),
                    do(lu, "first", 2),
                ],
                "asked": [
                    do(la, "third", 1),
                    do(la, "first", 2),
                    do(lu, "third", 2),
                    do(lu, "drain", 0),
                    do(lu, "drain", 1),
                    do(la, "drain", 0),
                ],
                2: [do(ru, "second", 0)],
                4: [do(la, "third", 2), lambda: finish_sum(e, 1, 0, PACK_COLS, 0, True)],
                6: [do(ru, "third", 0), do(ru, "first", 1)],
                "attended": [
                    do(ru, "third", 1),
                    do(ru, "first", 2),
                    late_done,
                    do(ru, "third", 2),
                    lambda: finish_sum(e, 0, GATE_AT, PACK_COLS, 1, True),
                ],
                "mixed": [do(ra, "first", 0)],
                "swapped": [units_done],
            }
        ),
        None,
    )
    gain_start(e, 0)

    def sum_step_one():
        gain_finish(e, 0)
        gain_start(e, 1)
        each(ra, "third", 0)
        each(ra, "first", 1)

    def sum_step_two():
        gain_finish(e, 1)
        gain_start(e, 2)
        each(ra, "third", 1)
        each(ra, "first", 2)

    def sum_step_three():
        each(ra, "third", 2)
        finish_sum(e, 0, 0, GATE_AT, 2, True)
        finish_sum(e, 0, 0, GATE_AT, 2, False)
        muon.update_moment(0, 0, GATE_AT)
        for m in range(4):
            muon.send(m)
        gain_finish(e, 2)
        gain_start(e, 3)

    sum_step_one()
    each(lu, "drain", 2)
    each(la, "drain", 1)
    each(la, "drain", 2)
    muon.serve_all([sum_step_two, sum_step_three])
    for lanes in (ru, ra):
        for phase in range(3):
            each(lanes, "drain", phase)
    gain_finish(e, 3)
    pl.when(jnp.logical_not(own_stays))(lambda: hand_over(0).wait_send())
    muon.finish()


REF_TABLE = [
    ("rows_in", "in", (TOKENS_HERE, D), bf16),
    ("grad_in", "in", (TOKENS_HERE, D), bf16),
    ("lengths", "in", (1, 3), jnp.int32),
    ("weights_own", "in", (LAYERS * ROW_SHARD, PACK_COLS), f32),
    ("moment", "in", (LAYERS * ROW_SHARD, PACK_COLS), f32),
    ("gains", "in", (LAYERS, 2, D), f32),
    ("rows_out", "out", (2, TOKENS_HERE, D), f32),
    ("grad_out", "out", (2, TOKENS_HERE, D), f32),
    ("gain_total", "out", (8, D), f32),
    ("moment_new", "out", (LAYERS * ROW_SHARD, PACK_COLS), f32),
    ("weights_new", "out", (LAYERS * ROW_SHARD, PACK_COLS), f32),
    ("full", "hbm", (LAYERS, 2, 4, 4, PAIR_ROWS, PACK_COLS), bf16),
    ("weights", "vmem", (2, 4, 4, PAIR_ROWS, PACK_COLS), bf16),
    ("grads", "vmem", (LAYERS, 2, 4, 4, PAIR_ROWS, PACK_COLS), bf16),
    ("own", "vmem", (LAYERS * ROW_SHARD, PACK_COLS), bf16),
    ("twin", "vmem", (2, LAYERS * ROW_SHARD, PACK_COLS), bf16),
    ("pair_more", "vmem", (ROW_SHARD, PACK_COLS), f32),

    ("piece", "vmem", (PAIR_ROWS, PACK_COLS), bf16),
    ("tables", "vmem", (2, TOKENS_HERE, 256), f32),
    ("rows_mid", "vmem", (TOKENS_HERE, D), f32),
    ("grad_mid", "vmem", (TOKENS_HERE, D), f32),
    ("mid_grad", "vmem", (TOKENS_HERE, D), f32),
    ("mid_rows", "vmem", (LAYERS, TOKENS_HERE, D), f32),
    ("normed", "vmem", (LAYERS, 2, TOKENS_HERE, D), bf16),
    ("normed_mid", "vmem", (LAYERS, 2, TOKENS_HERE, D), bf16),
    ("attended", "vmem", (LAYERS, 2, CHIP_TOKENS, 256), bf16),
    ("queries", "vmem", (LAYERS, GROUP, 128), bf16),
    ("keys_values", "vmem", (LAYERS, GROUP, 128), bf16),
    ("kept_output", "vmem", (LAYERS, GROUP, 2 * HEAD_DIM), f32),
    ("score_box", "vmem", (2 * GROUP, 128), f32),
    ("output_grad", "vmem", (GROUP, 128), bf16),
    ("partial", "vmem", (CHIP_TOKENS, D), f32),
    ("partial_out", "vmem", (CHIP_TOKENS, D), bf16),
    ("left_t", "vmem", (2, 4, D // 4, CHIP_TOKENS), bf16),
    ("partial_in", "vmem", (2, TOKENS_HERE, D), bf16),
    ("grad_swap", "vmem", (2, 2, TOKENS_HERE, D), bf16),
    ("mixed_grad", "vmem", (2, CHIP_TOKENS, IN_COLS), bf16),
    ("ask_out", "vmem", (HEADS_HERE, 2, ASK_ROWS, 128), bf16),
    ("ask_in", "vmem", (16, ASK_ROWS, 128), bf16),
    ("reply_out", "vmem", (16, REPLY_ROWS, 128), bf16),
    ("reply_in", "vmem", (HEADS_HERE, 2, REPLY_ROWS, 128), bf16),
    ("back_ask_in", "vmem", (16, REPLY_ROWS, 128), bf16),
    ("gain_box", "vmem", (12, 8, D), f32),
    ("square", "vmem", (SQUARE_COUNT, 32, 256), bf16),
    ("wide", "vmem", (WIDE_COUNT, PAIR_ROWS, 256), bf16),
    ("square_new", "vmem", (SQUARE_COUNT, 32, 256), bf16),
    ("wide_new", "vmem", (WIDE_COUNT, PAIR_ROWS, 256), bf16),
    ("slots", "vmem", (DEVICES, PAIR_ROWS, 256), bf16),
]
REF_TABLE += [(name, "vmem", shape, bf16) for name, shape in BOX_SHAPES.items()]
REF_TABLE += [
    ("gather_send", "dma", (144,), None),
    ("gather_recv", "dma", (144,), None),
    ("reduce_send", "dma", (144,), None),
    ("reduce_recv", "dma", (144,), None),
    ("load_sem", "dma", (4,), None),
    ("swap_send", "dma", (16,), None),
    ("swap_recv", "dma", (16,), None),
    ("ask_send", "dma", (HEADS_HERE, 2), None),
    ("reply_send", "dma", (16,), None),
    ("traffic_recv", "dma", (8,), None),
    ("pair_send", "dma", (8,), None),
    ("pair_recv", "dma", (6,), None),
    ("gain_send", "dma", (12,), None),
    ("gain_recv", "dma", (12,), None),
    ("tile_send", "dma", (COPIES, OWNERS), None),
    ("tile_recv", "dma", (OWNERS,), None),
    ("slot_recv", "dma", (2,), None),
    ("credit", "regular", (3, 2), None),
]
REF_NAMES = [row[0] for row in REF_TABLE]


def train_step(*inputs):
    scratch = []
    for name, where, shape, dtype in REF_TABLE:
        if where == "vmem":
            scratch.append(pltpu.VMEM(shape, dtype))
        elif where == "dma":
            scratch.append(pltpu.SemaphoreType.DMA(shape))
        elif where == "regular":
            scratch.append(pltpu.SemaphoreType.REGULAR(shape))
    outs = [row for row in REF_TABLE if row[1] in ("out", "hbm")]
    return pl.pallas_call(
        step_kernel,
        out_shape=[jax.ShapeDtypeStruct(shape, dtype) for _, _, shape, dtype in outs],
        in_specs=[pl.BlockSpec(memory_space=pltpu.VMEM)] * len(inputs),
        out_specs=[
            pl.BlockSpec(memory_space=pltpu.HBM if where == "hbm" else pltpu.VMEM)
            for _, where, _, _ in outs
        ],
        scratch_shapes=scratch,
        compiler_params=pltpu.CompilerParams(
            collective_id=0, has_side_effects=True, vmem_limit_bytes=63 * MIB + MIB // 2
        ),
        name="train_step",
    )(*inputs)


def pack_layers(attend_in, attend_out, expand, shrink):
    query_key = jnp.stack(
        [attend_in[:, k].reshape(LAYERS, ROW_SHARD, 3, HEAD_DIM) for k in range(2)], axis=3
    )
    return jnp.concatenate(
        [
            query_key.reshape(LAYERS, ROW_SHARD, 384),
            attend_in[:, 2],
            jnp.swapaxes(attend_out, 1, 2),
            expand[:, 0],
            expand[:, 1],
            jnp.swapaxes(shrink, 1, 2),
        ],
        axis=2,
    )


def four_squares(packed):
    query_key = packed[:, :, 0:384].reshape(LAYERS, ROW_SHARD, 3, 2, HEAD_DIM)
    return [
        query_key[:, :, :, 0].reshape(LAYERS, ROW_SHARD, 192),
        query_key[:, :, :, 1].reshape(LAYERS, ROW_SHARD, 192),
        packed[:, :, 384:576],
        packed[:, :, 576:768],
    ]


def unpack_layers(packed):
    query, key, value, out = four_squares(packed)
    return (
        jnp.stack([query, key, value], axis=1),
        jnp.swapaxes(out, 1, 2),
        jnp.stack([packed[:, :, 768:1280], packed[:, :, 1280:1792]], axis=1),
        jnp.swapaxes(packed[:, :, 1792:2304], 1, 2),
    )


def body(
    hidden_in,
    out_grad,
    seq_lengths,
    norm_gains,
    gain_first,
    gain_second,
    attend_in,
    attend_out,
    expand,
    shrink,
    attend_in_moment,
    attend_out_moment,
    expand_moment,
    shrink_moment,
):
    flat = (LAYERS * ROW_SHARD, PACK_COLS)
    rows, rows_grad, gain_total, moment_new, weights_new, _ = train_step(
        hidden_in,
        out_grad,
        seq_lengths,
        pack_layers(attend_in, attend_out, expand, shrink).reshape(flat),
        pack_layers(attend_in_moment, attend_out_moment, expand_moment, shrink_moment).reshape(flat),
        norm_gains,
    )
    split = (LAYERS, ROW_SHARD, PACK_COLS)
    gain_grad = gain_total[0:4].reshape(LAYERS, 2, D)
    gain_first_new = first_decay * gain_first + (1.0 - first_decay) * gain_grad
    gain_second_new = second_decay * gain_second + (1.0 - second_decay) * gain_grad * gain_grad
    gains_new = norm_gains - gain_rate * (gain_first_new / (1.0 - first_decay**STEP)) / (
        jnp.sqrt(gain_second_new / (1.0 - second_decay**STEP)) + adam_eps
    )
    return (
        rows[0] + rows[1],
        rows_grad[0] + rows_grad[1],
        gain_first_new,
        gain_second_new,
        gains_new,
        *unpack_layers(moment_new.reshape(split)),
        *unpack_layers(weights_new.reshape(split)),
    )


def solution(mesh):
    placed = (
        P(("fsdp", "ctx", "tp"), None),
        P(("fsdp", "ctx", "tp"), None),
        P("fsdp", None),
        P(),
        P(),
        P(),
        P(None, None, ("fsdp", "ctx"), "tp"),
        P(None, "tp", ("fsdp", "ctx")),
        P(None, None, ("fsdp", "ctx"), "tp"),
        P(None, "tp", ("fsdp", "ctx")),
        P(None, None, ("fsdp", "ctx"), "tp"),
        P(None, "tp", ("fsdp", "ctx")),
        P(None, None, ("fsdp", "ctx"), "tp"),
        P(None, "tp", ("fsdp", "ctx")),
    )
    return jax.shard_map(
        body,
        mesh=mesh,
        in_specs=placed,
        out_specs=(
            P(("fsdp", "ctx", "tp"), None),
            P(("fsdp", "ctx", "tp"), None),
            P(),
            P(),
            P(),
            P(None, None, ("fsdp", "ctx"), "tp"),
            P(None, "tp", ("fsdp", "ctx")),
            P(None, None, ("fsdp", "ctx"), "tp"),
            P(None, "tp", ("fsdp", "ctx")),
            P(None, None, ("fsdp", "ctx"), "tp"),
            P(None, "tp", ("fsdp", "ctx")),
            P(None, None, ("fsdp", "ctx"), "tp"),
            P(None, "tp", ("fsdp", "ctx")),
        ),
        check_vma=False,
    )
```
